32 devices in a mesh: batch: 8 (over y, x, core), seq: 4 (over z).
Axes of the slice: x: 2, y: 2, z: 4, core: 2. Of those that a mesh axis runs over, the one named last changes fastest.
Arguments:
- hidden: bfloat16 [8, 2048, 1024], P('batch', 'seq'), may hold values from -6 to 6
- token_ids: int32 [8, 2048], P('batch', 'seq'), may hold values from 3 to 31
- offsets: int32 [8], P('batch'), may hold values from 0 to 59999, as said below
- end_places: int32 [8], P('batch'), may hold values from 1 to 2048, as said below
- token_table: bfloat16 [32, 1024], replicated, may hold values from -6 to 6
- norm_gain: float32 [1024], replicated, may hold values from 0.5 to 1.5
- norm_bias: float32 [1024], replicated, may hold values from -2 to 2
- qkv_weight: bfloat16 [1024, 3072], replicated, may hold values from -0.1875 to 0.1875
- out_weight: bfloat16 [1024, 1024], replicated, may hold values from -1.5 to 1.5
- in_weight: bfloat16 [1024, 4096], replicated, may hold values from -0.1875 to 0.1875
- in_bias: float32 [4096], replicated, may hold values from -3 to 3
- down_weight: bfloat16 [4096, 1024], replicated, may hold values from -0.09375 to 0.09375
- down_bias: float32 [1024], replicated, may hold values from -3 to 3
- cotangent: bfloat16 [8, 2048, 1024], P('batch', 'seq'), may hold values from -6 to 6
Outputs:
- output: bfloat16 [8, 2048, 1024], P('batch', 'seq')
- hidden_grad: float32 [8, 2048, 1024], P('batch', 'seq')
- norm_gain_grad: float32 [1024], P('seq')
- norm_bias_grad: float32 [1024], P('seq')
- qkv_weight_grad: float32 [1024, 3072], P('seq')
- out_weight_grad: float32 [1024, 1024], P('seq')
- in_weight_grad: float32 [1024, 4096], P('seq')
- in_bias_grad: float32 [4096], P('seq')
- down_weight_grad: float32 [4096, 1024], P('seq')
- down_bias_grad: float32 [1024], P('seq')
The draws below stay inside these ranges and needn't reach their ends.
Inputs may be any that keep to these rules, and one draw needn't show every extreme that they name: `offsets`: offset 0 means that the window begins at its protein's first residue; a window begins at or before residue 59999 of its protein. `end_places`: 2048 means that the protein runs past the window's end. Of the 1 windows on each index of batch, at least one has its value at 1537 or above.
All inputs are finite; a program needn't handle non-finite values.
Results may differ from the reference program's by a relative error of at most 0.025.
Values may be sent and summed in bfloat16 or wider, within the bound.
No kernel may reach another device: no remote copies, remote signals or barrier semaphores. Data moves between devices by JAX's collectives and lax.ppermute only.
A program may use at most 320 MiB of HBM per device.

```python
import jax
import jax.numpy as jnp
from jax import lax

D = 1024
HEADS = 16
HEAD_DIM = 64
ROT = 32
FF = 4096
VOCAB = 32
LENGTH = 2048
SEQ_DEV = 512
WIN_DEV = 1
WINDOWS = 8


def draw_offsets(key, part):
    key = jax.random.fold_in(key, 11)
    begin_key, zero_key, pick_key = jax.random.split(key, 3)
    begins = jax.random.randint(begin_key, (WINDOWS,), 1, 60000)
    at_start = jax.random.randint(zero_key, (WINDOWS,), 0, 3) == 0
    picked = jax.random.permutation(pick_key, WINDOWS)
    numbers = jnp.arange(WINDOWS)
    offsets = jnp.where(at_start, 0, begins)
    offsets = jnp.where(numbers == picked[0], 59999, offsets)
    offsets = jnp.where(numbers == picked[1], 0, offsets)
    return offsets.astype(jnp.int32)


def draw_end_places(key, part):
    key = jax.random.fold_in(key, 23)
    cut_key, has_key, pick_key, last_key = jax.random.split(key, 4)
    cut_places = jax.random.randint(cut_key, (WINDOWS,), 1, LENGTH)
    has_end = jax.random.randint(has_key, (WINDOWS,), 0, 2) == 0
    places = jnp.where(has_end, cut_places, LENGTH)
    late_places = jax.random.randint(last_key, (WINDOWS,), LENGTH - SEQ_DEV + 1, LENGTH + 1)
    chosen = jax.random.randint(pick_key, (WINDOWS // WIN_DEV, 1), 0, WIN_DEV)
    spanning = (jnp.arange(WIN_DEV)[None, :] == chosen).reshape(WINDOWS)
    return jnp.where(spanning, late_places, places).astype(jnp.int32)


def touch_ends(drawn, own_key, least, high):
    place = [jax.random.randint(jax.random.fold_in(own_key, axis), (), 0, length) for axis, length in enumerate(drawn.shape)]
    longest = drawn.shape.index(max(drawn.shape))
    beside = place[:longest] + [(place[longest] + 1) % drawn.shape[longest]] + place[longest + 1:]
    return drawn.at[tuple(place)].set(least).at[tuple(beside)].set(high)


def strengthened(values, rng, source, target, parts, factor):
    def block_of(dim):
        return (jnp.arange(values.shape[dim]) // (values.shape[dim] // parts)).reshape((-1,) + (1,) * (values.ndim - 1 - dim))

    first = jax.random.permutation(rng, parts)[block_of(target)]
    far = (block_of(target) + parts // 2) % parts
    return jnp.where((block_of(source) == first) | (block_of(source) == far), factor * values, values)


def levels(stream_key, shape, cuts, low, largest):
    def one(axis_at, shards_of):
        draws = jax.random.uniform(jax.random.fold_in(jax.random.fold_in(stream_key, 6), axis_at), (shards_of,), jnp.float32, low / len(cuts), largest / len(cuts))
        return jnp.repeat(jnp.exp(draws), shape[axis_at] // shards_of).reshape((-1,) + (1,) * (len(shape) - axis_at - 1))

    factor_of = one(*cuts[0])
    for cut in cuts[1:]:
        factor_of = factor_of * one(*cut)
    return factor_of


def scatter_about(key, shape, width, bound, shards=(), kind=jnp.bfloat16):
    gain = levels(key, shape, shards, -0.22, 0.18) if shards else 1.0
    values = jax.random.normal(key, shape, jnp.float32) * width * gain
    return jnp.minimum(jnp.maximum(values, -bound), bound).astype(kind)


def heavy_noise(rng, dims, scale, most, pieces, heavy, held_as=jnp.bfloat16):
    values = scale * jax.random.normal(rng, dims, jnp.float32)
    if pieces:
        values = values * levels(rng, dims, pieces, -0.22, 0.18)
    return jnp.clip(strengthened(values, jax.random.fold_in(rng, 3), *heavy), -most, most).astype(held_as)


def setup_inputs(seed: int = 0) -> dict:
    streams_of = jax.random.split(jax.random.key(seed), 15)
    return {
        "hidden": scatter_about(streams_of[0], (WINDOWS, LENGTH, D), 1.0, 6.0, ((0, 8), (1, 4))),
        "token_ids": touch_ends(jax.random.randint(streams_of[1], (WINDOWS, LENGTH), 3, VOCAB), jax.random.fold_in(streams_of[1], 1), 3, VOCAB - 1).astype(jnp.int32),
        "offsets": draw_offsets(jax.random.fold_in(streams_of[14], 71), 0),
        "end_places": draw_end_places(jax.random.fold_in(streams_of[14], 71), 0),
        "token_table": scatter_about(streams_of[4], (VOCAB, D), 1.0, 6.0),
        "norm_gain": jnp.clip(1.0 + 0.1 * jax.random.normal(streams_of[5], (D,), jnp.float32), 0.5, 1.5),
        "norm_bias": scatter_about(streams_of[6], (D,), 0.3, 2.0, (), jnp.float32),
        "qkv_weight": scatter_about(streams_of[7], (D, 3 * D), D ** -0.5, 0.1875),
        "out_weight": scatter_about(streams_of[8], (D, D), (D // 64) ** -0.5, 1.5),
        "in_weight": scatter_about(streams_of[9], (D, FF), D ** -0.5, 0.1875),
        "in_bias": scatter_about(streams_of[10], (FF,), 0.5, 3.0, (), jnp.float32),
        "down_weight": scatter_about(streams_of[11], (FF, D), FF ** -0.5, 0.09375),
        "down_bias": scatter_about(streams_of[12], (D,), 0.5, 3.0, (), jnp.float32),
        "cotangent": heavy_noise(streams_of[13], (WINDOWS, LENGTH, D), 1.0, 6.0, ((0, 8), (1, 4)), (1, 2, 4, 2.0)),
    }


EPSILON = 1e-05
BLOCKED = -1e+30
HIGHEST = lax.Precision.HIGHEST

@jax.custom_vjp
def low(v):
    return lax.optimization_barrier(v.astype(jnp.bfloat16)).astype(jnp.float32)

@jax.custom_vjp
def low_back(v):
    return v

def low_keep(v):
    return (low(v), None)

def low_pass(kept, grad):
    return (grad,)

def back_keep(v):
    return (v, None)

def back_low(kept, grad):
    return (low(grad),)
low.defvjp(low_keep, low_pass)
low_back.defvjp(back_keep, back_low)

def product(left, right):
    return jnp.dot(left, right, precision=HIGHEST, preferred_element_type=jnp.float32)

def rotate(vectors, cosine_table, sine_table):
    even_part = vectors[..., 0:ROT:2]
    odd_part = vectors[..., 1:ROT:2]
    turned = jnp.stack([even_part * cosine_table - odd_part * sine_table, odd_part * cosine_table + even_part * sine_table], axis=-1)
    turned = turned.reshape(vectors.shape[:-1] + (ROT,))
    return jnp.concatenate([turned, vectors[..., ROT:]], axis=-1)

def angles(places):
    inverse = 10000.0 ** (-(jnp.arange(ROT // 2, dtype=jnp.float32) * 2.0) / ROT)
    phases = places.astype(jnp.float32)[:, None] * inverse[None, :]
    return (jnp.cos(phases), jnp.sin(phases))

def visible(query_places, key_places, end_places):
    query_after = query_places[None, :, None] > end_places[:, None, None]
    key_after = key_places[None, None, :] > end_places[:, None, None]
    return (key_places[None, None, :] <= query_places[None, :, None]) & (query_after == key_after)

def window_layer(params, stream, end_place):
    norm_gain, norm_bias, qkv_weight, out_weight, in_weight, in_bias, down_weight, down_bias = params
    centre = stream - lax.optimization_barrier(jnp.mean(stream, axis=-1, keepdims=True))
    spread = lax.optimization_barrier(jnp.mean(centre * centre, axis=-1, keepdims=True))
    normed = low(centre * lax.rsqrt(spread + EPSILON) * norm_gain + norm_bias)
    projected = low_back(product(normed, qkv_weight))
    places = jnp.arange(LENGTH, dtype=jnp.int32)
    cosine_table, sine_table = angles(places)
    cosine_table = cosine_table[:, None, :]
    sine_table = sine_table[:, None, :]
    divided = projected.reshape(LENGTH, 3, HEADS, HEAD_DIM)
    queries = low(rotate(divided[:, 0], cosine_table, sine_table))
    key_rows = low(rotate(divided[:, 1], cosine_table, sine_table))
    values = low(divided[:, 2])
    scores = low_back(jnp.einsum('qhd,khd->hqk', queries, key_rows, precision=HIGHEST) * 0.125)
    scores = jnp.where(visible(places, places, end_place[None]), scores, BLOCKED)
    highest = lax.optimization_barrier(jnp.max(scores, axis=-1, keepdims=True))
    raised = jnp.exp(scores - highest)
    weighting = raised / lax.optimization_barrier(jnp.sum(raised, axis=-1, keepdims=True))
    mixed_rows = jnp.einsum('hqk,khd->qhd', low(weighting), values, precision=HIGHEST).reshape(LENGTH, D)
    mixed_rows = low(low_back(mixed_rows))
    attended = product(mixed_rows, out_weight)
    pre_active = low_back(product(normed, in_weight) + in_bias)
    active = low(jax.nn.gelu(pre_active, approximate=True))
    return stream + attended + product(active, down_weight) + down_bias

def reference(hidden, token_ids, offsets, end_places, token_table, norm_gain, norm_bias, qkv_weight, out_weight, in_weight, in_bias, down_weight, down_bias, cotangent):
    places = jnp.arange(LENGTH, dtype=jnp.int32)[None, :]
    marked = jnp.where(places == end_places[:, None], 2, token_ids)
    marked = jnp.where(places == end_places[:, None] + 1, 1, marked)
    marked = jnp.where((places == 0) & (offsets[:, None] == 0), 1, marked)
    stream = hidden.astype(jnp.float32) + token_table.astype(jnp.float32)[marked]
    params = jax.tree.map(lambda array: array.astype(jnp.float32), (norm_gain, norm_bias, qkv_weight, out_weight, in_weight, in_bias, down_weight, down_bias))

    def forward(stream, params):
        layer = jax.checkpoint(window_layer)
        return lax.map(lambda window: layer(params, window[0], window[1]), (stream, end_places))
    result, pullback = jax.vjp(forward, stream, params)
    stream_grad, grads = pullback(cotangent.astype(jnp.float32))
    return (result.astype(jnp.bfloat16), stream_grad, grads[0], grads[1], grads[2], grads[3], grads[4], grads[5], grads[6], grads[7])
```

```python
import math

import jax
import jax.numpy as jnp
import numpy as np
from jax import lax
from jax.experimental import pallas as pl
from jax.experimental.pallas import tpu as pltpu
from jax.sharding import PartitionSpec as P

HEAD_DIM = 64
ROT = 32
PAIR = 2 * HEAD_DIM

EPSILON = 1e-05
BLOCKED = -1e30
LOG2E = math.log2(math.e)
BF16 = jnp.bfloat16
F32 = jnp.float32
MIB = 1 << 20


def dot_nn(left, right):
    return lax.dot_general(left, right, (((1,), (0,)), ((), ())), preferred_element_type=F32)


def dot_nt(left, right):
    return lax.dot_general(left, right, (((1,), (1,)), ((), ())), preferred_element_type=F32)


def dot_tn(left, right):
    return lax.dot_general(left, right, (((0,), (0,)), ((), ())), preferred_element_type=F32)


def swap_pairs(rows):
    width = rows.shape[1]
    lanes = lax.broadcasted_iota(jnp.int32, rows.shape, 1)
    return jnp.where(lanes % 2 == 0, pltpu.roll(rows, width - 1, 1), pltpu.roll(rows, 1, 1))


def trig_tables(length):
    inverse = 10000.0 ** (-(np.arange(ROT // 2, dtype=np.float32) * np.float32(2.0)) / np.float32(ROT))
    phases = np.arange(length, dtype=np.float32)[:, None] * inverse.astype(np.float32)[None, :]
    cosine = np.ones((length, HEAD_DIM), np.float32)
    sine = np.zeros((length, HEAD_DIM), np.float32)
    cosine[:, :ROT] = np.repeat(np.cos(phases), 2, axis=1)
    sine[:, :ROT] = np.repeat(np.sin(phases), 2, axis=1) * np.tile(np.array([-1.0, 1.0], np.float32), ROT // 2)
    return np.tile(cosine, (1, 2)), np.tile(sine, (1, 2))


def prep_kernel(hidden_ref, mark_ref, table_ref, gain_ref, bias_ref, stream_ref, normed_ref, turned_ref):
    rows = hidden_ref.shape[0]
    vocab = table_ref.shape[0]
    onehot = (mark_ref[...] == lax.broadcasted_iota(jnp.int32, (rows, vocab), 1)).astype(F32).astype(BF16)
    stream = hidden_ref[...].astype(F32) + dot_nn(onehot, table_ref[...])
    centre = stream - jnp.mean(stream, axis=-1, keepdims=True)
    spread = jnp.mean(centre * centre, axis=-1, keepdims=True)
    normed = centre * lax.rsqrt(spread + EPSILON) * gain_ref[...] + bias_ref[...]
    stream_ref[...] = stream
    normed_ref[...] = normed.astype(BF16)
    turned_ref[...] = normed.astype(BF16).T


def prepare(hidden, marked, table, gain, bias):
    rows, width = hidden.shape
    step = 128
    return pl.pallas_call(
        prep_kernel,
        grid=(rows // step,),
        in_specs=[
            pl.BlockSpec((step, width), lambda i: (i, 0)),
            pl.BlockSpec((step, 1), lambda i: (i, 0)),
            pl.BlockSpec(table.shape, lambda i: (0, 0)),
            pl.BlockSpec((1, width), lambda i: (0, 0)),
            pl.BlockSpec((1, width), lambda i: (0, 0)),
        ],
        out_specs=[
            pl.BlockSpec((step, width), lambda i: (i, 0)),
            pl.BlockSpec((step, width), lambda i: (i, 0)),
            pl.BlockSpec((width, step), lambda i: (0, i)),
        ],
        out_shape=[
            jax.ShapeDtypeStruct((rows, width), F32),
            jax.ShapeDtypeStruct((rows, width), BF16),
            jax.ShapeDtypeStruct((width, rows), BF16),
        ],
        name="prep",
    )(hidden, marked, table, gain, bias)


def heads_kernel(place_ref, normed_ref, cot_ref, wq_ref, wk_ref, wv_ref, wo_ref, cos_ref, sin_ref, *out_refs):
    normed = normed_ref[...]
    chunks = len(out_refs)
    cosine = jnp.concatenate([cos_ref[...]] * chunks, axis=1)
    sine = jnp.concatenate([sin_ref[...]] * chunks, axis=1)

    def turned(rows):
        return rows * cosine + swap_pairs(rows) * sine

    parts = (
        turned(dot_nn(normed, wq_ref[...])).astype(BF16),
        turned(dot_nn(normed, wk_ref[...])).astype(BF16),
        dot_nn(normed, wv_ref[...]).astype(BF16),
        dot_nt(cot_ref[...], wo_ref[...]).astype(BF16),
    )
    for chunk in range(chunks):
        for number, part in enumerate(parts):
            out_refs[chunk][:, number * PAIR : (number + 1) * PAIR] = part[:, chunk * PAIR : (chunk + 1) * PAIR]


def heads_of(owner, normed, cot, qkv_weight, out_weight, cosine, sine, owners):
    rows, width = normed.shape
    wide = width // owners
    chunks = wide // PAIR
    return pl.pallas_call(
        heads_kernel,
        grid_spec=pltpu.PrefetchScalarGridSpec(
            num_scalar_prefetch=1,
            grid=(1,),
            in_specs=[
                pl.BlockSpec((rows, width), lambda i, o: (0, 0)),
                pl.BlockSpec((rows, width), lambda i, o: (0, 0)),
                pl.BlockSpec((width, wide), lambda i, o: (0, o[0])),
                pl.BlockSpec((width, wide), lambda i, o: (0, owners + o[0])),
                pl.BlockSpec((width, wide), lambda i, o: (0, 2 * owners + o[0])),
                pl.BlockSpec((wide, width), lambda i, o: (o[0], 0)),
                pl.BlockSpec((rows, PAIR), lambda i, o: (0, 0)),
                pl.BlockSpec((rows, PAIR), lambda i, o: (0, 0)),
            ],
            out_specs=[pl.BlockSpec((rows, 4 * PAIR), lambda i, o: (0, 0))] * chunks,
        ),
        out_shape=[jax.ShapeDtypeStruct((rows, 4 * PAIR), BF16)] * chunks,
        name="heads",
    )(owner, normed, cot, qkv_weight, qkv_weight, qkv_weight, out_weight, cosine, sine)


QUERY_ROWS = 256
KEY_ROWS = 256


def attention_kernel(pieces, info_ref, *refs):
    piece_refs = refs[:pieces]
    cos_ref, sin_ref = refs[pieces : pieces + 2]
    out_refs = refs[pieces + 2 : 2 * pieces + 2]
    held, results, key_turned, value_turned, raised_ref, key_sum, value_sum = refs[2 * pieces + 2 :]
    me, end = info_ref[0], info_ref[1]
    rows = piece_refs[0].shape[0]
    length = rows * pieces
    for shift in range(pieces):
        start = pl.multiple_of(lax.rem(me - shift + pieces, pieces) * rows, rows)
        held[pl.ds(start, rows), :] = piece_refs[shift][...]
    key_turned[...] = held[:, PAIR : 2 * PAIR].T
    value_turned[...] = held[:, 2 * PAIR : 3 * PAIR].T
    key_sum[...] = jnp.zeros_like(key_sum)
    value_sum[...] = jnp.zeros_like(value_sum)
    scale = 0.125 * LOG2E
    halves = lax.broadcasted_iota(jnp.int32, (QUERY_ROWS, PAIR), 1) // HEAD_DIM

    def query_block(number, carry):
        first = pl.multiple_of(number * QUERY_ROWS, QUERY_ROWS)
        query_rows = held[pl.ds(first, QUERY_ROWS), 0:PAIR]
        grad_rows = held[pl.ds(first, QUERY_ROWS), 3 * PAIR : 4 * PAIR]
        zero = jnp.zeros_like(query_rows)
        queries = [jnp.where(halves == head, query_rows, zero) for head in range(2)]
        grads = [jnp.where(halves == head, grad_rows, zero) for head in range(2)]
        query_places = first + lax.broadcasted_iota(jnp.int32, (1, QUERY_ROWS), 1)
        lowest = jnp.where(query_places > end, end + 1, 0)
        blocks = (number + 1) * (QUERY_ROWS // KEY_ROWS) if QUERY_ROWS >= KEY_ROWS else lax.div(
            number * QUERY_ROWS, KEY_ROWS
        ) + 1

        def scores_of(block, highest):
            start = pl.multiple_of(block * KEY_ROWS, KEY_ROWS)
            keys = held[pl.ds(start, KEY_ROWS), PAIR : 2 * PAIR]
            key_places = start + lax.broadcasted_iota(jnp.int32, (KEY_ROWS, QUERY_ROWS), 0)
            seen = (key_places <= query_places) & (key_places >= lowest)
            after = []
            for head in range(2):
                scores = jnp.where(seen, dot_nt(keys, queries[head]) * scale, BLOCKED)
                raised_ref[head, pl.ds(start, KEY_ROWS), :] = scores
                after.append(jnp.maximum(highest[head], jnp.max(scores, axis=0, keepdims=True)))
            return tuple(after)

        start_row = jnp.full((1, QUERY_ROWS), BLOCKED, F32)
        highest = lax.fori_loop(0, blocks, scores_of, (start_row, start_row))

        def mix(block, carried):
            start = pl.multiple_of(block * KEY_ROWS, KEY_ROWS)
            after = []
            for head in range(2):
                total, mixed = carried[head]
                raised = jnp.exp2(raised_ref[head, pl.ds(start, KEY_ROWS), :] - highest[head])
                raised_ref[head, pl.ds(start, KEY_ROWS), :] = raised
                values = value_turned[head * HEAD_DIM : (head + 1) * HEAD_DIM, pl.ds(start, KEY_ROWS)]
                after.append(
                    (total + jnp.sum(raised, axis=0, keepdims=True), mixed + dot_nn(values, raised.astype(BF16)))
                )
            return tuple(after)

        empty = (jnp.zeros((1, QUERY_ROWS), F32), jnp.zeros((HEAD_DIM, QUERY_ROWS), F32))
        mixes = lax.fori_loop(0, blocks, mix, (empty, empty))
        inverse = [1.0 / mixes[head][0] for head in range(2)]
        mixed = jnp.concatenate([mixes[head][1] * inverse[head] for head in range(2)], axis=0)
        grad_turned = grad_rows.astype(F32).T
        products = mixed * grad_turned
        delta = [
            jnp.sum(products[head * HEAD_DIM : (head + 1) * HEAD_DIM], axis=0, keepdims=True) for head in range(2)
        ]

        def back(block, carried):
            start = pl.multiple_of(block * KEY_ROWS, KEY_ROWS)
            values = held[pl.ds(start, KEY_ROWS), 2 * PAIR : 3 * PAIR]
            after, key_terms, value_terms = [], [], []
            for head in range(2):
                probs = raised_ref[head, pl.ds(start, KEY_ROWS), :] * inverse[head]
                prob_grad = dot_nt(values, grads[head])
                score_grad = (probs * (prob_grad - delta[head])).astype(BF16)
                value_terms.append(dot_nn(probs.astype(BF16), grads[head]))
                key_terms.append(dot_nn(score_grad, queries[head]))
                keys = key_turned[head * HEAD_DIM : (head + 1) * HEAD_DIM, pl.ds(start, KEY_ROWS)]
                after.append(carried[head] + dot_nn(keys, score_grad))
            value_sum[pl.ds(start, KEY_ROWS), :] += value_terms[0] + value_terms[1]
            key_sum[pl.ds(start, KEY_ROWS), :] += key_terms[0] + key_terms[1]
            return tuple(after)

        query_grads = lax.fori_loop(0, blocks, back, (empty[1], empty[1]))
        query_grad = jnp.concatenate(query_grads, axis=0).T * 0.125
        cosine = cos_ref[pl.ds(first, QUERY_ROWS), :]
        sine = sin_ref[pl.ds(first, QUERY_ROWS), :]
        results[pl.ds(first, QUERY_ROWS), 0:PAIR] = (query_grad * cosine - swap_pairs(query_grad) * sine).astype(BF16)
        results[pl.ds(first, QUERY_ROWS), 3 * PAIR : 4 * PAIR] = mixed.T.astype(BF16)
        return carry

    lax.fori_loop(0, length // QUERY_ROWS, query_block, 0)
    key_grad = key_sum[...] * 0.125
    results[:, PAIR : 2 * PAIR] = (key_grad * cos_ref[...] - swap_pairs(key_grad) * sin_ref[...]).astype(BF16)
    results[:, 2 * PAIR : 3 * PAIR] = value_sum[...].astype(BF16)
    for shift in range(pieces):
        start = pl.multiple_of(lax.rem(me + shift, pieces) * rows, rows)
        out_refs[shift][...] = results[pl.ds(start, rows), :]


def attention(info, parts, cosine, sine):
    pieces = len(parts)
    rows, wide = parts[0].shape
    length = rows * pieces
    whole = pl.BlockSpec(memory_space=pltpu.VMEM)
    blocks = length // QUERY_ROWS
    pairs_of = 2 * blocks * (blocks + 1) // 2 * QUERY_ROWS * KEY_ROWS
    return pl.pallas_call(
        lambda *refs: attention_kernel(pieces, *refs),
        in_specs=[pl.BlockSpec(memory_space=pltpu.SMEM)] + [whole] * (pieces + 2),
        out_specs=[whole] * pieces,
        out_shape=[jax.ShapeDtypeStruct((rows, wide), BF16)] * pieces,
        scratch_shapes=[
            pltpu.VMEM((length, wide), BF16),
            pltpu.VMEM((length, wide), BF16),
            pltpu.VMEM((PAIR, length), BF16),
            pltpu.VMEM((PAIR, length), BF16),
            pltpu.VMEM((2, length, QUERY_ROWS), F32),
            pltpu.VMEM((length, PAIR), F32),
            pltpu.VMEM((length, PAIR), F32),
        ],
        compiler_params=pltpu.CompilerParams(vmem_limit_bytes=40 * MIB),
        cost_estimate=pl.CostEstimate(
            flops=12 * 256 * pairs_of, bytes_accessed=2 * 2 * length * wide * 2, transcendentals=pairs_of
        ),
        name="attention",
    )(info, *parts, cosine, sine)


def feed_kernel(
    cells, normed_ref, turned_ref, cot_ref, in_ref, bias_ref, down_ref, in_grad, down_grad, bias_grad, out_sum, norm_sum
):
    step = pl.program_id(0)
    up = math.sqrt(2.0 / math.pi)
    weights = in_ref[...]
    downs = down_ref[...]
    cot = cot_ref[...]
    pre = dot_nn(normed_ref[...], weights) + bias_ref[...]
    square = pre * pre
    tanh = jnp.tanh(up * pre * (1.0 + 0.044715 * square))
    half = 0.5 * (1.0 + tanh)
    active = (pre * half).astype(BF16)
    slope = half + 0.5 * pre * (1.0 - tanh * tanh) * (up * (1.0 + 3 * 0.044715 * square))
    pre_grad_full = (dot_nt(cot, downs) * slope).astype(BF16)
    in_grad[0] = dot_nn(turned_ref[...], pre_grad_full).astype(BF16)
    down_grad[0] = dot_tn(active, cot).astype(BF16)
    bias_grad[0] = jnp.sum(pre_grad_full.astype(F32), axis=0, keepdims=True)
    out_term = dot_nn(active, downs)
    norm_term = dot_nt(pre_grad_full, weights)

    @pl.when(step == 0)
    def _():
        out_sum[...] = out_term
        norm_sum[...] = norm_term

    @pl.when(step > 0)
    def _():
        out_sum[...] += out_term
        norm_sum[...] += norm_term


def feed_half(cells, normed, turned, cot, in_weight, in_bias, down_weight):
    rows, width = normed.shape
    tiles = cells.shape[0]
    hidden_units = in_weight.shape[1]
    tile = hidden_units // (2 * tiles)
    return pl.pallas_call(
        feed_kernel,
        grid_spec=pltpu.PrefetchScalarGridSpec(
            num_scalar_prefetch=1,
            grid=(tiles,),
            in_specs=[
                pl.BlockSpec((rows, width), lambda i, c: (0, 0)),
                pl.BlockSpec((width, rows), lambda i, c: (0, 0)),
                pl.BlockSpec((rows, width), lambda i, c: (0, 0)),
                pl.BlockSpec((width, tile), lambda i, c: (0, c[i])),
                pl.BlockSpec((1, tile), lambda i, c: (0, c[i])),
                pl.BlockSpec((tile, width), lambda i, c: (c[i], 0)),
            ],
            out_specs=[
                pl.BlockSpec((1, width, tile), lambda i, c: (i, 0, 0)),
                pl.BlockSpec((1, tile, width), lambda i, c: (i, 0, 0)),
                pl.BlockSpec((1, 1, tile), lambda i, c: (i, 0, 0)),
                pl.BlockSpec((rows, width), lambda i, c: (0, 0)),
                pl.BlockSpec((rows, width), lambda i, c: (0, 0)),
            ],
        ),
        out_shape=[
            jax.ShapeDtypeStruct((tiles, width, tile), BF16),
            jax.ShapeDtypeStruct((tiles, tile, width), BF16),
            jax.ShapeDtypeStruct((tiles, 1, tile), F32),
            jax.ShapeDtypeStruct((rows, width), F32),
            jax.ShapeDtypeStruct((rows, width), F32),
        ],
        compiler_params=pltpu.CompilerParams(vmem_limit_bytes=56 * MIB),
        cost_estimate=pl.CostEstimate(
            flops=12 * rows * width * hidden_units // 2,
            bytes_accessed=8 * width * hidden_units // 2,
            transcendentals=rows * hidden_units // 2,
        ),
        name="feed",
    )(cells, normed, turned, cot, in_weight, in_bias, down_weight)


def exchange(rows, axis, mask):
    size = lax.axis_size(axis)
    return lax.ppermute(rows, axis, [(place, place ^ mask) for place in range(size)])


def halves_of(rows, dim, bit):
    shape = rows.shape[:dim] + (2, rows.shape[dim] // 2) + rows.shape[dim + 1 :]
    split = rows.reshape(shape)
    return (
        lax.dynamic_index_in_dim(split, 1 - bit, dim, keepdims=False),
        lax.dynamic_index_in_dim(split, bit, dim, keepdims=False),
    )


def added(left, right):
    return (left.astype(F32) + right.astype(F32)).astype(BF16)


def joined(mine, other, dim, bit):
    low = jnp.where(bit == 0, mine, other)
    high = jnp.where(bit == 0, other, mine)
    return jnp.concatenate([low, high], axis=dim)


def bits_of(axis):
    return lax.axis_size(axis).bit_length() - 1


def reduce_over(rows, order):
    place = lax.axis_index("batch")
    for bit_number in order:
        bit = (place >> bit_number) & 1
        sent, kept = halves_of(rows, 2, bit)
        rows = added(kept, exchange(sent, "batch", 1 << bit_number))
    place = lax.axis_index("seq")
    for bit_number in range(bits_of("seq")):
        bit = (place >> bit_number) & 1
        shape = rows.shape
        split = rows.reshape((shape[0], shape[1] // 2, 2) + shape[2:])
        sent = lax.dynamic_index_in_dim(split, 1 - bit, 2, keepdims=False)
        kept = lax.dynamic_index_in_dim(split, bit, 2, keepdims=False)
        rows = added(kept, exchange(sent, "seq", 1 << bit_number))
    return rows


def gather_over(rows, order):
    place = lax.axis_index("batch")
    for bit_number in reversed(order):
        bit = (place >> bit_number) & 1
        rows = joined(rows, exchange(rows, "batch", 1 << bit_number), 2, bit)
    return rows


def sum_over_devices(sent, kept):
    rows = added(kept, exchange(sent, "batch", 1))
    order = list(range(1, bits_of("batch")))
    middle = rows.shape[2] // 2
    ends = []
    for part, bits in ((rows[:, :, :middle], order), (rows[:, :, middle:], order[::-1])):
        ends.append(gather_over(reduce_over(part, bits), bits))
    mine = jnp.concatenate(ends, axis=2)[:, 0]
    other = exchange(mine, "batch", 1)
    return joined(mine[None], other[None], 0, lax.axis_index("batch") & 1)


def fast_body(
    hidden,
    token_ids,
    offsets,
    end_places,
    token_table,
    norm_gain,
    norm_bias,
    qkv_weight,
    out_weight,
    in_weight,
    in_bias,
    down_weight,
    down_bias,
    cotangent,
):
    width = hidden.shape[2]
    rows = hidden.shape[1]
    owners = lax.axis_size("seq")
    me = lax.axis_index("seq")
    core = lax.axis_index("batch") & 1
    length = rows * owners
    chunks = width // owners // PAIR
    end = end_places[0]

    places = me * rows + jnp.arange(rows, dtype=jnp.int32)[:, None]
    marked = token_ids.reshape(rows, 1)
    marked = jnp.where(places == end, 2, marked)
    marked = jnp.where(places == end + 1, 1, marked)
    marked = jnp.where((places == 0) & (offsets[0] == 0), 1, marked)
    cot = cotangent.reshape(rows, width)
    stream, normed, turned = prepare(
        hidden.reshape(rows, width), marked, token_table, norm_gain[None], norm_bias[None]
    )
    cosine, sine = (jnp.asarray(table) for table in trig_tables(length))
    own_cosine = lax.dynamic_slice_in_dim(cosine, me * rows, rows)
    own_sine = lax.dynamic_slice_in_dim(sine, me * rows, rows)

    parts = [[None] * owners for _ in range(chunks)]
    for shift in list(range(1, owners)) + [0]:
        owner = lax.rem(me + shift, owners)
        blocks = heads_of(owner[None], normed, cot, qkv_weight, out_weight, own_cosine, own_sine, owners)
        for chunk in range(chunks):
            parts[chunk][shift] = blocks[chunk]

    def shifted(block, shift):
        if shift == 0:
            return block
        return lax.ppermute(block, "seq", [(place, (place + shift) % owners) for place in range(owners)])

    heads = [[shifted(parts[chunk][shift], shift) for shift in range(owners)] for chunk in range(chunks)]

    cells = 2 * jnp.arange(owners, dtype=jnp.int32)
    feed = [
        feed_half(cells + half, normed, turned, cot, in_weight, in_bias[None], down_weight)
        for half in (1 - core, core)
    ]
    tile = in_weight.shape[1] // (2 * owners)

    def in_view(grad):
        return grad.reshape(owners, owners, width // owners, tile)

    def down_view(grad):
        return grad.reshape(1, owners, tile, width)

    in_sum = sum_over_devices(in_view(feed[0][0]), in_view(feed[1][0]))
    down_sum = sum_over_devices(down_view(feed[0][1]), down_view(feed[1][1]))
    in_weight_grad = jnp.transpose(in_sum, (2, 1, 0, 3)).reshape(width // owners, in_weight.shape[1]).astype(F32)
    down_weight_grad = down_sum.reshape(2 * tile, width).astype(F32)
    bias_low = jnp.where(core == 0, feed[1][2], feed[0][2])
    bias_high = jnp.where(core == 0, feed[0][2], feed[1][2])
    in_bias_grad = jnp.concatenate([bias_low, bias_high], axis=1).reshape(-1)

    info = jnp.stack([me, end]).astype(jnp.int32)
    back = []
    for chunk in range(chunks):
        results = attention(info, heads[chunk], cosine, sine)
        back.append([shifted(results[shift], shift) for shift in range(owners)])

    ordered = []
    for owner in range(owners):
        ordered.append([])
        for chunk in range(chunks):
            stacked = jnp.stack(back[chunk])
            slot = lax.rem(me - owner + owners, owners)
            ordered[owner].append(lax.dynamic_index_in_dim(stacked, slot, 0, keepdims=False))

    def columns(part):
        return [
            block[:, part * PAIR : (part + 1) * PAIR] for blocks in ordered for block in blocks
        ]

    joined_grad = jnp.concatenate(columns(0) + columns(1) + columns(2), axis=1)
    mixed = jnp.concatenate(columns(3), axis=1)

    qkv_weight_grad = dot_nn(turned, joined_grad).astype(BF16)
    out_weight_grad = dot_tn(mixed, cot).astype(BF16)
    normed_grad = dot_nt(joined_grad, qkv_weight) + feed[0][4] + feed[1][4]

    def core_halves(grad):
        split = grad.reshape(1, owners, 2, grad.shape[0] // (2 * owners), grad.shape[1])
        return (
            lax.dynamic_index_in_dim(split, 1 - core, 2, keepdims=False),
            lax.dynamic_index_in_dim(split, core, 2, keepdims=False),
        )

    qkv_sum = sum_over_devices(*core_halves(qkv_weight_grad))
    out_sum = sum_over_devices(*core_halves(out_weight_grad))
    qkv_weight_grad = qkv_sum.reshape(width // owners, -1).astype(F32)
    out_weight_grad = out_sum.reshape(width // owners, -1).astype(F32)

    output = stream + dot_nn(mixed, out_weight) + feed[0][3] + feed[1][3] + down_bias[None]
    centre = stream - jnp.mean(stream, axis=-1, keepdims=True)
    spread = jnp.mean(centre * centre, axis=-1, keepdims=True)
    inverse = lax.rsqrt(spread + EPSILON)
    hat = centre * inverse
    gained = normed_grad * norm_gain[None]
    stream_part = inverse * (
        gained
        - jnp.mean(gained, axis=-1, keepdims=True)
        - hat * jnp.mean(gained * hat, axis=-1, keepdims=True)
    )
    hidden_grad = cot.astype(F32) + stream_part
    small = jnp.concatenate(
        [
            in_bias_grad.reshape(owners, -1),
            jnp.sum(cot.astype(F32), axis=0).reshape(owners, -1),
            jnp.sum(normed_grad * hat, axis=0).reshape(owners, -1),
            jnp.sum(normed_grad, axis=0).reshape(owners, -1),
        ],
        axis=1,
    )
    small = lax.dynamic_index_in_dim(lax.psum(small, ("batch", "seq")), me, 0, keepdims=False)
    few = width // owners
    many = in_bias.shape[0] // owners
    return (
        output.astype(BF16)[None],
        hidden_grad[None],
        small[many + few : many + 2 * few],
        small[many + 2 * few :],
        qkv_weight_grad,
        out_weight_grad,
        in_weight_grad,
        small[:many],
        down_weight_grad,
        small[many : many + few],
    )


def rotate(vectors, cosine_table, sine_table):
    even_part = vectors[..., 0:ROT:2]
    odd_part = vectors[..., 1:ROT:2]
    turned = jnp.stack(
        [
            even_part * cosine_table - odd_part * sine_table,
            odd_part * cosine_table + even_part * sine_table,
        ],
        axis=-1,
    )
    turned = turned.reshape(vectors.shape[:-1] + (ROT,))
    return jnp.concatenate([turned, vectors[..., ROT:]], axis=-1)


def angles(places):
    inverse = 10000.0 ** (-(jnp.arange(ROT // 2, dtype=jnp.float32) * 2.0) / ROT)
    phases = places.astype(jnp.float32)[:, None] * inverse[None, :]
    return (jnp.cos(phases), jnp.sin(phases))


def visible(query_places, key_places, end_places):
    query_after = query_places[None, :, None] > end_places[:, None, None]
    key_after = key_places[None, None, :] > end_places[:, None, None]
    return (key_places[None, None, :] <= query_places[None, :, None]) & (query_after == key_after)


def norm_rows(stream, gain_row, bias_row):
    centre = stream - jnp.mean(stream, axis=-1, keepdims=True)
    spread = jnp.mean(centre * centre, axis=-1, keepdims=True)
    return centre * lax.rsqrt(spread + EPSILON) * gain_row + bias_row


def gelu_rows(pre_active):
    return jax.nn.gelu(pre_active, approximate=True)


def plain_body(
    hidden,
    token_ids,
    offsets,
    end_places,
    token_table,
    norm_gain,
    norm_bias,
    qkv_weight,
    out_weight,
    in_weight,
    in_bias,
    down_weight,
    down_bias,
    cotangent,
):
    windows_here, shard_rows, model_width = hidden.shape
    head_count = model_width // HEAD_DIM
    seq_count = lax.axis_size("seq")
    seq_place = lax.axis_index("seq")
    home_places = seq_place * shard_rows + jnp.arange(shard_rows, dtype=jnp.int32)
    token_rows = shard_rows * windows_here
    marked = token_ids.T
    marked = jnp.where(home_places[:, None] == end_places[None, :], 2, marked)
    marked = jnp.where(home_places[:, None] == end_places[None, :] + 1, 1, marked)
    marked = jnp.where((home_places[:, None] == 0) & (offsets[None, :] == 0), 1, marked)
    onehot = (marked[..., None] == jnp.arange(token_table.shape[0], dtype=jnp.int32)).astype(
        jnp.bfloat16
    )
    embedded = jnp.einsum("swv,vd->swd", onehot, token_table, preferred_element_type=jnp.float32)
    stream_three = jnp.transpose(hidden, (1, 0, 2)).astype(jnp.float32) + embedded
    cot_three = jnp.transpose(cotangent, (1, 0, 2))
    own_high = jnp.max(home_places)
    stream_rows = stream_three.reshape(token_rows, model_width)
    normed, norm_back = jax.vjp(norm_rows, stream_rows, norm_gain, norm_bias)
    normed_low = normed.astype(jnp.bfloat16)
    projected = jnp.dot(normed_low, qkv_weight, preferred_element_type=jnp.float32)
    cosine_table, sine_table = angles(home_places)
    cosine_table = cosine_table[:, None, None, :]
    sine_table = sine_table[:, None, None, :]

    def turn_heads(projected_rows):
        divided = projected_rows.reshape(shard_rows, windows_here, 3, head_count, HEAD_DIM)
        return (
            rotate(divided[:, :, 0], cosine_table, sine_table),
            rotate(divided[:, :, 1], cosine_table, sine_table),
            divided[:, :, 2],
        )

    (queries, key_rows, values), turn_back = jax.vjp(turn_heads, projected)
    query_low = queries.astype(jnp.bfloat16)
    key_value = jnp.concatenate(
        [
            key_rows.reshape(shard_rows, windows_here, model_width),
            values.reshape(shard_rows, windows_here, model_width),
        ],
        axis=-1,
    ).astype(jnp.bfloat16)

    def split_block(key_block):
        row_count = key_block.shape[0]
        return (
            key_block[..., :model_width].reshape(row_count, windows_here, head_count, HEAD_DIM),
            key_block[..., model_width:].reshape(row_count, windows_here, head_count, HEAD_DIM),
        )

    def block_places(row_start, row_count):
        return row_start + jnp.arange(row_count, dtype=jnp.int32)

    def block_scores(key_block, key_start):
        key_part, value_part = split_block(key_block)
        key_places = block_places(key_start, key_block.shape[0])
        scores = (
            jnp.einsum("qwhd,kwhd->whqk", query_low, key_part, preferred_element_type=jnp.float32)
            * 0.125
        )
        scores = jnp.where(visible(home_places, key_places, end_places)[:, None], scores, BLOCKED)
        return (scores, key_part, value_part)

    def attend(carried, key_block, key_start):
        running, totals, accumulated = carried
        scores, key_part, value_part = block_scores(key_block, key_start)
        highest = jnp.maximum(running, jnp.max(scores, axis=-1))
        factor = jnp.exp(running - highest)
        raised = jnp.exp(scores - highest[..., None])
        totals = totals * factor + jnp.sum(raised, axis=-1)
        accumulated = accumulated * factor[..., None] + jnp.einsum(
            "whqk,kwhd->whqd",
            raised.astype(jnp.bfloat16),
            value_part,
            preferred_element_type=jnp.float32,
        )
        return (highest, totals, accumulated)

    start_state = (
        jnp.full((windows_here, head_count, shard_rows), BLOCKED, jnp.float32),
        jnp.zeros((windows_here, head_count, shard_rows), jnp.float32),
        jnp.zeros((windows_here, head_count, shard_rows, HEAD_DIM), jnp.float32),
    )
    carried = start_state
    fetched_rows = lax.all_gather(key_value, "seq", axis=0, tiled=True)
    row_count = fetched_rows.shape[0]
    blocks = fetched_rows.reshape((row_count // shard_rows, shard_rows) + fetched_rows.shape[1:])

    def visit_block(held_state, element):
        number, key_block = element
        key_start = number * shard_rows
        dead = jnp.min(block_places(key_start, shard_rows)) > own_high
        held_state = lax.cond(
            dead,
            lambda kept_state: kept_state,
            lambda kept_state: attend(kept_state, key_block, key_start),
            held_state,
        )
        return (held_state, None)

    carried, unused = lax.scan(
        visit_block, carried, (jnp.arange(blocks.shape[0], dtype=jnp.int32), blocks)
    )
    running, totals, accumulated = carried
    attention = accumulated / totals[..., None]
    log_total = running + jnp.log(totals)
    attention_rows = jnp.transpose(attention, (2, 0, 1, 3))
    mixed_low = attention_rows.reshape(token_rows, model_width).astype(jnp.bfloat16)
    attended = jnp.dot(mixed_low, out_weight, preferred_element_type=jnp.float32)
    pre_active = jnp.dot(normed_low, in_weight, preferred_element_type=jnp.float32) + in_bias
    active, gelu_back = jax.vjp(gelu_rows, pre_active)
    active_low = active.astype(jnp.bfloat16)
    result = (
        stream_rows
        + attended
        + jnp.dot(active_low, down_weight, preferred_element_type=jnp.float32)
        + down_bias
    )
    grad_rows = cot_three.reshape(token_rows, model_width)
    down_weight_grad = jnp.dot(active_low.T, grad_rows, preferred_element_type=jnp.float32)
    down_bias_grad = jnp.sum(grad_rows.astype(jnp.float32), axis=0)
    out_weight_grad = jnp.dot(mixed_low.T, grad_rows, preferred_element_type=jnp.float32)
    active_grad = jnp.dot(grad_rows, down_weight.T, preferred_element_type=jnp.float32)
    pre_grad = gelu_back(active_grad)[0].astype(jnp.bfloat16)
    in_weight_grad = jnp.dot(normed_low.T, pre_grad, preferred_element_type=jnp.float32)
    in_bias_grad = jnp.sum(pre_grad.astype(jnp.float32), axis=0)
    mixed_grad = jnp.dot(grad_rows, out_weight.T, preferred_element_type=jnp.float32).astype(
        jnp.bfloat16
    )
    grad_heads = mixed_grad.reshape(shard_rows, windows_here, head_count, HEAD_DIM)
    delta_rows = jnp.sum(grad_heads.astype(jnp.float32) * attention_rows, axis=-1)
    row_delta = jnp.transpose(delta_rows, (1, 2, 0))
    whole_keys = lax.all_gather(key_value, "seq", axis=0, tiled=True)
    blocks = whole_keys.reshape((seq_count, shard_rows) + whole_keys.shape[1:])
    zero_heads = jnp.zeros((shard_rows, windows_here, head_count, HEAD_DIM), jnp.float32)

    def back_block(query_grad, element):
        number, key_block = element
        key_start = number * shard_rows

        def live_block(held_grad):
            scores, key_part, value_part = block_scores(key_block, key_start)
            weighting = jnp.exp(scores - log_total[..., None])
            prob_grad = jnp.einsum(
                "qwhd,kwhd->whqk", grad_heads, value_part, preferred_element_type=jnp.float32
            )
            score_low = (weighting * (prob_grad - row_delta[..., None])).astype(jnp.bfloat16)
            held_grad = held_grad + 0.125 * jnp.einsum(
                "whqk,kwhd->qwhd", score_low, key_part, preferred_element_type=jnp.float32
            )
            key_grad = 0.125 * jnp.einsum(
                "whqk,qwhd->kwhd", score_low, query_low, preferred_element_type=jnp.float32
            )
            value_grad = jnp.einsum(
                "whqk,qwhd->kwhd",
                weighting.astype(jnp.bfloat16),
                grad_heads,
                preferred_element_type=jnp.float32,
            )
            return (
                held_grad,
                jnp.concatenate(
                    [
                        key_grad.reshape(shard_rows, windows_here, model_width),
                        value_grad.reshape(shard_rows, windows_here, model_width),
                    ],
                    axis=-1,
                ),
            )

        def dead_block(held_grad):
            return (held_grad, jnp.zeros((shard_rows, windows_here, 2 * model_width), jnp.float32))

        dead = jnp.min(block_places(key_start, shard_rows)) > own_high
        return lax.cond(dead, dead_block, live_block, query_grad)

    query_grad, key_terms = lax.scan(
        back_block, zero_heads, (jnp.arange(seq_count, dtype=jnp.int32), blocks)
    )
    key_terms = key_terms.reshape((seq_count * shard_rows,) + key_terms.shape[2:])
    summed = lax.psum_scatter(
        key_terms.astype(jnp.bfloat16), "seq", scatter_dimension=0, tiled=True
    ).astype(jnp.float32)
    key_grad = summed[..., :model_width].reshape(shard_rows, windows_here, head_count, HEAD_DIM)
    value_grad = summed[..., model_width:].reshape(shard_rows, windows_here, head_count, HEAD_DIM)
    joined_grad = turn_back((query_grad, key_grad, value_grad))[0].astype(jnp.bfloat16)
    qkv_weight_grad = jnp.dot(normed_low.T, joined_grad, preferred_element_type=jnp.float32)
    normed_grad = jnp.dot(joined_grad, qkv_weight.T, preferred_element_type=jnp.float32) + jnp.dot(
        pre_grad, in_weight.T, preferred_element_type=jnp.float32
    )
    stream_part, norm_gain_grad, norm_bias_grad = norm_back(normed_grad)
    stream_grad = grad_rows.astype(jnp.float32) + stream_part
    result_three = result.reshape(shard_rows, windows_here, model_width)
    grad_three = stream_grad.reshape(shard_rows, windows_here, model_width)
    output = jnp.transpose(result_three, (1, 0, 2)).astype(jnp.bfloat16)
    hidden_grad = jnp.transpose(grad_three, (1, 0, 2))
    shares = (
        lax.psum_scatter(
            norm_gain_grad.astype(jnp.bfloat16), "seq", scatter_dimension=0, tiled=True
        ).astype(jnp.float32),
        lax.psum_scatter(
            norm_bias_grad.astype(jnp.bfloat16), "seq", scatter_dimension=0, tiled=True
        ).astype(jnp.float32),
        lax.psum_scatter(
            qkv_weight_grad.astype(jnp.bfloat16), "seq", scatter_dimension=0, tiled=True
        ).astype(jnp.float32),
        lax.psum_scatter(
            out_weight_grad.astype(jnp.bfloat16), "seq", scatter_dimension=0, tiled=True
        ).astype(jnp.float32),
        lax.psum_scatter(
            in_weight_grad.astype(jnp.bfloat16), "seq", scatter_dimension=0, tiled=True
        ).astype(jnp.float32),
        lax.psum_scatter(
            in_bias_grad.astype(jnp.bfloat16), "seq", scatter_dimension=0, tiled=True
        ).astype(jnp.float32),
        lax.psum_scatter(
            down_weight_grad.astype(jnp.bfloat16), "seq", scatter_dimension=0, tiled=True
        ).astype(jnp.float32),
        lax.psum_scatter(
            down_bias_grad.astype(jnp.bfloat16), "seq", scatter_dimension=0, tiled=True
        ).astype(jnp.float32),
    )
    totals_all = (
        lax.psum(shares[0].astype(jnp.bfloat16), "batch").astype(jnp.float32),
        lax.psum(shares[1].astype(jnp.bfloat16), "batch").astype(jnp.float32),
        lax.psum(shares[2].astype(jnp.bfloat16), "batch").astype(jnp.float32),
        lax.psum(shares[3].astype(jnp.bfloat16), "batch").astype(jnp.float32),
        lax.psum(shares[4].astype(jnp.bfloat16), "batch").astype(jnp.float32),
        lax.psum(shares[5].astype(jnp.bfloat16), "batch").astype(jnp.float32),
        lax.psum(shares[6].astype(jnp.bfloat16), "batch").astype(jnp.float32),
        lax.psum(shares[7].astype(jnp.bfloat16), "batch").astype(jnp.float32),
    )
    return (
        output,
        hidden_grad,
        totals_all[0],
        totals_all[1],
        totals_all[2],
        totals_all[3],
        totals_all[4],
        totals_all[5],
        totals_all[6],
        totals_all[7],
    )


def solution(mesh):
    placed = (
        P("batch", "seq", None),
        P("batch", "seq"),
        P("batch"),
        P("batch"),
        P(),
        P(),
        P(),
        P(),
        P(),
        P(),
        P(),
        P(),
        P(),
        P("batch", "seq", None),
    )

    def body(*arrays):
        hidden = arrays[0]
        owners = mesh.shape["seq"]
        wide = hidden.shape[2] // owners
        if hidden.shape[0] == 1 and wide % PAIR == 0:
            return fast_body(*arrays)
        return plain_body(*arrays)

    return jax.shard_map(
        body,
        mesh=mesh,
        in_specs=placed,
        out_specs=(
            P("batch", "seq", None),
            P("batch", "seq", None),
            P("seq"),
            P("seq"),
            P("seq", None),
            P("seq", None),
            P("seq", None),
            P("seq"),
            P("seq", None),
            P("seq"),
        ),
        check_vma=False,
    )
```

```python
import math

import jax
import jax.numpy as jnp
import numpy as np
from jax import lax
from jax.experimental import pallas as pl
from jax.experimental.pallas import tpu as pltpu
from jax.sharding import PartitionSpec as P

HEAD_DIM = 64
ROT = 32
PAIR = 2 * HEAD_DIM

EPSILON = 1e-05
BLOCKED = -1e30
LOG2E = math.log2(math.e)
BF16 = jnp.bfloat16
F32 = jnp.float32
MIB = 1 << 20


def dot_nn(left, right):
    return lax.dot_general(left, right, (((1,), (0,)), ((), ())), preferred_element_type=F32)


def dot_nt(left, right):
    return lax.dot_general(left, right, (((1,), (1,)), ((), ())), preferred_element_type=F32)


def dot_tn(left, right):
    return lax.dot_general(left, right, (((0,), (0,)), ((), ())), preferred_element_type=F32)


def swap_pairs(rows):
    width = rows.shape[1]
    lanes = lax.broadcasted_iota(jnp.int32, rows.shape, 1)
    return jnp.where(lanes % 2 == 0, pltpu.roll(rows, width - 1, 1), pltpu.roll(rows, 1, 1))


def trig_tables(length):
    inverse = 10000.0 ** (-(np.arange(ROT // 2, dtype=np.float32) * np.float32(2.0)) / np.float32(ROT))
    phases = np.arange(length, dtype=np.float32)[:, None] * inverse.astype(np.float32)[None, :]
    cosine = np.ones((length, HEAD_DIM), np.float32)
    sine = np.zeros((length, HEAD_DIM), np.float32)
    cosine[:, :ROT] = np.repeat(np.cos(phases), 2, axis=1)
    sine[:, :ROT] = np.repeat(np.sin(phases), 2, axis=1) * np.tile(np.array([-1.0, 1.0], np.float32), ROT // 2)
    return np.tile(cosine, (1, 2)), np.tile(sine, (1, 2))


def prep_kernel(hidden_ref, mark_ref, table_ref, gain_ref, bias_ref, stream_ref, normed_ref, turned_ref):
    rows = hidden_ref.shape[0]
    vocab = table_ref.shape[0]
    onehot = (mark_ref[...] == lax.broadcasted_iota(jnp.int32, (rows, vocab), 1)).astype(F32).astype(BF16)
    stream = hidden_ref[...].astype(F32) + dot_nn(onehot, table_ref[...])
    centre = stream - jnp.mean(stream, axis=-1, keepdims=True)
    spread = jnp.mean(centre * centre, axis=-1, keepdims=True)
    normed = centre * lax.rsqrt(spread + EPSILON) * gain_ref[...] + bias_ref[...]
    stream_ref[...] = stream
    normed_ref[...] = normed.astype(BF16)
    turned_ref[...] = normed.astype(BF16).T


def prepare(hidden, marked, table, gain, bias):
    rows, width = hidden.shape
    step = 128
    return pl.pallas_call(
        prep_kernel,
        grid=(rows // step,),
        in_specs=[
            pl.BlockSpec((step, width), lambda i: (i, 0)),
            pl.BlockSpec((step, 1), lambda i: (i, 0)),
            pl.BlockSpec(table.shape, lambda i: (0, 0)),
            pl.BlockSpec((1, width), lambda i: (0, 0)),
            pl.BlockSpec((1, width), lambda i: (0, 0)),
        ],
        out_specs=[
            pl.BlockSpec((step, width), lambda i: (i, 0)),
            pl.BlockSpec((step, width), lambda i: (i, 0)),
            pl.BlockSpec((width, step), lambda i: (0, i)),
        ],
        out_shape=[
            jax.ShapeDtypeStruct((rows, width), F32),
            jax.ShapeDtypeStruct((rows, width), BF16),
            jax.ShapeDtypeStruct((width, rows), BF16),
        ],
        name="prep",
    )(hidden, marked, table, gain, bias)


def heads_kernel(place_ref, normed_ref, cot_ref, wq_ref, wk_ref, wv_ref, wo_ref, cos_ref, sin_ref, *out_refs):
    normed = normed_ref[...]
    chunks = len(out_refs)
    cosine = jnp.concatenate([cos_ref[...]] * chunks, axis=1)
    sine = jnp.concatenate([sin_ref[...]] * chunks, axis=1)

    def turned(rows):
        return rows * cosine + swap_pairs(rows) * sine

    parts = (
        turned(dot_nn(normed, wq_ref[...])).astype(BF16),
        turned(dot_nn(normed, wk_ref[...])).astype(BF16),
        dot_nn(normed, wv_ref[...]).astype(BF16),
        dot_nt(cot_ref[...], wo_ref[...]).astype(BF16),
    )
    for chunk in range(chunks):
        for number, part in enumerate(parts):
            out_refs[chunk][:, number * PAIR : (number + 1) * PAIR] = part[:, chunk * PAIR : (chunk + 1) * PAIR]


def heads_of(owner, normed, cot, qkv_weight, out_weight, cosine, sine, owners):
    rows, width = normed.shape
    wide = width // owners
    chunks = wide // PAIR
    return pl.pallas_call(
        heads_kernel,
        grid_spec=pltpu.PrefetchScalarGridSpec(
            num_scalar_prefetch=1,
            grid=(1,),
            in_specs=[
                pl.BlockSpec((rows, width), lambda i, o: (0, 0)),
                pl.BlockSpec((rows, width), lambda i, o: (0, 0)),
                pl.BlockSpec((width, wide), lambda i, o: (0, o[0])),
                pl.BlockSpec((width, wide), lambda i, o: (0, owners + o[0])),
                pl.BlockSpec((width, wide), lambda i, o: (0, 2 * owners + o[0])),
                pl.BlockSpec((wide, width), lambda i, o: (o[0], 0)),
                pl.BlockSpec((rows, PAIR), lambda i, o: (0, 0)),
                pl.BlockSpec((rows, PAIR), lambda i, o: (0, 0)),
            ],
            out_specs=[pl.BlockSpec((rows, 4 * PAIR), lambda i, o: (0, 0))] * chunks,
        ),
        out_shape=[jax.ShapeDtypeStruct((rows, 4 * PAIR), BF16)] * chunks,
        name="heads",
    )(owner, normed, cot, qkv_weight, qkv_weight, qkv_weight, out_weight, cosine, sine)


QUERY_ROWS = 512
KEY_ROWS = 512


def attention_kernel(pieces, info_ref, *refs):
    piece_refs = refs[:pieces]
    cos_ref, sin_ref = refs[pieces : pieces + 2]
    out_refs = refs[pieces + 2 : 2 * pieces + 2]
    held, results, key_turned, value_turned, raised_ref, key_sum, value_sum = refs[2 * pieces + 2 :]
    me, end = info_ref[0], info_ref[1]
    rows = piece_refs[0].shape[0]
    length = rows * pieces
    for shift in range(pieces):
        start = pl.multiple_of(lax.rem(me - shift + pieces, pieces) * rows, rows)
        held[pl.ds(start, rows), :] = piece_refs[shift][...]
    key_turned[...] = held[:, PAIR : 2 * PAIR].T
    value_turned[...] = held[:, 2 * PAIR : 3 * PAIR].T
    key_sum[...] = jnp.zeros_like(key_sum)
    value_sum[...] = jnp.zeros_like(value_sum)
    scale = 0.125 * LOG2E
    halves = lax.broadcasted_iota(jnp.int32, (QUERY_ROWS, PAIR), 1) // HEAD_DIM

    def query_block(number, carry):
        first = pl.multiple_of(number * QUERY_ROWS, QUERY_ROWS)
        query_rows = held[pl.ds(first, QUERY_ROWS), 0:PAIR]
        grad_rows = held[pl.ds(first, QUERY_ROWS), 3 * PAIR : 4 * PAIR]
        zero = jnp.zeros_like(query_rows)
        queries = [jnp.where(halves == head, query_rows, zero) for head in range(2)]
        grads = [jnp.where(halves == head, grad_rows, zero) for head in range(2)]
        query_places = first + lax.broadcasted_iota(jnp.int32, (1, QUERY_ROWS), 1)
        lowest = jnp.where(query_places > end, end + 1, 0)
        blocks = (number + 1) * (QUERY_ROWS // KEY_ROWS)

        def scores_of(block, highest):
            start = pl.multiple_of(block * KEY_ROWS, KEY_ROWS)
            keys = held[pl.ds(start, KEY_ROWS), PAIR : 2 * PAIR]
            key_places = start + lax.broadcasted_iota(jnp.int32, (KEY_ROWS, QUERY_ROWS), 0)
            seen = (key_places <= query_places) & (key_places >= lowest)
            after = []
            for head in range(2):
                scores = jnp.where(seen, dot_nt(keys, queries[head]) * scale, BLOCKED)
                raised_ref[head, pl.ds(start, KEY_ROWS), :] = scores
                after.append(jnp.maximum(highest[head], jnp.max(scores, axis=0, keepdims=True)))
            return tuple(after)

        start_row = jnp.full((1, QUERY_ROWS), BLOCKED, F32)
        highest = lax.fori_loop(0, blocks, scores_of, (start_row, start_row))

        def mix(block, carried):
            start = pl.multiple_of(block * KEY_ROWS, KEY_ROWS)
            after = []
            for head in range(2):
                total, mixed = carried[head]
                raised = jnp.exp2(raised_ref[head, pl.ds(start, KEY_ROWS), :] - highest[head])
                raised_ref[head, pl.ds(start, KEY_ROWS), :] = raised
                values = value_turned[head * HEAD_DIM : (head + 1) * HEAD_DIM, pl.ds(start, KEY_ROWS)]
                after.append(
                    (total + jnp.sum(raised, axis=0, keepdims=True), mixed + dot_nn(values, raised.astype(BF16)))
                )
            return tuple(after)

        empty = (jnp.zeros((1, QUERY_ROWS), F32), jnp.zeros((HEAD_DIM, QUERY_ROWS), F32))
        mixes = lax.fori_loop(0, blocks, mix, (empty, empty))
        inverse = [1.0 / mixes[head][0] for head in range(2)]
        mixed = jnp.concatenate([mixes[head][1] * inverse[head] for head in range(2)], axis=0)
        grad_turned = grad_rows.astype(F32).T
        products = mixed * grad_turned
        delta = [
            jnp.sum(products[head * HEAD_DIM : (head + 1) * HEAD_DIM], axis=0, keepdims=True) for head in range(2)
        ]

        def back(block, carried):
            start = pl.multiple_of(block * KEY_ROWS, KEY_ROWS)
            values = held[pl.ds(start, KEY_ROWS), 2 * PAIR : 3 * PAIR]
            after, key_terms, value_terms = [], [], []
            for head in range(2):
                probs = raised_ref[head, pl.ds(start, KEY_ROWS), :] * inverse[head]
                prob_grad = dot_nt(values, grads[head])
                score_grad = (probs * (prob_grad - delta[head])).astype(BF16)
                value_terms.append(dot_nn(probs.astype(BF16), grads[head]))
                key_terms.append(dot_nn(score_grad, queries[head]))
                keys = key_turned[head * HEAD_DIM : (head + 1) * HEAD_DIM, pl.ds(start, KEY_ROWS)]
                after.append(carried[head] + dot_nn(keys, score_grad))
            value_sum[pl.ds(start, KEY_ROWS), :] += value_terms[0] + value_terms[1]
            key_sum[pl.ds(start, KEY_ROWS), :] += key_terms[0] + key_terms[1]
            return tuple(after)

        query_grads = lax.fori_loop(0, blocks, back, (empty[1], empty[1]))
        query_grad = jnp.concatenate(query_grads, axis=0).T * 0.125
        cosine = cos_ref[pl.ds(first, QUERY_ROWS), :]
        sine = sin_ref[pl.ds(first, QUERY_ROWS), :]
        results[pl.ds(first, QUERY_ROWS), 0:PAIR] = (query_grad * cosine - swap_pairs(query_grad) * sine).astype(BF16)
        results[pl.ds(first, QUERY_ROWS), 3 * PAIR : 4 * PAIR] = mixed.T.astype(BF16)
        return carry

    lax.fori_loop(0, length // QUERY_ROWS, query_block, 0)
    key_grad = key_sum[...] * 0.125
    results[:, PAIR : 2 * PAIR] = (key_grad * cos_ref[...] - swap_pairs(key_grad) * sin_ref[...]).astype(BF16)
    results[:, 2 * PAIR : 3 * PAIR] = value_sum[...].astype(BF16)
    for shift in range(pieces):
        start = pl.multiple_of(lax.rem(me + shift, pieces) * rows, rows)
        out_refs[shift][...] = results[pl.ds(start, rows), :]


def attention(info, parts, cosine, sine):
    pieces = len(parts)
    rows, wide = parts[0].shape
    length = rows * pieces
    whole = pl.BlockSpec(memory_space=pltpu.VMEM)
    blocks = length // QUERY_ROWS
    pairs_of = 2 * blocks * (blocks + 1) // 2 * QUERY_ROWS * KEY_ROWS
    return pl.pallas_call(
        lambda *refs: attention_kernel(pieces, *refs),
        in_specs=[pl.BlockSpec(memory_space=pltpu.SMEM)] + [whole] * (pieces + 2),
        out_specs=[whole] * pieces,
        out_shape=[jax.ShapeDtypeStruct((rows, wide), BF16)] * pieces,
        scratch_shapes=[
            pltpu.VMEM((length, wide), BF16),
            pltpu.VMEM((length, wide), BF16),
            pltpu.VMEM((PAIR, length), BF16),
            pltpu.VMEM((PAIR, length), BF16),
            pltpu.VMEM((2, length, QUERY_ROWS), F32),
            pltpu.VMEM((length, PAIR), F32),
            pltpu.VMEM((length, PAIR), F32),
        ],
        compiler_params=pltpu.CompilerParams(vmem_limit_bytes=40 * MIB),
        cost_estimate=pl.CostEstimate(
            flops=12 * 256 * pairs_of, bytes_accessed=2 * 2 * length * wide * 2, transcendentals=pairs_of
        ),
        name="attention",
    )(info, *parts, cosine, sine)


def feed_kernel(first, *refs):
    normed_ref, turned_ref, cot_ref, in_ref, bias_ref, down_ref = refs[1:7]
    in_grad, down_grad, bias_grad, out_sum, norm_sum = refs[-5:]
    step = pl.program_id(0)
    up = math.sqrt(2.0 / math.pi)

    @pl.when(step == 0)
    def _():
        if first:
            out_sum[...] = jnp.zeros_like(out_sum)
            norm_sum[...] = jnp.zeros_like(norm_sum)
        else:
            out_sum[...] = refs[7][...]
            norm_sum[...] = refs[8][...]

    weights = in_ref[...]
    downs = down_ref[...]
    cot = cot_ref[...]
    pre = dot_nn(normed_ref[...], weights) + bias_ref[...]
    square = pre * pre
    tanh = jnp.tanh(up * pre * (1.0 + 0.044715 * square))
    half = 0.5 * (1.0 + tanh)
    active = (pre * half).astype(BF16)
    slope = half + 0.5 * pre * (1.0 - tanh * tanh) * (up * (1.0 + 3 * 0.044715 * square))
    pre_grad = (dot_nt(cot, downs) * slope).astype(BF16)
    pieces, owners, kept, tile = in_grad.shape
    term = dot_nn(turned_ref[...], pre_grad).astype(BF16)
    for owner in range(owners):
        for piece in range(pieces):
            start = (owner * pieces + piece) * kept
            in_grad[piece, owner] = term[start : start + kept]
    term = dot_tn(active, cot).astype(BF16)
    kept = tile // pieces
    for group in range(term.shape[1] // tile):
        for piece in range(pieces):
            down_grad[piece, 0, group * kept : (group + 1) * kept] = term[
                piece * kept : (piece + 1) * kept, group * tile : (group + 1) * tile
            ]
    bias_grad[0] = jnp.sum(pre_grad.astype(F32), axis=0, keepdims=True)
    out_sum[...] += dot_nn(active, downs)
    norm_sum[...] += dot_nt(pre_grad, weights)


def feed_half(cells, normed, turned, cot, in_weight, in_bias, down_weight, pieces, sums=()):
    rows, width = normed.shape
    owners = cells.shape[0]
    hidden_units = in_weight.shape[1]
    tile = hidden_units // (2 * owners)
    kept = width // owners // pieces
    tall = owners * kept
    wide = tile // pieces * (width // tile)
    fixed = pl.BlockSpec((rows, width), lambda i, c: (0, 0))
    return pl.pallas_call(
        lambda *refs: feed_kernel(not sums, *refs),
        grid_spec=pltpu.PrefetchScalarGridSpec(
            num_scalar_prefetch=1,
            grid=(owners,),
            in_specs=[
                fixed,
                pl.BlockSpec((width, rows), lambda i, c: (0, 0)),
                fixed,
                pl.BlockSpec((width, tile), lambda i, c: (0, c[i])),
                pl.BlockSpec((1, tile), lambda i, c: (0, c[i])),
                pl.BlockSpec((tile, width), lambda i, c: (c[i], 0)),
            ]
            + [fixed] * len(sums),
            out_specs=[
                pl.BlockSpec((pieces, owners, kept, tile), lambda i, c: (0, 0, i, 0)),
                pl.BlockSpec((pieces, 1, wide, tile), lambda i, c: (0, i, 0, 0)),
                pl.BlockSpec((1, 1, tile), lambda i, c: (i, 0, 0)),
                fixed,
                fixed,
            ],
        ),
        out_shape=[
            jax.ShapeDtypeStruct((pieces, owners, tall, tile), BF16),
            jax.ShapeDtypeStruct((pieces, owners, wide, tile), BF16),
            jax.ShapeDtypeStruct((owners, 1, tile), F32),
            jax.ShapeDtypeStruct((rows, width), F32),
            jax.ShapeDtypeStruct((rows, width), F32),
        ],
        compiler_params=pltpu.CompilerParams(vmem_limit_bytes=60 * MIB),
        cost_estimate=pl.CostEstimate(
            flops=12 * rows * width * hidden_units // 2,
            bytes_accessed=8 * width * hidden_units // 2,
            transcendentals=rows * hidden_units // 2,
        ),
        name="feed",
    )(cells, normed, turned, cot, in_weight, in_bias, down_weight, *sums)


def place_columns(me_ref, piece_refs, held):
    owners = len(piece_refs)
    for shift in range(owners):
        owner = lax.rem(me_ref[0] - shift + owners, owners)
        start = pl.multiple_of(owner * PAIR, PAIR)
        for part in range(4):
            held[part, :, pl.ds(start, PAIR)] = piece_refs[shift][:, part * PAIR : (part + 1) * PAIR]


def weight_kernel(pieces, me_ref, turned_ref, cot_ref, *refs):
    owners = len(refs) - 2
    grad_ref, held = refs[-2:]
    place_columns(me_ref, refs[:owners], held)
    kept = PAIR // pieces
    turned = turned_ref[...]
    for part in range(3):
        term = dot_nn(turned, held[part]).astype(BF16)
        for owner in range(owners):
            for core in range(2):
                for piece in range(pieces):
                    start = ((owner * 2 + core) * pieces + piece) * kept
                    grad_ref[core, piece, owner, part * kept : (part + 1) * kept] = term[start : start + kept]
    term = dot_tn(held[3], cot_ref[...]).astype(BF16)
    half = term.shape[1] // 2
    for owner in range(owners):
        for core in range(2):
            for piece in range(pieces):
                start = (owner * pieces + piece) * kept
                grad_ref[core, piece, owner, 3 * kept :] = term[
                    start : start + kept, core * half : (core + 1) * half
                ]


def weight_grads(me, turned, cot, parts, pieces):
    owners = len(parts)
    rows, width = cot.shape
    kept = PAIR // pieces
    whole = pl.BlockSpec(memory_space=pltpu.VMEM)
    return pl.pallas_call(
        lambda *refs: weight_kernel(pieces, *refs),
        in_specs=[pl.BlockSpec(memory_space=pltpu.SMEM)] + [whole] * (2 + owners),
        out_specs=whole,
        out_shape=jax.ShapeDtypeStruct((2, pieces, owners, 4 * kept, owners * PAIR), BF16),
        scratch_shapes=[pltpu.VMEM((4, rows, owners * PAIR), BF16)],
        compiler_params=pltpu.CompilerParams(vmem_limit_bytes=40 * MIB),
        cost_estimate=pl.CostEstimate(
            flops=8 * rows * width * owners * PAIR, bytes_accessed=12 * MIB, transcendentals=0
        ),
        name="weight_grads",
    )(me[None], turned, cot, *parts)


def sums_kernel(last, owners, me_ref, *refs):
    piece_refs, refs = refs[:owners], refs[owners:]
    weight_refs, refs = refs[: 3 * owners], refs[3 * owners :]
    out_weight_refs, refs = refs[:owners], refs[owners:]
    out_in, norm_in = refs[:2]
    held = refs[-1]
    place_columns(me_ref, piece_refs, held)
    norm = norm_in[...]
    for part in range(3):
        weights = jnp.concatenate([ref[...] for ref in weight_refs[part * owners : (part + 1) * owners]], axis=1)
        norm = norm + dot_nt(held[part], weights)
    weights = jnp.concatenate([ref[...] for ref in out_weight_refs], axis=0)
    out = out_in[...] + dot_nn(held[3], weights)
    if not last:
        out_ref, norm_ref = refs[2:4]
        out_ref[...] = out
        norm_ref[...] = norm
        return
    stream_ref, cot_ref, gain_ref, down_bias_ref, out_ref, hidden_ref, gain_grad, bias_grad, cot_sum = refs[2:-1]
    stream = stream_ref[...]
    cot = cot_ref[...].astype(F32)
    out_ref[...] = (stream + out + down_bias_ref[...]).astype(BF16)
    centre = stream - jnp.mean(stream, axis=-1, keepdims=True)
    spread = jnp.mean(centre * centre, axis=-1, keepdims=True)
    inverse = lax.rsqrt(spread + EPSILON)
    hat = centre * inverse
    gained = norm * gain_ref[...]
    hidden_ref[...] = cot + inverse * (
        gained
        - jnp.mean(gained, axis=-1, keepdims=True)
        - hat * jnp.mean(gained * hat, axis=-1, keepdims=True)
    )
    gain_grad[...] = jnp.sum(norm * hat, axis=0, keepdims=True)
    bias_grad[...] = jnp.sum(norm, axis=0, keepdims=True)
    cot_sum[...] = jnp.sum(cot, axis=0, keepdims=True)


def sums_of(me, chunk, chunks, parts, qkv_weight, out_weight, sums, final=()):
    owners = len(parts)
    rows = parts[0].shape[0]
    width = qkv_weight.shape[0]
    whole = pl.BlockSpec(memory_space=pltpu.VMEM)
    last = bool(final)

    def columns(part, owner):
        at = (part * owners + owner) * chunks + chunk
        return pl.BlockSpec((width, PAIR), lambda i: (0, at))

    def weight_rows(owner):
        return pl.BlockSpec((PAIR, width), lambda i: (owner * chunks + chunk, 0))

    full = jax.ShapeDtypeStruct((rows, width), F32)
    row = jax.ShapeDtypeStruct((1, width), F32)
    return pl.pallas_call(
        lambda *refs: sums_kernel(last, owners, *refs),
        grid=(1,),
        in_specs=[pl.BlockSpec(memory_space=pltpu.SMEM)]
        + [whole] * owners
        + [columns(part, owner) for part in range(3) for owner in range(owners)]
        + [weight_rows(owner) for owner in range(owners)]
        + [whole] * (2 + len(final)),
        out_specs=[whole] * (5 if last else 2),
        out_shape=[jax.ShapeDtypeStruct((rows, width), BF16), full, row, row, row] if last else [full, full],
        scratch_shapes=[pltpu.VMEM((4, rows, owners * PAIR), BF16)],
        compiler_params=pltpu.CompilerParams(vmem_limit_bytes=56 * MIB),
        cost_estimate=pl.CostEstimate(
            flops=8 * rows * width * owners * PAIR, bytes_accessed=16 * MIB, transcendentals=0
        ),
        name="sums",
    )(me[None], *parts, *([qkv_weight] * (3 * owners)), *([out_weight] * owners), *sums, *final)


def exchange(rows, axis, mask):
    size = lax.axis_size(axis)
    return lax.ppermute(rows, axis, [(place, place ^ mask) for place in range(size)])


def added(left, right):
    return (left.astype(F32) + right.astype(F32)).astype(BF16)


def joined(mine, other, bit):
    low = jnp.where(bit == 0, mine, other)
    high = jnp.where(bit == 0, other, mine)
    return jnp.stack([low, high])


def bits_of(axis):
    return lax.axis_size(axis).bit_length() - 1


def picked(rows, index):
    return lax.dynamic_index_in_dim(rows, index, 0, keepdims=False)


class DeviceSum:
    def __init__(self):
        place = lax.axis_index("batch")
        self.bits = [(place >> number) & 1 for number in range(bits_of("batch"))]
        place = lax.axis_index("seq")
        self.seq_bits = [(place >> number) & 1 for number in range(bits_of("seq"))]
        order = list(range(1, len(self.bits)))
        self.orders = (order, order[::-1])

    def send_core(self, arrays):
        self.arrived = [exchange(array, "batch", 1) for array in arrays]

    def take_core(self, kept):
        self.ends = []
        depth = len(self.orders[0])
        for half, order in enumerate(self.orders):
            bit = self.bits[order[0]]

            def side(index):
                terms = []
                for mine, other in zip(kept, self.arrived):
                    shape = (2, 2, mine.shape[0] // 4) + mine.shape[1:]
                    terms.append(
                        added(picked(mine.reshape(shape)[half], index), picked(other.reshape(shape)[half], index))
                    )
                return terms[0] if len(terms) == 1 else jnp.concatenate(terms, axis=2)

            self.ends.append((side(1 - bit), side(bit)))
        self.level = 0
        return self

    def send(self):
        self.arrived = [
            exchange(end[0], "batch", 1 << order[self.level]) for end, order in zip(self.ends, self.orders)
        ]

    def take(self):
        ends = []
        self.level += 1
        for (_, kept), arrived, order in zip(self.ends, self.arrived, self.orders):
            total = added(kept, arrived)
            if self.level < len(order):
                shape = (2, total.shape[0] // 2) + total.shape[1:]
                bit = self.bits[order[self.level]]
                ends.append((picked(total.reshape(shape), 1 - bit), picked(total.reshape(shape), bit)))
            else:
                ends.append(total[0])
        self.ends = ends
        if self.level == len(self.orders[0]):
            self.split_seq(jnp.concatenate(ends, axis=1), 0)

    def split_seq(self, rows, number):
        self.level = number
        split = rows.reshape((rows.shape[0] // 2, 2) + rows.shape[1:])
        bit = self.seq_bits[number]
        self.ends = tuple(
            lax.dynamic_index_in_dim(split, index, 1, keepdims=False) for index in (1 - bit, bit)
        )

    def send_seq(self):
        self.arrived = exchange(self.ends[0], "seq", 1 << self.level)

    def take_seq(self):
        total = added(self.ends[1], self.arrived)
        if self.level + 1 < len(self.seq_bits):
            self.split_seq(total, self.level + 1)
        else:
            rows = total[0]
            middle = rows.shape[0] // 2
            self.ends = [rows[:middle], rows[middle:]]

    def gather(self, level):
        ends = []
        for rows, order in zip(self.ends, self.orders):
            number = order[len(order) - 1 - level]
            ends.append(joined(rows, exchange(rows, "batch", 1 << number), self.bits[number]))
        self.ends = ends

    def gather_core(self):
        mine = jnp.stack(self.ends)
        return joined(mine, exchange(mine, "batch", 1), self.bits[0])


def all_sum(rows):
    for axis in ("batch", "seq"):
        for number in range(bits_of(axis)):
            rows = rows + exchange(rows, axis, 1 << number)
    return rows


def tied(*groups):
    return lax.optimization_barrier(groups)


def fast_body(
    hidden,
    token_ids,
    offsets,
    end_places,
    token_table,
    norm_gain,
    norm_bias,
    qkv_weight,
    out_weight,
    in_weight,
    in_bias,
    down_weight,
    down_bias,
    cotangent,
):
    width = hidden.shape[2]
    rows = hidden.shape[1]
    owners = lax.axis_size("seq")
    pieces = lax.axis_size("batch")
    me = lax.axis_index("seq")
    core = lax.axis_index("batch") & 1
    length = rows * owners
    own_rows = width // owners
    chunks = own_rows // PAIR
    end = end_places[0]

    places = me * rows + jnp.arange(rows, dtype=jnp.int32)[:, None]
    marked = token_ids.reshape(rows, 1)
    marked = jnp.where(places == end, 2, marked)
    marked = jnp.where(places == end + 1, 1, marked)
    marked = jnp.where((places == 0) & (offsets[0] == 0), 1, marked)
    cot = cotangent.reshape(rows, width)
    stream, normed, turned = prepare(
        hidden.reshape(rows, width), marked, token_table, norm_gain[None], norm_bias[None]
    )
    cosine, sine = (jnp.asarray(table) for table in trig_tables(length))
    own_cosine = lax.dynamic_slice_in_dim(cosine, me * rows, rows)
    own_sine = lax.dynamic_slice_in_dim(sine, me * rows, rows)

    parts = [[None] * owners for _ in range(chunks)]
    far_first = sorted(range(1, owners), key=lambda shift: abs(2 * shift - owners)) + [0]
    for shift in far_first:
        owner = lax.rem(me + shift, owners)
        blocks = heads_of(owner[None], normed, cot, qkv_weight, out_weight, own_cosine, own_sine, owners)
        for chunk in range(chunks):
            parts[chunk][shift] = blocks[chunk]

    def shifted(blocks):
        around = [blocks[0]]
        for shift in range(1, owners):
            around.append(
                lax.ppermute(blocks[shift], "seq", [(place, (place + shift) % owners) for place in range(owners)])
            )
        return around

    heads = [shifted(parts[0])]
    for chunk in range(1, chunks):
        parts[chunk], _ = tied(parts[chunk], parts[0])
        heads.append(shifted(parts[chunk]))

    cells = 2 * jnp.arange(owners, dtype=jnp.int32)
    feed_args = (normed, turned, cot, in_weight, in_bias[None], down_weight, pieces)
    away = feed_half(cells + 1 - core, *feed_args)
    here = feed_half(cells + core, *feed_args, sums=tuple(away[3:]))
    bias_low = jnp.where(core == 0, here[2], away[2])
    bias_high = jnp.where(core == 0, away[2], here[2])
    in_bias_grad = jnp.concatenate([bias_low, bias_high], axis=1)
    feed_sum = DeviceSum()
    feed_sum.send_core(away[:2])
    feed_sum.take_core(here[:2])
    out_total, norm_total = here[3:]

    info = jnp.stack([me, end]).astype(jnp.int32)
    back = []
    for chunk in range(chunks):
        heads[chunk], feed_sum.ends = tied(heads[chunk], feed_sum.ends)
        feed_sum.send()
        results = attention(info, heads[chunk], cosine, sine)
        back.append(shifted(results))
        results, feed_sum.arrived = tied(results, feed_sum.arrived)
        feed_sum.take()

    grads = []
    for chunk in range(chunks):
        last = chunk == chunks - 1
        back[chunk], feed_sum.ends = tied(back[chunk], feed_sum.ends)
        feed_sum.send_seq()
        grad = weight_grads(me, turned, cot, back[chunk], pieces)
        grads.append(DeviceSum())
        grads[chunk].send_core([picked(grad, 1 - core)])
        final = (stream, cot, norm_gain[None], down_bias[None]) if last else ()
        totals = sums_of(me, chunk, chunks, back[chunk], qkv_weight, out_weight, (out_total, norm_total), final)
        if not last:
            out_total, norm_total = totals
        grads[chunk].take_core([picked(grad, core)])
        grads[chunk].send()
        feed_sum.take_seq()
    output, hidden_grad, gain_grad, bias_grad, cot_sum = totals

    for grad in grads:
        for level in range(1, len(grad.orders[0])):
            grad.take()
            grad.send()
        grad.take()
        for _ in grad.seq_bits:
            grad.send_seq()
            grad.take_seq()
    small = jnp.concatenate(
        [
            in_bias_grad.reshape(owners, -1),
            cot_sum.reshape(owners, -1),
            gain_grad.reshape(owners, -1),
            bias_grad.reshape(owners, -1),
        ],
        axis=1,
    )
    small = picked(all_sum(small), me)
    for total in [feed_sum] + grads:
        for level in range(len(total.orders[0])):
            total.gather(level)

    tile = in_weight.shape[1] // (2 * owners)
    total = feed_sum.gather_core()
    total = total.reshape((2, pieces) + total.shape[-2:])
    tall = owners * (own_rows // pieces)
    in_weight_grad = total[:, :, :tall].reshape(2, pieces, owners, own_rows // pieces, tile)
    in_weight_grad = jnp.transpose(in_weight_grad, (1, 3, 2, 0, 4)).reshape(own_rows, -1).astype(F32)
    down_weight_grad = total[:, :, tall:].reshape(2, pieces, width // tile, tile // pieces, tile)
    down_weight_grad = jnp.transpose(down_weight_grad, (0, 1, 3, 2, 4)).reshape(2 * tile, width).astype(F32)
    kept = PAIR // pieces
    totals = jnp.stack([grad.gather_core() for grad in grads])
    totals = totals.reshape((chunks, 2, pieces, 4, kept) + totals.shape[-1:])
    qkv_weight_grad = totals[:, :, :, :3].reshape(chunks, 2, pieces, 3, kept, owners, PAIR)
    qkv_weight_grad = jnp.transpose(qkv_weight_grad, (1, 2, 4, 3, 5, 0, 6)).reshape(own_rows, -1).astype(F32)
    out_weight_grad = jnp.transpose(totals[:, :, :, 3], (0, 2, 3, 1, 4)).reshape(own_rows, width).astype(F32)

    few = own_rows
    many = in_bias.shape[0] // owners
    return (
        output[None],
        hidden_grad[None],
        small[many + few : many + 2 * few],
        small[many + 2 * few :],
        qkv_weight_grad,
        out_weight_grad,
        in_weight_grad,
        small[:many],
        down_weight_grad,
        small[many : many + few],
    )


def rotate(vectors, cosine_table, sine_table):
    even_part = vectors[..., 0:ROT:2]
    odd_part = vectors[..., 1:ROT:2]
    turned = jnp.stack(
        [
            even_part * cosine_table - odd_part * sine_table,
            odd_part * cosine_table + even_part * sine_table,
        ],
        axis=-1,
    )
    turned = turned.reshape(vectors.shape[:-1] + (ROT,))
    return jnp.concatenate([turned, vectors[..., ROT:]], axis=-1)


def angles(places):
    inverse = 10000.0 ** (-(jnp.arange(ROT // 2, dtype=jnp.float32) * 2.0) / ROT)
    phases = places.astype(jnp.float32)[:, None] * inverse[None, :]
    return (jnp.cos(phases), jnp.sin(phases))


def visible(query_places, key_places, end_places):
    query_after = query_places[None, :, None] > end_places[:, None, None]
    key_after = key_places[None, None, :] > end_places[:, None, None]
    return (key_places[None, None, :] <= query_places[None, :, None]) & (query_after == key_after)


def norm_rows(stream, gain_row, bias_row):
    centre = stream - jnp.mean(stream, axis=-1, keepdims=True)
    spread = jnp.mean(centre * centre, axis=-1, keepdims=True)
    return centre * lax.rsqrt(spread + EPSILON) * gain_row + bias_row


def gelu_rows(pre_active):
    return jax.nn.gelu(pre_active, approximate=True)


def plain_body(
    hidden,
    token_ids,
    offsets,
    end_places,
    token_table,
    norm_gain,
    norm_bias,
    qkv_weight,
    out_weight,
    in_weight,
    in_bias,
    down_weight,
    down_bias,
    cotangent,
):
    windows_here, shard_rows, model_width = hidden.shape
    head_count = model_width // HEAD_DIM
    seq_count = lax.axis_size("seq")
    seq_place = lax.axis_index("seq")
    home_places = seq_place * shard_rows + jnp.arange(shard_rows, dtype=jnp.int32)
    token_rows = shard_rows * windows_here
    marked = token_ids.T
    marked = jnp.where(home_places[:, None] == end_places[None, :], 2, marked)
    marked = jnp.where(home_places[:, None] == end_places[None, :] + 1, 1, marked)
    marked = jnp.where((home_places[:, None] == 0) & (offsets[None, :] == 0), 1, marked)
    onehot = (marked[..., None] == jnp.arange(token_table.shape[0], dtype=jnp.int32)).astype(
        jnp.bfloat16
    )
    embedded = jnp.einsum("swv,vd->swd", onehot, token_table, preferred_element_type=jnp.float32)
    stream_three = jnp.transpose(hidden, (1, 0, 2)).astype(jnp.float32) + embedded
    cot_three = jnp.transpose(cotangent, (1, 0, 2))
    own_high = jnp.max(home_places)
    stream_rows = stream_three.reshape(token_rows, model_width)
    normed, norm_back = jax.vjp(norm_rows, stream_rows, norm_gain, norm_bias)
    normed_low = normed.astype(jnp.bfloat16)
    projected = jnp.dot(normed_low, qkv_weight, preferred_element_type=jnp.float32)
    cosine_table, sine_table = angles(home_places)
    cosine_table = cosine_table[:, None, None, :]
    sine_table = sine_table[:, None, None, :]

    def turn_heads(projected_rows):
        divided = projected_rows.reshape(shard_rows, windows_here, 3, head_count, HEAD_DIM)
        return (
            rotate(divided[:, :, 0], cosine_table, sine_table),
            rotate(divided[:, :, 1], cosine_table, sine_table),
            divided[:, :, 2],
        )

    (queries, key_rows, values), turn_back = jax.vjp(turn_heads, projected)
    query_low = queries.astype(jnp.bfloat16)
    key_value = jnp.concatenate(
        [
            key_rows.reshape(shard_rows, windows_here, model_width),
            values.reshape(shard_rows, windows_here, model_width),
        ],
        axis=-1,
    ).astype(jnp.bfloat16)

    def split_block(key_block):
        row_count = key_block.shape[0]
        return (
            key_block[..., :model_width].reshape(row_count, windows_here, head_count, HEAD_DIM),
            key_block[..., model_width:].reshape(row_count, windows_here, head_count, HEAD_DIM),
        )

    def block_places(row_start, row_count):
        return row_start + jnp.arange(row_count, dtype=jnp.int32)

    def block_scores(key_block, key_start):
        key_part, value_part = split_block(key_block)
        key_places = block_places(key_start, key_block.shape[0])
        scores = (
            jnp.einsum("qwhd,kwhd->whqk", query_low, key_part, preferred_element_type=jnp.float32)
            * 0.125
        )
        scores = jnp.where(visible(home_places, key_places, end_places)[:, None], scores, BLOCKED)
        return (scores, key_part, value_part)

    def attend(carried, key_block, key_start):
        running, totals, accumulated = carried
        scores, key_part, value_part = block_scores(key_block, key_start)
        highest = jnp.maximum(running, jnp.max(scores, axis=-1))
        factor = jnp.exp(running - highest)
        raised = jnp.exp(scores - highest[..., None])
        totals = totals * factor + jnp.sum(raised, axis=-1)
        accumulated = accumulated * factor[..., None] + jnp.einsum(
            "whqk,kwhd->whqd",
            raised.astype(jnp.bfloat16),
            value_part,
            preferred_element_type=jnp.float32,
        )
        return (highest, totals, accumulated)

    start_state = (
        jnp.full((windows_here, head_count, shard_rows), BLOCKED, jnp.float32),
        jnp.zeros((windows_here, head_count, shard_rows), jnp.float32),
        jnp.zeros((windows_here, head_count, shard_rows, HEAD_DIM), jnp.float32),
    )
    carried = start_state
    fetched_rows = lax.all_gather(key_value, "seq", axis=0, tiled=True)
    row_count = fetched_rows.shape[0]
    blocks = fetched_rows.reshape((row_count // shard_rows, shard_rows) + fetched_rows.shape[1:])

    def visit_block(held_state, element):
        number, key_block = element
        key_start = number * shard_rows
        dead = jnp.min(block_places(key_start, shard_rows)) > own_high
        held_state = lax.cond(
            dead,
            lambda kept_state: kept_state,
            lambda kept_state: attend(kept_state, key_block, key_start),
            held_state,
        )
        return (held_state, None)

    carried, unused = lax.scan(
        visit_block, carried, (jnp.arange(blocks.shape[0], dtype=jnp.int32), blocks)
    )
    running, totals, accumulated = carried
    attention = accumulated / totals[..., None]
    log_total = running + jnp.log(totals)
    attention_rows = jnp.transpose(attention, (2, 0, 1, 3))
    mixed_low = attention_rows.reshape(token_rows, model_width).astype(jnp.bfloat16)
    attended = jnp.dot(mixed_low, out_weight, preferred_element_type=jnp.float32)
    pre_active = jnp.dot(normed_low, in_weight, preferred_element_type=jnp.float32) + in_bias
    active, gelu_back = jax.vjp(gelu_rows, pre_active)
    active_low = active.astype(jnp.bfloat16)
    result = (
        stream_rows
        + attended
        + jnp.dot(active_low, down_weight, preferred_element_type=jnp.float32)
        + down_bias
    )
    grad_rows = cot_three.reshape(token_rows, model_width)
    down_weight_grad = jnp.dot(active_low.T, grad_rows, preferred_element_type=jnp.float32)
    down_bias_grad = jnp.sum(grad_rows.astype(jnp.float32), axis=0)
    out_weight_grad = jnp.dot(mixed_low.T, grad_rows, preferred_element_type=jnp.float32)
    active_grad = jnp.dot(grad_rows, down_weight.T, preferred_element_type=jnp.float32)
    pre_grad = gelu_back(active_grad)[0].astype(jnp.bfloat16)
    in_weight_grad = jnp.dot(normed_low.T, pre_grad, preferred_element_type=jnp.float32)
    in_bias_grad = jnp.sum(pre_grad.astype(jnp.float32), axis=0)
    mixed_grad = jnp.dot(grad_rows, out_weight.T, preferred_element_type=jnp.float32).astype(
        jnp.bfloat16
    )
    grad_heads = mixed_grad.reshape(shard_rows, windows_here, head_count, HEAD_DIM)
    delta_rows = jnp.sum(grad_heads.astype(jnp.float32) * attention_rows, axis=-1)
    row_delta = jnp.transpose(delta_rows, (1, 2, 0))
    whole_keys = lax.all_gather(key_value, "seq", axis=0, tiled=True)
    blocks = whole_keys.reshape((seq_count, shard_rows) + whole_keys.shape[1:])
    zero_heads = jnp.zeros((shard_rows, windows_here, head_count, HEAD_DIM), jnp.float32)

    def back_block(query_grad, element):
        number, key_block = element
        key_start = number * shard_rows

        def live_block(held_grad):
            scores, key_part, value_part = block_scores(key_block, key_start)
            weighting = jnp.exp(scores - log_total[..., None])
            prob_grad = jnp.einsum(
                "qwhd,kwhd->whqk", grad_heads, value_part, preferred_element_type=jnp.float32
            )
            score_low = (weighting * (prob_grad - row_delta[..., None])).astype(jnp.bfloat16)
            held_grad = held_grad + 0.125 * jnp.einsum(
                "whqk,kwhd->qwhd", score_low, key_part, preferred_element_type=jnp.float32
            )
            key_grad = 0.125 * jnp.einsum(
                "whqk,qwhd->kwhd", score_low, query_low, preferred_element_type=jnp.float32
            )
            value_grad = jnp.einsum(
                "whqk,qwhd->kwhd",
                weighting.astype(jnp.bfloat16),
                grad_heads,
                preferred_element_type=jnp.float32,
            )
            return (
                held_grad,
                jnp.concatenate(
                    [
                        key_grad.reshape(shard_rows, windows_here, model_width),
                        value_grad.reshape(shard_rows, windows_here, model_width),
                    ],
                    axis=-1,
                ),
            )

        def dead_block(held_grad):
            return (held_grad, jnp.zeros((shard_rows, windows_here, 2 * model_width), jnp.float32))

        dead = jnp.min(block_places(key_start, shard_rows)) > own_high
        return lax.cond(dead, dead_block, live_block, query_grad)

    query_grad, key_terms = lax.scan(
        back_block, zero_heads, (jnp.arange(seq_count, dtype=jnp.int32), blocks)
    )
    key_terms = key_terms.reshape((seq_count * shard_rows,) + key_terms.shape[2:])
    summed = lax.psum_scatter(
        key_terms.astype(jnp.bfloat16), "seq", scatter_dimension=0, tiled=True
    ).astype(jnp.float32)
    key_grad = summed[..., :model_width].reshape(shard_rows, windows_here, head_count, HEAD_DIM)
    value_grad = summed[..., model_width:].reshape(shard_rows, windows_here, head_count, HEAD_DIM)
    joined_grad = turn_back((query_grad, key_grad, value_grad))[0].astype(jnp.bfloat16)
    qkv_weight_grad = jnp.dot(normed_low.T, joined_grad, preferred_element_type=jnp.float32)
    normed_grad = jnp.dot(joined_grad, qkv_weight.T, preferred_element_type=jnp.float32) + jnp.dot(
        pre_grad, in_weight.T, preferred_element_type=jnp.float32
    )
    stream_part, norm_gain_grad, norm_bias_grad = norm_back(normed_grad)
    stream_grad = grad_rows.astype(jnp.float32) + stream_part
    result_three = result.reshape(shard_rows, windows_here, model_width)
    grad_three = stream_grad.reshape(shard_rows, windows_here, model_width)
    output = jnp.transpose(result_three, (1, 0, 2)).astype(jnp.bfloat16)
    hidden_grad = jnp.transpose(grad_three, (1, 0, 2))
    shares = (
        lax.psum_scatter(
            norm_gain_grad.astype(jnp.bfloat16), "seq", scatter_dimension=0, tiled=True
        ).astype(jnp.float32),
        lax.psum_scatter(
            norm_bias_grad.astype(jnp.bfloat16), "seq", scatter_dimension=0, tiled=True
        ).astype(jnp.float32),
        lax.psum_scatter(
            qkv_weight_grad.astype(jnp.bfloat16), "seq", scatter_dimension=0, tiled=True
        ).astype(jnp.float32),
        lax.psum_scatter(
            out_weight_grad.astype(jnp.bfloat16), "seq", scatter_dimension=0, tiled=True
        ).astype(jnp.float32),
        lax.psum_scatter(
            in_weight_grad.astype(jnp.bfloat16), "seq", scatter_dimension=0, tiled=True
        ).astype(jnp.float32),
        lax.psum_scatter(
            in_bias_grad.astype(jnp.bfloat16), "seq", scatter_dimension=0, tiled=True
        ).astype(jnp.float32),
        lax.psum_scatter(
            down_weight_grad.astype(jnp.bfloat16), "seq", scatter_dimension=0, tiled=True
        ).astype(jnp.float32),
        lax.psum_scatter(
            down_bias_grad.astype(jnp.bfloat16), "seq", scatter_dimension=0, tiled=True
        ).astype(jnp.float32),
    )
    totals_all = (
        lax.psum(shares[0].astype(jnp.bfloat16), "batch").astype(jnp.float32),
        lax.psum(shares[1].astype(jnp.bfloat16), "batch").astype(jnp.float32),
        lax.psum(shares[2].astype(jnp.bfloat16), "batch").astype(jnp.float32),
        lax.psum(shares[3].astype(jnp.bfloat16), "batch").astype(jnp.float32),
        lax.psum(shares[4].astype(jnp.bfloat16), "batch").astype(jnp.float32),
        lax.psum(shares[5].astype(jnp.bfloat16), "batch").astype(jnp.float32),
        lax.psum(shares[6].astype(jnp.bfloat16), "batch").astype(jnp.float32),
        lax.psum(shares[7].astype(jnp.bfloat16), "batch").astype(jnp.float32),
    )
    return (
        output,
        hidden_grad,
        totals_all[0],
        totals_all[1],
        totals_all[2],
        totals_all[3],
        totals_all[4],
        totals_all[5],
        totals_all[6],
        totals_all[7],
    )


def solution(mesh):
    placed = (
        P("batch", "seq", None),
        P("batch", "seq"),
        P("batch"),
        P("batch"),
        P(),
        P(),
        P(),
        P(),
        P(),
        P(),
        P(),
        P(),
        P(),
        P("batch", "seq", None),
    )

    def body(*arrays):
        hidden = arrays[0]
        owners = mesh.shape["seq"]
        wide = hidden.shape[2] // owners
        pieces = mesh.shape["batch"]
        if hidden.shape[0] == 1 and wide % PAIR == 0 and wide // 2 >= 16 * pieces and pieces >= 4:
            return fast_body(*arrays)
        return plain_body(*arrays)

    return jax.shard_map(
        body,
        mesh=mesh,
        in_specs=placed,
        out_specs=(
            P("batch", "seq", None),
            P("batch", "seq", None),
            P("seq"),
            P("seq"),
            P("seq", None),
            P("seq", None),
            P("seq", None),
            P("seq"),
            P("seq", None),
            P("seq"),
        ),
        check_vma=False,
    )
```

```python
import math

import jax
import jax.numpy as jnp
import numpy as np
from jax import lax
from jax.experimental import pallas as pl
from jax.experimental.pallas import tpu as pltpu
from jax.sharding import PartitionSpec as P

HEAD_DIM = 64
ROT = 32
PAIR = 2 * HEAD_DIM

EPSILON = 1e-05
BLOCKED = -1e30
LOG2E = math.log2(math.e)
BF16 = jnp.bfloat16
F32 = jnp.float32
MIB = 1 << 20
SHORT = pl.CostEstimate(flops=1000, bytes_accessed=1000, transcendentals=0)


def dot_nn(left, right):
    return lax.dot_general(left, right, (((1,), (0,)), ((), ())), preferred_element_type=F32)


def dot_nt(left, right):
    return lax.dot_general(left, right, (((1,), (1,)), ((), ())), preferred_element_type=F32)


def dot_tn(left, right):
    return lax.dot_general(left, right, (((0,), (0,)), ((), ())), preferred_element_type=F32)


def swap_pairs(rows):
    width = rows.shape[1]
    lanes = lax.broadcasted_iota(jnp.int32, rows.shape, 1)
    return jnp.where(lanes % 2 == 0, pltpu.roll(rows, width - 1, 1), pltpu.roll(rows, 1, 1))


def trig_tables(length):
    inverse = 10000.0 ** (-(np.arange(ROT // 2, dtype=np.float32) * np.float32(2.0)) / np.float32(ROT))
    phases = np.arange(length, dtype=np.float32)[:, None] * inverse.astype(np.float32)[None, :]
    cosine = np.ones((length, HEAD_DIM), np.float32)
    sine = np.zeros((length, HEAD_DIM), np.float32)
    cosine[:, :ROT] = np.repeat(np.cos(phases), 2, axis=1)
    sine[:, :ROT] = np.repeat(np.sin(phases), 2, axis=1) * np.tile(np.array([-1.0, 1.0], np.float32), ROT // 2)
    return np.tile(cosine, (1, 2)), np.tile(sine, (1, 2))


def whole(array):
    shape = array.shape
    return pl.BlockSpec(shape, lambda i: (0,) * len(shape))


SCALARS = pl.BlockSpec(memory_space=pltpu.SMEM)


def prep_kernel(hidden_ref, mark_ref, table_ref, gain_ref, bias_ref, stream_ref, normed_ref, turned_ref):
    rows = hidden_ref.shape[0]
    vocab = table_ref.shape[0]
    onehot = (mark_ref[...] == lax.broadcasted_iota(jnp.int32, (rows, vocab), 1)).astype(F32).astype(BF16)
    stream = hidden_ref[...].astype(F32) + dot_nn(onehot, table_ref[...])
    centre = stream - jnp.mean(stream, axis=-1, keepdims=True)
    spread = jnp.mean(centre * centre, axis=-1, keepdims=True)
    normed = centre * lax.rsqrt(spread + EPSILON) * gain_ref[...] + bias_ref[...]
    stream_ref[...] = stream
    normed_ref[...] = normed.astype(BF16)
    turned_ref[...] = normed.astype(BF16).T


def prepare(hidden, marked, table, gain, bias):
    rows, width = hidden.shape
    step = 128
    return pl.pallas_call(
        prep_kernel,
        grid=(rows // step,),
        in_specs=[
            pl.BlockSpec((step, width), lambda i: (i, 0)),
            pl.BlockSpec((step, 1), lambda i: (i, 0)),
            pl.BlockSpec(table.shape, lambda i: (0, 0)),
            pl.BlockSpec((1, width), lambda i: (0, 0)),
            pl.BlockSpec((1, width), lambda i: (0, 0)),
        ],
        out_specs=[
            pl.BlockSpec((step, width), lambda i: (i, 0)),
            pl.BlockSpec((step, width), lambda i: (i, 0)),
            pl.BlockSpec((width, step), lambda i: (0, i)),
        ],
        out_shape=[
            jax.ShapeDtypeStruct((rows, width), F32),
            jax.ShapeDtypeStruct((rows, width), BF16),
            jax.ShapeDtypeStruct((width, rows), BF16),
        ],
        cost_estimate=SHORT,
        name="prep",
    )(hidden, marked, table, gain, bias)


def mixed_grad_kernel(owners_ref, cot_ref, weight_ref, *out_refs):
    for shift, out_ref in enumerate(out_refs):

        @pl.when(pl.program_id(0) == shift)
        def _():
            out_ref[...] = dot_nt(cot_ref[...], weight_ref[...]).astype(BF16)


def mixed_grads(order, cot, out_weight):
    rows, width = cot.shape
    owners = order.shape[0]
    wide = width // owners
    return pl.pallas_call(
        mixed_grad_kernel,
        grid_spec=pltpu.PrefetchScalarGridSpec(
            num_scalar_prefetch=1,
            grid=(owners,),
            in_specs=[
                pl.BlockSpec((rows, width), lambda i, o: (0, 0)),
                pl.BlockSpec((wide, width), lambda i, o: (o[i], 0)),
            ],
            out_specs=[pl.BlockSpec((rows, wide), lambda i, o: (0, 0))] * owners,
        ),
        out_shape=[jax.ShapeDtypeStruct((rows, wide), BF16)] * owners,
        cost_estimate=SHORT,
        name="mixed_grads",
    )(order, cot, out_weight)


def heads_kernel(owners, me_ref, *refs):
    below, above = refs[:owners], (None,) + refs[owners : 2 * owners - 1]
    wq_ref, wk_ref, wv_ref, cos_ref, sin_ref, normed_ref = refs[2 * owners - 1 : 2 * owners + 5]
    out_refs = refs[2 * owners + 5 :]
    me = me_ref[0]
    rows = below[0].shape[0]
    chunks = len(out_refs)
    for shift in range(owners):
        block = below[shift][...]
        if shift:
            block = jnp.where(me >= shift, block, above[owners - shift][...])
        start = pl.multiple_of(lax.rem(me - shift + owners, owners) * rows, rows)
        places = pl.ds(start, rows)
        normed_ref[places, :] = block
        cosine = jnp.concatenate([cos_ref[places, :]] * chunks, axis=1)
        sine = jnp.concatenate([sin_ref[places, :]] * chunks, axis=1)
        for number, ref in enumerate((wq_ref, wk_ref, wv_ref)):
            part = dot_nn(block, ref[...])
            if number < 2:
                part = part * cosine + swap_pairs(part) * sine
            part = part.astype(BF16)
            for chunk in range(chunks):
                out_refs[chunk][places, number * PAIR : (number + 1) * PAIR] = part[
                    :, chunk * PAIR : (chunk + 1) * PAIR
                ]


def heads_of(me, below, above, qkv_weight, cosine, sine):
    owners = len(below)
    rows, width = below[0].shape
    wide = width // owners
    chunks = wide // PAIR

    def all_of(array):
        return pl.BlockSpec(array.shape, lambda i, o: (0, 0))

    def columns(part):
        return pl.BlockSpec((width, wide), lambda i, o: (0, part * owners + o[0]))

    shapes = [jax.ShapeDtypeStruct((rows * owners, width), BF16)] + [
        jax.ShapeDtypeStruct((rows * owners, 3 * PAIR), BF16)
    ] * chunks
    blocks = (*below, *above)
    return pl.pallas_call(
        lambda *refs: heads_kernel(owners, *refs),
        grid_spec=pltpu.PrefetchScalarGridSpec(
            num_scalar_prefetch=1,
            grid=(1,),
            in_specs=[all_of(block) for block in blocks]
            + [columns(part) for part in range(3)]
            + [all_of(cosine), all_of(sine)],
            out_specs=[all_of(shape) for shape in shapes],
        ),
        out_shape=shapes,
        compiler_params=pltpu.CompilerParams(vmem_limit_bytes=56 * MIB),
        cost_estimate=SHORT,
        name="heads",
    )(me, *blocks, qkv_weight, qkv_weight, qkv_weight, cosine, sine)


QUERY_ROWS = 512
KEY_ROWS = 512


def attention_kernel(pieces, chunk, info_ref, held, *refs):
    piece_refs = refs[:pieces]
    cos_ref, sin_ref = refs[pieces : pieces + 2]
    out_refs = refs[pieces + 2 : -7]
    grads_held, results, key_turned, value_turned, raised_ref, key_sum, value_sum = refs[-7:]
    me, end = info_ref[0], info_ref[1]
    rows = piece_refs[0].shape[0]
    length = rows * pieces
    for shift in range(pieces):
        start = pl.multiple_of(lax.rem(me - shift + pieces, pieces) * rows, rows)
        grads_held[pl.ds(start, rows), :] = piece_refs[shift][:, chunk * PAIR : (chunk + 1) * PAIR]
    key_turned[...] = held[:, PAIR : 2 * PAIR].T
    value_turned[...] = held[:, 2 * PAIR : 3 * PAIR].T
    key_sum[...] = jnp.zeros_like(key_sum)
    value_sum[...] = jnp.zeros_like(value_sum)
    scale = 0.125 * LOG2E
    halves = lax.broadcasted_iota(jnp.int32, (QUERY_ROWS, PAIR), 1) // HEAD_DIM

    def query_block(number, carry):
        first = pl.multiple_of(number * QUERY_ROWS, QUERY_ROWS)
        query_rows = held[pl.ds(first, QUERY_ROWS), 0:PAIR]
        grad_rows = grads_held[pl.ds(first, QUERY_ROWS), :]
        zero = jnp.zeros_like(query_rows)
        queries = [jnp.where(halves == head, query_rows, zero) for head in range(2)]
        grads = [jnp.where(halves == head, grad_rows, zero) for head in range(2)]
        query_places = first + lax.broadcasted_iota(jnp.int32, (1, QUERY_ROWS), 1)
        lowest = jnp.where(query_places > end, end + 1, 0)
        blocks = (number + 1) * (QUERY_ROWS // KEY_ROWS)

        def scores_of(block, highest):
            start = pl.multiple_of(block * KEY_ROWS, KEY_ROWS)
            keys = held[pl.ds(start, KEY_ROWS), PAIR : 2 * PAIR]
            key_places = start + lax.broadcasted_iota(jnp.int32, (KEY_ROWS, QUERY_ROWS), 0)
            seen = (key_places <= query_places) & (key_places >= lowest)
            after = []
            for head in range(2):
                scores = jnp.where(seen, dot_nt(keys, queries[head]) * scale, BLOCKED)
                raised_ref[head, pl.ds(start, KEY_ROWS), :] = scores
                after.append(jnp.maximum(highest[head], jnp.max(scores, axis=0, keepdims=True)))
            return tuple(after)

        start_row = jnp.full((1, QUERY_ROWS), BLOCKED, F32)
        highest = lax.fori_loop(0, blocks, scores_of, (start_row, start_row))

        def mix(block, carried):
            start = pl.multiple_of(block * KEY_ROWS, KEY_ROWS)
            after = []
            for head in range(2):
                total, mixed = carried[head]
                raised = jnp.exp2(raised_ref[head, pl.ds(start, KEY_ROWS), :] - highest[head])
                raised_ref[head, pl.ds(start, KEY_ROWS), :] = raised
                values = value_turned[head * HEAD_DIM : (head + 1) * HEAD_DIM, pl.ds(start, KEY_ROWS)]
                after.append(
                    (total + jnp.sum(raised, axis=0, keepdims=True), mixed + dot_nn(values, raised.astype(BF16)))
                )
            return tuple(after)

        empty = (jnp.zeros((1, QUERY_ROWS), F32), jnp.zeros((HEAD_DIM, QUERY_ROWS), F32))
        mixes = lax.fori_loop(0, blocks, mix, (empty, empty))
        inverse = [1.0 / mixes[head][0] for head in range(2)]
        mixed = jnp.concatenate([mixes[head][1] * inverse[head] for head in range(2)], axis=0)
        grad_turned = grad_rows.astype(F32).T
        products = mixed * grad_turned
        delta = [
            jnp.sum(products[head * HEAD_DIM : (head + 1) * HEAD_DIM], axis=0, keepdims=True) for head in range(2)
        ]

        def back(block, carried):
            start = pl.multiple_of(block * KEY_ROWS, KEY_ROWS)
            values = held[pl.ds(start, KEY_ROWS), 2 * PAIR : 3 * PAIR]
            after, key_terms, value_terms = [], [], []
            for head in range(2):
                probs = raised_ref[head, pl.ds(start, KEY_ROWS), :] * inverse[head]
                prob_grad = dot_nt(values, grads[head])
                score_grad = (probs * (prob_grad - delta[head])).astype(BF16)
                value_terms.append(dot_nn(probs.astype(BF16), grads[head]))
                key_terms.append(dot_nn(score_grad, queries[head]))
                keys = key_turned[head * HEAD_DIM : (head + 1) * HEAD_DIM, pl.ds(start, KEY_ROWS)]
                after.append(carried[head] + dot_nn(keys, score_grad))
            value_sum[pl.ds(start, KEY_ROWS), :] += value_terms[0] + value_terms[1]
            key_sum[pl.ds(start, KEY_ROWS), :] += key_terms[0] + key_terms[1]
            return tuple(after)

        query_grads = lax.fori_loop(0, blocks, back, (empty[1], empty[1]))
        query_grad = jnp.concatenate(query_grads, axis=0).T * 0.125
        cosine = cos_ref[pl.ds(first, QUERY_ROWS), :]
        sine = sin_ref[pl.ds(first, QUERY_ROWS), :]
        results[pl.ds(first, QUERY_ROWS), 0:PAIR] = (query_grad * cosine - swap_pairs(query_grad) * sine).astype(BF16)
        results[pl.ds(first, QUERY_ROWS), 3 * PAIR : 4 * PAIR] = mixed.T.astype(BF16)
        return carry

    lax.fori_loop(0, length // QUERY_ROWS, query_block, 0)
    key_grad = key_sum[...] * 0.125
    results[:, PAIR : 2 * PAIR] = (key_grad * cos_ref[...] - swap_pairs(key_grad) * sin_ref[...]).astype(BF16)
    results[:, 2 * PAIR : 3 * PAIR] = value_sum[...].astype(BF16)
    for shift in range(pieces):
        start = pl.multiple_of(lax.rem(me + shift, pieces) * rows, rows)
        wide = out_refs[shift].shape[1]
        out_refs[shift][...] = results[pl.ds(start, rows), :wide]
        if len(out_refs) > pieces:
            out_refs[pieces + shift][...] = results[pl.ds(start, rows), wide:]


def attention(info, chunk, heads, parts, cosine, sine, apart):
    pieces = len(parts)
    rows = parts[0].shape[0]
    length = rows * pieces
    arrays = (heads, *parts, cosine, sine)
    shapes = [jax.ShapeDtypeStruct((rows, 4 * PAIR), BF16)] * pieces
    if apart:
        shapes = [jax.ShapeDtypeStruct((rows, wide * PAIR), BF16) for wide in (3, 1) for _ in range(pieces)]
    return pl.pallas_call(
        lambda *refs: attention_kernel(pieces, chunk, *refs),
        grid=(1,),
        in_specs=[SCALARS] + [whole(array) for array in arrays],
        out_specs=[whole(shape) for shape in shapes],
        out_shape=shapes,
        scratch_shapes=[
            pltpu.VMEM((length, PAIR), BF16),
            pltpu.VMEM((length, 4 * PAIR), BF16),
            pltpu.VMEM((PAIR, length), BF16),
            pltpu.VMEM((PAIR, length), BF16),
            pltpu.VMEM((2, length, QUERY_ROWS), F32),
            pltpu.VMEM((length, PAIR), F32),
            pltpu.VMEM((length, PAIR), F32),
        ],
        compiler_params=pltpu.CompilerParams(vmem_limit_bytes=48 * MIB),
        cost_estimate=SHORT,
        name="attention",
    )(info, *arrays)


def feed_kernel(first, *refs):
    normed_ref, turned_ref, cot_ref, in_ref, bias_ref, down_ref = refs[1:7]
    in_grad, down_grad, bias_grad, out_sum, norm_sum = refs[-5:]
    step = pl.program_id(0)
    up = math.sqrt(2.0 / math.pi)

    @pl.when(step == 0)
    def _():
        if first:
            out_sum[...] = jnp.zeros_like(out_sum)
            norm_sum[...] = jnp.zeros_like(norm_sum)
        else:
            out_sum[...] = refs[7][...]
            norm_sum[...] = refs[8][...]

    weights = in_ref[...]
    downs = down_ref[...]
    cot = cot_ref[...]
    pre = dot_nn(normed_ref[...], weights) + bias_ref[...]
    square = pre * pre
    tanh = jnp.tanh(up * pre * (1.0 + 0.044715 * square))
    half = 0.5 * (1.0 + tanh)
    active = (pre * half).astype(BF16)
    slope = half + 0.5 * pre * (1.0 - tanh * tanh) * (up * (1.0 + 3 * 0.044715 * square))
    pre_grad = (dot_nt(cot, downs) * slope).astype(BF16)
    pieces, owners, kept, tile = in_grad.shape
    term = dot_nn(turned_ref[...], pre_grad).astype(BF16)
    for owner in range(owners):
        for piece in range(pieces):
            start = (owner * pieces + piece) * kept
            in_grad[piece, owner] = term[start : start + kept]
    term = dot_tn(active, cot).astype(BF16)
    kept = tile // pieces
    for group in range(term.shape[1] // tile):
        for piece in range(pieces):
            down_grad[piece, 0, group * kept : (group + 1) * kept] = term[
                piece * kept : (piece + 1) * kept, group * tile : (group + 1) * tile
            ]
    bias_grad[0] = jnp.sum(pre_grad.astype(F32), axis=0, keepdims=True)
    out_sum[...] += dot_nn(active, downs)
    norm_sum[...] += dot_nt(pre_grad, weights)


def feed_half(cells, normed, turned, cot, in_weight, in_bias, down_weight, pieces, sums=()):
    rows, width = normed.shape
    owners = cells.shape[0]
    hidden_units = in_weight.shape[1]
    tile = hidden_units // (2 * owners)
    kept = width // owners // pieces
    tall = owners * kept
    wide = tile // pieces * (width // tile)
    fixed = pl.BlockSpec((rows, width), lambda i, c: (0, 0))
    return pl.pallas_call(
        lambda *refs: feed_kernel(not sums, *refs),
        grid_spec=pltpu.PrefetchScalarGridSpec(
            num_scalar_prefetch=1,
            grid=(owners,),
            in_specs=[
                fixed,
                pl.BlockSpec((width, rows), lambda i, c: (0, 0)),
                fixed,
                pl.BlockSpec((width, tile), lambda i, c: (0, c[i])),
                pl.BlockSpec((1, tile), lambda i, c: (0, c[i])),
                pl.BlockSpec((tile, width), lambda i, c: (c[i], 0)),
            ]
            + [fixed] * len(sums),
            out_specs=[
                pl.BlockSpec((pieces, owners, kept, tile), lambda i, c: (0, 0, i, 0)),
                pl.BlockSpec((pieces, 1, wide, tile), lambda i, c: (0, i, 0, 0)),
                pl.BlockSpec((1, 1, tile), lambda i, c: (i, 0, 0)),
                fixed,
                fixed,
            ],
        ),
        out_shape=[
            jax.ShapeDtypeStruct((pieces, owners, tall, tile), BF16),
            jax.ShapeDtypeStruct((pieces, owners, wide, tile), BF16),
            jax.ShapeDtypeStruct((owners, 1, tile), F32),
            jax.ShapeDtypeStruct((rows, width), F32),
            jax.ShapeDtypeStruct((rows, width), F32),
        ],
        compiler_params=pltpu.CompilerParams(vmem_limit_bytes=60 * MIB),
        cost_estimate=SHORT,
        name="feed",
    )(cells, normed, turned, cot, in_weight, in_bias, down_weight, *sums)


def qkv_grad_kernel(info_ref, normed_ref, *refs):
    kept_ref, sent_ref, turned = refs[-3:]
    chunks = kept_ref.shape[-1] // PAIR
    owners = (len(refs) - 3) // chunks
    pieces, kept = kept_ref.shape[0], kept_ref.shape[2] // 3
    rows = refs[0].shape[0]
    for chunk in range(chunks):
        total = None
        for shift in range(owners):
            start = pl.multiple_of(lax.rem(info_ref[0] + shift, owners) * rows, rows)
            term = dot_tn(refs[chunk * owners + shift][:, : 3 * PAIR], normed_ref[pl.ds(start, rows), :])
            total = term if total is None else total + term
        turned[...] = total.T.astype(BF16)
        for side, ref in enumerate((kept_ref, sent_ref)):
            core = info_ref[1] ^ side
            for owner in range(owners):
                for piece in range(pieces):
                    start = pl.multiple_of(((owner * 2 + core) * pieces + piece) * kept, kept)
                    rows_of = turned[pl.ds(start, kept), :]
                    for part in range(3):
                        ref[piece, owner, part * kept : (part + 1) * kept, chunk * PAIR : (chunk + 1) * PAIR] = rows_of[
                            :, part * PAIR : (part + 1) * PAIR
                        ]


def qkv_grads(info, normed, parts, pieces):
    owners, chunks = len(parts[0]), len(parts)
    length, width = normed.shape
    kept = width // owners // 2 // pieces
    arrays = (normed, *[block for blocks in parts for block in blocks])
    shape = jax.ShapeDtypeStruct((pieces, owners, 3 * kept, chunks * PAIR), BF16)
    return pl.pallas_call(
        qkv_grad_kernel,
        grid=(1,),
        in_specs=[SCALARS] + [whole(array) for array in arrays],
        out_specs=[whole(shape)] * 2,
        out_shape=[shape] * 2,
        scratch_shapes=[pltpu.VMEM((width, 3 * PAIR), BF16)],
        compiler_params=pltpu.CompilerParams(vmem_limit_bytes=48 * MIB),
        cost_estimate=SHORT,
        name="qkv_grads",
    )(info, *arrays)


def out_kernel(owners, chunks, info_ref, *refs):
    piece_refs, refs = refs[: owners * chunks], refs[owners * chunks :]
    stream_ref, cot_ref, weight_ref, sum_ref, bias_ref, out_ref, kept_ref, sent_ref, held, grad = refs
    for chunk in range(chunks):
        for shift in range(owners):
            owner = lax.rem(info_ref[0] - shift + owners, owners)
            start = pl.multiple_of((owner * chunks + chunk) * PAIR, PAIR)
            held[:, pl.ds(start, PAIR)] = piece_refs[chunk * owners + shift][:, -PAIR:]
    cot = cot_ref[...]
    mixed = held[...]
    grad[...] = dot_tn(mixed, cot).astype(BF16)
    pieces, total, wide = kept_ref.shape[0], kept_ref.shape[2], kept_ref.shape[3]
    kept = grad.shape[0] // owners // pieces
    groups = total // kept
    for side, ref in enumerate((kept_ref, sent_ref)):
        core = info_ref[1] ^ side
        for group in range(groups):
            columns = pl.ds(pl.multiple_of((core * groups + group) * wide, wide), wide)
            for owner in range(owners):
                for piece in range(pieces):
                    start = (owner * pieces + piece) * kept
                    ref[piece, owner, group * kept : (group + 1) * kept] = grad[start : start + kept, columns]
    out_ref[...] = (stream_ref[...] + sum_ref[...] + dot_nn(mixed, weight_ref[...]) + bias_ref[...]).astype(BF16)


def out_parts(info, parts, stream, cot, out_weight, out_sum, down_bias, pieces):
    owners, chunks = len(parts[0]), len(parts)
    rows, width = cot.shape
    kept = width // owners // pieces
    wide = chunks * PAIR
    arrays = (*[block for blocks in parts for block in blocks], stream, cot, out_weight, out_sum, down_bias)
    side = jax.ShapeDtypeStruct((pieces, owners, kept * (width // 2 // wide), wide), BF16)
    shapes = [jax.ShapeDtypeStruct((rows, width), BF16), side, side]
    return pl.pallas_call(
        lambda *refs: out_kernel(owners, chunks, *refs),
        grid=(1,),
        in_specs=[SCALARS] + [whole(array) for array in arrays],
        out_specs=[whole(shape) for shape in shapes],
        out_shape=shapes,
        scratch_shapes=[pltpu.VMEM((rows, width), BF16), pltpu.VMEM((width, width), BF16)],
        compiler_params=pltpu.CompilerParams(vmem_limit_bytes=48 * MIB),
        cost_estimate=SHORT,
        name="out_parts",
    )(info, *arrays)


def norm_kernel(last, owners, me_ref, *refs):
    piece_refs, refs = refs[:owners], refs[owners:]
    weight_refs, refs = refs[: 3 * owners], refs[3 * owners :]
    norm_in, held = refs[0], refs[-1]
    for shift in range(owners):
        owner = lax.rem(me_ref[0] - shift + owners, owners)
        start = pl.multiple_of(owner * PAIR, PAIR)
        for part in range(3):
            held[part, :, pl.ds(start, PAIR)] = piece_refs[shift][:, part * PAIR : (part + 1) * PAIR]
    norm = norm_in[...]
    for part in range(3):
        weights = jnp.concatenate([ref[...] for ref in weight_refs[part * owners : (part + 1) * owners]], axis=1)
        norm = norm + dot_nt(held[part], weights)
    if not last:
        refs[1][...] = norm
        return
    stream_ref, cot_ref, gain_ref, hidden_ref, gain_grad, bias_grad = refs[1:-1]
    stream = stream_ref[...]
    centre = stream - jnp.mean(stream, axis=-1, keepdims=True)
    spread = jnp.mean(centre * centre, axis=-1, keepdims=True)
    inverse = lax.rsqrt(spread + EPSILON)
    hat = centre * inverse
    gained = norm * gain_ref[...]
    hidden_ref[...] = cot_ref[...].astype(F32) + inverse * (
        gained
        - jnp.mean(gained, axis=-1, keepdims=True)
        - hat * jnp.mean(gained * hat, axis=-1, keepdims=True)
    )
    gain_grad[...] = jnp.sum(norm * hat, axis=0, keepdims=True)
    bias_grad[...] = jnp.sum(norm, axis=0, keepdims=True)


def norm_parts(me, chunk, chunks, parts, qkv_weight, norm_sum, final=()):
    owners = len(parts)
    rows = parts[0].shape[0]
    width = qkv_weight.shape[0]
    last = bool(final)

    def columns(part, owner):
        at = (part * owners + owner) * chunks + chunk
        return pl.BlockSpec((width, PAIR), lambda i: (0, at))

    full = jax.ShapeDtypeStruct((rows, width), F32)
    row = jax.ShapeDtypeStruct((1, width), F32)
    shapes = [full, row, row] if last else [full]
    return pl.pallas_call(
        lambda *refs: norm_kernel(last, owners, *refs),
        grid=(1,),
        in_specs=[SCALARS]
        + [whole(part) for part in parts]
        + [columns(part, owner) for part in range(3) for owner in range(owners)]
        + [whole(array) for array in (norm_sum, *final)],
        out_specs=[whole(shape) for shape in shapes],
        out_shape=shapes,
        scratch_shapes=[pltpu.VMEM((3, rows, owners * PAIR), BF16)],
        compiler_params=pltpu.CompilerParams(vmem_limit_bytes=56 * MIB),
        cost_estimate=SHORT,
        name="norm_parts",
    )(me[None], *parts, *([qkv_weight] * (3 * owners)), norm_sum, *final)


def piece_of(device, half):
    first, second = (device >> 1) & 1, device >> 2
    return (half * 2 + (second if half else first)) * 2 + (first if half else second)


def feed_place_kernel(info_ref, mine_ref, other_ref, in_ref, down_ref):
    masks, total, tile = mine_ref.shape
    own_rows = in_ref.shape[0]
    kept = own_rows // 2 // masks
    tiles = in_ref.shape[1] // (2 * tile)
    rows_here = down_ref.shape[0] // 2
    down_kept = rows_here // 2 // masks
    for source, ref in enumerate((mine_ref, other_ref)):
        for mask in range(masks):
            device = info_ref[0] ^ (2 * mask + source)
            core = device & 1
            for half in range(2):
                piece = piece_of(device, half)
                at = half * (total // 2)
                rows = pl.ds(pl.multiple_of(piece * kept, kept), kept)
                for number in range(tiles):
                    columns = pl.ds(pl.multiple_of((2 * number + core) * tile, tile), tile)
                    in_ref[rows, columns] = ref[mask, at + number * kept : at + (number + 1) * kept].astype(F32)
                at += tiles * kept
                rows = pl.ds(pl.multiple_of(core * rows_here + piece * down_kept, down_kept), down_kept)
                for group in range(down_ref.shape[1] // tile):
                    down_ref[rows, group * tile : (group + 1) * tile] = ref[
                        mask, at + group * down_kept : at + (group + 1) * down_kept
                    ].astype(F32)


def place_feed(info, mine, other, in_shape, down_shape):
    shapes = [jax.ShapeDtypeStruct(in_shape, F32), jax.ShapeDtypeStruct(down_shape, F32)]
    return pl.pallas_call(
        feed_place_kernel,
        grid=(1,),
        in_specs=[SCALARS, whole(mine), whole(other)],
        out_specs=[whole(shape) for shape in shapes],
        out_shape=shapes,
        compiler_params=pltpu.CompilerParams(vmem_limit_bytes=48 * MIB),
        cost_estimate=SHORT,
        name="place_feed",
    )(info, mine, other)


def heads_place_kernel(info_ref, mine_ref, other_ref, qkv_ref, out_ref):
    masks, total, wide = mine_ref.shape
    own_rows, width = out_ref.shape
    owners = width // wide
    kept = own_rows // 4 // masks
    out_kept = own_rows // 2 // masks
    groups = width // 2 // wide
    for source, ref in enumerate((mine_ref, other_ref)):
        for mask in range(masks):
            device = info_ref[0] ^ (2 * mask + source)
            core = device & 1
            for half in range(2):
                piece = piece_of(device, half)
                rows = pl.ds(pl.multiple_of(core * (own_rows // 2) + piece * kept, kept), kept)
                for seq_mask in range(owners):
                    owner = info_ref[1] ^ seq_mask
                    for part in range(3):
                        columns = pl.ds(pl.multiple_of(part * width + owner * wide, wide), wide)
                        at = (seq_mask * 2 + half) * 3 * kept + part * kept
                        qkv_ref[rows, columns] = ref[mask, at : at + kept].astype(F32)
                rows = pl.ds(pl.multiple_of(piece * out_kept, out_kept), out_kept)
                for group in range(groups):
                    columns = pl.ds(pl.multiple_of(core * (width // 2) + group * wide, wide), wide)
                    at = owners * 2 * 3 * kept + (half * groups + group) * out_kept
                    out_ref[rows, columns] = ref[mask, at : at + out_kept].astype(F32)


def place_heads(info, mine, other, own_rows, width):
    shapes = [jax.ShapeDtypeStruct((own_rows, 3 * width), F32), jax.ShapeDtypeStruct((own_rows, width), F32)]
    return pl.pallas_call(
        heads_place_kernel,
        grid=(1,),
        in_specs=[SCALARS, whole(mine), whole(other)],
        out_specs=[whole(shape) for shape in shapes],
        out_shape=shapes,
        compiler_params=pltpu.CompilerParams(vmem_limit_bytes=48 * MIB),
        cost_estimate=SHORT,
        name="place_heads",
    )(info, mine, other)


def exchange(rows, axis, mask):
    size = lax.axis_size(axis)
    return lax.ppermute(rows, axis, [(place, place ^ mask) for place in range(size)])


def around(rows, shift):
    owners = lax.axis_size("seq")
    return lax.ppermute(rows, "seq", [(place, (place + shift) % owners) for place in range(owners)])


def total_of(*terms):
    return sum(term.astype(F32) for term in terms).astype(BF16)


def picked(rows, index, dim=0):
    return lax.dynamic_index_in_dim(rows, index, dim, keepdims=False)


def add_kernel(places, bits_ref, *refs):
    outs = refs[len(refs) - len(places) :]
    for out_ref, terms in zip(outs, places):
        at = 0
        for left, right in terms:
            rows = refs[left].shape[-2]
            total = refs[left][...].astype(F32) + refs[right][...].astype(F32)
            out_ref[..., at : at + rows, :] = total.reshape(out_ref.shape[:-2] + total.shape[-2:]).astype(BF16)
            at += rows


def add_after_core(bits, kept, arrived):
    pairs = len(kept)
    owners = kept[0].shape[1]
    specs, places, arrays = [], [], []
    for half in range(2):
        for side in (1, 0):
            terms = []
            for mine, other in zip(kept, arrived):
                block = (1, 1) + mine.shape[2:]

                def index(i, j, b, half=half, side=side):
                    return (half * 4 + (b[half] ^ side) * 2 + i, j, 0, 0)

                terms.append((len(arrays), len(arrays) + 1))
                arrays += [mine, other]
                specs += [pl.BlockSpec(block, index)] * 2
            places.append(terms)
    rows = sum(array.shape[2] for array in kept)
    columns = kept[0].shape[3]
    out = jax.ShapeDtypeStruct((2, owners, rows, columns), BF16)
    results = pl.pallas_call(
        lambda *refs: add_kernel(places, *refs),
        grid_spec=pltpu.PrefetchScalarGridSpec(
            num_scalar_prefetch=1,
            grid=(2, owners),
            in_specs=specs,
            out_specs=[pl.BlockSpec((1, 1, rows, columns), lambda i, j, b: (i, j, 0, 0))] * 4,
        ),
        out_shape=[out] * 4,
        cost_estimate=SHORT,
        name="add_after_core",
    )(bits, *arrays)
    return [results[:2], results[2:]]


def add_after_first(bits, held, arrived):
    specs, places, arrays = [], [], []
    owners, rows, columns = held[0][1].shape[1:]
    for half in range(2):
        for side in (1, 0):

            def index(j, b, half=half, side=side):
                return (b[1 - half] ^ side, j, 0, 0)

            places.append([(len(arrays), len(arrays) + 1)])
            arrays += [held[half][1], arrived[half]]
            specs += [pl.BlockSpec((1, 1, rows, columns), index)] * 2
    out = jax.ShapeDtypeStruct((owners, rows, columns), BF16)
    results = pl.pallas_call(
        lambda *refs: add_kernel(places, *refs),
        grid_spec=pltpu.PrefetchScalarGridSpec(
            num_scalar_prefetch=1,
            grid=(owners,),
            in_specs=specs,
            out_specs=[pl.BlockSpec((1, rows, columns), lambda j, b: (j, 0, 0))] * 4,
        ),
        out_shape=[out] * 4,
        cost_estimate=SHORT,
        name="add_after_first",
    )(bits, *arrays)
    return [results[:2], results[2:]]


def add_after_second(held, arrived):
    owners, rows, columns = held[0][1].shape
    arrays = [held[0][1], arrived[0], held[1][1], arrived[1]]
    return pl.pallas_call(
        lambda *refs: add_kernel([[(0, 1), (2, 3)]], None, *refs),
        grid=(owners,),
        in_specs=[pl.BlockSpec((1, rows, columns), lambda j: (j, 0, 0))] * 4,
        out_specs=pl.BlockSpec((1, 2 * rows, columns), lambda j: (j, 0, 0)),
        out_shape=jax.ShapeDtypeStruct((owners, 2 * rows, columns), BF16),
        cost_estimate=SHORT,
        name="add_after_second",
    )(*arrays)


def cross(held, level):
    return [exchange(held[half][0], "batch", 2 << (half ^ level)) for half in range(2)]


def all_sum(rows):
    rows = rows + exchange(rows, "batch", 1)
    rows = sum((exchange(rows, "batch", mask) for mask in range(2, lax.axis_size("batch"), 2)), rows)
    return sum((around(rows, shift) for shift in range(1, lax.axis_size("seq"))), rows)


class Order:
    token = None

    def __call__(self, value):
        if self.token is None:
            return value
        return lax.optimization_barrier((value, self.token))[0]

    def done(self, token):
        self.token = token
        return token

    def also(self, *tokens):
        self.token = (self.token, tokens)


def fast_body(
    hidden,
    token_ids,
    offsets,
    end_places,
    token_table,
    norm_gain,
    norm_bias,
    qkv_weight,
    out_weight,
    in_weight,
    in_bias,
    down_weight,
    down_bias,
    cotangent,
):
    width = hidden.shape[2]
    rows = hidden.shape[1]
    owners = lax.axis_size("seq")
    pieces = lax.axis_size("batch")
    me = lax.axis_index("seq")
    core = lax.axis_index("batch") & 1
    length = rows * owners
    own_rows = width // owners
    chunks = own_rows // PAIR
    end = end_places[0]

    places = me * rows + jnp.arange(rows, dtype=jnp.int32)[:, None]
    marked = token_ids.reshape(rows, 1)
    marked = jnp.where(places == end, 2, marked)
    marked = jnp.where(places == end + 1, 1, marked)
    marked = jnp.where((places == 0) & (offsets[0] == 0), 1, marked)
    cot = cotangent.reshape(rows, width)
    stream, normed, turned = prepare(
        hidden.reshape(rows, width), marked, token_table, norm_gain[None], norm_bias[None]
    )
    cosine, sine = (jnp.asarray(table) for table in trig_tables(length))

    def up(block):
        return lax.ppermute(block, "seq", [(place, place + 1) for place in range(owners - 1)])

    def down(block):
        return lax.ppermute(block, "seq", [(place + 1, place) for place in range(owners - 1)])

    def far_first(blocks):
        moved = {shift: around(blocks[shift], shift) for shift in (2, 1, 3)}
        return [blocks[0]] + [moved[shift] for shift in (1, 2, 3)]

    def back(rows):
        return [exchange(rows, "batch", mask) for mask in (2, 4, 6)]

    place = lax.axis_index("batch")
    info = jnp.stack([me, core]).astype(jnp.int32)
    batch_info = jnp.stack([place, me]).astype(jnp.int32)
    bits = jnp.stack([(place >> 1) & 1, place >> 2]).astype(jnp.int32)
    order = Order()

    order.done(normed)
    below, above = [normed, up(normed)], [down(normed)]
    shifts = lax.rem(me + jnp.arange(owners, dtype=jnp.int32), owners)
    grads = order.done(mixed_grads(shifts, order(cot), out_weight))
    head_grads = [grads[0], None, around(grads[2], 2), None]
    cells = 2 * jnp.arange(owners, dtype=jnp.int32)
    feed_args = (turned, cot, in_weight, in_bias[None], down_weight, pieces)
    away = order.done(feed_half(cells + 1 - core, order(normed), *feed_args))
    order.also(below[1], above[0], head_grads[2])

    feed_arrived = [exchange(array, "batch", 1) for array in order(away[:2])]
    below.append(up(order(below[1])))
    above.append(down(order(above[0])))
    head_grads[1] = around(order(grads[1]), 1)
    here = order.done(feed_half(cells + core, order(normed), *feed_args, sums=tuple(away[3:])))
    order.also(below[2], above[1], head_grads[1], feed_arrived)
    out_sum, norm_sum = here[3:]

    below.append(up(order(below[2])))
    above.append(down(order(above[1])))
    head_grads[3] = around(order(grads[3]), 3)
    feed_held = order.done(add_after_core(bits, order(here[:2]), feed_arrived))
    order.also(below[3], above[2], head_grads[3])

    feed_arrived = cross(order(feed_held), 0)
    normed_all, *heads = order.done(heads_of(me[None], order(below), above, qkv_weight, cosine, sine))
    spots = jnp.stack([me, end]).astype(jnp.int32)
    first = order.done(attention(spots, 0, order(heads[0]), head_grads, cosine, sine, False))
    first_back = far_first(first)
    order.also(feed_arrived)
    feed_held = order.done(add_after_first(bits, order(feed_held), feed_arrived))

    feed_arrived = cross(feed_held, 1)
    second = order.done(attention(spots, 1, order(heads[1]), head_grads, cosine, sine, True))
    order.also(feed_arrived)
    feed_rows = order.done(add_after_second(order(feed_held), feed_arrived))

    def halve_seq(rows, number):
        bit = (me >> number) & 1
        split = rows.reshape((rows.shape[0] // 2, 2) + rows.shape[1:])
        return picked(split, bit, 1), exchange(picked(split, 1 - bit, 1), "seq", 1 << number)

    head_kept, head_sent = order.done(qkv_grads(info, order(normed_all), (first, second[:owners]), pieces))
    order.also(first_back)

    feed_rows, feed_arrived = halve_seq(order(feed_rows), 0)
    mixed_back = far_first(order(second[owners:]))
    norm_sum = order.done(norm_parts(me, 0, chunks, order(first_back), qkv_weight, norm_sum)[0])
    order.also(mixed_back, feed_arrived)
    feed_rows = order.done(total_of(order(feed_rows), feed_arrived))

    feed_rows, feed_arrived = halve_seq(order(feed_rows), 1)
    second_back = [second[0], None, around(order(second[2]), 2), None]
    output, out_kept, out_sent = order.done(
        out_parts(info, (first_back, order(mixed_back)), stream, cot, out_weight, out_sum, down_bias[None], pieces)
    )
    order.also(feed_arrived)
    feed_rows = order.done(total_of(order(feed_rows), feed_arrived))[0]

    feed_back = back(order(feed_rows))
    grad_arrived = [exchange(array, "batch", 1) for array in order((head_sent, out_sent))]
    order.also(grad_arrived)
    grad_held = order.done(add_after_core(bits, order((head_kept, out_kept)), grad_arrived))

    grad_arrived = cross(order(grad_held), 0)
    order.also(second_back[2], feed_back)
    second_back[1] = around(order(second[1]), 1)
    feed_mine = order.done(jnp.stack([feed_rows] + order(feed_back)))
    order.also(grad_arrived)
    grad_held = order.done(add_after_first(bits, order(grad_held), grad_arrived))

    feed_other = exchange(order(feed_mine), "batch", 1)
    grad_arrived = cross(order(grad_held), 1)
    order.also(feed_other)
    in_weight_grad, down_weight_grad = order.done(
        place_feed(
            batch_info,
            order(feed_mine),
            feed_other,
            (own_rows, in_weight.shape[1]),
            (down_weight.shape[0] // owners, width),
        )
    )
    order.also(second_back[1], grad_arrived)
    second_back[3] = around(order(second[3]), 3)
    grad_rows = order.done(add_after_second(order(grad_held), grad_arrived))

    complete = head_kept.shape[2]
    half = grad_rows.shape[1] // 2
    at_start = (slice(0, complete), slice(half, half + complete))
    at_end = (slice(complete, half), slice(half + complete, 2 * half))
    mine, other = halve_seq(order(grad_rows), 0)
    order.also(other)
    other = order(other)
    grad_rows = jnp.concatenate(
        [mine[:, part] for part in at_start]
        + [other[:, part] for part in at_start]
        + [total_of(mine[:, part], other[:, part]) for part in at_end],
        axis=1,
    )
    order.done(grad_rows)
    complete *= 4
    mine, other = halve_seq(order(grad_rows), 1)
    order.also(second_back[3], other)
    mine, other = mine[0], order(other)[0]
    grad_rows = jnp.concatenate(
        [mine[:complete], other[:complete], total_of(mine[complete:], other[complete:])], axis=0
    )
    order.done(grad_rows)
    grad_back = back(order(grad_rows))
    hidden_grad, gain_grad, bias_grad = order.done(
        norm_parts(me, 1, chunks, order(second_back), qkv_weight, norm_sum, (stream, cot, norm_gain[None]))
    )
    order.also(grad_back)
    grad_mine = order.done(jnp.stack([grad_rows] + order(grad_back)))
    qkv_weight_grad, out_weight_grad = place_heads(
        batch_info, grad_mine, exchange(grad_mine, "batch", 1), own_rows, width
    )

    bias_low = jnp.where(core == 0, here[2], away[2])
    bias_high = jnp.where(core == 0, away[2], here[2])
    in_bias_grad = jnp.concatenate([bias_low, bias_high], axis=1)
    cot_sum = jnp.sum(cot.astype(F32), axis=0)
    small = jnp.concatenate(
        [
            in_bias_grad.reshape(owners, -1),
            cot_sum.reshape(owners, -1),
            gain_grad.reshape(owners, -1),
            bias_grad.reshape(owners, -1),
        ],
        axis=1,
    )
    small = picked(all_sum(small), me)
    few = own_rows
    many = in_bias.shape[0] // owners
    return (
        output[None],
        hidden_grad[None],
        small[many + few : many + 2 * few],
        small[many + 2 * few :],
        qkv_weight_grad,
        out_weight_grad,
        in_weight_grad,
        small[:many],
        down_weight_grad,
        small[many : many + few],
    )


def rotate(vectors, cosine_table, sine_table):
    even_part = vectors[..., 0:ROT:2]
    odd_part = vectors[..., 1:ROT:2]
    turned = jnp.stack(
        [
            even_part * cosine_table - odd_part * sine_table,
            odd_part * cosine_table + even_part * sine_table,
        ],
        axis=-1,
    )
    turned = turned.reshape(vectors.shape[:-1] + (ROT,))
    return jnp.concatenate([turned, vectors[..., ROT:]], axis=-1)


def angles(places):
    inverse = 10000.0 ** (-(jnp.arange(ROT // 2, dtype=jnp.float32) * 2.0) / ROT)
    phases = places.astype(jnp.float32)[:, None] * inverse[None, :]
    return (jnp.cos(phases), jnp.sin(phases))


def visible(query_places, key_places, end_places):
    query_after = query_places[None, :, None] > end_places[:, None, None]
    key_after = key_places[None, None, :] > end_places[:, None, None]
    return (key_places[None, None, :] <= query_places[None, :, None]) & (query_after == key_after)


def norm_rows(stream, gain_row, bias_row):
    centre = stream - jnp.mean(stream, axis=-1, keepdims=True)
    spread = jnp.mean(centre * centre, axis=-1, keepdims=True)
    return centre * lax.rsqrt(spread + EPSILON) * gain_row + bias_row


def gelu_rows(pre_active):
    return jax.nn.gelu(pre_active, approximate=True)


def plain_body(
    hidden,
    token_ids,
    offsets,
    end_places,
    token_table,
    norm_gain,
    norm_bias,
    qkv_weight,
    out_weight,
    in_weight,
    in_bias,
    down_weight,
    down_bias,
    cotangent,
):
    windows_here, shard_rows, model_width = hidden.shape
    head_count = model_width // HEAD_DIM
    seq_count = lax.axis_size("seq")
    seq_place = lax.axis_index("seq")
    home_places = seq_place * shard_rows + jnp.arange(shard_rows, dtype=jnp.int32)
    token_rows = shard_rows * windows_here
    marked = token_ids.T
    marked = jnp.where(home_places[:, None] == end_places[None, :], 2, marked)
    marked = jnp.where(home_places[:, None] == end_places[None, :] + 1, 1, marked)
    marked = jnp.where((home_places[:, None] == 0) & (offsets[None, :] == 0), 1, marked)
    onehot = (marked[..., None] == jnp.arange(token_table.shape[0], dtype=jnp.int32)).astype(
        jnp.bfloat16
    )
    embedded = jnp.einsum("swv,vd->swd", onehot, token_table, preferred_element_type=jnp.float32)
    stream_three = jnp.transpose(hidden, (1, 0, 2)).astype(jnp.float32) + embedded
    cot_three = jnp.transpose(cotangent, (1, 0, 2))
    own_high = jnp.max(home_places)
    stream_rows = stream_three.reshape(token_rows, model_width)
    normed, norm_back = jax.vjp(norm_rows, stream_rows, norm_gain, norm_bias)
    normed_low = normed.astype(jnp.bfloat16)
    projected = jnp.dot(normed_low, qkv_weight, preferred_element_type=jnp.float32)
    cosine_table, sine_table = angles(home_places)
    cosine_table = cosine_table[:, None, None, :]
    sine_table = sine_table[:, None, None, :]

    def turn_heads(projected_rows):
        divided = projected_rows.reshape(shard_rows, windows_here, 3, head_count, HEAD_DIM)
        return (
            rotate(divided[:, :, 0], cosine_table, sine_table),
            rotate(divided[:, :, 1], cosine_table, sine_table),
            divided[:, :, 2],
        )

    (queries, key_rows, values), turn_back = jax.vjp(turn_heads, projected)
    query_low = queries.astype(jnp.bfloat16)
    key_value = jnp.concatenate(
        [
            key_rows.reshape(shard_rows, windows_here, model_width),
            values.reshape(shard_rows, windows_here, model_width),
        ],
        axis=-1,
    ).astype(jnp.bfloat16)

    def split_block(key_block):
        row_count = key_block.shape[0]
        return (
            key_block[..., :model_width].reshape(row_count, windows_here, head_count, HEAD_DIM),
            key_block[..., model_width:].reshape(row_count, windows_here, head_count, HEAD_DIM),
        )

    def block_places(row_start, row_count):
        return row_start + jnp.arange(row_count, dtype=jnp.int32)

    def block_scores(key_block, key_start):
        key_part, value_part = split_block(key_block)
        key_places = block_places(key_start, key_block.shape[0])
        scores = (
            jnp.einsum("qwhd,kwhd->whqk", query_low, key_part, preferred_element_type=jnp.float32)
            * 0.125
        )
        scores = jnp.where(visible(home_places, key_places, end_places)[:, None], scores, BLOCKED)
        return (scores, key_part, value_part)

    def attend(carried, key_block, key_start):
        running, totals, accumulated = carried
        scores, key_part, value_part = block_scores(key_block, key_start)
        highest = jnp.maximum(running, jnp.max(scores, axis=-1))
        factor = jnp.exp(running - highest)
        raised = jnp.exp(scores - highest[..., None])
        totals = totals * factor + jnp.sum(raised, axis=-1)
        accumulated = accumulated * factor[..., None] + jnp.einsum(
            "whqk,kwhd->whqd",
            raised.astype(jnp.bfloat16),
            value_part,
            preferred_element_type=jnp.float32,
        )
        return (highest, totals, accumulated)

    start_state = (
        jnp.full((windows_here, head_count, shard_rows), BLOCKED, jnp.float32),
        jnp.zeros((windows_here, head_count, shard_rows), jnp.float32),
        jnp.zeros((windows_here, head_count, shard_rows, HEAD_DIM), jnp.float32),
    )
    carried = start_state
    fetched_rows = lax.all_gather(key_value, "seq", axis=0, tiled=True)
    row_count = fetched_rows.shape[0]
    blocks = fetched_rows.reshape((row_count // shard_rows, shard_rows) + fetched_rows.shape[1:])

    def visit_block(held_state, element):
        number, key_block = element
        key_start = number * shard_rows
        dead = jnp.min(block_places(key_start, shard_rows)) > own_high
        held_state = lax.cond(
            dead,
            lambda kept_state: kept_state,
            lambda kept_state: attend(kept_state, key_block, key_start),
            held_state,
        )
        return (held_state, None)

    carried, unused = lax.scan(
        visit_block, carried, (jnp.arange(blocks.shape[0], dtype=jnp.int32), blocks)
    )
    running, totals, accumulated = carried
    attention = accumulated / totals[..., None]
    log_total = running + jnp.log(totals)
    attention_rows = jnp.transpose(attention, (2, 0, 1, 3))
    mixed_low = attention_rows.reshape(token_rows, model_width).astype(jnp.bfloat16)
    attended = jnp.dot(mixed_low, out_weight, preferred_element_type=jnp.float32)
    pre_active = jnp.dot(normed_low, in_weight, preferred_element_type=jnp.float32) + in_bias
    active, gelu_back = jax.vjp(gelu_rows, pre_active)
    active_low = active.astype(jnp.bfloat16)
    result = (
        stream_rows
        + attended
        + jnp.dot(active_low, down_weight, preferred_element_type=jnp.float32)
        + down_bias
    )
    grad_rows = cot_three.reshape(token_rows, model_width)
    down_weight_grad = jnp.dot(active_low.T, grad_rows, preferred_element_type=jnp.float32)
    down_bias_grad = jnp.sum(grad_rows.astype(jnp.float32), axis=0)
    out_weight_grad = jnp.dot(mixed_low.T, grad_rows, preferred_element_type=jnp.float32)
    active_grad = jnp.dot(grad_rows, down_weight.T, preferred_element_type=jnp.float32)
    pre_grad = gelu_back(active_grad)[0].astype(jnp.bfloat16)
    in_weight_grad = jnp.dot(normed_low.T, pre_grad, preferred_element_type=jnp.float32)
    in_bias_grad = jnp.sum(pre_grad.astype(jnp.float32), axis=0)
    mixed_grad = jnp.dot(grad_rows, out_weight.T, preferred_element_type=jnp.float32).astype(
        jnp.bfloat16
    )
    grad_heads = mixed_grad.reshape(shard_rows, windows_here, head_count, HEAD_DIM)
    delta_rows = jnp.sum(grad_heads.astype(jnp.float32) * attention_rows, axis=-1)
    row_delta = jnp.transpose(delta_rows, (1, 2, 0))
    whole_keys = lax.all_gather(key_value, "seq", axis=0, tiled=True)
    blocks = whole_keys.reshape((seq_count, shard_rows) + whole_keys.shape[1:])
    zero_heads = jnp.zeros((shard_rows, windows_here, head_count, HEAD_DIM), jnp.float32)

    def back_block(query_grad, element):
        number, key_block = element
        key_start = number * shard_rows

        def live_block(held_grad):
            scores, key_part, value_part = block_scores(key_block, key_start)
            weighting = jnp.exp(scores - log_total[..., None])
            prob_grad = jnp.einsum(
                "qwhd,kwhd->whqk", grad_heads, value_part, preferred_element_type=jnp.float32
            )
            score_low = (weighting * (prob_grad - row_delta[..., None])).astype(jnp.bfloat16)
            held_grad = held_grad + 0.125 * jnp.einsum(
                "whqk,kwhd->qwhd", score_low, key_part, preferred_element_type=jnp.float32
            )
            key_grad = 0.125 * jnp.einsum(
                "whqk,qwhd->kwhd", score_low, query_low, preferred_element_type=jnp.float32
            )
            value_grad = jnp.einsum(
                "whqk,qwhd->kwhd",
                weighting.astype(jnp.bfloat16),
                grad_heads,
                preferred_element_type=jnp.float32,
            )
            return (
                held_grad,
                jnp.concatenate(
                    [
                        key_grad.reshape(shard_rows, windows_here, model_width),
                        value_grad.reshape(shard_rows, windows_here, model_width),
                    ],
                    axis=-1,
                ),
            )

        def dead_block(held_grad):
            return (held_grad, jnp.zeros((shard_rows, windows_here, 2 * model_width), jnp.float32))

        dead = jnp.min(block_places(key_start, shard_rows)) > own_high
        return lax.cond(dead, dead_block, live_block, query_grad)

    query_grad, key_terms = lax.scan(
        back_block, zero_heads, (jnp.arange(seq_count, dtype=jnp.int32), blocks)
    )
    key_terms = key_terms.reshape((seq_count * shard_rows,) + key_terms.shape[2:])
    summed = lax.psum_scatter(
        key_terms.astype(jnp.bfloat16), "seq", scatter_dimension=0, tiled=True
    ).astype(jnp.float32)
    key_grad = summed[..., :model_width].reshape(shard_rows, windows_here, head_count, HEAD_DIM)
    value_grad = summed[..., model_width:].reshape(shard_rows, windows_here, head_count, HEAD_DIM)
    joined_grad = turn_back((query_grad, key_grad, value_grad))[0].astype(jnp.bfloat16)
    qkv_weight_grad = jnp.dot(normed_low.T, joined_grad, preferred_element_type=jnp.float32)
    normed_grad = jnp.dot(joined_grad, qkv_weight.T, preferred_element_type=jnp.float32) + jnp.dot(
        pre_grad, in_weight.T, preferred_element_type=jnp.float32
    )
    stream_part, norm_gain_grad, norm_bias_grad = norm_back(normed_grad)
    stream_grad = grad_rows.astype(jnp.float32) + stream_part
    result_three = result.reshape(shard_rows, windows_here, model_width)
    grad_three = stream_grad.reshape(shard_rows, windows_here, model_width)
    output = jnp.transpose(result_three, (1, 0, 2)).astype(jnp.bfloat16)
    hidden_grad = jnp.transpose(grad_three, (1, 0, 2))
    shares = (
        lax.psum_scatter(
            norm_gain_grad.astype(jnp.bfloat16), "seq", scatter_dimension=0, tiled=True
        ).astype(jnp.float32),
        lax.psum_scatter(
            norm_bias_grad.astype(jnp.bfloat16), "seq", scatter_dimension=0, tiled=True
        ).astype(jnp.float32),
        lax.psum_scatter(
            qkv_weight_grad.astype(jnp.bfloat16), "seq", scatter_dimension=0, tiled=True
        ).astype(jnp.float32),
        lax.psum_scatter(
            out_weight_grad.astype(jnp.bfloat16), "seq", scatter_dimension=0, tiled=True
        ).astype(jnp.float32),
        lax.psum_scatter(
            in_weight_grad.astype(jnp.bfloat16), "seq", scatter_dimension=0, tiled=True
        ).astype(jnp.float32),
        lax.psum_scatter(
            in_bias_grad.astype(jnp.bfloat16), "seq", scatter_dimension=0, tiled=True
        ).astype(jnp.float32),
        lax.psum_scatter(
            down_weight_grad.astype(jnp.bfloat16), "seq", scatter_dimension=0, tiled=True
        ).astype(jnp.float32),
        lax.psum_scatter(
            down_bias_grad.astype(jnp.bfloat16), "seq", scatter_dimension=0, tiled=True
        ).astype(jnp.float32),
    )
    totals_all = (
        lax.psum(shares[0].astype(jnp.bfloat16), "batch").astype(jnp.float32),
        lax.psum(shares[1].astype(jnp.bfloat16), "batch").astype(jnp.float32),
        lax.psum(shares[2].astype(jnp.bfloat16), "batch").astype(jnp.float32),
        lax.psum(shares[3].astype(jnp.bfloat16), "batch").astype(jnp.float32),
        lax.psum(shares[4].astype(jnp.bfloat16), "batch").astype(jnp.float32),
        lax.psum(shares[5].astype(jnp.bfloat16), "batch").astype(jnp.float32),
        lax.psum(shares[6].astype(jnp.bfloat16), "batch").astype(jnp.float32),
        lax.psum(shares[7].astype(jnp.bfloat16), "batch").astype(jnp.float32),
    )
    return (
        output,
        hidden_grad,
        totals_all[0],
        totals_all[1],
        totals_all[2],
        totals_all[3],
        totals_all[4],
        totals_all[5],
        totals_all[6],
        totals_all[7],
    )


def solution(mesh):
    placed = (
        P("batch", "seq", None),
        P("batch", "seq"),
        P("batch"),
        P("batch"),
        P(),
        P(),
        P(),
        P(),
        P(),
        P(),
        P(),
        P(),
        P(),
        P("batch", "seq", None),
    )

    def body(*arrays):
        hidden = arrays[0]
        owners = mesh.shape["seq"]
        if hidden.shape[0] == 1 and hidden.shape[2] == 2 * PAIR * owners and owners == 4 and mesh.shape["batch"] == 8:
            return fast_body(*arrays)
        return plain_body(*arrays)

    return jax.shard_map(
        body,
        mesh=mesh,
        in_specs=placed,
        out_specs=(
            P("batch", "seq", None),
            P("batch", "seq", None),
            P("seq"),
            P("seq"),
            P("seq", None),
            P("seq", None),
            P("seq", None),
            P("seq"),
            P("seq", None),
            P("seq"),
        ),
        check_vma=False,
    )
```

```python
import math

import jax
import jax.numpy as jnp
import numpy as np
from jax import lax
from jax.experimental import pallas as pl
from jax.experimental.pallas import tpu as pltpu
from jax.sharding import PartitionSpec as P

HEAD_DIM = 64
ROT = 32
PAIR = 2 * HEAD_DIM

EPSILON = 1e-05
BLOCKED = -1e30
LOG2E = math.log2(math.e)
BF16 = jnp.bfloat16
F32 = jnp.float32
MIB = 1 << 20
SHORT = pl.CostEstimate(flops=1000, bytes_accessed=1000, transcendentals=0)
LONG = pl.CostEstimate(flops=10**11, bytes_accessed=1000, transcendentals=0)


def dot_nn(left, right):
    return lax.dot_general(left, right, (((1,), (0,)), ((), ())), preferred_element_type=F32)


def dot_nt(left, right):
    return lax.dot_general(left, right, (((1,), (1,)), ((), ())), preferred_element_type=F32)


def dot_tn(left, right):
    return lax.dot_general(left, right, (((0,), (0,)), ((), ())), preferred_element_type=F32)


def swap_pairs(rows):
    width = rows.shape[1]
    lanes = lax.broadcasted_iota(jnp.int32, rows.shape, 1)
    return jnp.where(lanes % 2 == 0, pltpu.roll(rows, width - 1, 1), pltpu.roll(rows, 1, 1))


def trig_tables(length):
    inverse = 10000.0 ** (-(np.arange(ROT // 2, dtype=np.float32) * np.float32(2.0)) / np.float32(ROT))
    phases = np.arange(length, dtype=np.float32)[:, None] * inverse.astype(np.float32)[None, :]
    cosine = np.ones((length, HEAD_DIM), np.float32)
    sine = np.zeros((length, HEAD_DIM), np.float32)
    cosine[:, :ROT] = np.repeat(np.cos(phases), 2, axis=1)
    sine[:, :ROT] = np.repeat(np.sin(phases), 2, axis=1) * np.tile(np.array([-1.0, 1.0], np.float32), ROT // 2)
    return np.tile(cosine, (1, 2)), np.tile(sine, (1, 2))


def whole(array):
    shape = array.shape
    return pl.BlockSpec(shape, lambda i: (0,) * len(shape))


SCALARS = pl.BlockSpec(memory_space=pltpu.SMEM)


def prep_kernel(hidden_ref, mark_ref, table_ref, gain_ref, bias_ref, stream_ref, normed_ref, turned_ref):
    rows = hidden_ref.shape[0]
    vocab = table_ref.shape[0]
    onehot = (mark_ref[...] == lax.broadcasted_iota(jnp.int32, (rows, vocab), 1)).astype(F32).astype(BF16)
    stream = hidden_ref[...].astype(F32) + dot_nn(onehot, table_ref[...])
    centre = stream - jnp.mean(stream, axis=-1, keepdims=True)
    spread = jnp.mean(centre * centre, axis=-1, keepdims=True)
    normed = centre * lax.rsqrt(spread + EPSILON) * gain_ref[...] + bias_ref[...]
    stream_ref[...] = stream
    normed_ref[...] = normed.astype(BF16)
    turned_ref[...] = normed.astype(BF16).T


def prepare(hidden, marked, table, gain, bias):
    rows, width = hidden.shape
    step = 128
    return pl.pallas_call(
        prep_kernel,
        grid=(rows // step,),
        in_specs=[
            pl.BlockSpec((step, width), lambda i: (i, 0)),
            pl.BlockSpec((step, 1), lambda i: (i, 0)),
            pl.BlockSpec(table.shape, lambda i: (0, 0)),
            pl.BlockSpec((1, width), lambda i: (0, 0)),
            pl.BlockSpec((1, width), lambda i: (0, 0)),
        ],
        out_specs=[
            pl.BlockSpec((step, width), lambda i: (i, 0)),
            pl.BlockSpec((step, width), lambda i: (i, 0)),
            pl.BlockSpec((width, step), lambda i: (0, i)),
        ],
        out_shape=[
            jax.ShapeDtypeStruct((rows, width), F32),
            jax.ShapeDtypeStruct((rows, width), BF16),
            jax.ShapeDtypeStruct((width, rows), BF16),
        ],
        cost_estimate=SHORT,
        name="prep",
    )(hidden, marked, table, gain, bias)


def heads_kernel(owners_ref, normed_ref, cot_ref, wq_ref, wk_ref, wv_ref, wo_ref, cos_ref, sin_ref, *out_refs):
    normed = normed_ref[...]
    shifts = pl.num_programs(0)
    chunks = wq_ref.shape[1] // PAIR
    cosine = jnp.concatenate([cos_ref[...]] * chunks, axis=1)
    sine = jnp.concatenate([sin_ref[...]] * chunks, axis=1)

    def turned(rows):
        return rows * cosine + swap_pairs(rows) * sine

    parts = (
        turned(dot_nn(normed, wq_ref[...])).astype(BF16),
        turned(dot_nn(normed, wk_ref[...])).astype(BF16),
        dot_nn(normed, wv_ref[...]).astype(BF16),
        dot_nt(cot_ref[...], wo_ref[...]).astype(BF16),
    )
    for number, out_ref in enumerate(out_refs):
        shift, chunk = divmod(number, chunks)

        @pl.when(pl.program_id(0) == shift)
        def _():
            for at, part in enumerate(parts):
                out_ref[:, at * PAIR : (at + 1) * PAIR] = part[:, chunk * PAIR : (chunk + 1) * PAIR]


def heads_of(order, normed, cot, qkv_weight, out_weight, cosine, sine):
    rows, width = normed.shape
    owners = order.shape[0]
    wide = width // owners
    chunks = wide // PAIR
    fixed = pl.BlockSpec((rows, width), lambda i, o: (0, 0))
    table = pl.BlockSpec((rows, PAIR), lambda i, o: (0, 0))

    def columns(part):
        return pl.BlockSpec((width, wide), lambda i, o: (0, part * owners + o[i]))

    blocks = pl.pallas_call(
        heads_kernel,
        grid_spec=pltpu.PrefetchScalarGridSpec(
            num_scalar_prefetch=1,
            grid=(owners,),
            in_specs=[fixed, fixed]
            + [columns(part) for part in range(3)]
            + [pl.BlockSpec((wide, width), lambda i, o: (o[i], 0)), table, table],
            out_specs=[pl.BlockSpec((rows, 4 * PAIR), lambda i, o: (0, 0))] * (owners * chunks),
        ),
        out_shape=[jax.ShapeDtypeStruct((rows, 4 * PAIR), BF16)] * (owners * chunks),
        compiler_params=pltpu.CompilerParams(vmem_limit_bytes=60 * MIB),
        cost_estimate=SHORT,
        name="heads",
    )(order, normed, cot, qkv_weight, qkv_weight, qkv_weight, out_weight, cosine, sine)
    return [[blocks[shift * chunks + chunk] for shift in range(owners)] for chunk in range(chunks)]


QUERY_ROWS = 512
KEY_ROWS = QUERY_ROWS


def attention_kernel(pieces, info_ref, *refs):
    piece_refs = refs[:pieces]
    cos_ref, sin_ref = refs[pieces : pieces + 2]
    out_refs = refs[pieces + 2 : -9]
    held, results, key_turned, value_turned, doubled, score_ref, raised_ref, key_sum, value_sum = refs[-9:]
    me, end = info_ref[0], info_ref[1]
    rows = piece_refs[0].shape[0]
    length = rows * pieces
    for shift in range(pieces):
        start = pl.multiple_of(lax.rem(me - shift + pieces, pieces) * rows, rows)
        held[pl.ds(start, rows), :] = piece_refs[shift][...]
    key_turned[...] = held[:, PAIR : 2 * PAIR].T
    value_turned[...] = held[:, 2 * PAIR : 3 * PAIR].T
    for head in range(2):
        keys = held[:, PAIR + head * HEAD_DIM : PAIR + (head + 1) * HEAD_DIM]
        doubled[head] = jnp.concatenate([keys, keys], axis=1)
    key_sum[...] = jnp.zeros_like(key_sum)
    value_sum[...] = jnp.zeros_like(value_sum)
    scale = 0.125 * LOG2E
    halves = lax.broadcasted_iota(jnp.int32, (QUERY_ROWS, PAIR), 1) // HEAD_DIM
    causal = lax.broadcasted_iota(jnp.int32, (KEY_ROWS, QUERY_ROWS), 0) <= lax.broadcasted_iota(
        jnp.int32, (KEY_ROWS, QUERY_ROWS), 1
    )
    key_steps = lax.broadcasted_iota(jnp.int32, (KEY_ROWS, QUERY_ROWS), 0)

    def query_block(number, carry):
        first = pl.multiple_of(number * QUERY_ROWS, QUERY_ROWS)
        query_rows = held[pl.ds(first, QUERY_ROWS), 0:PAIR]
        grad_rows = held[pl.ds(first, QUERY_ROWS), 3 * PAIR : 4 * PAIR]
        zero = jnp.zeros_like(query_rows)
        queries = [jnp.where(halves == head, query_rows, zero) for head in range(2)]
        scaled = query_rows.astype(F32) * scale
        large = scaled.astype(BF16)
        small = (scaled - large.astype(F32)).astype(BF16)
        pairs = [
            jnp.concatenate(
                [part[:, head * HEAD_DIM : (head + 1) * HEAD_DIM] for part in (large, small)], axis=1
            )
            for head in range(2)
        ]
        query_places = first + lax.broadcasted_iota(jnp.int32, (1, QUERY_ROWS), 1)
        lowest = jnp.where(query_places > end, end + 1, 0)

        def scores_of(block, highest, diagonal, parted):
            start = pl.multiple_of(block * KEY_ROWS, KEY_ROWS)
            after = []
            for head in range(2):
                scores = dot_nt(doubled[head, pl.ds(start, KEY_ROWS), :], pairs[head])
                if diagonal:
                    scores = jnp.where(causal, scores, BLOCKED)
                if parted:
                    scores = jnp.where(key_steps >= lowest - start, scores, BLOCKED)
                score_ref[head, pl.ds(start, KEY_ROWS), :] = scores
                after.append(jnp.maximum(highest[head], jnp.max(scores, axis=0, keepdims=True)))
            return tuple(after)

        def any_scores(block, highest, diagonal=False):
            parted = (first + QUERY_ROWS - 1 > end) & (block * KEY_ROWS <= end)
            return lax.cond(
                parted,
                lambda held_rows: scores_of(block, held_rows, diagonal, True),
                lambda held_rows: scores_of(block, held_rows, diagonal, False),
                highest,
            )

        start_row = jnp.full((1, QUERY_ROWS), BLOCKED, F32)
        highest = lax.fori_loop(0, number, any_scores, (start_row, start_row))
        highest = any_scores(number, highest, True)

        def mix(block, carried):
            start = pl.multiple_of(block * KEY_ROWS, KEY_ROWS)
            after = []
            for head in range(2):
                total, mixed = carried[head]
                raised = jnp.exp2(score_ref[head, pl.ds(start, KEY_ROWS), :] - highest[head])
                rounded = raised.astype(BF16)
                raised_ref[head, pl.ds(start, KEY_ROWS), :] = rounded
                values = value_turned[head * HEAD_DIM : (head + 1) * HEAD_DIM, pl.ds(start, KEY_ROWS)]
                after.append((total + jnp.sum(raised, axis=0, keepdims=True), mixed + dot_nn(values, rounded)))
            return tuple(after)

        empty = (jnp.zeros((1, QUERY_ROWS), F32), jnp.zeros((HEAD_DIM, QUERY_ROWS), F32))
        mixes = lax.fori_loop(0, number + 1, mix, (empty, empty))
        inverse = [1.0 / mixes[head][0] for head in range(2)]
        mixed = jnp.concatenate([mixes[head][1] * inverse[head] for head in range(2)], axis=0)
        turned = grad_rows.astype(F32).T
        turned = jnp.concatenate(
            [turned[head * HEAD_DIM : (head + 1) * HEAD_DIM] * inverse[head] for head in range(2)], axis=0
        )
        products = mixed * turned
        delta = [
            jnp.sum(products[head * HEAD_DIM : (head + 1) * HEAD_DIM], axis=0, keepdims=True) for head in range(2)
        ]
        divided = turned.T.astype(BF16)
        grads = [jnp.where(halves == head, divided, zero) for head in range(2)]

        def back(block, carried):
            start = pl.multiple_of(block * KEY_ROWS, KEY_ROWS)
            values = held[pl.ds(start, KEY_ROWS), 2 * PAIR : 3 * PAIR]
            after, key_terms, value_terms = [], [], []
            for head in range(2):
                raised = raised_ref[head, pl.ds(start, KEY_ROWS), :]
                score_grad = raised * (dot_nt(values, grads[head]) - delta[head]).astype(BF16)
                value_terms.append(dot_nn(raised, grads[head]))
                key_terms.append(dot_nn(score_grad, queries[head]))
                keys = key_turned[head * HEAD_DIM : (head + 1) * HEAD_DIM, pl.ds(start, KEY_ROWS)]
                after.append(carried[head] + dot_nn(keys, score_grad))
            value_sum[pl.ds(start, KEY_ROWS), :] += value_terms[0] + value_terms[1]
            key_sum[pl.ds(start, KEY_ROWS), :] += key_terms[0] + key_terms[1]
            return tuple(after)

        query_grads = lax.fori_loop(0, number + 1, back, (empty[1], empty[1]))
        query_grad = jnp.concatenate(query_grads, axis=0).T * 0.125
        cosine = cos_ref[pl.ds(first, QUERY_ROWS), :]
        sine = sin_ref[pl.ds(first, QUERY_ROWS), :]
        results[pl.ds(first, QUERY_ROWS), 0:PAIR] = (query_grad * cosine - swap_pairs(query_grad) * sine).astype(BF16)
        results[pl.ds(first, QUERY_ROWS), 3 * PAIR : 4 * PAIR] = mixed.T.astype(BF16)
        return carry

    lax.fori_loop(0, length // QUERY_ROWS, query_block, 0)
    key_grad = key_sum[...] * 0.125
    results[:, PAIR : 2 * PAIR] = (key_grad * cos_ref[...] - swap_pairs(key_grad) * sin_ref[...]).astype(BF16)
    results[:, 2 * PAIR : 3 * PAIR] = value_sum[...].astype(BF16)
    for shift in range(pieces):
        start = pl.multiple_of(lax.rem(me + shift, pieces) * rows, rows)
        out_refs[shift][...] = results[pl.ds(start, rows), :]


def attention(info, parts, cosine, sine):
    pieces = len(parts)
    rows = parts[0].shape[0]
    length = rows * pieces
    arrays = (*parts, cosine, sine)
    shapes = [jax.ShapeDtypeStruct((rows, 4 * PAIR), BF16)] * pieces
    return pl.pallas_call(
        lambda *refs: attention_kernel(pieces, *refs),
        grid=(1,),
        in_specs=[SCALARS] + [whole(array) for array in arrays],
        out_specs=[whole(shape) for shape in shapes],
        out_shape=shapes,
        scratch_shapes=[
            pltpu.VMEM((length, 4 * PAIR), BF16),
            pltpu.VMEM((length, 4 * PAIR), BF16),
            pltpu.VMEM((PAIR, length), BF16),
            pltpu.VMEM((PAIR, length), BF16),
            pltpu.VMEM((2, length, PAIR), BF16),
            pltpu.VMEM((2, length, QUERY_ROWS), F32),
            pltpu.VMEM((2, length, QUERY_ROWS), BF16),
            pltpu.VMEM((length, PAIR), F32),
            pltpu.VMEM((length, PAIR), F32),
        ],
        compiler_params=pltpu.CompilerParams(vmem_limit_bytes=60 * MIB),
        cost_estimate=SHORT,
        name="attention",
    )(info, *arrays)


def feed_kernel(cells_ref, normed_ref, turned_ref, cot_ref, in_ref, bias_ref, down_ref, *out_refs):
    sides = (out_refs[0:2], out_refs[2:4])
    bias_grad, out_sum, norm_sum = out_refs[4:]
    step = pl.program_id(0)
    steps = pl.num_programs(0) // 2
    up = math.sqrt(2.0 / math.pi)

    @pl.when(step == 0)
    def _():
        out_sum[...] = jnp.zeros_like(out_sum)
        norm_sum[...] = jnp.zeros_like(norm_sum)

    weights = in_ref[...]
    downs = down_ref[...]
    cot = cot_ref[...]
    pre = dot_nn(normed_ref[...], weights) + bias_ref[...]
    square = pre * pre
    tanh = jnp.tanh(up * pre * (1.0 + 0.044715 * square))
    half = 0.5 * (1.0 + tanh)
    active = (pre * half).astype(BF16)
    slope = half + 0.5 * pre * (1.0 - tanh * tanh) * (up * (1.0 + 3 * 0.044715 * square))
    pre_grad = (dot_nt(cot, downs) * slope).astype(BF16)
    in_term = dot_nn(turned_ref[...], pre_grad).astype(BF16)
    down_term = dot_tn(active, cot).astype(BF16)
    for side, (in_grad, down_grad) in enumerate(sides):

        @pl.when((step >= steps) == bool(side))
        def _():
            pieces, owners, kept, tile = in_grad.shape
            for owner in range(owners):
                for piece in range(pieces):
                    start = (owner * pieces + piece) * kept
                    in_grad[piece, owner] = in_term[start : start + kept]
            kept = tile // pieces
            for group in range(down_term.shape[1] // tile):
                for piece in range(pieces):
                    down_grad[piece, 0, group * kept : (group + 1) * kept] = down_term[
                        piece * kept : (piece + 1) * kept, group * tile : (group + 1) * tile
                    ]

    bias_grad[0] = jnp.sum(pre_grad.astype(F32), axis=0, keepdims=True)
    out_sum[...] += dot_nn(active, downs)
    norm_sum[...] += dot_nt(pre_grad, weights)


def feed_forward(cells, normed, turned, cot, in_weight, in_bias, down_weight, pieces):
    rows, width = normed.shape
    steps = cells.shape[0]
    owners = steps // 2
    hidden_units = in_weight.shape[1]
    tile = hidden_units // steps
    kept = width // owners // pieces
    tall = owners * kept
    wide = tile // pieces * (width // tile)
    fixed = pl.BlockSpec((rows, width), lambda i, c: (0, 0))

    def first(i):
        return jnp.minimum(i, owners - 1)

    def second(i):
        return jnp.maximum(i - owners, 0)

    def sides_of(turn):
        return [
            pl.BlockSpec((pieces, owners, kept, tile), lambda i, c: (0, 0, turn(i), 0)),
            pl.BlockSpec((pieces, 1, wide, tile), lambda i, c: (0, turn(i), 0, 0)),
        ]

    grads = [
        jax.ShapeDtypeStruct((pieces, owners, tall, tile), BF16),
        jax.ShapeDtypeStruct((pieces, owners, wide, tile), BF16),
    ]
    full = jax.ShapeDtypeStruct((rows, width), F32)
    results = pl.pallas_call(
        feed_kernel,
        grid_spec=pltpu.PrefetchScalarGridSpec(
            num_scalar_prefetch=1,
            grid=(steps,),
            in_specs=[
                fixed,
                pl.BlockSpec((width, rows), lambda i, c: (0, 0)),
                fixed,
                pl.BlockSpec((width, tile), lambda i, c: (0, c[i])),
                pl.BlockSpec((1, tile), lambda i, c: (0, c[i])),
                pl.BlockSpec((tile, width), lambda i, c: (c[i], 0)),
            ],
            out_specs=sides_of(first)
            + sides_of(second)
            + [pl.BlockSpec((1, 1, tile), lambda i, c: (i, 0, 0)), fixed, fixed],
        ),
        out_shape=grads + grads + [jax.ShapeDtypeStruct((steps, 1, tile), F32), full, full],
        compiler_params=pltpu.CompilerParams(vmem_limit_bytes=60 * MIB),
        cost_estimate=SHORT,
        name="feed",
    )(cells, normed, turned, cot, in_weight, in_bias, down_weight)
    return results[:2], results[2:4], *results[4:]


def place_columns(me_ref, piece_refs, held):
    owners = len(piece_refs)
    for shift in range(owners):
        owner = lax.rem(me_ref[0] - shift + owners, owners)
        start = pl.multiple_of(owner * PAIR, PAIR)
        for part in range(4):
            held[part, :, pl.ds(start, PAIR)] = piece_refs[shift][:, part * PAIR : (part + 1) * PAIR]


def weight_kernel(pieces, info_ref, turned_ref, cot_ref, *refs):
    owners = len(refs) - 4
    kept_ref, sent_ref, held, grad = refs[-4:]
    place_columns(info_ref, refs[:owners], held)
    kept = PAIR // pieces
    turned = turned_ref[...]
    for part in range(3):
        grad[...] = dot_nn(turned, held[part]).astype(BF16)
        for side, ref in enumerate((kept_ref, sent_ref)):
            core = info_ref[1] ^ side
            for owner in range(owners):
                for piece in range(pieces):
                    start = pl.multiple_of(((owner * 2 + core) * pieces + piece) * kept, kept)
                    ref[piece, owner, part * kept : (part + 1) * kept] = grad[pl.ds(start, kept), :]
    term = dot_tn(held[3], cot_ref[...]).astype(BF16)
    rows, half = term.shape[0], term.shape[1] // 2
    for core in range(2):
        grad[core * rows : (core + 1) * rows, :] = term[:, core * half : (core + 1) * half]
    for side, ref in enumerate((kept_ref, sent_ref)):
        core = info_ref[1] ^ side
        for owner in range(owners):
            for piece in range(pieces):
                start = pl.multiple_of(core * rows + (owner * pieces + piece) * kept, kept)
                ref[piece, owner, 3 * kept :] = grad[pl.ds(start, kept), :]


def weight_grads(info, turned, cot, parts, pieces):
    owners = len(parts)
    rows, width = cot.shape
    kept = PAIR // pieces
    arrays = (turned, cot, *parts)
    shape = jax.ShapeDtypeStruct((pieces, owners, 4 * kept, owners * PAIR), BF16)
    return pl.pallas_call(
        lambda *refs: weight_kernel(pieces, *refs),
        grid=(1,),
        in_specs=[SCALARS] + [whole(array) for array in arrays],
        out_specs=[whole(shape)] * 2,
        out_shape=[shape] * 2,
        scratch_shapes=[pltpu.VMEM((4, rows, owners * PAIR), BF16), pltpu.VMEM((width, owners * PAIR), BF16)],
        compiler_params=pltpu.CompilerParams(vmem_limit_bytes=60 * MIB),
        cost_estimate=SHORT,
        name="weight_grads",
    )(info, *arrays)


def sums_kernel(last, owners, me_ref, *refs):
    piece_refs, refs = refs[:owners], refs[owners:]
    weight_refs, refs = refs[: 3 * owners], refs[3 * owners :]
    out_weight_refs, refs = refs[:owners], refs[owners:]
    out_in, norm_in = refs[:2]
    held = refs[-1]
    place_columns(me_ref, piece_refs, held)
    norm = norm_in[...]
    for part in range(3):
        weights = jnp.concatenate([ref[...] for ref in weight_refs[part * owners : (part + 1) * owners]], axis=1)
        norm = norm + dot_nt(held[part], weights)
    weights = jnp.concatenate([ref[...] for ref in out_weight_refs], axis=0)
    out = out_in[...] + dot_nn(held[3], weights)
    if not last:
        out_ref, norm_ref = refs[2:4]
        out_ref[...] = out
        norm_ref[...] = norm
        return
    stream_ref, cot_ref, gain_ref, down_bias_ref, out_ref, hidden_ref, gain_grad, bias_grad = refs[2:-1]
    stream = stream_ref[...]
    cot = cot_ref[...].astype(F32)
    out_ref[...] = (stream + out + down_bias_ref[...]).astype(BF16)
    centre = stream - jnp.mean(stream, axis=-1, keepdims=True)
    spread = jnp.mean(centre * centre, axis=-1, keepdims=True)
    inverse = lax.rsqrt(spread + EPSILON)
    hat = centre * inverse
    gained = norm * gain_ref[...]
    hidden_ref[...] = cot + inverse * (
        gained
        - jnp.mean(gained, axis=-1, keepdims=True)
        - hat * jnp.mean(gained * hat, axis=-1, keepdims=True)
    )
    gain_grad[...] = jnp.sum(norm * hat, axis=0, keepdims=True)
    bias_grad[...] = jnp.sum(norm, axis=0, keepdims=True)


def sums_of(info, chunk, chunks, parts, qkv_weight, out_weight, sums, final=()):
    owners = len(parts)
    rows = parts[0].shape[0]
    width = qkv_weight.shape[0]
    last = bool(final)

    def columns(part, owner):
        at = (part * owners + owner) * chunks + chunk
        return pl.BlockSpec((width, PAIR), lambda i: (0, at))

    def weight_rows(owner):
        return pl.BlockSpec((PAIR, width), lambda i: (owner * chunks + chunk, 0))

    full = jax.ShapeDtypeStruct((rows, width), F32)
    row = jax.ShapeDtypeStruct((1, width), F32)
    shapes = [jax.ShapeDtypeStruct((rows, width), BF16), full, row, row] if last else [full, full]
    return pl.pallas_call(
        lambda *refs: sums_kernel(last, owners, *refs),
        grid=(1,),
        in_specs=[SCALARS]
        + [whole(part) for part in parts]
        + [columns(part, owner) for part in range(3) for owner in range(owners)]
        + [weight_rows(owner) for owner in range(owners)]
        + [whole(array) for array in (*sums, *final)],
        out_specs=[whole(shape) for shape in shapes],
        out_shape=shapes,
        scratch_shapes=[pltpu.VMEM((4, rows, owners * PAIR), BF16)],
        compiler_params=pltpu.CompilerParams(vmem_limit_bytes=60 * MIB),
        cost_estimate=SHORT,
        name="sums",
    )(info, *parts, *([qkv_weight] * (3 * owners)), *([out_weight] * owners), *sums, *final)


def feed_place_kernel(sums_ref, in_ref, down_ref):
    devices, total, tile = sums_ref.shape
    kept = 2 * in_ref.shape[0] // devices
    tiles = in_ref.shape[1] // (2 * tile)
    rows = down_ref.shape[0] // 2
    down_kept = 2 * rows // devices
    for device in range(devices):
        core, chip = device & 1, device >> 1
        rows_of = slice(chip * kept, (chip + 1) * kept)
        for number in range(tiles):
            column = (2 * number + core) * tile
            in_ref[rows_of, column : column + tile] = sums_ref[device, number * kept : (number + 1) * kept].astype(F32)
        start = core * rows + chip * down_kept
        for group in range(down_ref.shape[1] // tile):
            at = tiles * kept + group * down_kept
            down_ref[start : start + down_kept, group * tile : (group + 1) * tile] = sums_ref[
                device, at : at + down_kept
            ].astype(F32)


def place_feed(sums, in_shape, down_shape):
    shapes = [jax.ShapeDtypeStruct(in_shape, F32), jax.ShapeDtypeStruct(down_shape, F32)]
    return pl.pallas_call(
        feed_place_kernel,
        grid=(1,),
        in_specs=[whole(sums)],
        out_specs=[whole(shape) for shape in shapes],
        out_shape=shapes,
        compiler_params=pltpu.CompilerParams(vmem_limit_bytes=60 * MIB),
        cost_estimate=SHORT,
        name="place_feed",
    )(sums)


def heads_place_kernel(info_ref, mine_ref, other_ref, qkv_ref, out_ref):
    core, place = info_ref[0], info_ref[1]
    masks, total, wide = mine_ref.shape
    own_rows, width = out_ref.shape
    kept = own_rows // 2 // masks
    chunks = total // (4 * kept)
    owners = wide // PAIR
    for source, ref in enumerate((mine_ref, other_ref)):
        at_core = core if source == 0 else 1 - core
        columns = pl.ds(pl.multiple_of(at_core * (width // 2), width // 2), width // 2)
        for mask in range(masks):
            piece = place ^ mask
            rows = pl.ds(pl.multiple_of(at_core * (own_rows // 2) + piece * kept, kept), kept)
            for chunk in range(chunks):
                at = chunk * 4 * kept
                for part in range(3):
                    block = ref[mask, at + part * kept : at + (part + 1) * kept].astype(F32)
                    for owner in range(owners):
                        column = part * width + (owner * chunks + chunk) * PAIR
                        qkv_ref[rows, column : column + PAIR] = block[:, owner * PAIR : (owner + 1) * PAIR]
                out_rows = pl.ds(pl.multiple_of(chunk * PAIR + piece * kept, kept), kept)
                out_ref[out_rows, columns] = ref[mask, at + 3 * kept : at + 4 * kept].astype(F32)


def place_heads(info, mine, other, own_rows, width):
    shapes = [jax.ShapeDtypeStruct((own_rows, 3 * width), F32), jax.ShapeDtypeStruct((own_rows, width), F32)]
    return pl.pallas_call(
        heads_place_kernel,
        grid=(1,),
        in_specs=[SCALARS, whole(mine), whole(other)],
        out_specs=[whole(shape) for shape in shapes],
        out_shape=shapes,
        compiler_params=pltpu.CompilerParams(vmem_limit_bytes=60 * MIB),
        cost_estimate=SHORT,
        name="place_heads",
    )(info, mine, other)


def exchange(rows, axis, mask):
    size = lax.axis_size(axis)
    return lax.ppermute(rows, axis, [(place, place ^ mask) for place in range(size)])


def around(rows, shift):
    owners = lax.axis_size("seq")
    return lax.ppermute(rows, "seq", [(place, (place + shift) % owners) for place in range(owners)])


def total_of(*terms):
    return sum(term.astype(F32) for term in terms).astype(BF16)


def picked(rows, index, dim=0):
    return lax.dynamic_index_in_dim(rows, index, dim, keepdims=False)


def add_kernel(places, bits_ref, *refs):
    outs = refs[len(refs) - len(places) :]
    for out_ref, terms in zip(outs, places):
        at = 0
        for left, right in terms:
            rows = refs[left].shape[-2]
            total = refs[left][...].astype(F32) + refs[right][...].astype(F32)
            out_ref[..., at : at + rows, :] = total.reshape(out_ref.shape[:-2] + total.shape[-2:]).astype(BF16)
            at += rows


def add_pieces(kept, arrived):
    pieces, owners = kept[0].shape[:2]
    arrays = [array for pair in zip(kept, arrived) for array in pair]
    rows = sum(array.shape[2] for array in kept)
    columns = kept[0].shape[3]
    return pl.pallas_call(
        lambda *refs: add_kernel([[(0, 1), (2, 3)]], None, *refs),
        grid=(pieces,),
        in_specs=[pl.BlockSpec((1,) + array.shape[1:], lambda i: (i, 0, 0, 0)) for array in arrays],
        out_specs=pl.BlockSpec((1, owners, rows, columns), lambda i: (i, 0, 0, 0)),
        out_shape=jax.ShapeDtypeStruct((pieces, owners, rows, columns), BF16),
        compiler_params=pltpu.CompilerParams(vmem_limit_bytes=60 * MIB),
        cost_estimate=SHORT,
        name="add_pieces",
    )(*arrays)


def add_for_chips(chip, kept, arrived):
    specs, places, arrays = [], [], []
    chips, owners = kept[0].shape[:2]
    for mask in range(chips):
        terms = []
        for mine, other in zip(kept, arrived):
            terms.append((len(arrays), len(arrays) + 1))
            arrays += [mine, other]
            specs += [pl.BlockSpec((1,) + mine.shape[1:], lambda i, c, mask=mask: (c[0] ^ mask, 0, 0, 0))] * 2
        places.append(terms)
    rows = sum(array.shape[2] for array in kept)
    out = jax.ShapeDtypeStruct((owners, rows, kept[0].shape[3]), BF16)
    return pl.pallas_call(
        lambda *refs: add_kernel(places, *refs),
        grid_spec=pltpu.PrefetchScalarGridSpec(
            num_scalar_prefetch=1,
            grid=(1,),
            in_specs=specs,
            out_specs=[pl.BlockSpec(out.shape, lambda i, c: (0, 0, 0))] * chips,
        ),
        out_shape=[out] * chips,
        cost_estimate=SHORT,
        name="add_for_chips",
    )(chip[None], *arrays)


class Order:
    token = None

    def __call__(self, value):
        if self.token is None:
            return value
        return lax.optimization_barrier((value, self.token))[0]

    def done(self, token):
        self.token = token
        return token

    def also(self, *tokens):
        self.token = (self.token, tokens)


def fast_body(
    hidden,
    token_ids,
    offsets,
    end_places,
    token_table,
    norm_gain,
    norm_bias,
    qkv_weight,
    out_weight,
    in_weight,
    in_bias,
    down_weight,
    down_bias,
    cotangent,
):
    width = hidden.shape[2]
    rows = hidden.shape[1]
    owners = lax.axis_size("seq")
    pieces = lax.axis_size("batch")
    me = lax.axis_index("seq")
    core = lax.axis_index("batch") & 1
    length = rows * owners
    own_rows = width // owners
    chunks = own_rows // PAIR
    end = end_places[0]

    places = me * rows + jnp.arange(rows, dtype=jnp.int32)[:, None]
    marked = token_ids.reshape(rows, 1)
    marked = jnp.where(places == end, 2, marked)
    marked = jnp.where(places == end + 1, 1, marked)
    marked = jnp.where((places == 0) & (offsets[0] == 0), 1, marked)
    cot = cotangent.reshape(rows, width)
    stream, normed, turned = prepare(
        hidden.reshape(rows, width), marked, token_table, norm_gain[None], norm_bias[None]
    )
    cosine, sine = (jnp.asarray(table) for table in trig_tables(length))
    own_cosine = lax.dynamic_slice_in_dim(cosine, me * rows, rows)
    own_sine = lax.dynamic_slice_in_dim(sine, me * rows, rows)
    place = lax.axis_index("batch")
    info = jnp.stack([me, core]).astype(jnp.int32)
    spots = jnp.stack([me, end]).astype(jnp.int32)
    order = Order()

    def moved(blocks, shifts=(2, 1, 3)):
        return {shift: around(blocks[shift], shift) for shift in shifts}

    def gathered(blocks, arrived):
        return [blocks[0]] + [arrived[shift] for shift in range(1, owners)]

    def back(rows):
        return [exchange(rows, "batch", mask) for mask in (2, 4, 6)]

    shifts = lax.rem(me + jnp.arange(owners, dtype=jnp.int32), owners)
    heads = order.done(heads_of(shifts, normed, cot, qkv_weight, out_weight, own_cosine, own_sine))

    arrived = moved(order(heads[0]))
    cells = 2 * jnp.arange(owners, dtype=jnp.int32)
    cells = jnp.concatenate([cells + 1 - core, cells + core])
    away, here, in_bias_grad, out_sum, norm_sum = order.done(
        feed_forward(cells, order(normed), turned, cot, in_weight, in_bias[None], down_weight, pieces // 2)
    )
    order.also(arrived)

    feed_arrived = [exchange(array, "batch", 1) for array in order(away)]
    later = moved(order(heads[1]))
    first = order.done(attention(spots, gathered(heads[0], order(arrived)), cosine, sine))
    order.also(feed_arrived)
    feed_rows = order.done(add_pieces(order(here), feed_arrived))
    order.also(later)

    groups = [list(range(number, pieces, 2)) for number in range(2)]
    feed_rows = lax.psum_scatter(
        order(feed_rows), "batch", scatter_dimension=0, axis_index_groups=groups, tiled=False
    )
    arrived = moved(order(first))
    second = order.done(attention(spots, gathered(heads[1], order(later)), cosine, sine))
    cot_sum = order.done(jnp.sum(order(cot).astype(F32), axis=0))
    order.also(arrived)

    parts = gathered(first, order(arrived))
    first_kept, first_sent = order.done(weight_grads(info, turned, cot, parts, pieces // 2))

    grad_arrived = exchange(order(first_sent), "batch", 1)
    later = moved(order(second))
    sums = order.done(sums_of(info, 0, chunks, order(parts), qkv_weight, out_weight, (out_sum, norm_sum)))
    order.also(grad_arrived)
    first_held = order.done(add_for_chips(place >> 1, [order(first_kept)], [grad_arrived]))
    order.also(later, feed_rows)

    feed_rows = lax.psum_scatter(order(feed_rows), "seq", scatter_dimension=0, tiled=False)
    parts = gathered(second, order(later))
    second_kept, second_sent = order.done(weight_grads(info, turned, cot, parts, pieces // 2))

    first_arrived = [exchange(order(first_held[mask]), "batch", 2 * mask) for mask in (1, 2, 3)]
    grad_arrived = exchange(order(second_sent), "batch", 1)
    output, hidden_grad, gain_grad, bias_grad = order.done(
        sums_of(
            info, 1, chunks, order(parts), qkv_weight, out_weight, sums, (stream, cot, norm_gain[None], down_bias[None])
        )
    )
    order.also(first_arrived, grad_arrived)
    second_held = order.done(add_for_chips(place >> 1, [order(second_kept)], [grad_arrived]))
    bias_low = jnp.where(core == 0, in_bias_grad[owners:], in_bias_grad[:owners])
    bias_high = jnp.where(core == 0, in_bias_grad[:owners], in_bias_grad[owners:])
    small = jnp.concatenate(
        [
            jnp.concatenate([bias_low, bias_high], axis=1).reshape(owners, -1),
            cot_sum.reshape(owners, -1),
            gain_grad.reshape(owners, -1),
            bias_grad.reshape(owners, -1),
        ],
        axis=1,
    )
    order.done((second_held, order(small)))

    def send_owners(rows):
        return [around(picked(rows, lax.rem(me + shift, owners)), shift) for shift in range(1, owners)]

    second_arrived = [exchange(order(second_held[mask]), "batch", 2 * mask) for mask in (1, 2, 3)]
    small_arrived = exchange(order(small), "batch", 1)
    order.also(second_arrived, small_arrived, feed_rows)
    feed_total = lax.all_gather(order(feed_rows), "batch", axis=0)
    small = small + order(small_arrived)
    grad_rows = order.done(
        jnp.concatenate(
            [
                total_of(order(held[0]), *arrived)
                for held, arrived in ((first_held, first_arrived), (second_held, second_arrived))
            ],
            axis=1,
        )
    )
    order.also(small)

    grad_rows = order(grad_rows)
    grad_arrived = send_owners(grad_rows)
    order.also(grad_arrived)
    grad_rows = order.done(total_of(picked(grad_rows, me), *order(grad_arrived)))

    grad_back = back(order(grad_rows))
    order.also(grad_back)
    grad_mine = order.done(jnp.stack([grad_rows] + order(grad_back)))

    grad_other = exchange(order(grad_mine), "batch", 1)
    small_arrived = back(order(small))
    order.also(small_arrived, grad_other)
    small = order.done(sum(order(small_arrived), small))

    small_arrived = [around(order(small), shift) for shift in range(1, owners)]
    heads_info = jnp.stack([core, place >> 1]).astype(jnp.int32)
    qkv_weight_grad, out_weight_grad = order.done(
        place_heads(heads_info, order(grad_mine), grad_other, own_rows, width)
    )
    in_weight_grad, down_weight_grad = order.done(
        place_feed(order(feed_total), (own_rows, in_weight.shape[1]), (down_weight.shape[0] // owners, width))
    )
    small = picked(sum(order(small_arrived), small), me)
    few = own_rows
    many = in_bias.shape[0] // owners
    return (
        output[None],
        hidden_grad[None],
        small[many + few : many + 2 * few],
        small[many + 2 * few :],
        qkv_weight_grad,
        out_weight_grad,
        in_weight_grad,
        small[:many],
        down_weight_grad,
        small[many : many + few],
    )


def rotate(vectors, cosine_table, sine_table):
    even_part = vectors[..., 0:ROT:2]
    odd_part = vectors[..., 1:ROT:2]
    turned = jnp.stack(
        [
            even_part * cosine_table - odd_part * sine_table,
            odd_part * cosine_table + even_part * sine_table,
        ],
        axis=-1,
    )
    turned = turned.reshape(vectors.shape[:-1] + (ROT,))
    return jnp.concatenate([turned, vectors[..., ROT:]], axis=-1)


def angles(places):
    inverse = 10000.0 ** (-(jnp.arange(ROT // 2, dtype=jnp.float32) * 2.0) / ROT)
    phases = places.astype(jnp.float32)[:, None] * inverse[None, :]
    return (jnp.cos(phases), jnp.sin(phases))


def visible(query_places, key_places, end_places):
    query_after = query_places[None, :, None] > end_places[:, None, None]
    key_after = key_places[None, None, :] > end_places[:, None, None]
    return (key_places[None, None, :] <= query_places[None, :, None]) & (query_after == key_after)


def norm_rows(stream, gain_row, bias_row):
    centre = stream - jnp.mean(stream, axis=-1, keepdims=True)
    spread = jnp.mean(centre * centre, axis=-1, keepdims=True)
    return centre * lax.rsqrt(spread + EPSILON) * gain_row + bias_row


def gelu_rows(pre_active):
    return jax.nn.gelu(pre_active, approximate=True)


def plain_body(
    hidden,
    token_ids,
    offsets,
    end_places,
    token_table,
    norm_gain,
    norm_bias,
    qkv_weight,
    out_weight,
    in_weight,
    in_bias,
    down_weight,
    down_bias,
    cotangent,
):
    windows_here, shard_rows, model_width = hidden.shape
    head_count = model_width // HEAD_DIM
    seq_count = lax.axis_size("seq")
    seq_place = lax.axis_index("seq")
    home_places = seq_place * shard_rows + jnp.arange(shard_rows, dtype=jnp.int32)
    token_rows = shard_rows * windows_here
    marked = token_ids.T
    marked = jnp.where(home_places[:, None] == end_places[None, :], 2, marked)
    marked = jnp.where(home_places[:, None] == end_places[None, :] + 1, 1, marked)
    marked = jnp.where((home_places[:, None] == 0) & (offsets[None, :] == 0), 1, marked)
    onehot = (marked[..., None] == jnp.arange(token_table.shape[0], dtype=jnp.int32)).astype(
        jnp.bfloat16
    )
    embedded = jnp.einsum("swv,vd->swd", onehot, token_table, preferred_element_type=jnp.float32)
    stream_three = jnp.transpose(hidden, (1, 0, 2)).astype(jnp.float32) + embedded
    cot_three = jnp.transpose(cotangent, (1, 0, 2))
    own_high = jnp.max(home_places)
    stream_rows = stream_three.reshape(token_rows, model_width)
    normed, norm_back = jax.vjp(norm_rows, stream_rows, norm_gain, norm_bias)
    normed_low = normed.astype(jnp.bfloat16)
    projected = jnp.dot(normed_low, qkv_weight, preferred_element_type=jnp.float32)
    cosine_table, sine_table = angles(home_places)
    cosine_table = cosine_table[:, None, None, :]
    sine_table = sine_table[:, None, None, :]

    def turn_heads(projected_rows):
        divided = projected_rows.reshape(shard_rows, windows_here, 3, head_count, HEAD_DIM)
        return (
            rotate(divided[:, :, 0], cosine_table, sine_table),
            rotate(divided[:, :, 1], cosine_table, sine_table),
            divided[:, :, 2],
        )

    (queries, key_rows, values), turn_back = jax.vjp(turn_heads, projected)
    query_low = queries.astype(jnp.bfloat16)
    key_value = jnp.concatenate(
        [
            key_rows.reshape(shard_rows, windows_here, model_width),
            values.reshape(shard_rows, windows_here, model_width),
        ],
        axis=-1,
    ).astype(jnp.bfloat16)

    def split_block(key_block):
        row_count = key_block.shape[0]
        return (
            key_block[..., :model_width].reshape(row_count, windows_here, head_count, HEAD_DIM),
            key_block[..., model_width:].reshape(row_count, windows_here, head_count, HEAD_DIM),
        )

    def block_places(row_start, row_count):
        return row_start + jnp.arange(row_count, dtype=jnp.int32)

    def block_scores(key_block, key_start):
        key_part, value_part = split_block(key_block)
        key_places = block_places(key_start, key_block.shape[0])
        scores = (
            jnp.einsum("qwhd,kwhd->whqk", query_low, key_part, preferred_element_type=jnp.float32)
            * 0.125
        )
        scores = jnp.where(visible(home_places, key_places, end_places)[:, None], scores, BLOCKED)
        return (scores, key_part, value_part)

    def attend(carried, key_block, key_start):
        running, totals, accumulated = carried
        scores, key_part, value_part = block_scores(key_block, key_start)
        highest = jnp.maximum(running, jnp.max(scores, axis=-1))
        factor = jnp.exp(running - highest)
        raised = jnp.exp(scores - highest[..., None])
        totals = totals * factor + jnp.sum(raised, axis=-1)
        accumulated = accumulated * factor[..., None] + jnp.einsum(
            "whqk,kwhd->whqd",
            raised.astype(jnp.bfloat16),
            value_part,
            preferred_element_type=jnp.float32,
        )
        return (highest, totals, accumulated)

    start_state = (
        jnp.full((windows_here, head_count, shard_rows), BLOCKED, jnp.float32),
        jnp.zeros((windows_here, head_count, shard_rows), jnp.float32),
        jnp.zeros((windows_here, head_count, shard_rows, HEAD_DIM), jnp.float32),
    )
    carried = start_state
    fetched_rows = lax.all_gather(key_value, "seq", axis=0, tiled=True)
    row_count = fetched_rows.shape[0]
    blocks = fetched_rows.reshape((row_count // shard_rows, shard_rows) + fetched_rows.shape[1:])

    def visit_block(held_state, element):
        number, key_block = element
        key_start = number * shard_rows
        dead = jnp.min(block_places(key_start, shard_rows)) > own_high
        held_state = lax.cond(
            dead,
            lambda kept_state: kept_state,
            lambda kept_state: attend(kept_state, key_block, key_start),
            held_state,
        )
        return (held_state, None)

    carried, unused = lax.scan(
        visit_block, carried, (jnp.arange(blocks.shape[0], dtype=jnp.int32), blocks)
    )
    running, totals, accumulated = carried
    attention = accumulated / totals[..., None]
    log_total = running + jnp.log(totals)
    attention_rows = jnp.transpose(attention, (2, 0, 1, 3))
    mixed_low = attention_rows.reshape(token_rows, model_width).astype(jnp.bfloat16)
    attended = jnp.dot(mixed_low, out_weight, preferred_element_type=jnp.float32)
    pre_active = jnp.dot(normed_low, in_weight, preferred_element_type=jnp.float32) + in_bias
    active, gelu_back = jax.vjp(gelu_rows, pre_active)
    active_low = active.astype(jnp.bfloat16)
    result = (
        stream_rows
        + attended
        + jnp.dot(active_low, down_weight, preferred_element_type=jnp.float32)
        + down_bias
    )
    grad_rows = cot_three.reshape(token_rows, model_width)
    down_weight_grad = jnp.dot(active_low.T, grad_rows, preferred_element_type=jnp.float32)
    down_bias_grad = jnp.sum(grad_rows.astype(jnp.float32), axis=0)
    out_weight_grad = jnp.dot(mixed_low.T, grad_rows, preferred_element_type=jnp.float32)
    active_grad = jnp.dot(grad_rows, down_weight.T, preferred_element_type=jnp.float32)
    pre_grad = gelu_back(active_grad)[0].astype(jnp.bfloat16)
    in_weight_grad = jnp.dot(normed_low.T, pre_grad, preferred_element_type=jnp.float32)
    in_bias_grad = jnp.sum(pre_grad.astype(jnp.float32), axis=0)
    mixed_grad = jnp.dot(grad_rows, out_weight.T, preferred_element_type=jnp.float32).astype(
        jnp.bfloat16
    )
    grad_heads = mixed_grad.reshape(shard_rows, windows_here, head_count, HEAD_DIM)
    delta_rows = jnp.sum(grad_heads.astype(jnp.float32) * attention_rows, axis=-1)
    row_delta = jnp.transpose(delta_rows, (1, 2, 0))
    whole_keys = lax.all_gather(key_value, "seq", axis=0, tiled=True)
    blocks = whole_keys.reshape((seq_count, shard_rows) + whole_keys.shape[1:])
    zero_heads = jnp.zeros((shard_rows, windows_here, head_count, HEAD_DIM), jnp.float32)

    def back_block(query_grad, element):
        number, key_block = element
        key_start = number * shard_rows

        def live_block(held_grad):
            scores, key_part, value_part = block_scores(key_block, key_start)
            weighting = jnp.exp(scores - log_total[..., None])
            prob_grad = jnp.einsum(
                "qwhd,kwhd->whqk", grad_heads, value_part, preferred_element_type=jnp.float32
            )
            score_low = (weighting * (prob_grad - row_delta[..., None])).astype(jnp.bfloat16)
            held_grad = held_grad + 0.125 * jnp.einsum(
                "whqk,kwhd->qwhd", score_low, key_part, preferred_element_type=jnp.float32
            )
            key_grad = 0.125 * jnp.einsum(
                "whqk,qwhd->kwhd", score_low, query_low, preferred_element_type=jnp.float32
            )
            value_grad = jnp.einsum(
                "whqk,qwhd->kwhd",
                weighting.astype(jnp.bfloat16),
                grad_heads,
                preferred_element_type=jnp.float32,
            )
            return (
                held_grad,
                jnp.concatenate(
                    [
                        key_grad.reshape(shard_rows, windows_here, model_width),
                        value_grad.reshape(shard_rows, windows_here, model_width),
                    ],
                    axis=-1,
                ),
            )

        def dead_block(held_grad):
            return (held_grad, jnp.zeros((shard_rows, windows_here, 2 * model_width), jnp.float32))

        dead = jnp.min(block_places(key_start, shard_rows)) > own_high
        return lax.cond(dead, dead_block, live_block, query_grad)

    query_grad, key_terms = lax.scan(
        back_block, zero_heads, (jnp.arange(seq_count, dtype=jnp.int32), blocks)
    )
    key_terms = key_terms.reshape((seq_count * shard_rows,) + key_terms.shape[2:])
    summed = lax.psum_scatter(
        key_terms.astype(jnp.bfloat16), "seq", scatter_dimension=0, tiled=True
    ).astype(jnp.float32)
    key_grad = summed[..., :model_width].reshape(shard_rows, windows_here, head_count, HEAD_DIM)
    value_grad = summed[..., model_width:].reshape(shard_rows, windows_here, head_count, HEAD_DIM)
    joined_grad = turn_back((query_grad, key_grad, value_grad))[0].astype(jnp.bfloat16)
    qkv_weight_grad = jnp.dot(normed_low.T, joined_grad, preferred_element_type=jnp.float32)
    normed_grad = jnp.dot(joined_grad, qkv_weight.T, preferred_element_type=jnp.float32) + jnp.dot(
        pre_grad, in_weight.T, preferred_element_type=jnp.float32
    )
    stream_part, norm_gain_grad, norm_bias_grad = norm_back(normed_grad)
    stream_grad = grad_rows.astype(jnp.float32) + stream_part
    result_three = result.reshape(shard_rows, windows_here, model_width)
    grad_three = stream_grad.reshape(shard_rows, windows_here, model_width)
    output = jnp.transpose(result_three, (1, 0, 2)).astype(jnp.bfloat16)
    hidden_grad = jnp.transpose(grad_three, (1, 0, 2))
    shares = (
        lax.psum_scatter(
            norm_gain_grad.astype(jnp.bfloat16), "seq", scatter_dimension=0, tiled=True
        ).astype(jnp.float32),
        lax.psum_scatter(
            norm_bias_grad.astype(jnp.bfloat16), "seq", scatter_dimension=0, tiled=True
        ).astype(jnp.float32),
        lax.psum_scatter(
            qkv_weight_grad.astype(jnp.bfloat16), "seq", scatter_dimension=0, tiled=True
        ).astype(jnp.float32),
        lax.psum_scatter(
            out_weight_grad.astype(jnp.bfloat16), "seq", scatter_dimension=0, tiled=True
        ).astype(jnp.float32),
        lax.psum_scatter(
            in_weight_grad.astype(jnp.bfloat16), "seq", scatter_dimension=0, tiled=True
        ).astype(jnp.float32),
        lax.psum_scatter(
            in_bias_grad.astype(jnp.bfloat16), "seq", scatter_dimension=0, tiled=True
        ).astype(jnp.float32),
        lax.psum_scatter(
            down_weight_grad.astype(jnp.bfloat16), "seq", scatter_dimension=0, tiled=True
        ).astype(jnp.float32),
        lax.psum_scatter(
            down_bias_grad.astype(jnp.bfloat16), "seq", scatter_dimension=0, tiled=True
        ).astype(jnp.float32),
    )
    totals_all = (
        lax.psum(shares[0].astype(jnp.bfloat16), "batch").astype(jnp.float32),
        lax.psum(shares[1].astype(jnp.bfloat16), "batch").astype(jnp.float32),
        lax.psum(shares[2].astype(jnp.bfloat16), "batch").astype(jnp.float32),
        lax.psum(shares[3].astype(jnp.bfloat16), "batch").astype(jnp.float32),
        lax.psum(shares[4].astype(jnp.bfloat16), "batch").astype(jnp.float32),
        lax.psum(shares[5].astype(jnp.bfloat16), "batch").astype(jnp.float32),
        lax.psum(shares[6].astype(jnp.bfloat16), "batch").astype(jnp.float32),
        lax.psum(shares[7].astype(jnp.bfloat16), "batch").astype(jnp.float32),
    )
    return (
        output,
        hidden_grad,
        totals_all[0],
        totals_all[1],
        totals_all[2],
        totals_all[3],
        totals_all[4],
        totals_all[5],
        totals_all[6],
        totals_all[7],
    )


def solution(mesh):
    placed = (
        P("batch", "seq", None),
        P("batch", "seq"),
        P("batch"),
        P("batch"),
        P(),
        P(),
        P(),
        P(),
        P(),
        P(),
        P(),
        P(),
        P(),
        P("batch", "seq", None),
    )

    def body(*arrays):
        hidden = arrays[0]
        owners = mesh.shape["seq"]
        if hidden.shape[0] == 1 and hidden.shape[2] == 2 * PAIR * owners and owners == 4 and mesh.shape["batch"] == 8:
            return fast_body(*arrays)
        return plain_body(*arrays)

    return jax.shard_map(
        body,
        mesh=mesh,
        in_specs=placed,
        out_specs=(
            P("batch", "seq", None),
            P("batch", "seq", None),
            P("seq"),
            P("seq"),
            P("seq", None),
            P("seq", None),
            P("seq", None),
            P("seq"),
            P("seq", None),
            P("seq"),
        ),
        check_vma=False,
    )
```

```python
import math

import jax
import jax.numpy as jnp
import numpy as np
from jax import lax
from jax.experimental import pallas as pl
from jax.experimental.pallas import tpu as pltpu
from jax.sharding import PartitionSpec as P

HEAD_DIM = 64
ROT = 32
PAIR = 2 * HEAD_DIM

EPSILON = 1e-05
BLOCKED = -1e30
LOG2E = math.log2(math.e)
BF16 = jnp.bfloat16
F32 = jnp.float32
MIB = 1 << 20
SHORT = pl.CostEstimate(flops=1000, bytes_accessed=1000, transcendentals=0)
LONG = pl.CostEstimate(flops=10**11, bytes_accessed=1000, transcendentals=0)


def dot_nn(left, right):
    return lax.dot_general(left, right, (((1,), (0,)), ((), ())), preferred_element_type=F32)


def dot_nt(left, right):
    return lax.dot_general(left, right, (((1,), (1,)), ((), ())), preferred_element_type=F32)


def dot_tn(left, right):
    return lax.dot_general(left, right, (((0,), (0,)), ((), ())), preferred_element_type=F32)


def swap_pairs(rows):
    width = rows.shape[1]
    lanes = lax.broadcasted_iota(jnp.int32, rows.shape, 1)
    return jnp.where(lanes % 2 == 0, pltpu.roll(rows, width - 1, 1), pltpu.roll(rows, 1, 1))


def trig_tables(length):
    inverse = 10000.0 ** (-(np.arange(ROT // 2, dtype=np.float32) * np.float32(2.0)) / np.float32(ROT))
    phases = np.arange(length, dtype=np.float32)[:, None] * inverse.astype(np.float32)[None, :]
    cosine = np.ones((length, HEAD_DIM), np.float32)
    sine = np.zeros((length, HEAD_DIM), np.float32)
    cosine[:, :ROT] = np.repeat(np.cos(phases), 2, axis=1)
    sine[:, :ROT] = np.repeat(np.sin(phases), 2, axis=1) * np.tile(np.array([-1.0, 1.0], np.float32), ROT // 2)
    return np.tile(cosine, (1, 2)), np.tile(sine, (1, 2))


def whole(array):
    shape = array.shape
    return pl.BlockSpec(shape, lambda i: (0,) * len(shape))


SCALARS = pl.BlockSpec(memory_space=pltpu.SMEM)


def prep_kernel(hidden_ref, mark_ref, table_ref, gain_ref, bias_ref, stream_ref, normed_ref, turned_ref):
    rows = hidden_ref.shape[0]
    vocab = table_ref.shape[0]
    onehot = (mark_ref[...] == lax.broadcasted_iota(jnp.int32, (rows, vocab), 1)).astype(F32).astype(BF16)
    stream = hidden_ref[...].astype(F32) + dot_nn(onehot, table_ref[...])
    centre = stream - jnp.mean(stream, axis=-1, keepdims=True)
    spread = jnp.mean(centre * centre, axis=-1, keepdims=True)
    normed = centre * lax.rsqrt(spread + EPSILON) * gain_ref[...] + bias_ref[...]
    stream_ref[...] = stream
    normed_ref[...] = normed.astype(BF16)
    turned_ref[...] = normed.astype(BF16).T


def prepare(hidden, marked, table, gain, bias):
    rows, width = hidden.shape
    step = 128
    return pl.pallas_call(
        prep_kernel,
        grid=(rows // step,),
        in_specs=[
            pl.BlockSpec((step, width), lambda i: (i, 0)),
            pl.BlockSpec((step, 1), lambda i: (i, 0)),
            pl.BlockSpec(table.shape, lambda i: (0, 0)),
            pl.BlockSpec((1, width), lambda i: (0, 0)),
            pl.BlockSpec((1, width), lambda i: (0, 0)),
        ],
        out_specs=[
            pl.BlockSpec((step, width), lambda i: (i, 0)),
            pl.BlockSpec((step, width), lambda i: (i, 0)),
            pl.BlockSpec((width, step), lambda i: (0, i)),
        ],
        out_shape=[
            jax.ShapeDtypeStruct((rows, width), F32),
            jax.ShapeDtypeStruct((rows, width), BF16),
            jax.ShapeDtypeStruct((width, rows), BF16),
        ],
        cost_estimate=SHORT,
        name="prep",
    )(hidden, marked, table, gain, bias)


def heads_kernel(owners_ref, normed_ref, cot_ref, wq_ref, wk_ref, wv_ref, wo_ref, cos_ref, sin_ref, *out_refs):
    normed = normed_ref[...]
    shifts = pl.num_programs(0)
    chunks = wq_ref.shape[1] // PAIR
    cosine = jnp.concatenate([cos_ref[...]] * chunks, axis=1)
    sine = jnp.concatenate([sin_ref[...]] * chunks, axis=1)

    def turned(rows):
        return rows * cosine + swap_pairs(rows) * sine

    parts = (
        turned(dot_nn(normed, wq_ref[...])).astype(BF16),
        turned(dot_nn(normed, wk_ref[...])).astype(BF16),
        dot_nn(normed, wv_ref[...]).astype(BF16),
        dot_nt(cot_ref[...], wo_ref[...]).astype(BF16),
    )
    for number, out_ref in enumerate(out_refs):
        shift, chunk = divmod(number, chunks)

        @pl.when(pl.program_id(0) == shift)
        def _():
            for at, part in enumerate(parts):
                out_ref[:, at * PAIR : (at + 1) * PAIR] = part[:, chunk * PAIR : (chunk + 1) * PAIR]


def heads_of(order, normed, cot, qkv_weight, out_weight, cosine, sine):
    rows, width = normed.shape
    owners = order.shape[0]
    wide = width // owners
    chunks = wide // PAIR
    fixed = pl.BlockSpec((rows, width), lambda i, o: (0, 0))
    table = pl.BlockSpec((rows, PAIR), lambda i, o: (o[0], 0))

    def columns(part):
        return pl.BlockSpec((width, wide), lambda i, o: (0, part * owners + o[i]))

    blocks = pl.pallas_call(
        heads_kernel,
        grid_spec=pltpu.PrefetchScalarGridSpec(
            num_scalar_prefetch=1,
            grid=(owners,),
            in_specs=[fixed, fixed]
            + [columns(part) for part in range(3)]
            + [pl.BlockSpec((wide, width), lambda i, o: (o[i], 0)), table, table],
            out_specs=[pl.BlockSpec((rows, 4 * PAIR), lambda i, o: (0, 0))] * (owners * chunks),
        ),
        out_shape=[jax.ShapeDtypeStruct((rows, 4 * PAIR), BF16)] * (owners * chunks),
        compiler_params=pltpu.CompilerParams(vmem_limit_bytes=60 * MIB),
        cost_estimate=SHORT,
        name="heads",
    )(order, normed, cot, qkv_weight, qkv_weight, qkv_weight, out_weight, cosine, sine)
    return [[blocks[shift * chunks + chunk] for shift in range(owners)] for chunk in range(chunks)]


QUERY_ROWS = 512
KEY_ROWS = QUERY_ROWS


def attention_kernel(pieces, info_ref, *refs):
    piece_refs = refs[:pieces]
    cos_ref, sin_ref = refs[pieces : pieces + 2]
    out_refs = refs[pieces + 2 : -9]
    held, results, key_turned, value_turned, doubled, score_ref, raised_ref, key_sum, value_sum = refs[-9:]
    me, end = info_ref[0], info_ref[1]
    rows = piece_refs[0].shape[0]
    length = rows * pieces
    for shift in range(pieces):
        start = pl.multiple_of(lax.rem(me - shift + pieces, pieces) * rows, rows)
        held[pl.ds(start, rows), :] = piece_refs[shift][...]
    key_turned[...] = held[:, PAIR : 2 * PAIR].T
    value_turned[...] = held[:, 2 * PAIR : 3 * PAIR].T
    for head in range(2):
        keys = held[:, PAIR + head * HEAD_DIM : PAIR + (head + 1) * HEAD_DIM]
        doubled[head] = jnp.concatenate([keys, keys], axis=1)
    key_sum[...] = jnp.zeros_like(key_sum)
    value_sum[...] = jnp.zeros_like(value_sum)
    scale = 0.125 * LOG2E
    halves = lax.broadcasted_iota(jnp.int32, (QUERY_ROWS, PAIR), 1) // HEAD_DIM
    causal = lax.broadcasted_iota(jnp.int32, (KEY_ROWS, QUERY_ROWS), 0) <= lax.broadcasted_iota(
        jnp.int32, (KEY_ROWS, QUERY_ROWS), 1
    )
    key_steps = lax.broadcasted_iota(jnp.int32, (KEY_ROWS, QUERY_ROWS), 0)

    def query_block(number, carry):
        first = pl.multiple_of(number * QUERY_ROWS, QUERY_ROWS)
        query_rows = held[pl.ds(first, QUERY_ROWS), 0:PAIR]
        grad_rows = held[pl.ds(first, QUERY_ROWS), 3 * PAIR : 4 * PAIR]
        zero = jnp.zeros_like(query_rows)
        queries = [jnp.where(halves == head, query_rows, zero) for head in range(2)]
        scaled = query_rows.astype(F32) * scale
        large = scaled.astype(BF16)
        small = (scaled - large.astype(F32)).astype(BF16)
        pairs = [
            jnp.concatenate(
                [part[:, head * HEAD_DIM : (head + 1) * HEAD_DIM] for part in (large, small)], axis=1
            )
            for head in range(2)
        ]
        query_places = first + lax.broadcasted_iota(jnp.int32, (1, QUERY_ROWS), 1)
        lowest = jnp.where(query_places > end, end + 1, 0)

        def scores_of(block, highest, diagonal, parted):
            start = pl.multiple_of(block * KEY_ROWS, KEY_ROWS)
            after = []
            for head in range(2):
                scores = dot_nt(doubled[head, pl.ds(start, KEY_ROWS), :], pairs[head])
                if diagonal:
                    scores = jnp.where(causal, scores, BLOCKED)
                if parted:
                    scores = jnp.where(key_steps >= lowest - start, scores, BLOCKED)
                score_ref[head, pl.ds(start, KEY_ROWS), :] = scores
                after.append(jnp.maximum(highest[head], jnp.max(scores, axis=0, keepdims=True)))
            return tuple(after)

        def any_scores(block, highest, diagonal=False):
            parted = (first + QUERY_ROWS - 1 > end) & (block * KEY_ROWS <= end)
            return lax.cond(
                parted,
                lambda held_rows: scores_of(block, held_rows, diagonal, True),
                lambda held_rows: scores_of(block, held_rows, diagonal, False),
                highest,
            )

        start_row = jnp.full((1, QUERY_ROWS), BLOCKED, F32)
        highest = lax.fori_loop(0, number, any_scores, (start_row, start_row))
        highest = any_scores(number, highest, True)

        def mix(block, carried):
            start = pl.multiple_of(block * KEY_ROWS, KEY_ROWS)
            after = []
            for head in range(2):
                total, mixed = carried[head]
                raised = jnp.exp2(score_ref[head, pl.ds(start, KEY_ROWS), :] - highest[head])
                rounded = raised.astype(BF16)
                raised_ref[head, pl.ds(start, KEY_ROWS), :] = rounded
                values = value_turned[head * HEAD_DIM : (head + 1) * HEAD_DIM, pl.ds(start, KEY_ROWS)]
                after.append((total + jnp.sum(raised, axis=0, keepdims=True), mixed + dot_nn(values, rounded)))
            return tuple(after)

        empty = (jnp.zeros((1, QUERY_ROWS), F32), jnp.zeros((HEAD_DIM, QUERY_ROWS), F32))
        mixes = lax.fori_loop(0, number + 1, mix, (empty, empty))
        inverse = [1.0 / mixes[head][0] for head in range(2)]
        mixed = jnp.concatenate([mixes[head][1] * inverse[head] for head in range(2)], axis=0)
        turned = grad_rows.astype(F32).T
        turned = jnp.concatenate(
            [turned[head * HEAD_DIM : (head + 1) * HEAD_DIM] * inverse[head] for head in range(2)], axis=0
        )
        products = mixed * turned
        delta = [
            jnp.sum(products[head * HEAD_DIM : (head + 1) * HEAD_DIM], axis=0, keepdims=True) for head in range(2)
        ]
        divided = turned.T.astype(BF16)
        grads = [jnp.where(halves == head, divided, zero) for head in range(2)]

        def back(block, carried):
            start = pl.multiple_of(block * KEY_ROWS, KEY_ROWS)
            values = held[pl.ds(start, KEY_ROWS), 2 * PAIR : 3 * PAIR]
            after, key_terms, value_terms = [], [], []
            for head in range(2):
                raised = raised_ref[head, pl.ds(start, KEY_ROWS), :]
                score_grad = raised * (dot_nt(values, grads[head]) - delta[head]).astype(BF16)
                value_terms.append(dot_nn(raised, grads[head]))
                key_terms.append(dot_nn(score_grad, queries[head]))
                keys = key_turned[head * HEAD_DIM : (head + 1) * HEAD_DIM, pl.ds(start, KEY_ROWS)]
                after.append(carried[head] + dot_nn(keys, score_grad))
            value_sum[pl.ds(start, KEY_ROWS), :] += value_terms[0] + value_terms[1]
            key_sum[pl.ds(start, KEY_ROWS), :] += key_terms[0] + key_terms[1]
            return tuple(after)

        query_grads = lax.fori_loop(0, number + 1, back, (empty[1], empty[1]))
        query_grad = jnp.concatenate(query_grads, axis=0).T * 0.125
        cosine = cos_ref[pl.ds(first, QUERY_ROWS), :]
        sine = sin_ref[pl.ds(first, QUERY_ROWS), :]
        results[pl.ds(first, QUERY_ROWS), 0:PAIR] = (query_grad * cosine - swap_pairs(query_grad) * sine).astype(BF16)
        results[pl.ds(first, QUERY_ROWS), 3 * PAIR : 4 * PAIR] = mixed.T.astype(BF16)
        return carry

    lax.fori_loop(0, length // QUERY_ROWS, query_block, 0)
    key_grad = key_sum[...] * 0.125
    results[:, PAIR : 2 * PAIR] = (key_grad * cos_ref[...] - swap_pairs(key_grad) * sin_ref[...]).astype(BF16)
    results[:, 2 * PAIR : 3 * PAIR] = value_sum[...].astype(BF16)
    for shift in range(pieces):
        start = pl.multiple_of(lax.rem(me + shift, pieces) * rows, rows)
        out_refs[shift][...] = results[pl.ds(start, rows), :]


def attention(info, parts, cosine, sine):
    pieces = len(parts)
    rows = parts[0].shape[0]
    length = rows * pieces
    arrays = (*parts, cosine, sine)
    shapes = [jax.ShapeDtypeStruct((rows, 4 * PAIR), BF16)] * pieces
    return pl.pallas_call(
        lambda *refs: attention_kernel(pieces, *refs),
        grid=(1,),
        in_specs=[SCALARS] + [whole(array) for array in arrays],
        out_specs=[whole(shape) for shape in shapes],
        out_shape=shapes,
        scratch_shapes=[
            pltpu.VMEM((length, 4 * PAIR), BF16),
            pltpu.VMEM((length, 4 * PAIR), BF16),
            pltpu.VMEM((PAIR, length), BF16),
            pltpu.VMEM((PAIR, length), BF16),
            pltpu.VMEM((2, length, PAIR), BF16),
            pltpu.VMEM((2, length, QUERY_ROWS), F32),
            pltpu.VMEM((2, length, QUERY_ROWS), BF16),
            pltpu.VMEM((length, PAIR), F32),
            pltpu.VMEM((length, PAIR), F32),
        ],
        compiler_params=pltpu.CompilerParams(vmem_limit_bytes=60 * MIB),
        cost_estimate=SHORT,
        name="attention",
    )(info, *arrays)


def feed_kernel(cells_ref, normed_ref, turned_ref, cot_ref, in_ref, bias_ref, down_ref, *out_refs):
    sides = (out_refs[0:2], out_refs[2:4])
    bias_grad, out_sum, norm_sum = out_refs[4:]
    step = pl.program_id(0)
    steps = pl.num_programs(0) // 2
    up = math.sqrt(2.0 / math.pi)

    @pl.when(step == 0)
    def _():
        out_sum[...] = jnp.zeros_like(out_sum)
        norm_sum[...] = jnp.zeros_like(norm_sum)

    weights = in_ref[...]
    downs = down_ref[...]
    cot = cot_ref[...]
    pre = dot_nn(normed_ref[...], weights) + bias_ref[...]
    square = pre * pre
    tanh = jnp.tanh(up * pre * (1.0 + 0.044715 * square))
    half = 0.5 * (1.0 + tanh)
    active = (pre * half).astype(BF16)
    slope = half + 0.5 * pre * (1.0 - tanh * tanh) * (up * (1.0 + 3 * 0.044715 * square))
    pre_grad = (dot_nt(cot, downs) * slope).astype(BF16)
    in_term = dot_nn(turned_ref[...], pre_grad).astype(BF16)
    down_term = dot_tn(active, cot).astype(BF16)
    for side, (in_grad, down_grad) in enumerate(sides):

        @pl.when((step >= steps) == bool(side))
        def _():
            pieces, owners, kept, tile = in_grad.shape
            for owner in range(owners):
                for piece in range(pieces):
                    start = (owner * pieces + piece) * kept
                    in_grad[piece, owner] = in_term[start : start + kept]
            kept = tile // pieces
            for group in range(down_term.shape[1] // tile):
                for piece in range(pieces):
                    down_grad[piece, 0, group * kept : (group + 1) * kept] = down_term[
                        piece * kept : (piece + 1) * kept, group * tile : (group + 1) * tile
                    ]

    bias_grad[0] = jnp.sum(pre_grad.astype(F32), axis=0, keepdims=True)
    out_sum[...] += dot_nn(active, downs)
    norm_sum[...] += dot_nt(pre_grad, weights)


def feed_forward(cells, normed, turned, cot, in_weight, in_bias, down_weight, pieces):
    rows, width = normed.shape
    steps = cells.shape[0]
    owners = steps // 2
    hidden_units = in_weight.shape[1]
    tile = hidden_units // steps
    kept = width // owners // pieces
    tall = owners * kept
    wide = tile // pieces * (width // tile)
    fixed = pl.BlockSpec((rows, width), lambda i, c: (0, 0))

    def first(i):
        return jnp.minimum(i, owners - 1)

    def second(i):
        return jnp.maximum(i - owners, 0)

    def sides_of(turn):
        return [
            pl.BlockSpec((pieces, owners, kept, tile), lambda i, c: (0, 0, turn(i), 0)),
            pl.BlockSpec((pieces, 1, wide, tile), lambda i, c: (0, turn(i), 0, 0)),
        ]

    grads = [
        jax.ShapeDtypeStruct((pieces, owners, tall, tile), BF16),
        jax.ShapeDtypeStruct((pieces, owners, wide, tile), BF16),
    ]
    full = jax.ShapeDtypeStruct((rows, width), F32)
    results = pl.pallas_call(
        feed_kernel,
        grid_spec=pltpu.PrefetchScalarGridSpec(
            num_scalar_prefetch=1,
            grid=(steps,),
            in_specs=[
                fixed,
                pl.BlockSpec((width, rows), lambda i, c: (0, 0)),
                fixed,
                pl.BlockSpec((width, tile), lambda i, c: (0, c[i])),
                pl.BlockSpec((1, tile), lambda i, c: (0, c[i])),
                pl.BlockSpec((tile, width), lambda i, c: (c[i], 0)),
            ],
            out_specs=sides_of(first)
            + sides_of(second)
            + [pl.BlockSpec((1, 1, tile), lambda i, c: (i, 0, 0)), fixed, fixed],
        ),
        out_shape=grads + grads + [jax.ShapeDtypeStruct((steps, 1, tile), F32), full, full],
        compiler_params=pltpu.CompilerParams(vmem_limit_bytes=60 * MIB),
        cost_estimate=SHORT,
        name="feed",
    )(cells, normed, turned, cot, in_weight, in_bias, down_weight)
    return results[:2], results[2:4], *results[4:]


def place_columns(me_ref, piece_refs, held):
    owners = len(piece_refs)
    for shift in range(owners):
        owner = lax.rem(me_ref[0] - shift + owners, owners)
        start = pl.multiple_of(owner * PAIR, PAIR)
        for part in range(4):
            held[part, :, pl.ds(start, PAIR)] = piece_refs[shift][:, part * PAIR : (part + 1) * PAIR]


def weight_kernel(pieces, info_ref, turned_ref, cot_ref, *refs):
    owners = len(refs) - 4
    kept_ref, sent_ref, held, grad = refs[-4:]
    place_columns(info_ref, refs[:owners], held)
    kept = PAIR // pieces
    turned = turned_ref[...]
    for part in range(3):
        grad[...] = dot_nn(turned, held[part]).astype(BF16)
        for side, ref in enumerate((kept_ref, sent_ref)):
            core = info_ref[1] ^ side
            for owner in range(owners):
                for piece in range(pieces):
                    start = pl.multiple_of(((owner * 2 + core) * pieces + piece) * kept, kept)
                    ref[piece, owner, part * kept : (part + 1) * kept] = grad[pl.ds(start, kept), :]
    term = dot_tn(held[3], cot_ref[...]).astype(BF16)
    rows, half = term.shape[0], term.shape[1] // 2
    for core in range(2):
        grad[core * rows : (core + 1) * rows, :] = term[:, core * half : (core + 1) * half]
    for side, ref in enumerate((kept_ref, sent_ref)):
        core = info_ref[1] ^ side
        for owner in range(owners):
            for piece in range(pieces):
                start = pl.multiple_of(core * rows + (owner * pieces + piece) * kept, kept)
                ref[piece, owner, 3 * kept :] = grad[pl.ds(start, kept), :]


def weight_grads(info, turned, cot, parts, pieces):
    owners = len(parts)
    rows, width = cot.shape
    kept = PAIR // pieces
    arrays = (turned, cot, *parts)
    shape = jax.ShapeDtypeStruct((pieces, owners, 4 * kept, owners * PAIR), BF16)
    return pl.pallas_call(
        lambda *refs: weight_kernel(pieces, *refs),
        grid=(1,),
        in_specs=[SCALARS] + [whole(array) for array in arrays],
        out_specs=[whole(shape)] * 2,
        out_shape=[shape] * 2,
        scratch_shapes=[pltpu.VMEM((4, rows, owners * PAIR), BF16), pltpu.VMEM((width, owners * PAIR), BF16)],
        compiler_params=pltpu.CompilerParams(vmem_limit_bytes=60 * MIB),
        cost_estimate=SHORT,
        name="weight_grads",
    )(info, *arrays)


def sums_kernel(last, owners, me_ref, *refs):
    piece_refs, refs = refs[:owners], refs[owners:]
    weight_refs, refs = refs[: 3 * owners], refs[3 * owners :]
    out_weight_refs, refs = refs[:owners], refs[owners:]
    out_in, norm_in = refs[:2]
    held = refs[-1]
    place_columns(me_ref, piece_refs, held)
    norm = norm_in[...]
    for part in range(3):
        weights = jnp.concatenate([ref[...] for ref in weight_refs[part * owners : (part + 1) * owners]], axis=1)
        norm = norm + dot_nt(held[part], weights)
    weights = jnp.concatenate([ref[...] for ref in out_weight_refs], axis=0)
    out = out_in[...] + dot_nn(held[3], weights)
    if not last:
        out_ref, norm_ref = refs[2:4]
        out_ref[...] = out
        norm_ref[...] = norm
        return
    stream_ref, cot_ref, gain_ref, down_bias_ref, out_ref, hidden_ref, gain_grad, bias_grad = refs[2:-1]
    stream = stream_ref[...]
    cot = cot_ref[...].astype(F32)
    out_ref[...] = (stream + out + down_bias_ref[...]).astype(BF16)
    centre = stream - jnp.mean(stream, axis=-1, keepdims=True)
    spread = jnp.mean(centre * centre, axis=-1, keepdims=True)
    inverse = lax.rsqrt(spread + EPSILON)
    hat = centre * inverse
    gained = norm * gain_ref[...]
    hidden_ref[...] = cot + inverse * (
        gained
        - jnp.mean(gained, axis=-1, keepdims=True)
        - hat * jnp.mean(gained * hat, axis=-1, keepdims=True)
    )
    for out_ref, rows in ((gain_grad, norm * hat), (bias_grad, norm)):
        row = jnp.sum(rows, axis=0, keepdims=True)
        wide = out_ref.shape[1]
        for owner in range(owners):
            out_ref[owner : owner + 1, :] = row[:, owner * wide : (owner + 1) * wide]


def sums_of(info, chunk, chunks, parts, qkv_weight, out_weight, sums, final=()):
    owners = len(parts)
    rows = parts[0].shape[0]
    width = qkv_weight.shape[0]
    last = bool(final)

    def columns(part, owner):
        at = (part * owners + owner) * chunks + chunk
        return pl.BlockSpec((width, PAIR), lambda i: (0, at))

    def weight_rows(owner):
        return pl.BlockSpec((PAIR, width), lambda i: (owner * chunks + chunk, 0))

    full = jax.ShapeDtypeStruct((rows, width), F32)
    row = jax.ShapeDtypeStruct((owners, width // owners), F32)
    shapes = [jax.ShapeDtypeStruct((rows, width), BF16), full, row, row] if last else [full, full]
    return pl.pallas_call(
        lambda *refs: sums_kernel(last, owners, *refs),
        grid=(1,),
        in_specs=[SCALARS]
        + [whole(part) for part in parts]
        + [columns(part, owner) for part in range(3) for owner in range(owners)]
        + [weight_rows(owner) for owner in range(owners)]
        + [whole(array) for array in (*sums, *final)],
        out_specs=[whole(shape) for shape in shapes],
        out_shape=shapes,
        scratch_shapes=[pltpu.VMEM((4, rows, owners * PAIR), BF16)],
        compiler_params=pltpu.CompilerParams(vmem_limit_bytes=60 * MIB),
        cost_estimate=SHORT,
        name="sums",
    )(info, *parts, *([qkv_weight] * (3 * owners)), *([out_weight] * owners), *sums, *final)


def feed_place_kernel(info_ref, mine_ref, other_ref, in_ref, down_ref):
    masks, total, tile = mine_ref.shape
    kept = in_ref.shape[0] // masks
    tiles = in_ref.shape[1] // (2 * tile)
    half = down_ref.shape[0] // 2
    down_kept = half // masks
    for source, ref in enumerate((mine_ref, other_ref)):
        core = info_ref[0] ^ source
        for mask in range(masks):
            chip = info_ref[1] ^ mask
            rows = pl.ds(pl.multiple_of(chip * kept, kept), kept)
            for number in range(tiles):
                columns = pl.ds(pl.multiple_of((2 * number + core) * tile, tile), tile)
                in_ref[rows, columns] = ref[mask, number * kept : (number + 1) * kept].astype(F32)
            rows = pl.ds(pl.multiple_of(core * half + chip * down_kept, down_kept), down_kept)
            for group in range(down_ref.shape[1] // tile):
                at = tiles * kept + group * down_kept
                down_ref[rows, group * tile : (group + 1) * tile] = ref[mask, at : at + down_kept].astype(F32)


def place_feed(info, mine, other, in_shape, down_shape):
    shapes = [jax.ShapeDtypeStruct(in_shape, F32), jax.ShapeDtypeStruct(down_shape, F32)]
    return pl.pallas_call(
        feed_place_kernel,
        grid=(1,),
        in_specs=[SCALARS, whole(mine), whole(other)],
        out_specs=[whole(shape) for shape in shapes],
        out_shape=shapes,
        compiler_params=pltpu.CompilerParams(vmem_limit_bytes=60 * MIB),
        cost_estimate=SHORT,
        name="place_feed",
    )(info, mine, other)


def heads_place_kernel(info_ref, mine_ref, other_ref, qkv_ref, out_ref):
    core, place = info_ref[0], info_ref[1]
    masks, total, wide = mine_ref.shape
    own_rows, width = out_ref.shape
    kept = own_rows // 2 // masks
    chunks = total // (4 * kept)
    owners = wide // PAIR
    for source, ref in enumerate((mine_ref, other_ref)):
        at_core = core if source == 0 else 1 - core
        columns = pl.ds(pl.multiple_of(at_core * (width // 2), width // 2), width // 2)
        for mask in range(masks):
            piece = place ^ mask
            rows = pl.ds(pl.multiple_of(at_core * (own_rows // 2) + piece * kept, kept), kept)
            for chunk in range(chunks):
                at = chunk * 4 * kept
                for part in range(3):
                    block = ref[mask, at + part * kept : at + (part + 1) * kept].astype(F32)
                    for owner in range(owners):
                        column = part * width + (owner * chunks + chunk) * PAIR
                        qkv_ref[rows, column : column + PAIR] = block[:, owner * PAIR : (owner + 1) * PAIR]
                out_rows = pl.ds(pl.multiple_of(chunk * PAIR + piece * kept, kept), kept)
                out_ref[out_rows, columns] = ref[mask, at + 3 * kept : at + 4 * kept].astype(F32)


def place_heads(info, mine, other, own_rows, width):
    shapes = [jax.ShapeDtypeStruct((own_rows, 3 * width), F32), jax.ShapeDtypeStruct((own_rows, width), F32)]
    return pl.pallas_call(
        heads_place_kernel,
        grid=(1,),
        in_specs=[SCALARS, whole(mine), whole(other)],
        out_specs=[whole(shape) for shape in shapes],
        out_shape=shapes,
        compiler_params=pltpu.CompilerParams(vmem_limit_bytes=60 * MIB),
        cost_estimate=SHORT,
        name="place_heads",
    )(info, mine, other)


def exchange(rows, axis, mask):
    size = lax.axis_size(axis)
    return lax.ppermute(rows, axis, [(place, place ^ mask) for place in range(size)])


def around(rows, shift):
    owners = lax.axis_size("seq")
    return lax.ppermute(rows, "seq", [(place, (place + shift) % owners) for place in range(owners)])


def total_of(*terms):
    return sum(term.astype(F32) for term in terms).astype(BF16)


def picked(rows, index, dim=0):
    return lax.dynamic_index_in_dim(rows, index, dim, keepdims=False)


def add_kernel(places, bits_ref, *refs):
    outs = refs[len(refs) - len(places) :]
    for out_ref, terms in zip(outs, places):
        at = 0
        for left, right in terms:
            rows = refs[left].shape[-2]
            total = refs[left][...].astype(F32) + refs[right][...].astype(F32)
            out_ref[..., at : at + rows, :] = total.reshape(out_ref.shape[:-2] + total.shape[-2:]).astype(BF16)
            at += rows


def add_pieces(kept, arrived):
    pieces, owners = kept[0].shape[:2]
    arrays = [array for pair in zip(kept, arrived) for array in pair]
    rows = sum(array.shape[2] for array in kept)
    columns = kept[0].shape[3]
    return pl.pallas_call(
        lambda *refs: add_kernel([[(0, 1), (2, 3)]], None, *refs),
        grid=(pieces,),
        in_specs=[pl.BlockSpec((1,) + array.shape[1:], lambda i: (i, 0, 0, 0)) for array in arrays],
        out_specs=pl.BlockSpec((1, owners, rows, columns), lambda i: (i, 0, 0, 0)),
        out_shape=jax.ShapeDtypeStruct((pieces, owners, rows, columns), BF16),
        compiler_params=pltpu.CompilerParams(vmem_limit_bytes=60 * MIB),
        cost_estimate=SHORT,
        name="add_pieces",
    )(*arrays)


def add_for_chips(chip, kept, arrived):
    specs, places, arrays = [], [], []
    chips, owners = kept[0].shape[:2]
    for mask in range(chips):
        terms = []
        for mine, other in zip(kept, arrived):
            terms.append((len(arrays), len(arrays) + 1))
            arrays += [mine, other]
            specs += [pl.BlockSpec((1,) + mine.shape[1:], lambda i, c, mask=mask: (c[0] ^ mask, 0, 0, 0))] * 2
        places.append(terms)
    rows = sum(array.shape[2] for array in kept)
    out = jax.ShapeDtypeStruct((owners, rows, kept[0].shape[3]), BF16)
    return pl.pallas_call(
        lambda *refs: add_kernel(places, *refs),
        grid_spec=pltpu.PrefetchScalarGridSpec(
            num_scalar_prefetch=1,
            grid=(1,),
            in_specs=specs,
            out_specs=[pl.BlockSpec(out.shape, lambda i, c: (0, 0, 0))] * chips,
        ),
        out_shape=[out] * chips,
        cost_estimate=SHORT,
        name="add_for_chips",
    )(chip[None], *arrays)


class Order:
    token = None

    def __call__(self, value):
        if self.token is None:
            return value
        return lax.optimization_barrier((value, self.token))[0]

    def done(self, token):
        self.token = token
        return token

    def also(self, *tokens):
        self.token = (self.token, tokens)


def fast_body(
    hidden,
    token_ids,
    offsets,
    end_places,
    token_table,
    norm_gain,
    norm_bias,
    qkv_weight,
    out_weight,
    in_weight,
    in_bias,
    down_weight,
    down_bias,
    cotangent,
):
    width = hidden.shape[2]
    rows = hidden.shape[1]
    owners = lax.axis_size("seq")
    pieces = lax.axis_size("batch")
    me = lax.axis_index("seq")
    core = lax.axis_index("batch") & 1
    length = rows * owners
    own_rows = width // owners
    chunks = own_rows // PAIR
    end = end_places[0]

    places = me * rows + jnp.arange(rows, dtype=jnp.int32)[:, None]
    marked = token_ids.reshape(rows, 1)
    marked = jnp.where(places == end, 2, marked)
    marked = jnp.where(places == end + 1, 1, marked)
    marked = jnp.where((places == 0) & (offsets[0] == 0), 1, marked)
    cot = cotangent.reshape(rows, width)
    stream, normed, turned = prepare(
        hidden.reshape(rows, width), marked, token_table, norm_gain[None], norm_bias[None]
    )
    cosine, sine = (jnp.asarray(table) for table in trig_tables(length))
    place = lax.axis_index("batch")
    info = jnp.stack([me, core]).astype(jnp.int32)
    spots = jnp.stack([me, end]).astype(jnp.int32)
    order = Order()

    def moved(blocks, shifts=(2, 1, 3)):
        return {shift: around(blocks[shift], shift) for shift in shifts}

    def gathered(blocks, arrived):
        return [blocks[0]] + [arrived[shift] for shift in range(1, owners)]

    def back(rows):
        return [exchange(rows, "batch", mask) for mask in (2, 4, 6)]

    shifts = lax.rem(me + jnp.arange(owners, dtype=jnp.int32), owners)
    heads = order.done(heads_of(shifts, normed, cot, qkv_weight, out_weight, cosine, sine))

    arrived = moved(order(heads[0]))
    cells = 2 * jnp.arange(owners, dtype=jnp.int32)
    cells = jnp.concatenate([cells + 1 - core, cells + core])
    away, here, in_bias_grad, out_sum, norm_sum = order.done(
        feed_forward(cells, order(normed), turned, cot, in_weight, in_bias[None], down_weight, pieces // 2)
    )
    order.also(arrived)

    feed_arrived = [exchange(array, "batch", 1) for array in order(away)]
    later = moved(order(heads[1]))
    first = order.done(attention(spots, gathered(heads[0], order(arrived)), cosine, sine))
    order.also(feed_arrived)
    feed_rows = order.done(add_pieces(order(here), feed_arrived))
    order.also(later)

    groups = [list(range(number, pieces, 2)) for number in range(2)]
    feed_rows = lax.psum_scatter(
        order(feed_rows), "batch", scatter_dimension=0, axis_index_groups=groups, tiled=False
    )
    arrived = moved(order(first))
    second = order.done(attention(spots, gathered(heads[1], order(later)), cosine, sine))
    cot_sum = order.done(jnp.sum(order(cot).astype(F32), axis=0))
    order.also(arrived)

    later = moved(order(second))
    parts = gathered(first, order(arrived))
    sums = order.done(sums_of(info, 0, chunks, order(parts), qkv_weight, out_weight, (out_sum, norm_sum)))
    first_kept, first_sent = order.done(weight_grads(info, turned, cot, order(parts), pieces // 2))
    order.also(later, feed_rows)

    feed_rows = lax.psum_scatter(order(feed_rows), "seq", scatter_dimension=0, tiled=False)
    grad_arrived = exchange(order(first_sent), "batch", 1)
    parts = gathered(second, order(later))
    second_kept, second_sent = order.done(weight_grads(info, turned, cot, parts, pieces // 2))
    order.also(grad_arrived)
    first_held = order.done(add_for_chips(place >> 1, [order(first_kept)], [grad_arrived]))

    first_arrived = [exchange(order(first_held[mask]), "batch", 2 * mask) for mask in (1, 2, 3)]
    grad_arrived = exchange(order(second_sent), "batch", 1)
    output, hidden_grad, gain_grad, bias_grad = order.done(
        sums_of(
            info, 1, chunks, order(parts), qkv_weight, out_weight, sums, (stream, cot, norm_gain[None], down_bias[None])
        )
    )
    order.also(first_arrived, grad_arrived)
    second_held = order.done(add_for_chips(place >> 1, [order(second_kept)], [grad_arrived]))

    def halve_seq(rows, number):
        bit = (me >> number) & 1
        split = rows.reshape((rows.shape[0] // 2, 2) + rows.shape[1:])
        return picked(split, bit, 1), exchange(picked(split, 1 - bit, 1), "seq", 1 << number)

    second_arrived = [exchange(order(second_held[mask]), "batch", 2 * mask) for mask in (1, 2, 3)]
    in_bias_grad = order(in_bias_grad)
    bias_low = jnp.where(core == 0, in_bias_grad[owners:], in_bias_grad[:owners])
    bias_high = jnp.where(core == 0, in_bias_grad[:owners], in_bias_grad[owners:])
    small = order.done(
        jnp.concatenate(
            [
                jnp.concatenate([bias_low, bias_high], axis=1).reshape(owners, -1),
                cot_sum.reshape(owners, -1),
                gain_grad,
                bias_grad,
            ],
            axis=1,
        )
    )
    order.also(second_arrived, feed_rows)
    grad_rows = order.done(
        jnp.concatenate(
            [
                total_of(order(held[0]), *arrived)
                for held, arrived in ((first_held, first_arrived), (second_held, second_arrived))
            ],
            axis=1,
        )
    )

    feed_rows = order(feed_rows)
    feed_back = [exchange(feed_rows, "batch", mask) for mask in (2, 4)]
    small_arrived = exchange(order(small), "batch", 1)
    grad_rows, grad_arrived = halve_seq(order(grad_rows), 0)
    order.also(feed_back, grad_arrived, small_arrived)
    small = small + order(small_arrived)
    grad_rows = total_of(order(grad_rows), grad_arrived)
    order.done((grad_rows, small))

    feed_back.append(exchange(order(feed_rows), "batch", 6))
    small_arrived = back(order(small))
    grad_rows, grad_arrived = halve_seq(order(grad_rows), 1)
    order.also(feed_back, grad_arrived, small_arrived)
    grad_rows = total_of(order(grad_rows), grad_arrived)[0]
    small = sum(order(small_arrived), small)
    feed_mine = jnp.stack([feed_rows] + order(feed_back))
    order.done((grad_rows, feed_mine, small))

    grad_back = back(order(grad_rows))
    feed_other = exchange(order(feed_mine), "batch", 1)
    place_info = jnp.stack([core, place >> 1]).astype(jnp.int32)
    in_weight_grad, down_weight_grad = order.done(
        place_feed(
            place_info,
            order(feed_mine),
            feed_other,
            (own_rows, in_weight.shape[1]),
            (down_weight.shape[0] // owners, width),
        )
    )
    order.also(grad_back)
    grad_mine = order.done(jnp.stack([grad_rows] + order(grad_back)))

    grad_other = exchange(order(grad_mine), "batch", 1)
    small_arrived = [around(order(small), shift) for shift in range(1, owners)]
    qkv_weight_grad, out_weight_grad = place_heads(place_info, order(grad_mine), grad_other, own_rows, width)
    small = picked(sum(order(small_arrived), small), me)
    few = own_rows
    many = in_bias.shape[0] // owners
    return (
        output[None],
        hidden_grad[None],
        small[many + few : many + 2 * few],
        small[many + 2 * few :],
        qkv_weight_grad,
        out_weight_grad,
        in_weight_grad,
        small[:many],
        down_weight_grad,
        small[many : many + few],
    )


def rotate(vectors, cosine_table, sine_table):
    even_part = vectors[..., 0:ROT:2]
    odd_part = vectors[..., 1:ROT:2]
    turned = jnp.stack(
        [
            even_part * cosine_table - odd_part * sine_table,
            odd_part * cosine_table + even_part * sine_table,
        ],
        axis=-1,
    )
    turned = turned.reshape(vectors.shape[:-1] + (ROT,))
    return jnp.concatenate([turned, vectors[..., ROT:]], axis=-1)


def angles(places):
    inverse = 10000.0 ** (-(jnp.arange(ROT // 2, dtype=jnp.float32) * 2.0) / ROT)
    phases = places.astype(jnp.float32)[:, None] * inverse[None, :]
    return (jnp.cos(phases), jnp.sin(phases))


def visible(query_places, key_places, end_places):
    query_after = query_places[None, :, None] > end_places[:, None, None]
    key_after = key_places[None, None, :] > end_places[:, None, None]
    return (key_places[None, None, :] <= query_places[None, :, None]) & (query_after == key_after)


def norm_rows(stream, gain_row, bias_row):
    centre = stream - jnp.mean(stream, axis=-1, keepdims=True)
    spread = jnp.mean(centre * centre, axis=-1, keepdims=True)
    return centre * lax.rsqrt(spread + EPSILON) * gain_row + bias_row


def gelu_rows(pre_active):
    return jax.nn.gelu(pre_active, approximate=True)


def plain_body(
    hidden,
    token_ids,
    offsets,
    end_places,
    token_table,
    norm_gain,
    norm_bias,
    qkv_weight,
    out_weight,
    in_weight,
    in_bias,
    down_weight,
    down_bias,
    cotangent,
):
    windows_here, shard_rows, model_width = hidden.shape
    head_count = model_width // HEAD_DIM
    seq_count = lax.axis_size("seq")
    seq_place = lax.axis_index("seq")
    home_places = seq_place * shard_rows + jnp.arange(shard_rows, dtype=jnp.int32)
    token_rows = shard_rows * windows_here
    marked = token_ids.T
    marked = jnp.where(home_places[:, None] == end_places[None, :], 2, marked)
    marked = jnp.where(home_places[:, None] == end_places[None, :] + 1, 1, marked)
    marked = jnp.where((home_places[:, None] == 0) & (offsets[None, :] == 0), 1, marked)
    onehot = (marked[..., None] == jnp.arange(token_table.shape[0], dtype=jnp.int32)).astype(
        jnp.bfloat16
    )
    embedded = jnp.einsum("swv,vd->swd", onehot, token_table, preferred_element_type=jnp.float32)
    stream_three = jnp.transpose(hidden, (1, 0, 2)).astype(jnp.float32) + embedded
    cot_three = jnp.transpose(cotangent, (1, 0, 2))
    own_high = jnp.max(home_places)
    stream_rows = stream_three.reshape(token_rows, model_width)
    normed, norm_back = jax.vjp(norm_rows, stream_rows, norm_gain, norm_bias)
    normed_low = normed.astype(jnp.bfloat16)
    projected = jnp.dot(normed_low, qkv_weight, preferred_element_type=jnp.float32)
    cosine_table, sine_table = angles(home_places)
    cosine_table = cosine_table[:, None, None, :]
    sine_table = sine_table[:, None, None, :]

    def turn_heads(projected_rows):
        divided = projected_rows.reshape(shard_rows, windows_here, 3, head_count, HEAD_DIM)
        return (
            rotate(divided[:, :, 0], cosine_table, sine_table),
            rotate(divided[:, :, 1], cosine_table, sine_table),
            divided[:, :, 2],
        )

    (queries, key_rows, values), turn_back = jax.vjp(turn_heads, projected)
    query_low = queries.astype(jnp.bfloat16)
    key_value = jnp.concatenate(
        [
            key_rows.reshape(shard_rows, windows_here, model_width),
            values.reshape(shard_rows, windows_here, model_width),
        ],
        axis=-1,
    ).astype(jnp.bfloat16)

    def split_block(key_block):
        row_count = key_block.shape[0]
        return (
            key_block[..., :model_width].reshape(row_count, windows_here, head_count, HEAD_DIM),
            key_block[..., model_width:].reshape(row_count, windows_here, head_count, HEAD_DIM),
        )

    def block_places(row_start, row_count):
        return row_start + jnp.arange(row_count, dtype=jnp.int32)

    def block_scores(key_block, key_start):
        key_part, value_part = split_block(key_block)
        key_places = block_places(key_start, key_block.shape[0])
        scores = (
            jnp.einsum("qwhd,kwhd->whqk", query_low, key_part, preferred_element_type=jnp.float32)
            * 0.125
        )
        scores = jnp.where(visible(home_places, key_places, end_places)[:, None], scores, BLOCKED)
        return (scores, key_part, value_part)

    def attend(carried, key_block, key_start):
        running, totals, accumulated = carried
        scores, key_part, value_part = block_scores(key_block, key_start)
        highest = jnp.maximum(running, jnp.max(scores, axis=-1))
        factor = jnp.exp(running - highest)
        raised = jnp.exp(scores - highest[..., None])
        totals = totals * factor + jnp.sum(raised, axis=-1)
        accumulated = accumulated * factor[..., None] + jnp.einsum(
            "whqk,kwhd->whqd",
            raised.astype(jnp.bfloat16),
            value_part,
            preferred_element_type=jnp.float32,
        )
        return (highest, totals, accumulated)

    start_state = (
        jnp.full((windows_here, head_count, shard_rows), BLOCKED, jnp.float32),
        jnp.zeros((windows_here, head_count, shard_rows), jnp.float32),
        jnp.zeros((windows_here, head_count, shard_rows, HEAD_DIM), jnp.float32),
    )
    carried = start_state
    fetched_rows = lax.all_gather(key_value, "seq", axis=0, tiled=True)
    row_count = fetched_rows.shape[0]
    blocks = fetched_rows.reshape((row_count // shard_rows, shard_rows) + fetched_rows.shape[1:])

    def visit_block(held_state, element):
        number, key_block = element
        key_start = number * shard_rows
        dead = jnp.min(block_places(key_start, shard_rows)) > own_high
        held_state = lax.cond(
            dead,
            lambda kept_state: kept_state,
            lambda kept_state: attend(kept_state, key_block, key_start),
            held_state,
        )
        return (held_state, None)

    carried, unused = lax.scan(
        visit_block, carried, (jnp.arange(blocks.shape[0], dtype=jnp.int32), blocks)
    )
    running, totals, accumulated = carried
    attention = accumulated / totals[..., None]
    log_total = running + jnp.log(totals)
    attention_rows = jnp.transpose(attention, (2, 0, 1, 3))
    mixed_low = attention_rows.reshape(token_rows, model_width).astype(jnp.bfloat16)
    attended = jnp.dot(mixed_low, out_weight, preferred_element_type=jnp.float32)
    pre_active = jnp.dot(normed_low, in_weight, preferred_element_type=jnp.float32) + in_bias
    active, gelu_back = jax.vjp(gelu_rows, pre_active)
    active_low = active.astype(jnp.bfloat16)
    result = (
        stream_rows
        + attended
        + jnp.dot(active_low, down_weight, preferred_element_type=jnp.float32)
        + down_bias
    )
    grad_rows = cot_three.reshape(token_rows, model_width)
    down_weight_grad = jnp.dot(active_low.T, grad_rows, preferred_element_type=jnp.float32)
    down_bias_grad = jnp.sum(grad_rows.astype(jnp.float32), axis=0)
    out_weight_grad = jnp.dot(mixed_low.T, grad_rows, preferred_element_type=jnp.float32)
    active_grad = jnp.dot(grad_rows, down_weight.T, preferred_element_type=jnp.float32)
    pre_grad = gelu_back(active_grad)[0].astype(jnp.bfloat16)
    in_weight_grad = jnp.dot(normed_low.T, pre_grad, preferred_element_type=jnp.float32)
    in_bias_grad = jnp.sum(pre_grad.astype(jnp.float32), axis=0)
    mixed_grad = jnp.dot(grad_rows, out_weight.T, preferred_element_type=jnp.float32).astype(
        jnp.bfloat16
    )
    grad_heads = mixed_grad.reshape(shard_rows, windows_here, head_count, HEAD_DIM)
    delta_rows = jnp.sum(grad_heads.astype(jnp.float32) * attention_rows, axis=-1)
    row_delta = jnp.transpose(delta_rows, (1, 2, 0))
    whole_keys = lax.all_gather(key_value, "seq", axis=0, tiled=True)
    blocks = whole_keys.reshape((seq_count, shard_rows) + whole_keys.shape[1:])
    zero_heads = jnp.zeros((shard_rows, windows_here, head_count, HEAD_DIM), jnp.float32)

    def back_block(query_grad, element):
        number, key_block = element
        key_start = number * shard_rows

        def live_block(held_grad):
            scores, key_part, value_part = block_scores(key_block, key_start)
            weighting = jnp.exp(scores - log_total[..., None])
            prob_grad = jnp.einsum(
                "qwhd,kwhd->whqk", grad_heads, value_part, preferred_element_type=jnp.float32
            )
            score_low = (weighting * (prob_grad - row_delta[..., None])).astype(jnp.bfloat16)
            held_grad = held_grad + 0.125 * jnp.einsum(
                "whqk,kwhd->qwhd", score_low, key_part, preferred_element_type=jnp.float32
            )
            key_grad = 0.125 * jnp.einsum(
                "whqk,qwhd->kwhd", score_low, query_low, preferred_element_type=jnp.float32
            )
            value_grad = jnp.einsum(
                "whqk,qwhd->kwhd",
                weighting.astype(jnp.bfloat16),
                grad_heads,
                preferred_element_type=jnp.float32,
            )
            return (
                held_grad,
                jnp.concatenate(
                    [
                        key_grad.reshape(shard_rows, windows_here, model_width),
                        value_grad.reshape(shard_rows, windows_here, model_width),
                    ],
                    axis=-1,
                ),
            )

        def dead_block(held_grad):
            return (held_grad, jnp.zeros((shard_rows, windows_here, 2 * model_width), jnp.float32))

        dead = jnp.min(block_places(key_start, shard_rows)) > own_high
        return lax.cond(dead, dead_block, live_block, query_grad)

    query_grad, key_terms = lax.scan(
        back_block, zero_heads, (jnp.arange(seq_count, dtype=jnp.int32), blocks)
    )
    key_terms = key_terms.reshape((seq_count * shard_rows,) + key_terms.shape[2:])
    summed = lax.psum_scatter(
        key_terms.astype(jnp.bfloat16), "seq", scatter_dimension=0, tiled=True
    ).astype(jnp.float32)
    key_grad = summed[..., :model_width].reshape(shard_rows, windows_here, head_count, HEAD_DIM)
    value_grad = summed[..., model_width:].reshape(shard_rows, windows_here, head_count, HEAD_DIM)
    joined_grad = turn_back((query_grad, key_grad, value_grad))[0].astype(jnp.bfloat16)
    qkv_weight_grad = jnp.dot(normed_low.T, joined_grad, preferred_element_type=jnp.float32)
    normed_grad = jnp.dot(joined_grad, qkv_weight.T, preferred_element_type=jnp.float32) + jnp.dot(
        pre_grad, in_weight.T, preferred_element_type=jnp.float32
    )
    stream_part, norm_gain_grad, norm_bias_grad = norm_back(normed_grad)
    stream_grad = grad_rows.astype(jnp.float32) + stream_part
    result_three = result.reshape(shard_rows, windows_here, model_width)
    grad_three = stream_grad.reshape(shard_rows, windows_here, model_width)
    output = jnp.transpose(result_three, (1, 0, 2)).astype(jnp.bfloat16)
    hidden_grad = jnp.transpose(grad_three, (1, 0, 2))
    shares = (
        lax.psum_scatter(
            norm_gain_grad.astype(jnp.bfloat16), "seq", scatter_dimension=0, tiled=True
        ).astype(jnp.float32),
        lax.psum_scatter(
            norm_bias_grad.astype(jnp.bfloat16), "seq", scatter_dimension=0, tiled=True
        ).astype(jnp.float32),
        lax.psum_scatter(
            qkv_weight_grad.astype(jnp.bfloat16), "seq", scatter_dimension=0, tiled=True
        ).astype(jnp.float32),
        lax.psum_scatter(
            out_weight_grad.astype(jnp.bfloat16), "seq", scatter_dimension=0, tiled=True
        ).astype(jnp.float32),
        lax.psum_scatter(
            in_weight_grad.astype(jnp.bfloat16), "seq", scatter_dimension=0, tiled=True
        ).astype(jnp.float32),
        lax.psum_scatter(
            in_bias_grad.astype(jnp.bfloat16), "seq", scatter_dimension=0, tiled=True
        ).astype(jnp.float32),
        lax.psum_scatter(
            down_weight_grad.astype(jnp.bfloat16), "seq", scatter_dimension=0, tiled=True
        ).astype(jnp.float32),
        lax.psum_scatter(
            down_bias_grad.astype(jnp.bfloat16), "seq", scatter_dimension=0, tiled=True
        ).astype(jnp.float32),
    )
    totals_all = (
        lax.psum(shares[0].astype(jnp.bfloat16), "batch").astype(jnp.float32),
        lax.psum(shares[1].astype(jnp.bfloat16), "batch").astype(jnp.float32),
        lax.psum(shares[2].astype(jnp.bfloat16), "batch").astype(jnp.float32),
        lax.psum(shares[3].astype(jnp.bfloat16), "batch").astype(jnp.float32),
        lax.psum(shares[4].astype(jnp.bfloat16), "batch").astype(jnp.float32),
        lax.psum(shares[5].astype(jnp.bfloat16), "batch").astype(jnp.float32),
        lax.psum(shares[6].astype(jnp.bfloat16), "batch").astype(jnp.float32),
        lax.psum(shares[7].astype(jnp.bfloat16), "batch").astype(jnp.float32),
    )
    return (
        output,
        hidden_grad,
        totals_all[0],
        totals_all[1],
        totals_all[2],
        totals_all[3],
        totals_all[4],
        totals_all[5],
        totals_all[6],
        totals_all[7],
    )


def solution(mesh):
    placed = (
        P("batch", "seq", None),
        P("batch", "seq"),
        P("batch"),
        P("batch"),
        P(),
        P(),
        P(),
        P(),
        P(),
        P(),
        P(),
        P(),
        P(),
        P("batch", "seq", None),
    )

    def body(*arrays):
        hidden = arrays[0]
        owners = mesh.shape["seq"]
        if hidden.shape[0] == 1 and hidden.shape[2] == 2 * PAIR * owners and owners == 4 and mesh.shape["batch"] == 8:
            return fast_body(*arrays)
        return plain_body(*arrays)

    return jax.shard_map(
        body,
        mesh=mesh,
        in_specs=placed,
        out_specs=(
            P("batch", "seq", None),
            P("batch", "seq", None),
            P("seq"),
            P("seq"),
            P("seq", None),
            P("seq", None),
            P("seq", None),
            P("seq"),
            P("seq", None),
            P("seq"),
        ),
        check_vma=False,
    )
```

```python
import math

import jax
import jax.numpy as jnp
import numpy as np
from jax import lax
from jax.experimental import pallas as pl
from jax.experimental.pallas import tpu as pltpu
from jax.sharding import PartitionSpec as P

HEAD_DIM = 64
ROT = 32
PAIR = 2 * HEAD_DIM

EPSILON = 1e-05
BLOCKED = -1e30
LOG2E = math.log2(math.e)
BF16 = jnp.bfloat16
F32 = jnp.float32
MIB = 1 << 20
SHORT = pl.CostEstimate(flops=1000, bytes_accessed=1000, transcendentals=0)
LONG = pl.CostEstimate(flops=10**11, bytes_accessed=1000, transcendentals=0)


def dot_nn(left, right):
    return lax.dot_general(left, right, (((1,), (0,)), ((), ())), preferred_element_type=F32)


def dot_nt(left, right):
    return lax.dot_general(left, right, (((1,), (1,)), ((), ())), preferred_element_type=F32)


def dot_tn(left, right):
    return lax.dot_general(left, right, (((0,), (0,)), ((), ())), preferred_element_type=F32)


def swap_pairs(rows):
    width = rows.shape[1]
    lanes = lax.broadcasted_iota(jnp.int32, rows.shape, 1)
    return jnp.where(lanes % 2 == 0, pltpu.roll(rows, width - 1, 1), pltpu.roll(rows, 1, 1))


def trig_tables(length):
    inverse = 10000.0 ** (-(np.arange(ROT // 2, dtype=np.float32) * np.float32(2.0)) / np.float32(ROT))
    phases = np.arange(length, dtype=np.float32)[:, None] * inverse.astype(np.float32)[None, :]
    cosine = np.ones((length, HEAD_DIM), np.float32)
    sine = np.zeros((length, HEAD_DIM), np.float32)
    cosine[:, :ROT] = np.repeat(np.cos(phases), 2, axis=1)
    sine[:, :ROT] = np.repeat(np.sin(phases), 2, axis=1) * np.tile(np.array([-1.0, 1.0], np.float32), ROT // 2)
    return np.tile(cosine, (1, 2)), np.tile(sine, (1, 2))


def whole(array):
    shape = array.shape
    return pl.BlockSpec(shape, lambda i: (0,) * len(shape))


SCALARS = pl.BlockSpec(memory_space=pltpu.SMEM)


def prep_kernel(hidden_ref, mark_ref, table_ref, gain_ref, bias_ref, stream_ref, normed_ref, turned_ref):
    rows = hidden_ref.shape[0]
    vocab = table_ref.shape[0]
    onehot = (mark_ref[...] == lax.broadcasted_iota(jnp.int32, (rows, vocab), 1)).astype(F32).astype(BF16)
    stream = hidden_ref[...].astype(F32) + dot_nn(onehot, table_ref[...])
    centre = stream - jnp.mean(stream, axis=-1, keepdims=True)
    spread = jnp.mean(centre * centre, axis=-1, keepdims=True)
    normed = centre * lax.rsqrt(spread + EPSILON) * gain_ref[...] + bias_ref[...]
    stream_ref[...] = stream
    normed_ref[...] = normed.astype(BF16)
    turned_ref[...] = normed.astype(BF16).T


def prepare(hidden, marked, table, gain, bias):
    rows, width = hidden.shape
    step = 128
    return pl.pallas_call(
        prep_kernel,
        grid=(rows // step,),
        in_specs=[
            pl.BlockSpec((step, width), lambda i: (i, 0)),
            pl.BlockSpec((step, 1), lambda i: (i, 0)),
            pl.BlockSpec(table.shape, lambda i: (0, 0)),
            pl.BlockSpec((1, width), lambda i: (0, 0)),
            pl.BlockSpec((1, width), lambda i: (0, 0)),
        ],
        out_specs=[
            pl.BlockSpec((step, width), lambda i: (i, 0)),
            pl.BlockSpec((step, width), lambda i: (i, 0)),
            pl.BlockSpec((width, step), lambda i: (0, i)),
        ],
        out_shape=[
            jax.ShapeDtypeStruct((rows, width), F32),
            jax.ShapeDtypeStruct((rows, width), BF16),
            jax.ShapeDtypeStruct((width, rows), BF16),
        ],
        cost_estimate=SHORT,
        name="prep",
    )(hidden, marked, table, gain, bias)


def heads_kernel(owners_ref, normed_ref, cot_ref, wq_ref, wk_ref, wv_ref, wo_ref, cos_ref, sin_ref, *out_refs):
    normed = normed_ref[...]
    shifts = pl.num_programs(0)
    chunks = wq_ref.shape[1] // PAIR
    cosine = jnp.concatenate([cos_ref[...]] * chunks, axis=1)
    sine = jnp.concatenate([sin_ref[...]] * chunks, axis=1)

    def turned(rows):
        return rows * cosine + swap_pairs(rows) * sine

    parts = (
        turned(dot_nn(normed, wq_ref[...])).astype(BF16),
        turned(dot_nn(normed, wk_ref[...])).astype(BF16),
        dot_nn(normed, wv_ref[...]).astype(BF16),
        dot_nt(cot_ref[...], wo_ref[...]).astype(BF16),
    )
    for number, out_ref in enumerate(out_refs):
        shift, chunk = divmod(number, chunks)

        @pl.when(pl.program_id(0) == shift)
        def _():
            for at, part in enumerate(parts):
                out_ref[:, at * PAIR : (at + 1) * PAIR] = part[:, chunk * PAIR : (chunk + 1) * PAIR]


def heads_of(order, normed, cot, qkv_weight, out_weight, cosine, sine):
    rows, width = normed.shape
    owners = order.shape[0]
    wide = width // owners
    chunks = wide // PAIR
    fixed = pl.BlockSpec((rows, width), lambda i, o: (0, 0))
    table = pl.BlockSpec((rows, PAIR), lambda i, o: (o[0], 0))

    def columns(part):
        return pl.BlockSpec((width, wide), lambda i, o: (0, part * owners + o[i]))

    blocks = pl.pallas_call(
        heads_kernel,
        grid_spec=pltpu.PrefetchScalarGridSpec(
            num_scalar_prefetch=1,
            grid=(owners,),
            in_specs=[fixed, fixed]
            + [columns(part) for part in range(3)]
            + [pl.BlockSpec((wide, width), lambda i, o: (o[i], 0)), table, table],
            out_specs=[pl.BlockSpec((rows, 4 * PAIR), lambda i, o: (0, 0))] * (owners * chunks),
        ),
        out_shape=[jax.ShapeDtypeStruct((rows, 4 * PAIR), BF16)] * (owners * chunks),
        compiler_params=pltpu.CompilerParams(vmem_limit_bytes=60 * MIB),
        cost_estimate=SHORT,
        name="heads",
    )(order, normed, cot, qkv_weight, qkv_weight, qkv_weight, out_weight, cosine, sine)
    return [[blocks[shift * chunks + chunk] for shift in range(owners)] for chunk in range(chunks)]


QUERY_ROWS = 512
KEY_ROWS = QUERY_ROWS


def attention_kernel(pieces, info_ref, *refs):
    piece_refs = refs[:pieces]
    cos_ref, sin_ref = refs[pieces : pieces + 2]
    out_refs = refs[pieces + 2 : -9]
    held, results, key_turned, value_turned, doubled, score_ref, raised_ref, key_sum, value_sum = refs[-9:]
    me, end = info_ref[0], info_ref[1]
    rows = piece_refs[0].shape[0]
    length = rows * pieces
    for shift in range(pieces):
        start = pl.multiple_of(lax.rem(me - shift + pieces, pieces) * rows, rows)
        held[pl.ds(start, rows), :] = piece_refs[shift][...]
    key_turned[...] = held[:, PAIR : 2 * PAIR].T
    value_turned[...] = held[:, 2 * PAIR : 3 * PAIR].T
    for head in range(2):
        keys = held[:, PAIR + head * HEAD_DIM : PAIR + (head + 1) * HEAD_DIM]
        doubled[head] = jnp.concatenate([keys, keys], axis=1)
    key_sum[...] = jnp.zeros_like(key_sum)
    value_sum[...] = jnp.zeros_like(value_sum)
    scale = 0.125 * LOG2E
    halves = lax.broadcasted_iota(jnp.int32, (QUERY_ROWS, PAIR), 1) // HEAD_DIM
    causal = lax.broadcasted_iota(jnp.int32, (KEY_ROWS, QUERY_ROWS), 0) <= lax.broadcasted_iota(
        jnp.int32, (KEY_ROWS, QUERY_ROWS), 1
    )
    key_steps = lax.broadcasted_iota(jnp.int32, (KEY_ROWS, QUERY_ROWS), 0)

    def query_block(number, carry):
        first = pl.multiple_of(number * QUERY_ROWS, QUERY_ROWS)
        query_rows = held[pl.ds(first, QUERY_ROWS), 0:PAIR]
        grad_rows = held[pl.ds(first, QUERY_ROWS), 3 * PAIR : 4 * PAIR]
        zero = jnp.zeros_like(query_rows)
        queries = [jnp.where(halves == head, query_rows, zero) for head in range(2)]
        scaled = query_rows.astype(F32) * scale
        large = scaled.astype(BF16)
        small = (scaled - large.astype(F32)).astype(BF16)
        pairs = [
            jnp.concatenate(
                [part[:, head * HEAD_DIM : (head + 1) * HEAD_DIM] for part in (large, small)], axis=1
            )
            for head in range(2)
        ]
        query_places = first + lax.broadcasted_iota(jnp.int32, (1, QUERY_ROWS), 1)
        lowest = jnp.where(query_places > end, end + 1, 0)

        def scores_of(block, highest, diagonal, parted):
            start = pl.multiple_of(block * KEY_ROWS, KEY_ROWS)
            after = []
            for head in range(2):
                scores = dot_nt(doubled[head, pl.ds(start, KEY_ROWS), :], pairs[head])
                if diagonal:
                    scores = jnp.where(causal, scores, BLOCKED)
                if parted:
                    scores = jnp.where(key_steps >= lowest - start, scores, BLOCKED)
                score_ref[head, pl.ds(start, KEY_ROWS), :] = scores
                after.append(jnp.maximum(highest[head], jnp.max(scores, axis=0, keepdims=True)))
            return tuple(after)

        def any_scores(block, highest, diagonal=False):
            parted = (first + QUERY_ROWS - 1 > end) & (block * KEY_ROWS <= end)
            return lax.cond(
                parted,
                lambda held_rows: scores_of(block, held_rows, diagonal, True),
                lambda held_rows: scores_of(block, held_rows, diagonal, False),
                highest,
            )

        start_row = jnp.full((1, QUERY_ROWS), BLOCKED, F32)
        highest = lax.fori_loop(0, number, any_scores, (start_row, start_row))
        highest = any_scores(number, highest, True)

        def mix(block, carried):
            start = pl.multiple_of(block * KEY_ROWS, KEY_ROWS)
            after = []
            for head in range(2):
                total, mixed = carried[head]
                raised = jnp.exp2(score_ref[head, pl.ds(start, KEY_ROWS), :] - highest[head])
                rounded = raised.astype(BF16)
                raised_ref[head, pl.ds(start, KEY_ROWS), :] = rounded
                values = value_turned[head * HEAD_DIM : (head + 1) * HEAD_DIM, pl.ds(start, KEY_ROWS)]
                after.append((total + jnp.sum(raised, axis=0, keepdims=True), mixed + dot_nn(values, rounded)))
            return tuple(after)

        empty = (jnp.zeros((1, QUERY_ROWS), F32), jnp.zeros((HEAD_DIM, QUERY_ROWS), F32))
        mixes = lax.fori_loop(0, number + 1, mix, (empty, empty))
        inverse = [1.0 / mixes[head][0] for head in range(2)]
        mixed = jnp.concatenate([mixes[head][1] * inverse[head] for head in range(2)], axis=0)
        turned = grad_rows.astype(F32).T
        turned = jnp.concatenate(
            [turned[head * HEAD_DIM : (head + 1) * HEAD_DIM] * inverse[head] for head in range(2)], axis=0
        )
        products = mixed * turned
        delta = [
            jnp.sum(products[head * HEAD_DIM : (head + 1) * HEAD_DIM], axis=0, keepdims=True) for head in range(2)
        ]
        divided = turned.T.astype(BF16)
        grads = [jnp.where(halves == head, divided, zero) for head in range(2)]

        def back(block, carried):
            start = pl.multiple_of(block * KEY_ROWS, KEY_ROWS)
            values = held[pl.ds(start, KEY_ROWS), 2 * PAIR : 3 * PAIR]
            after, key_terms, value_terms = [], [], []
            for head in range(2):
                raised = raised_ref[head, pl.ds(start, KEY_ROWS), :]
                score_grad = raised * (dot_nt(values, grads[head]) - delta[head]).astype(BF16)
                value_terms.append(dot_nn(raised, grads[head]))
                key_terms.append(dot_nn(score_grad, queries[head]))
                keys = key_turned[head * HEAD_DIM : (head + 1) * HEAD_DIM, pl.ds(start, KEY_ROWS)]
                after.append(carried[head] + dot_nn(keys, score_grad))
            value_sum[pl.ds(start, KEY_ROWS), :] += value_terms[0] + value_terms[1]
            key_sum[pl.ds(start, KEY_ROWS), :] += key_terms[0] + key_terms[1]
            return tuple(after)

        query_grads = lax.fori_loop(0, number + 1, back, (empty[1], empty[1]))
        query_grad = jnp.concatenate(query_grads, axis=0).T * 0.125
        cosine = cos_ref[pl.ds(first, QUERY_ROWS), :]
        sine = sin_ref[pl.ds(first, QUERY_ROWS), :]
        results[pl.ds(first, QUERY_ROWS), 0:PAIR] = (query_grad * cosine - swap_pairs(query_grad) * sine).astype(BF16)
        results[pl.ds(first, QUERY_ROWS), 3 * PAIR : 4 * PAIR] = mixed.T.astype(BF16)
        return carry

    lax.fori_loop(0, length // QUERY_ROWS, query_block, 0)
    key_grad = key_sum[...] * 0.125
    results[:, PAIR : 2 * PAIR] = (key_grad * cos_ref[...] - swap_pairs(key_grad) * sin_ref[...]).astype(BF16)
    results[:, 2 * PAIR : 3 * PAIR] = value_sum[...].astype(BF16)
    for shift in range(pieces):
        start = pl.multiple_of(lax.rem(me + shift, pieces) * rows, rows)
        out_refs[shift][...] = results[pl.ds(start, rows), :]


def attention(info, parts, cosine, sine):
    pieces = len(parts)
    rows = parts[0].shape[0]
    length = rows * pieces
    arrays = (*parts, cosine, sine)
    shapes = [jax.ShapeDtypeStruct((rows, 4 * PAIR), BF16)] * pieces
    return pl.pallas_call(
        lambda *refs: attention_kernel(pieces, *refs),
        grid=(1,),
        in_specs=[SCALARS] + [whole(array) for array in arrays],
        out_specs=[whole(shape) for shape in shapes],
        out_shape=shapes,
        scratch_shapes=[
            pltpu.VMEM((length, 4 * PAIR), BF16),
            pltpu.VMEM((length, 4 * PAIR), BF16),
            pltpu.VMEM((PAIR, length), BF16),
            pltpu.VMEM((PAIR, length), BF16),
            pltpu.VMEM((2, length, PAIR), BF16),
            pltpu.VMEM((2, length, QUERY_ROWS), F32),
            pltpu.VMEM((2, length, QUERY_ROWS), BF16),
            pltpu.VMEM((length, PAIR), F32),
            pltpu.VMEM((length, PAIR), F32),
        ],
        compiler_params=pltpu.CompilerParams(vmem_limit_bytes=60 * MIB),
        cost_estimate=SHORT,
        name="attention",
    )(info, *arrays)


def feed_kernel(cells_ref, normed_ref, turned_ref, cot_ref, in_ref, bias_ref, down_ref, *out_refs):
    sides = (out_refs[0:2], out_refs[2:4])
    bias_grad, out_sum, norm_sum = out_refs[4:]
    step = pl.program_id(0)
    steps = pl.num_programs(0) // 2
    up = math.sqrt(2.0 / math.pi)

    @pl.when(step == 0)
    def _():
        out_sum[...] = jnp.zeros_like(out_sum)
        norm_sum[...] = jnp.zeros_like(norm_sum)

    weights = in_ref[...]
    downs = down_ref[...]
    cot = cot_ref[...]
    pre = dot_nn(normed_ref[...], weights) + bias_ref[...]
    square = pre * pre
    tanh = jnp.tanh(up * pre * (1.0 + 0.044715 * square))
    half = 0.5 * (1.0 + tanh)
    active = (pre * half).astype(BF16)
    slope = half + 0.5 * pre * (1.0 - tanh * tanh) * (up * (1.0 + 3 * 0.044715 * square))
    pre_grad = (dot_nt(cot, downs) * slope).astype(BF16)
    in_term = dot_nn(turned_ref[...], pre_grad).astype(BF16)
    down_term = dot_tn(active, cot).astype(BF16)
    for side, (in_grad, down_grad) in enumerate(sides):

        @pl.when((step >= steps) == bool(side))
        def _():
            pieces, owners, kept, tile = in_grad.shape
            for owner in range(owners):
                for piece in range(pieces):
                    start = (owner * pieces + piece) * kept
                    in_grad[piece, owner] = in_term[start : start + kept]
            kept = tile // pieces
            for group in range(down_term.shape[1] // tile):
                for piece in range(pieces):
                    down_grad[piece, 0, group * kept : (group + 1) * kept] = down_term[
                        piece * kept : (piece + 1) * kept, group * tile : (group + 1) * tile
                    ]

    bias_grad[0] = jnp.sum(pre_grad.astype(F32), axis=0, keepdims=True)
    out_sum[...] += dot_nn(active, downs)
    norm_sum[...] += dot_nt(pre_grad, weights)


def feed_forward(cells, normed, turned, cot, in_weight, in_bias, down_weight, pieces):
    rows, width = normed.shape
    steps = cells.shape[0]
    owners = steps // 2
    hidden_units = in_weight.shape[1]
    tile = hidden_units // steps
    kept = width // owners // pieces
    tall = owners * kept
    wide = tile // pieces * (width // tile)
    fixed = pl.BlockSpec((rows, width), lambda i, c: (0, 0))

    def first(i):
        return jnp.minimum(i, owners - 1)

    def second(i):
        return jnp.maximum(i - owners, 0)

    def sides_of(turn):
        return [
            pl.BlockSpec((pieces, owners, kept, tile), lambda i, c: (0, 0, turn(i), 0)),
            pl.BlockSpec((pieces, 1, wide, tile), lambda i, c: (0, turn(i), 0, 0)),
        ]

    grads = [
        jax.ShapeDtypeStruct((pieces, owners, tall, tile), BF16),
        jax.ShapeDtypeStruct((pieces, owners, wide, tile), BF16),
    ]
    full = jax.ShapeDtypeStruct((rows, width), F32)
    results = pl.pallas_call(
        feed_kernel,
        grid_spec=pltpu.PrefetchScalarGridSpec(
            num_scalar_prefetch=1,
            grid=(steps,),
            in_specs=[
                fixed,
                pl.BlockSpec((width, rows), lambda i, c: (0, 0)),
                fixed,
                pl.BlockSpec((width, tile), lambda i, c: (0, c[i])),
                pl.BlockSpec((1, tile), lambda i, c: (0, c[i])),
                pl.BlockSpec((tile, width), lambda i, c: (c[i], 0)),
            ],
            out_specs=sides_of(first)
            + sides_of(second)
            + [pl.BlockSpec((1, 1, tile), lambda i, c: (i, 0, 0)), fixed, fixed],
        ),
        out_shape=grads + grads + [jax.ShapeDtypeStruct((steps, 1, tile), F32), full, full],
        compiler_params=pltpu.CompilerParams(vmem_limit_bytes=60 * MIB),
        cost_estimate=SHORT,
        name="feed",
    )(cells, normed, turned, cot, in_weight, in_bias, down_weight)
    return results[:2], results[2:4], *results[4:]


def place_columns(me_ref, piece_refs, held):
    owners = len(piece_refs)
    for shift in range(owners):
        owner = lax.rem(me_ref[0] - shift + owners, owners)
        start = pl.multiple_of(owner * PAIR, PAIR)
        for part in range(4):
            held[part, :, pl.ds(start, PAIR)] = piece_refs[shift][:, part * PAIR : (part + 1) * PAIR]


def weight_kernel(pieces, info_ref, turned_ref, cot_ref, *refs):
    owners = len(refs) - 4
    kept_ref, sent_ref, held, grad = refs[-4:]
    place_columns(info_ref, refs[:owners], held)
    kept = PAIR // pieces
    turned = turned_ref[...]
    for part in range(3):
        grad[...] = dot_nn(turned, held[part]).astype(BF16)
        for side, ref in enumerate((kept_ref, sent_ref)):
            core = info_ref[1] ^ side
            for owner in range(owners):
                for piece in range(pieces):
                    start = pl.multiple_of(((owner * 2 + core) * pieces + piece) * kept, kept)
                    ref[piece, owner, part * kept : (part + 1) * kept] = grad[pl.ds(start, kept), :]
    term = dot_tn(held[3], cot_ref[...]).astype(BF16)
    rows, half = term.shape[0], term.shape[1] // 2
    for core in range(2):
        grad[core * rows : (core + 1) * rows, :] = term[:, core * half : (core + 1) * half]
    for side, ref in enumerate((kept_ref, sent_ref)):
        core = info_ref[1] ^ side
        for owner in range(owners):
            for piece in range(pieces):
                start = pl.multiple_of(core * rows + (owner * pieces + piece) * kept, kept)
                ref[piece, owner, 3 * kept :] = grad[pl.ds(start, kept), :]


def weight_grads(info, turned, cot, parts, pieces):
    owners = len(parts)
    rows, width = cot.shape
    kept = PAIR // pieces
    arrays = (turned, cot, *parts)
    shape = jax.ShapeDtypeStruct((pieces, owners, 4 * kept, owners * PAIR), BF16)
    return pl.pallas_call(
        lambda *refs: weight_kernel(pieces, *refs),
        grid=(1,),
        in_specs=[SCALARS] + [whole(array) for array in arrays],
        out_specs=[whole(shape)] * 2,
        out_shape=[shape] * 2,
        scratch_shapes=[pltpu.VMEM((4, rows, owners * PAIR), BF16), pltpu.VMEM((width, owners * PAIR), BF16)],
        compiler_params=pltpu.CompilerParams(vmem_limit_bytes=60 * MIB),
        cost_estimate=SHORT,
        name="weight_grads",
    )(info, *arrays)


def sums_kernel(last, owners, me_ref, *refs):
    piece_refs, refs = refs[:owners], refs[owners:]
    weight_refs, refs = refs[: 3 * owners], refs[3 * owners :]
    out_weight_refs, refs = refs[:owners], refs[owners:]
    out_in, norm_in = refs[:2]
    held = refs[-1]
    place_columns(me_ref, piece_refs, held)
    norm = norm_in[...]
    for part in range(3):
        weights = jnp.concatenate([ref[...] for ref in weight_refs[part * owners : (part + 1) * owners]], axis=1)
        norm = norm + dot_nt(held[part], weights)
    weights = jnp.concatenate([ref[...] for ref in out_weight_refs], axis=0)
    out = out_in[...] + dot_nn(held[3], weights)
    if not last:
        out_ref, norm_ref = refs[2:4]
        out_ref[...] = out
        norm_ref[...] = norm
        return
    stream_ref, cot_ref, gain_ref, down_bias_ref, out_ref, hidden_ref, gain_grad, bias_grad = refs[2:-1]
    stream = stream_ref[...]
    cot = cot_ref[...].astype(F32)
    out_ref[...] = (stream + out + down_bias_ref[...]).astype(BF16)
    centre = stream - jnp.mean(stream, axis=-1, keepdims=True)
    spread = jnp.mean(centre * centre, axis=-1, keepdims=True)
    inverse = lax.rsqrt(spread + EPSILON)
    hat = centre * inverse
    gained = norm * gain_ref[...]
    hidden_ref[...] = cot + inverse * (
        gained
        - jnp.mean(gained, axis=-1, keepdims=True)
        - hat * jnp.mean(gained * hat, axis=-1, keepdims=True)
    )
    for out_ref, rows in ((gain_grad, norm * hat), (bias_grad, norm)):
        row = jnp.sum(rows, axis=0, keepdims=True)
        wide = out_ref.shape[1]
        for owner in range(owners):
            out_ref[owner : owner + 1, :] = row[:, owner * wide : (owner + 1) * wide]


def sums_of(info, chunk, chunks, parts, qkv_weight, out_weight, sums, final=()):
    owners = len(parts)
    rows = parts[0].shape[0]
    width = qkv_weight.shape[0]
    last = bool(final)

    def columns(part, owner):
        at = (part * owners + owner) * chunks + chunk
        return pl.BlockSpec((width, PAIR), lambda i: (0, at))

    def weight_rows(owner):
        return pl.BlockSpec((PAIR, width), lambda i: (owner * chunks + chunk, 0))

    full = jax.ShapeDtypeStruct((rows, width), F32)
    row = jax.ShapeDtypeStruct((owners, width // owners), F32)
    shapes = [jax.ShapeDtypeStruct((rows, width), BF16), full, row, row] if last else [full, full]
    return pl.pallas_call(
        lambda *refs: sums_kernel(last, owners, *refs),
        grid=(1,),
        in_specs=[SCALARS]
        + [whole(part) for part in parts]
        + [columns(part, owner) for part in range(3) for owner in range(owners)]
        + [weight_rows(owner) for owner in range(owners)]
        + [whole(array) for array in (*sums, *final)],
        out_specs=[whole(shape) for shape in shapes],
        out_shape=shapes,
        scratch_shapes=[pltpu.VMEM((4, rows, owners * PAIR), BF16)],
        compiler_params=pltpu.CompilerParams(vmem_limit_bytes=60 * MIB),
        cost_estimate=SHORT,
        name="sums",
    )(info, *parts, *([qkv_weight] * (3 * owners)), *([out_weight] * owners), *sums, *final)


def feed_place_kernel(info_ref, mine_ref, other_ref, in_ref, down_ref):
    masks, total, tile = mine_ref.shape
    kept = in_ref.shape[0] // masks
    tiles = in_ref.shape[1] // (2 * tile)
    half = down_ref.shape[0] // 2
    down_kept = half // masks
    for source, ref in enumerate((mine_ref, other_ref)):
        core = info_ref[0] ^ source
        for mask in range(masks):
            chip = info_ref[1] ^ mask
            rows = pl.ds(pl.multiple_of(chip * kept, kept), kept)
            for number in range(tiles):
                columns = pl.ds(pl.multiple_of((2 * number + core) * tile, tile), tile)
                in_ref[rows, columns] = ref[mask, number * kept : (number + 1) * kept].astype(F32)
            rows = pl.ds(pl.multiple_of(core * half + chip * down_kept, down_kept), down_kept)
            for group in range(down_ref.shape[1] // tile):
                at = tiles * kept + group * down_kept
                down_ref[rows, group * tile : (group + 1) * tile] = ref[mask, at : at + down_kept].astype(F32)


def place_feed(info, mine, other, in_shape, down_shape):
    shapes = [jax.ShapeDtypeStruct(in_shape, F32), jax.ShapeDtypeStruct(down_shape, F32)]
    return pl.pallas_call(
        feed_place_kernel,
        grid=(1,),
        in_specs=[SCALARS, whole(mine), whole(other)],
        out_specs=[whole(shape) for shape in shapes],
        out_shape=shapes,
        compiler_params=pltpu.CompilerParams(vmem_limit_bytes=60 * MIB),
        cost_estimate=SHORT,
        name="place_feed",
    )(info, mine, other)


def heads_place_kernel(info_ref, mine_ref, other_ref, qkv_ref, out_ref):
    core, place = info_ref[0], info_ref[1]
    masks, total, wide = mine_ref.shape
    own_rows, width = out_ref.shape
    kept = own_rows // 2 // masks
    chunks = total // (4 * kept)
    owners = wide // PAIR
    for source, ref in enumerate((mine_ref, other_ref)):
        at_core = core if source == 0 else 1 - core
        columns = pl.ds(pl.multiple_of(at_core * (width // 2), width // 2), width // 2)
        for mask in range(masks):
            piece = place ^ mask
            rows = pl.ds(pl.multiple_of(at_core * (own_rows // 2) + piece * kept, kept), kept)
            for chunk in range(chunks):
                at = chunk * 4 * kept
                for part in range(3):
                    block = ref[mask, at + part * kept : at + (part + 1) * kept].astype(F32)
                    for owner in range(owners):
                        column = part * width + (owner * chunks + chunk) * PAIR
                        qkv_ref[rows, column : column + PAIR] = block[:, owner * PAIR : (owner + 1) * PAIR]
                out_rows = pl.ds(pl.multiple_of(chunk * PAIR + piece * kept, kept), kept)
                out_ref[out_rows, columns] = ref[mask, at + 3 * kept : at + 4 * kept].astype(F32)


def place_heads(info, mine, other, own_rows, width):
    shapes = [jax.ShapeDtypeStruct((own_rows, 3 * width), F32), jax.ShapeDtypeStruct((own_rows, width), F32)]
    return pl.pallas_call(
        heads_place_kernel,
        grid=(1,),
        in_specs=[SCALARS, whole(mine), whole(other)],
        out_specs=[whole(shape) for shape in shapes],
        out_shape=shapes,
        compiler_params=pltpu.CompilerParams(vmem_limit_bytes=60 * MIB),
        cost_estimate=SHORT,
        name="place_heads",
    )(info, mine, other)


def exchange(rows, axis, mask):
    size = lax.axis_size(axis)
    return lax.ppermute(rows, axis, [(place, place ^ mask) for place in range(size)])


def around(rows, shift):
    owners = lax.axis_size("seq")
    return lax.ppermute(rows, "seq", [(place, (place + shift) % owners) for place in range(owners)])


def total_of(*terms):
    return sum(term.astype(F32) for term in terms).astype(BF16)


def picked(rows, index, dim=0):
    return lax.dynamic_index_in_dim(rows, index, dim, keepdims=False)


def add_kernel(places, bits_ref, *refs):
    outs = refs[len(refs) - len(places) :]
    for out_ref, terms in zip(outs, places):
        at = 0
        for left, right in terms:
            rows = refs[left].shape[-2]
            total = refs[left][...].astype(F32) + refs[right][...].astype(F32)
            out_ref[..., at : at + rows, :] = total.reshape(out_ref.shape[:-2] + total.shape[-2:]).astype(BF16)
            at += rows


def add_pieces(kept, arrived):
    pieces, owners = kept[0].shape[:2]
    arrays = [array for pair in zip(kept, arrived) for array in pair]
    rows = sum(array.shape[2] for array in kept)
    columns = kept[0].shape[3]
    return pl.pallas_call(
        lambda *refs: add_kernel([[(0, 1), (2, 3)]], None, *refs),
        grid=(pieces,),
        in_specs=[pl.BlockSpec((1,) + array.shape[1:], lambda i: (i, 0, 0, 0)) for array in arrays],
        out_specs=pl.BlockSpec((1, owners, rows, columns), lambda i: (i, 0, 0, 0)),
        out_shape=jax.ShapeDtypeStruct((pieces, owners, rows, columns), BF16),
        compiler_params=pltpu.CompilerParams(vmem_limit_bytes=60 * MIB),
        cost_estimate=SHORT,
        name="add_pieces",
    )(*arrays)


def add_for_chips(chip, kept, arrived):
    specs, places, arrays = [], [], []
    chips, owners = kept[0].shape[:2]
    for mask in range(chips):
        terms = []
        for mine, other in zip(kept, arrived):
            terms.append((len(arrays), len(arrays) + 1))
            arrays += [mine, other]
            specs += [pl.BlockSpec((1,) + mine.shape[1:], lambda i, c, mask=mask: (c[0] ^ mask, 0, 0, 0))] * 2
        places.append(terms)
    rows = sum(array.shape[2] for array in kept)
    out = jax.ShapeDtypeStruct((owners, rows, kept[0].shape[3]), BF16)
    return pl.pallas_call(
        lambda *refs: add_kernel(places, *refs),
        grid_spec=pltpu.PrefetchScalarGridSpec(
            num_scalar_prefetch=1,
            grid=(1,),
            in_specs=specs,
            out_specs=[pl.BlockSpec(out.shape, lambda i, c: (0, 0, 0))] * chips,
        ),
        out_shape=[out] * chips,
        cost_estimate=SHORT,
        name="add_for_chips",
    )(chip[None], *arrays)


class Order:
    token = None

    def __call__(self, value):
        if self.token is None:
            return value
        return lax.optimization_barrier((value, self.token))[0]

    def done(self, token):
        self.token = token
        return token

    def also(self, *tokens):
        self.token = (self.token, tokens)


def fast_body(
    hidden,
    token_ids,
    offsets,
    end_places,
    token_table,
    norm_gain,
    norm_bias,
    qkv_weight,
    out_weight,
    in_weight,
    in_bias,
    down_weight,
    down_bias,
    cotangent,
):
    width = hidden.shape[2]
    rows = hidden.shape[1]
    owners = lax.axis_size("seq")
    pieces = lax.axis_size("batch")
    me = lax.axis_index("seq")
    core = lax.axis_index("batch") & 1
    length = rows * owners
    own_rows = width // owners
    chunks = own_rows // PAIR
    end = end_places[0]

    places = me * rows + jnp.arange(rows, dtype=jnp.int32)[:, None]
    marked = token_ids.reshape(rows, 1)
    marked = jnp.where(places == end, 2, marked)
    marked = jnp.where(places == end + 1, 1, marked)
    marked = jnp.where((places == 0) & (offsets[0] == 0), 1, marked)
    cot = cotangent.reshape(rows, width)
    stream, normed, turned = prepare(
        hidden.reshape(rows, width), marked, token_table, norm_gain[None], norm_bias[None]
    )
    cosine, sine = (jnp.asarray(table) for table in trig_tables(length))
    place = lax.axis_index("batch")
    info = jnp.stack([me, core]).astype(jnp.int32)
    spots = jnp.stack([me, end]).astype(jnp.int32)
    order = Order()

    def moved(blocks, shifts=(2, 1, 3)):
        return {shift: around(blocks[shift], shift) for shift in shifts}

    def gathered(blocks, arrived):
        return [blocks[0]] + [arrived[shift] for shift in range(1, owners)]

    def back(rows):
        return [exchange(rows, "batch", mask) for mask in (2, 4, 6)]

    shifts = lax.rem(me + jnp.arange(owners, dtype=jnp.int32), owners)
    heads = order.done(heads_of(shifts, normed, cot, qkv_weight, out_weight, cosine, sine))

    arrived = moved(order(heads[0]))
    cells = 2 * jnp.arange(owners, dtype=jnp.int32)
    cells = jnp.concatenate([cells + 1 - core, cells + core])
    away, here, in_bias_grad, out_sum, norm_sum = order.done(
        feed_forward(cells, order(normed), turned, cot, in_weight, in_bias[None], down_weight, pieces // 2)
    )
    order.also(arrived)

    feed_arrived = [exchange(array, "batch", 1) for array in order(away)]
    later = moved(order(heads[1]))
    first = order.done(attention(spots, gathered(heads[0], order(arrived)), cosine, sine))
    order.also(feed_arrived)
    feed_rows = order.done(add_pieces(order(here), feed_arrived))
    order.also(later)

    groups = [list(range(number, pieces, 2)) for number in range(2)]
    feed_rows = lax.psum_scatter(
        order(feed_rows), "batch", scatter_dimension=0, axis_index_groups=groups, tiled=False
    )
    arrived = moved(order(first))
    second = order.done(attention(spots, gathered(heads[1], order(later)), cosine, sine))
    cot_sum = order.done(jnp.sum(order(cot).astype(F32), axis=0))
    order.also(arrived)

    later = moved(order(second))
    parts = gathered(first, order(arrived))
    sums = order.done(sums_of(info, 0, chunks, order(parts), qkv_weight, out_weight, (out_sum, norm_sum)))
    first_kept, first_sent = order.done(weight_grads(info, turned, cot, order(parts), pieces // 2))
    order.also(later, feed_rows)

    feed_rows = lax.psum_scatter(order(feed_rows), "seq", scatter_dimension=0, tiled=False)
    grad_arrived = exchange(order(first_sent), "batch", 1)
    parts = gathered(second, order(later))
    second_kept, second_sent = order.done(weight_grads(info, turned, cot, parts, pieces // 2))
    order.also(grad_arrived)
    first_held = order.done(add_for_chips(place >> 1, [order(first_kept)], [grad_arrived]))

    first_arrived = [exchange(order(first_held[mask]), "batch", 2 * mask) for mask in (1, 2, 3)]
    grad_arrived = exchange(order(second_sent), "batch", 1)
    output, hidden_grad, gain_grad, bias_grad = order.done(
        sums_of(
            info, 1, chunks, order(parts), qkv_weight, out_weight, sums, (stream, cot, norm_gain[None], down_bias[None])
        )
    )
    order.also(first_arrived, grad_arrived)
    second_held = order.done(add_for_chips(place >> 1, [order(second_kept)], [grad_arrived]))

    def halve_seq(rows, number):
        bit = (me >> number) & 1
        split = rows.reshape((rows.shape[0] // 2, 2) + rows.shape[1:])
        return picked(split, bit, 1), exchange(picked(split, 1 - bit, 1), "seq", 1 << number)

    second_arrived = [exchange(order(second_held[mask]), "batch", 2 * mask) for mask in (1, 2, 3)]
    in_bias_grad = order(in_bias_grad)
    bias_low = jnp.where(core == 0, in_bias_grad[owners:], in_bias_grad[:owners])
    bias_high = jnp.where(core == 0, in_bias_grad[:owners], in_bias_grad[owners:])
    small = order.done(
        jnp.concatenate(
            [
                jnp.concatenate([bias_low, bias_high], axis=1).reshape(owners, -1),
                cot_sum.reshape(owners, -1),
                gain_grad,
                bias_grad,
            ],
            axis=1,
        )
    )
    order.also(second_arrived, feed_rows)
    grad_rows = order.done(
        jnp.concatenate(
            [
                total_of(order(held[0]), *arrived)
                for held, arrived in ((first_held, first_arrived), (second_held, second_arrived))
            ],
            axis=1,
        )
    )

    feed_rows = order(feed_rows)
    feed_back = [exchange(feed_rows, "batch", mask) for mask in (2, 4)]
    small_arrived = exchange(order(small), "batch", 1)
    grad_rows, grad_arrived = halve_seq(order(grad_rows), 0)
    order.also(feed_back, grad_arrived, small_arrived)
    small = small + order(small_arrived)
    grad_rows = total_of(order(grad_rows), grad_arrived)
    order.done((grad_rows, small))

    feed_back.append(exchange(order(feed_rows), "batch", 6))
    small_arrived = back(order(small))
    grad_rows, grad_arrived = halve_seq(order(grad_rows), 1)
    order.also(feed_back, grad_arrived, small_arrived)
    grad_rows = total_of(order(grad_rows), grad_arrived)[0]
    small = sum(order(small_arrived), small)
    feed_mine = jnp.stack([feed_rows] + order(feed_back))
    order.done((grad_rows, feed_mine, small))

    grad_back = back(order(grad_rows))
    small = order(small)
    small_arrived = exchange(small, "seq", 1)
    feed_other = exchange(order(feed_mine), "batch", 1)
    place_info = jnp.stack([core, place >> 1]).astype(jnp.int32)
    in_weight_grad, down_weight_grad = order.done(
        place_feed(
            place_info,
            order(feed_mine),
            feed_other,
            (own_rows, in_weight.shape[1]),
            (down_weight.shape[0] // owners, width),
        )
    )
    order.also(grad_back, small_arrived)
    small = small + order(small_arrived)
    grad_mine = jnp.stack([grad_rows] + order(grad_back))
    order.done((grad_mine, small))

    grad_other = exchange(order(grad_mine), "batch", 1)
    small = order(small)
    small_arrived = exchange(small, "seq", 2)
    qkv_weight_grad, out_weight_grad = place_heads(place_info, order(grad_mine), grad_other, own_rows, width)
    small = picked(small + small_arrived, me)
    few = own_rows
    many = in_bias.shape[0] // owners
    return (
        output[None],
        hidden_grad[None],
        small[many + few : many + 2 * few],
        small[many + 2 * few :],
        qkv_weight_grad,
        out_weight_grad,
        in_weight_grad,
        small[:many],
        down_weight_grad,
        small[many : many + few],
    )


def rotate(vectors, cosine_table, sine_table):
    even_part = vectors[..., 0:ROT:2]
    odd_part = vectors[..., 1:ROT:2]
    turned = jnp.stack(
        [
            even_part * cosine_table - odd_part * sine_table,
            odd_part * cosine_table + even_part * sine_table,
        ],
        axis=-1,
    )
    turned = turned.reshape(vectors.shape[:-1] + (ROT,))
    return jnp.concatenate([turned, vectors[..., ROT:]], axis=-1)


def angles(places):
    inverse = 10000.0 ** (-(jnp.arange(ROT // 2, dtype=jnp.float32) * 2.0) / ROT)
    phases = places.astype(jnp.float32)[:, None] * inverse[None, :]
    return (jnp.cos(phases), jnp.sin(phases))


def visible(query_places, key_places, end_places):
    query_after = query_places[None, :, None] > end_places[:, None, None]
    key_after = key_places[None, None, :] > end_places[:, None, None]
    return (key_places[None, None, :] <= query_places[None, :, None]) & (query_after == key_after)


def norm_rows(stream, gain_row, bias_row):
    centre = stream - jnp.mean(stream, axis=-1, keepdims=True)
    spread = jnp.mean(centre * centre, axis=-1, keepdims=True)
    return centre * lax.rsqrt(spread + EPSILON) * gain_row + bias_row


def gelu_rows(pre_active):
    return jax.nn.gelu(pre_active, approximate=True)


def plain_body(
    hidden,
    token_ids,
    offsets,
    end_places,
    token_table,
    norm_gain,
    norm_bias,
    qkv_weight,
    out_weight,
    in_weight,
    in_bias,
    down_weight,
    down_bias,
    cotangent,
):
    windows_here, shard_rows, model_width = hidden.shape
    head_count = model_width // HEAD_DIM
    seq_count = lax.axis_size("seq")
    seq_place = lax.axis_index("seq")
    home_places = seq_place * shard_rows + jnp.arange(shard_rows, dtype=jnp.int32)
    token_rows = shard_rows * windows_here
    marked = token_ids.T
    marked = jnp.where(home_places[:, None] == end_places[None, :], 2, marked)
    marked = jnp.where(home_places[:, None] == end_places[None, :] + 1, 1, marked)
    marked = jnp.where((home_places[:, None] == 0) & (offsets[None, :] == 0), 1, marked)
    onehot = (marked[..., None] == jnp.arange(token_table.shape[0], dtype=jnp.int32)).astype(
        jnp.bfloat16
    )
    embedded = jnp.einsum("swv,vd->swd", onehot, token_table, preferred_element_type=jnp.float32)
    stream_three = jnp.transpose(hidden, (1, 0, 2)).astype(jnp.float32) + embedded
    cot_three = jnp.transpose(cotangent, (1, 0, 2))
    own_high = jnp.max(home_places)
    stream_rows = stream_three.reshape(token_rows, model_width)
    normed, norm_back = jax.vjp(norm_rows, stream_rows, norm_gain, norm_bias)
    normed_low = normed.astype(jnp.bfloat16)
    projected = jnp.dot(normed_low, qkv_weight, preferred_element_type=jnp.float32)
    cosine_table, sine_table = angles(home_places)
    cosine_table = cosine_table[:, None, None, :]
    sine_table = sine_table[:, None, None, :]

    def turn_heads(projected_rows):
        divided = projected_rows.reshape(shard_rows, windows_here, 3, head_count, HEAD_DIM)
        return (
            rotate(divided[:, :, 0], cosine_table, sine_table),
            rotate(divided[:, :, 1], cosine_table, sine_table),
            divided[:, :, 2],
        )

    (queries, key_rows, values), turn_back = jax.vjp(turn_heads, projected)
    query_low = queries.astype(jnp.bfloat16)
    key_value = jnp.concatenate(
        [
            key_rows.reshape(shard_rows, windows_here, model_width),
            values.reshape(shard_rows, windows_here, model_width),
        ],
        axis=-1,
    ).astype(jnp.bfloat16)

    def split_block(key_block):
        row_count = key_block.shape[0]
        return (
            key_block[..., :model_width].reshape(row_count, windows_here, head_count, HEAD_DIM),
            key_block[..., model_width:].reshape(row_count, windows_here, head_count, HEAD_DIM),
        )

    def block_places(row_start, row_count):
        return row_start + jnp.arange(row_count, dtype=jnp.int32)

    def block_scores(key_block, key_start):
        key_part, value_part = split_block(key_block)
        key_places = block_places(key_start, key_block.shape[0])
        scores = (
            jnp.einsum("qwhd,kwhd->whqk", query_low, key_part, preferred_element_type=jnp.float32)
            * 0.125
        )
        scores = jnp.where(visible(home_places, key_places, end_places)[:, None], scores, BLOCKED)
        return (scores, key_part, value_part)

    def attend(carried, key_block, key_start):
        running, totals, accumulated = carried
        scores, key_part, value_part = block_scores(key_block, key_start)
        highest = jnp.maximum(running, jnp.max(scores, axis=-1))
        factor = jnp.exp(running - highest)
        raised = jnp.exp(scores - highest[..., None])
        totals = totals * factor + jnp.sum(raised, axis=-1)
        accumulated = accumulated * factor[..., None] + jnp.einsum(
            "whqk,kwhd->whqd",
            raised.astype(jnp.bfloat16),
            value_part,
            preferred_element_type=jnp.float32,
        )
        return (highest, totals, accumulated)

    start_state = (
        jnp.full((windows_here, head_count, shard_rows), BLOCKED, jnp.float32),
        jnp.zeros((windows_here, head_count, shard_rows), jnp.float32),
        jnp.zeros((windows_here, head_count, shard_rows, HEAD_DIM), jnp.float32),
    )
    carried = start_state
    fetched_rows = lax.all_gather(key_value, "seq", axis=0, tiled=True)
    row_count = fetched_rows.shape[0]
    blocks = fetched_rows.reshape((row_count // shard_rows, shard_rows) + fetched_rows.shape[1:])

    def visit_block(held_state, element):
        number, key_block = element
        key_start = number * shard_rows
        dead = jnp.min(block_places(key_start, shard_rows)) > own_high
        held_state = lax.cond(
            dead,
            lambda kept_state: kept_state,
            lambda kept_state: attend(kept_state, key_block, key_start),
            held_state,
        )
        return (held_state, None)

    carried, unused = lax.scan(
        visit_block, carried, (jnp.arange(blocks.shape[0], dtype=jnp.int32), blocks)
    )
    running, totals, accumulated = carried
    attention = accumulated / totals[..., None]
    log_total = running + jnp.log(totals)
    attention_rows = jnp.transpose(attention, (2, 0, 1, 3))
    mixed_low = attention_rows.reshape(token_rows, model_width).astype(jnp.bfloat16)
    attended = jnp.dot(mixed_low, out_weight, preferred_element_type=jnp.float32)
    pre_active = jnp.dot(normed_low, in_weight, preferred_element_type=jnp.float32) + in_bias
    active, gelu_back = jax.vjp(gelu_rows, pre_active)
    active_low = active.astype(jnp.bfloat16)
    result = (
        stream_rows
        + attended
        + jnp.dot(active_low, down_weight, preferred_element_type=jnp.float32)
        + down_bias
    )
    grad_rows = cot_three.reshape(token_rows, model_width)
    down_weight_grad = jnp.dot(active_low.T, grad_rows, preferred_element_type=jnp.float32)
    down_bias_grad = jnp.sum(grad_rows.astype(jnp.float32), axis=0)
    out_weight_grad = jnp.dot(mixed_low.T, grad_rows, preferred_element_type=jnp.float32)
    active_grad = jnp.dot(grad_rows, down_weight.T, preferred_element_type=jnp.float32)
    pre_grad = gelu_back(active_grad)[0].astype(jnp.bfloat16)
    in_weight_grad = jnp.dot(normed_low.T, pre_grad, preferred_element_type=jnp.float32)
    in_bias_grad = jnp.sum(pre_grad.astype(jnp.float32), axis=0)
    mixed_grad = jnp.dot(grad_rows, out_weight.T, preferred_element_type=jnp.float32).astype(
        jnp.bfloat16
    )
    grad_heads = mixed_grad.reshape(shard_rows, windows_here, head_count, HEAD_DIM)
    delta_rows = jnp.sum(grad_heads.astype(jnp.float32) * attention_rows, axis=-1)
    row_delta = jnp.transpose(delta_rows, (1, 2, 0))
    whole_keys = lax.all_gather(key_value, "seq", axis=0, tiled=True)
    blocks = whole_keys.reshape((seq_count, shard_rows) + whole_keys.shape[1:])
    zero_heads = jnp.zeros((shard_rows, windows_here, head_count, HEAD_DIM), jnp.float32)

    def back_block(query_grad, element):
        number, key_block = element
        key_start = number * shard_rows

        def live_block(held_grad):
            scores, key_part, value_part = block_scores(key_block, key_start)
            weighting = jnp.exp(scores - log_total[..., None])
            prob_grad = jnp.einsum(
                "qwhd,kwhd->whqk", grad_heads, value_part, preferred_element_type=jnp.float32
            )
            score_low = (weighting * (prob_grad - row_delta[..., None])).astype(jnp.bfloat16)
            held_grad = held_grad + 0.125 * jnp.einsum(
                "whqk,kwhd->qwhd", score_low, key_part, preferred_element_type=jnp.float32
            )
            key_grad = 0.125 * jnp.einsum(
                "whqk,qwhd->kwhd", score_low, query_low, preferred_element_type=jnp.float32
            )
            value_grad = jnp.einsum(
                "whqk,qwhd->kwhd",
                weighting.astype(jnp.bfloat16),
                grad_heads,
                preferred_element_type=jnp.float32,
            )
            return (
                held_grad,
                jnp.concatenate(
                    [
                        key_grad.reshape(shard_rows, windows_here, model_width),
                        value_grad.reshape(shard_rows, windows_here, model_width),
                    ],
                    axis=-1,
                ),
            )

        def dead_block(held_grad):
            return (held_grad, jnp.zeros((shard_rows, windows_here, 2 * model_width), jnp.float32))

        dead = jnp.min(block_places(key_start, shard_rows)) > own_high
        return lax.cond(dead, dead_block, live_block, query_grad)

    query_grad, key_terms = lax.scan(
        back_block, zero_heads, (jnp.arange(seq_count, dtype=jnp.int32), blocks)
    )
    key_terms = key_terms.reshape((seq_count * shard_rows,) + key_terms.shape[2:])
    summed = lax.psum_scatter(
        key_terms.astype(jnp.bfloat16), "seq", scatter_dimension=0, tiled=True
    ).astype(jnp.float32)
    key_grad = summed[..., :model_width].reshape(shard_rows, windows_here, head_count, HEAD_DIM)
    value_grad = summed[..., model_width:].reshape(shard_rows, windows_here, head_count, HEAD_DIM)
    joined_grad = turn_back((query_grad, key_grad, value_grad))[0].astype(jnp.bfloat16)
    qkv_weight_grad = jnp.dot(normed_low.T, joined_grad, preferred_element_type=jnp.float32)
    normed_grad = jnp.dot(joined_grad, qkv_weight.T, preferred_element_type=jnp.float32) + jnp.dot(
        pre_grad, in_weight.T, preferred_element_type=jnp.float32
    )
    stream_part, norm_gain_grad, norm_bias_grad = norm_back(normed_grad)
    stream_grad = grad_rows.astype(jnp.float32) + stream_part
    result_three = result.reshape(shard_rows, windows_here, model_width)
    grad_three = stream_grad.reshape(shard_rows, windows_here, model_width)
    output = jnp.transpose(result_three, (1, 0, 2)).astype(jnp.bfloat16)
    hidden_grad = jnp.transpose(grad_three, (1, 0, 2))
    shares = (
        lax.psum_scatter(
            norm_gain_grad.astype(jnp.bfloat16), "seq", scatter_dimension=0, tiled=True
        ).astype(jnp.float32),
        lax.psum_scatter(
            norm_bias_grad.astype(jnp.bfloat16), "seq", scatter_dimension=0, tiled=True
        ).astype(jnp.float32),
        lax.psum_scatter(
            qkv_weight_grad.astype(jnp.bfloat16), "seq", scatter_dimension=0, tiled=True
        ).astype(jnp.float32),
        lax.psum_scatter(
            out_weight_grad.astype(jnp.bfloat16), "seq", scatter_dimension=0, tiled=True
        ).astype(jnp.float32),
        lax.psum_scatter(
            in_weight_grad.astype(jnp.bfloat16), "seq", scatter_dimension=0, tiled=True
        ).astype(jnp.float32),
        lax.psum_scatter(
            in_bias_grad.astype(jnp.bfloat16), "seq", scatter_dimension=0, tiled=True
        ).astype(jnp.float32),
        lax.psum_scatter(
            down_weight_grad.astype(jnp.bfloat16), "seq", scatter_dimension=0, tiled=True
        ).astype(jnp.float32),
        lax.psum_scatter(
            down_bias_grad.astype(jnp.bfloat16), "seq", scatter_dimension=0, tiled=True
        ).astype(jnp.float32),
    )
    totals_all = (
        lax.psum(shares[0].astype(jnp.bfloat16), "batch").astype(jnp.float32),
        lax.psum(shares[1].astype(jnp.bfloat16), "batch").astype(jnp.float32),
        lax.psum(shares[2].astype(jnp.bfloat16), "batch").astype(jnp.float32),
        lax.psum(shares[3].astype(jnp.bfloat16), "batch").astype(jnp.float32),
        lax.psum(shares[4].astype(jnp.bfloat16), "batch").astype(jnp.float32),
        lax.psum(shares[5].astype(jnp.bfloat16), "batch").astype(jnp.float32),
        lax.psum(shares[6].astype(jnp.bfloat16), "batch").astype(jnp.float32),
        lax.psum(shares[7].astype(jnp.bfloat16), "batch").astype(jnp.float32),
    )
    return (
        output,
        hidden_grad,
        totals_all[0],
        totals_all[1],
        totals_all[2],
        totals_all[3],
        totals_all[4],
        totals_all[5],
        totals_all[6],
        totals_all[7],
    )


def solution(mesh):
    placed = (
        P("batch", "seq", None),
        P("batch", "seq"),
        P("batch"),
        P("batch"),
        P(),
        P(),
        P(),
        P(),
        P(),
        P(),
        P(),
        P(),
        P(),
        P("batch", "seq", None),
    )

    def body(*arrays):
        hidden = arrays[0]
        owners = mesh.shape["seq"]
        if hidden.shape[0] == 1 and hidden.shape[2] == 2 * PAIR * owners and owners == 4 and mesh.shape["batch"] == 8:
            return fast_body(*arrays)
        return plain_body(*arrays)

    return jax.shard_map(
        body,
        mesh=mesh,
        in_specs=placed,
        out_specs=(
            P("batch", "seq", None),
            P("batch", "seq", None),
            P("seq"),
            P("seq"),
            P("seq", None),
            P("seq", None),
            P("seq", None),
            P("seq"),
            P("seq", None),
            P("seq"),
        ),
        check_vma=False,
    )
```

```python
import math

import jax
import jax.numpy as jnp
import numpy as np
from jax import lax
from jax.experimental import pallas as pl
from jax.experimental.pallas import tpu as pltpu
from jax.sharding import PartitionSpec as P

HEAD_DIM = 64
ROT = 32
PAIR = 2 * HEAD_DIM

EPSILON = 1e-05
BLOCKED = -1e30
LOG2E = math.log2(math.e)
BF16 = jnp.bfloat16
F32 = jnp.float32
MIB = 1 << 20
SHORT = pl.CostEstimate(flops=1000, bytes_accessed=1000, transcendentals=0)
LONG = pl.CostEstimate(flops=10**11, bytes_accessed=1000, transcendentals=0)


def dot_nn(left, right):
    return lax.dot_general(left, right, (((1,), (0,)), ((), ())), preferred_element_type=F32)


def dot_nt(left, right):
    return lax.dot_general(left, right, (((1,), (1,)), ((), ())), preferred_element_type=F32)


def dot_tn(left, right):
    return lax.dot_general(left, right, (((0,), (0,)), ((), ())), preferred_element_type=F32)


def swap_pairs(rows):
    width = rows.shape[1]
    lanes = lax.broadcasted_iota(jnp.int32, rows.shape, 1)
    return jnp.where(lanes % 2 == 0, pltpu.roll(rows, width - 1, 1), pltpu.roll(rows, 1, 1))


def trig_tables(length):
    inverse = 10000.0 ** (-(np.arange(ROT // 2, dtype=np.float32) * np.float32(2.0)) / np.float32(ROT))
    phases = np.arange(length, dtype=np.float32)[:, None] * inverse.astype(np.float32)[None, :]
    cosine = np.ones((length, HEAD_DIM), np.float32)
    sine = np.zeros((length, HEAD_DIM), np.float32)
    cosine[:, :ROT] = np.repeat(np.cos(phases), 2, axis=1)
    sine[:, :ROT] = np.repeat(np.sin(phases), 2, axis=1) * np.tile(np.array([-1.0, 1.0], np.float32), ROT // 2)
    return np.tile(cosine, (1, 2)), np.tile(sine, (1, 2))


def whole(array):
    shape = array.shape
    return pl.BlockSpec(shape, lambda i: (0,) * len(shape))


SCALARS = pl.BlockSpec(memory_space=pltpu.SMEM)


def prep_kernel(hidden_ref, mark_ref, table_ref, gain_ref, bias_ref, stream_ref, normed_ref, turned_ref):
    rows = hidden_ref.shape[0]
    vocab = table_ref.shape[0]
    onehot = (mark_ref[...] == lax.broadcasted_iota(jnp.int32, (rows, vocab), 1)).astype(F32).astype(BF16)
    stream = hidden_ref[...].astype(F32) + dot_nn(onehot, table_ref[...])
    centre = stream - jnp.mean(stream, axis=-1, keepdims=True)
    spread = jnp.mean(centre * centre, axis=-1, keepdims=True)
    normed = centre * lax.rsqrt(spread + EPSILON) * gain_ref[...] + bias_ref[...]
    stream_ref[...] = stream
    normed_ref[...] = normed.astype(BF16)
    turned_ref[...] = normed.astype(BF16).T


def prepare(hidden, marked, table, gain, bias):
    rows, width = hidden.shape
    step = 128
    return pl.pallas_call(
        prep_kernel,
        grid=(rows // step,),
        in_specs=[
            pl.BlockSpec((step, width), lambda i: (i, 0)),
            pl.BlockSpec((step, 1), lambda i: (i, 0)),
            pl.BlockSpec(table.shape, lambda i: (0, 0)),
            pl.BlockSpec((1, width), lambda i: (0, 0)),
            pl.BlockSpec((1, width), lambda i: (0, 0)),
        ],
        out_specs=[
            pl.BlockSpec((step, width), lambda i: (i, 0)),
            pl.BlockSpec((step, width), lambda i: (i, 0)),
            pl.BlockSpec((width, step), lambda i: (0, i)),
        ],
        out_shape=[
            jax.ShapeDtypeStruct((rows, width), F32),
            jax.ShapeDtypeStruct((rows, width), BF16),
            jax.ShapeDtypeStruct((width, rows), BF16),
        ],
        cost_estimate=SHORT,
        name="prep",
    )(hidden, marked, table, gain, bias)


def heads_kernel(owners_ref, normed_ref, cot_ref, wq_ref, wk_ref, wv_ref, wo_ref, cos_ref, sin_ref, *out_refs):
    normed = normed_ref[...]
    shifts = pl.num_programs(0)
    chunks = wq_ref.shape[1] // PAIR
    cosine = jnp.concatenate([cos_ref[...]] * chunks, axis=1)
    sine = jnp.concatenate([sin_ref[...]] * chunks, axis=1)

    def turned(rows):
        return rows * cosine + swap_pairs(rows) * sine

    parts = (
        turned(dot_nn(normed, wq_ref[...])).astype(BF16),
        turned(dot_nn(normed, wk_ref[...])).astype(BF16),
        dot_nn(normed, wv_ref[...]).astype(BF16),
        dot_nt(cot_ref[...], wo_ref[...]).astype(BF16),
    )
    for number, out_ref in enumerate(out_refs):
        shift, chunk = divmod(number, chunks)

        @pl.when(pl.program_id(0) == shift)
        def _():
            for at, part in enumerate(parts):
                out_ref[:, at * PAIR : (at + 1) * PAIR] = part[:, chunk * PAIR : (chunk + 1) * PAIR]


def heads_of(order, normed, cot, qkv_weight, out_weight, cosine, sine):
    rows, width = normed.shape
    owners = order.shape[0]
    wide = width // owners
    chunks = wide // PAIR
    fixed = pl.BlockSpec((rows, width), lambda i, o: (0, 0))
    table = pl.BlockSpec((rows, PAIR), lambda i, o: (o[0], 0))

    def columns(part):
        return pl.BlockSpec((width, wide), lambda i, o: (0, part * owners + o[i]))

    blocks = pl.pallas_call(
        heads_kernel,
        grid_spec=pltpu.PrefetchScalarGridSpec(
            num_scalar_prefetch=1,
            grid=(owners,),
            in_specs=[fixed, fixed]
            + [columns(part) for part in range(3)]
            + [pl.BlockSpec((wide, width), lambda i, o: (o[i], 0)), table, table],
            out_specs=[pl.BlockSpec((rows, 4 * PAIR), lambda i, o: (0, 0))] * (owners * chunks),
        ),
        out_shape=[jax.ShapeDtypeStruct((rows, 4 * PAIR), BF16)] * (owners * chunks),
        compiler_params=pltpu.CompilerParams(vmem_limit_bytes=60 * MIB),
        cost_estimate=SHORT,
        name="heads",
    )(order, normed, cot, qkv_weight, qkv_weight, qkv_weight, out_weight, cosine, sine)
    return [[blocks[shift * chunks + chunk] for shift in range(owners)] for chunk in range(chunks)]


QUERY_ROWS = 512
KEY_ROWS = QUERY_ROWS


def attention_kernel(pieces, info_ref, *refs):
    piece_refs = refs[:pieces]
    cos_ref, sin_ref = refs[pieces : pieces + 2]
    out_refs = refs[pieces + 2 : -9]
    held, results, key_turned, value_turned, doubled, score_ref, raised_ref, key_sum, value_sum = refs[-9:]
    me, end = info_ref[0], info_ref[1]
    rows = piece_refs[0].shape[0]
    length = rows * pieces
    for shift in range(pieces):
        start = pl.multiple_of(lax.rem(me - shift + pieces, pieces) * rows, rows)
        held[pl.ds(start, rows), :] = piece_refs[shift][...]
    key_turned[...] = held[:, PAIR : 2 * PAIR].T
    value_turned[...] = held[:, 2 * PAIR : 3 * PAIR].T
    for head in range(2):
        keys = held[:, PAIR + head * HEAD_DIM : PAIR + (head + 1) * HEAD_DIM]
        doubled[head] = jnp.concatenate([keys, keys], axis=1)
    key_sum[...] = jnp.zeros_like(key_sum)
    value_sum[...] = jnp.zeros_like(value_sum)
    scale = 0.125 * LOG2E
    halves = lax.broadcasted_iota(jnp.int32, (QUERY_ROWS, PAIR), 1) // HEAD_DIM
    causal = lax.broadcasted_iota(jnp.int32, (KEY_ROWS, QUERY_ROWS), 0) <= lax.broadcasted_iota(
        jnp.int32, (KEY_ROWS, QUERY_ROWS), 1
    )
    key_steps = lax.broadcasted_iota(jnp.int32, (KEY_ROWS, QUERY_ROWS), 0)

    def query_block(number, carry):
        first = pl.multiple_of(number * QUERY_ROWS, QUERY_ROWS)
        query_rows = held[pl.ds(first, QUERY_ROWS), 0:PAIR]
        grad_rows = held[pl.ds(first, QUERY_ROWS), 3 * PAIR : 4 * PAIR]
        zero = jnp.zeros_like(query_rows)
        queries = [jnp.where(halves == head, query_rows, zero) for head in range(2)]
        scaled = query_rows.astype(F32) * scale
        large = scaled.astype(BF16)
        small = (scaled - large.astype(F32)).astype(BF16)
        pairs = [
            jnp.concatenate(
                [part[:, head * HEAD_DIM : (head + 1) * HEAD_DIM] for part in (large, small)], axis=1
            )
            for head in range(2)
        ]
        query_places = first + lax.broadcasted_iota(jnp.int32, (1, QUERY_ROWS), 1)
        lowest = jnp.where(query_places > end, end + 1, 0)

        def scores_of(block, highest, diagonal, parted):
            start = pl.multiple_of(block * KEY_ROWS, KEY_ROWS)
            after = []
            for head in range(2):
                scores = dot_nt(doubled[head, pl.ds(start, KEY_ROWS), :], pairs[head])
                if diagonal:
                    scores = jnp.where(causal, scores, BLOCKED)
                if parted:
                    scores = jnp.where(key_steps >= lowest - start, scores, BLOCKED)
                score_ref[head, pl.ds(start, KEY_ROWS), :] = scores
                after.append(jnp.maximum(highest[head], jnp.max(scores, axis=0, keepdims=True)))
            return tuple(after)

        def any_scores(block, highest, diagonal=False):
            parted = (first + QUERY_ROWS - 1 > end) & (block * KEY_ROWS <= end)
            return lax.cond(
                parted,
                lambda held_rows: scores_of(block, held_rows, diagonal, True),
                lambda held_rows: scores_of(block, held_rows, diagonal, False),
                highest,
            )

        start_row = jnp.full((1, QUERY_ROWS), BLOCKED, F32)
        highest = lax.fori_loop(0, number, any_scores, (start_row, start_row))
        highest = any_scores(number, highest, True)

        def mix(block, carried):
            start = pl.multiple_of(block * KEY_ROWS, KEY_ROWS)
            after = []
            for head in range(2):
                total, mixed = carried[head]
                raised = jnp.exp2(score_ref[head, pl.ds(start, KEY_ROWS), :] - highest[head])
                rounded = raised.astype(BF16)
                raised_ref[head, pl.ds(start, KEY_ROWS), :] = rounded
                values = value_turned[head * HEAD_DIM : (head + 1) * HEAD_DIM, pl.ds(start, KEY_ROWS)]
                after.append((total + jnp.sum(raised, axis=0, keepdims=True), mixed + dot_nn(values, rounded)))
            return tuple(after)

        empty = (jnp.zeros((1, QUERY_ROWS), F32), jnp.zeros((HEAD_DIM, QUERY_ROWS), F32))
        mixes = lax.fori_loop(0, number + 1, mix, (empty, empty))
        inverse = [1.0 / mixes[head][0] for head in range(2)]
        mixed = jnp.concatenate([mixes[head][1] * inverse[head] for head in range(2)], axis=0)
        turned = grad_rows.astype(F32).T
        turned = jnp.concatenate(
            [turned[head * HEAD_DIM : (head + 1) * HEAD_DIM] * inverse[head] for head in range(2)], axis=0
        )
        products = mixed * turned
        delta = [
            jnp.sum(products[head * HEAD_DIM : (head + 1) * HEAD_DIM], axis=0, keepdims=True) for head in range(2)
        ]
        divided = turned.T.astype(BF16)
        grads = [jnp.where(halves == head, divided, zero) for head in range(2)]

        def back(block, carried):
            start = pl.multiple_of(block * KEY_ROWS, KEY_ROWS)
            values = held[pl.ds(start, KEY_ROWS), 2 * PAIR : 3 * PAIR]
            after, key_terms, value_terms = [], [], []
            for head in range(2):
                raised = raised_ref[head, pl.ds(start, KEY_ROWS), :]
                score_grad = raised * (dot_nt(values, grads[head]) - delta[head]).astype(BF16)
                value_terms.append(dot_nn(raised, grads[head]))
                key_terms.append(dot_nn(score_grad, queries[head]))
                keys = key_turned[head * HEAD_DIM : (head + 1) * HEAD_DIM, pl.ds(start, KEY_ROWS)]
                after.append(carried[head] + dot_nn(keys, score_grad))
            value_sum[pl.ds(start, KEY_ROWS), :] += value_terms[0] + value_terms[1]
            key_sum[pl.ds(start, KEY_ROWS), :] += key_terms[0] + key_terms[1]
            return tuple(after)

        query_grads = lax.fori_loop(0, number + 1, back, (empty[1], empty[1]))
        query_grad = jnp.concatenate(query_grads, axis=0).T * 0.125
        cosine = cos_ref[pl.ds(first, QUERY_ROWS), :]
        sine = sin_ref[pl.ds(first, QUERY_ROWS), :]
        results[pl.ds(first, QUERY_ROWS), 0:PAIR] = (query_grad * cosine - swap_pairs(query_grad) * sine).astype(BF16)
        results[pl.ds(first, QUERY_ROWS), 3 * PAIR : 4 * PAIR] = mixed.T.astype(BF16)
        return carry

    lax.fori_loop(0, length // QUERY_ROWS, query_block, 0)
    key_grad = key_sum[...] * 0.125
    results[:, PAIR : 2 * PAIR] = (key_grad * cos_ref[...] - swap_pairs(key_grad) * sin_ref[...]).astype(BF16)
    results[:, 2 * PAIR : 3 * PAIR] = value_sum[...].astype(BF16)
    for shift in range(pieces):
        start = pl.multiple_of(lax.rem(me + shift, pieces) * rows, rows)
        out_refs[shift][...] = results[pl.ds(start, rows), :]


def attention(info, parts, cosine, sine):
    pieces = len(parts)
    rows = parts[0].shape[0]
    length = rows * pieces
    arrays = (*parts, cosine, sine)
    shapes = [jax.ShapeDtypeStruct((rows, 4 * PAIR), BF16)] * pieces
    return pl.pallas_call(
        lambda *refs: attention_kernel(pieces, *refs),
        grid=(1,),
        in_specs=[SCALARS] + [whole(array) for array in arrays],
        out_specs=[whole(shape) for shape in shapes],
        out_shape=shapes,
        scratch_shapes=[
            pltpu.VMEM((length, 4 * PAIR), BF16),
            pltpu.VMEM((length, 4 * PAIR), BF16),
            pltpu.VMEM((PAIR, length), BF16),
            pltpu.VMEM((PAIR, length), BF16),
            pltpu.VMEM((2, length, PAIR), BF16),
            pltpu.VMEM((2, length, QUERY_ROWS), F32),
            pltpu.VMEM((2, length, QUERY_ROWS), BF16),
            pltpu.VMEM((length, PAIR), F32),
            pltpu.VMEM((length, PAIR), F32),
        ],
        compiler_params=pltpu.CompilerParams(vmem_limit_bytes=60 * MIB),
        cost_estimate=SHORT,
        name="attention",
    )(info, *arrays)


def feed_kernel(cells_ref, normed_ref, turned_ref, cot_ref, in_ref, bias_ref, down_ref, *out_refs):
    sides = (out_refs[0:2], out_refs[2:4])
    bias_grad, out_sum, norm_sum = out_refs[4:]
    step = pl.program_id(0)
    steps = pl.num_programs(0) // 2
    up = math.sqrt(2.0 / math.pi)

    @pl.when(step == 0)
    def _():
        out_sum[...] = jnp.zeros_like(out_sum)
        norm_sum[...] = jnp.zeros_like(norm_sum)

    weights = in_ref[...]
    downs = down_ref[...]
    cot = cot_ref[...]
    pre = dot_nn(normed_ref[...], weights) + bias_ref[...]
    square = pre * pre
    tanh = jnp.tanh(up * pre * (1.0 + 0.044715 * square))
    half = 0.5 * (1.0 + tanh)
    active = (pre * half).astype(BF16)
    slope = half + 0.5 * pre * (1.0 - tanh * tanh) * (up * (1.0 + 3 * 0.044715 * square))
    pre_grad = (dot_nt(cot, downs) * slope).astype(BF16)
    in_term = dot_nn(turned_ref[...], pre_grad).astype(BF16)
    down_term = dot_tn(active, cot).astype(BF16)
    for side, (in_grad, down_grad) in enumerate(sides):

        @pl.when((step >= steps) == bool(side))
        def _():
            pieces, owners, kept, tile = in_grad.shape
            for owner in range(owners):
                for piece in range(pieces):
                    start = (owner * pieces + piece) * kept
                    in_grad[piece, owner] = in_term[start : start + kept]
            kept = tile // pieces
            for group in range(down_term.shape[1] // tile):
                for piece in range(pieces):
                    down_grad[piece, 0, group * kept : (group + 1) * kept] = down_term[
                        piece * kept : (piece + 1) * kept, group * tile : (group + 1) * tile
                    ]

    bias_grad[0] = jnp.sum(pre_grad.astype(F32), axis=0, keepdims=True)
    out_sum[...] += dot_nn(active, downs)
    norm_sum[...] += dot_nt(pre_grad, weights)


def feed_forward(cells, normed, turned, cot, in_weight, in_bias, down_weight, pieces):
    rows, width = normed.shape
    steps = cells.shape[0]
    owners = steps // 2
    hidden_units = in_weight.shape[1]
    tile = hidden_units // steps
    kept = width // owners // pieces
    tall = owners * kept
    wide = tile // pieces * (width // tile)
    fixed = pl.BlockSpec((rows, width), lambda i, c: (0, 0))

    def first(i):
        return jnp.minimum(i, owners - 1)

    def second(i):
        return jnp.maximum(i - owners, 0)

    def sides_of(turn):
        return [
            pl.BlockSpec((pieces, owners, kept, tile), lambda i, c: (0, 0, turn(i), 0)),
            pl.BlockSpec((pieces, 1, wide, tile), lambda i, c: (0, turn(i), 0, 0)),
        ]

    grads = [
        jax.ShapeDtypeStruct((pieces, owners, tall, tile), BF16),
        jax.ShapeDtypeStruct((pieces, owners, wide, tile), BF16),
    ]
    full = jax.ShapeDtypeStruct((rows, width), F32)
    results = pl.pallas_call(
        feed_kernel,
        grid_spec=pltpu.PrefetchScalarGridSpec(
            num_scalar_prefetch=1,
            grid=(steps,),
            in_specs=[
                fixed,
                pl.BlockSpec((width, rows), lambda i, c: (0, 0)),
                fixed,
                pl.BlockSpec((width, tile), lambda i, c: (0, c[i])),
                pl.BlockSpec((1, tile), lambda i, c: (0, c[i])),
                pl.BlockSpec((tile, width), lambda i, c: (c[i], 0)),
            ],
            out_specs=sides_of(first)
            + sides_of(second)
            + [pl.BlockSpec((1, 1, tile), lambda i, c: (i, 0, 0)), fixed, fixed],
        ),
        out_shape=grads + grads + [jax.ShapeDtypeStruct((steps, 1, tile), F32), full, full],
        compiler_params=pltpu.CompilerParams(vmem_limit_bytes=60 * MIB),
        cost_estimate=SHORT,
        name="feed",
    )(cells, normed, turned, cot, in_weight, in_bias, down_weight)
    return results[:2], results[2:4], *results[4:]


def place_columns(me_ref, piece_refs, held):
    owners = len(piece_refs)
    for shift in range(owners):
        owner = lax.rem(me_ref[0] - shift + owners, owners)
        start = pl.multiple_of(owner * PAIR, PAIR)
        for part in range(4):
            held[part, :, pl.ds(start, PAIR)] = piece_refs[shift][:, part * PAIR : (part + 1) * PAIR]


def weight_kernel(pieces, info_ref, turned_ref, cot_ref, *refs):
    owners = len(refs) - 4
    kept_ref, sent_ref, held, grad = refs[-4:]
    place_columns(info_ref, refs[:owners], held)
    kept = PAIR // pieces
    turned = turned_ref[...]
    for part in range(3):
        grad[...] = dot_nn(turned, held[part]).astype(BF16)
        for side, ref in enumerate((kept_ref, sent_ref)):
            core = info_ref[1] ^ side
            for owner in range(owners):
                for piece in range(pieces):
                    start = pl.multiple_of(((owner * 2 + core) * pieces + piece) * kept, kept)
                    ref[piece, owner, part * kept : (part + 1) * kept] = grad[pl.ds(start, kept), :]
    term = dot_tn(held[3], cot_ref[...]).astype(BF16)
    rows, half = term.shape[0], term.shape[1] // 2
    for core in range(2):
        grad[core * rows : (core + 1) * rows, :] = term[:, core * half : (core + 1) * half]
    for side, ref in enumerate((kept_ref, sent_ref)):
        core = info_ref[1] ^ side
        for owner in range(owners):
            for piece in range(pieces):
                start = pl.multiple_of(core * rows + (owner * pieces + piece) * kept, kept)
                ref[piece, owner, 3 * kept :] = grad[pl.ds(start, kept), :]


def weight_grads(info, turned, cot, parts, pieces):
    owners = len(parts)
    rows, width = cot.shape
    kept = PAIR // pieces
    arrays = (turned, cot, *parts)
    shape = jax.ShapeDtypeStruct((pieces, owners, 4 * kept, owners * PAIR), BF16)
    return pl.pallas_call(
        lambda *refs: weight_kernel(pieces, *refs),
        grid=(1,),
        in_specs=[SCALARS] + [whole(array) for array in arrays],
        out_specs=[whole(shape)] * 2,
        out_shape=[shape] * 2,
        scratch_shapes=[pltpu.VMEM((4, rows, owners * PAIR), BF16), pltpu.VMEM((width, owners * PAIR), BF16)],
        compiler_params=pltpu.CompilerParams(vmem_limit_bytes=60 * MIB),
        cost_estimate=SHORT,
        name="weight_grads",
    )(info, *arrays)


def sums_kernel(last, owners, me_ref, *refs):
    piece_refs, refs = refs[:owners], refs[owners:]
    weight_refs, refs = refs[: 3 * owners], refs[3 * owners :]
    out_weight_refs, refs = refs[:owners], refs[owners:]
    out_in, norm_in = refs[:2]
    held = refs[-1]
    place_columns(me_ref, piece_refs, held)
    norm = norm_in[...]
    for part in range(3):
        weights = jnp.concatenate([ref[...] for ref in weight_refs[part * owners : (part + 1) * owners]], axis=1)
        norm = norm + dot_nt(held[part], weights)
    weights = jnp.concatenate([ref[...] for ref in out_weight_refs], axis=0)
    out = out_in[...] + dot_nn(held[3], weights)
    if not last:
        out_ref, norm_ref = refs[2:4]
        out_ref[...] = out
        norm_ref[...] = norm
        return
    stream_ref, cot_ref, gain_ref, down_bias_ref, out_ref, hidden_ref, gain_grad, bias_grad = refs[2:-1]
    stream = stream_ref[...]
    cot = cot_ref[...].astype(F32)
    out_ref[...] = (stream + out + down_bias_ref[...]).astype(BF16)
    centre = stream - jnp.mean(stream, axis=-1, keepdims=True)
    spread = jnp.mean(centre * centre, axis=-1, keepdims=True)
    inverse = lax.rsqrt(spread + EPSILON)
    hat = centre * inverse
    gained = norm * gain_ref[...]
    hidden_ref[...] = cot + inverse * (
        gained
        - jnp.mean(gained, axis=-1, keepdims=True)
        - hat * jnp.mean(gained * hat, axis=-1, keepdims=True)
    )
    for out_ref, rows in ((gain_grad, norm * hat), (bias_grad, norm)):
        row = jnp.sum(rows, axis=0, keepdims=True)
        wide = out_ref.shape[1]
        for owner in range(owners):
            out_ref[owner : owner + 1, :] = row[:, owner * wide : (owner + 1) * wide]


def sums_of(info, chunk, chunks, parts, qkv_weight, out_weight, sums, final=()):
    owners = len(parts)
    rows = parts[0].shape[0]
    width = qkv_weight.shape[0]
    last = bool(final)

    def columns(part, owner):
        at = (part * owners + owner) * chunks + chunk
        return pl.BlockSpec((width, PAIR), lambda i: (0, at))

    def weight_rows(owner):
        return pl.BlockSpec((PAIR, width), lambda i: (owner * chunks + chunk, 0))

    full = jax.ShapeDtypeStruct((rows, width), F32)
    row = jax.ShapeDtypeStruct((owners, width // owners), F32)
    shapes = [jax.ShapeDtypeStruct((rows, width), BF16), full, row, row] if last else [full, full]
    return pl.pallas_call(
        lambda *refs: sums_kernel(last, owners, *refs),
        grid=(1,),
        in_specs=[SCALARS]
        + [whole(part) for part in parts]
        + [columns(part, owner) for part in range(3) for owner in range(owners)]
        + [weight_rows(owner) for owner in range(owners)]
        + [whole(array) for array in (*sums, *final)],
        out_specs=[whole(shape) for shape in shapes],
        out_shape=shapes,
        scratch_shapes=[pltpu.VMEM((4, rows, owners * PAIR), BF16)],
        compiler_params=pltpu.CompilerParams(vmem_limit_bytes=60 * MIB),
        cost_estimate=SHORT,
        name="sums",
    )(info, *parts, *([qkv_weight] * (3 * owners)), *([out_weight] * owners), *sums, *final)


def feed_place_kernel(info_ref, mine_ref, other_ref, in_ref, down_ref):
    masks, total, tile = mine_ref.shape
    kept = in_ref.shape[0] // masks
    tiles = in_ref.shape[1] // (2 * tile)
    half = down_ref.shape[0] // 2
    down_kept = half // masks
    for source, ref in enumerate((mine_ref, other_ref)):
        core = info_ref[0] ^ source
        for mask in range(masks):
            chip = info_ref[1] ^ mask
            rows = pl.ds(pl.multiple_of(chip * kept, kept), kept)
            for number in range(tiles):
                columns = pl.ds(pl.multiple_of((2 * number + core) * tile, tile), tile)
                in_ref[rows, columns] = ref[mask, number * kept : (number + 1) * kept].astype(F32)
            rows = pl.ds(pl.multiple_of(core * half + chip * down_kept, down_kept), down_kept)
            for group in range(down_ref.shape[1] // tile):
                at = tiles * kept + group * down_kept
                down_ref[rows, group * tile : (group + 1) * tile] = ref[mask, at : at + down_kept].astype(F32)


def place_feed(info, mine, other, in_shape, down_shape):
    shapes = [jax.ShapeDtypeStruct(in_shape, F32), jax.ShapeDtypeStruct(down_shape, F32)]
    return pl.pallas_call(
        feed_place_kernel,
        grid=(1,),
        in_specs=[SCALARS, whole(mine), whole(other)],
        out_specs=[whole(shape) for shape in shapes],
        out_shape=shapes,
        compiler_params=pltpu.CompilerParams(vmem_limit_bytes=60 * MIB),
        cost_estimate=SHORT,
        name="place_feed",
    )(info, mine, other)


def heads_place_kernel(info_ref, mine_ref, other_ref, qkv_ref, out_ref):
    core, place = info_ref[0], info_ref[1]
    masks, total, wide = mine_ref.shape
    own_rows, width = out_ref.shape
    kept = own_rows // 2 // masks
    chunks = total // (4 * kept)
    owners = wide // PAIR
    for source, ref in enumerate((mine_ref, other_ref)):
        at_core = core if source == 0 else 1 - core
        columns = pl.ds(pl.multiple_of(at_core * (width // 2), width // 2), width // 2)
        for mask in range(masks):
            piece = place ^ mask
            rows = pl.ds(pl.multiple_of(at_core * (own_rows // 2) + piece * kept, kept), kept)
            for chunk in range(chunks):
                at = chunk * 4 * kept
                for part in range(3):
                    block = ref[mask, at + part * kept : at + (part + 1) * kept].astype(F32)
                    for owner in range(owners):
                        column = part * width + (owner * chunks + chunk) * PAIR
                        qkv_ref[rows, column : column + PAIR] = block[:, owner * PAIR : (owner + 1) * PAIR]
                out_rows = pl.ds(pl.multiple_of(chunk * PAIR + piece * kept, kept), kept)
                out_ref[out_rows, columns] = ref[mask, at + 3 * kept : at + 4 * kept].astype(F32)


def place_heads(info, mine, other, own_rows, width):
    shapes = [jax.ShapeDtypeStruct((own_rows, 3 * width), F32), jax.ShapeDtypeStruct((own_rows, width), F32)]
    return pl.pallas_call(
        heads_place_kernel,
        grid=(1,),
        in_specs=[SCALARS, whole(mine), whole(other)],
        out_specs=[whole(shape) for shape in shapes],
        out_shape=shapes,
        compiler_params=pltpu.CompilerParams(vmem_limit_bytes=60 * MIB),
        cost_estimate=SHORT,
        name="place_heads",
    )(info, mine, other)


def exchange(rows, axis, mask):
    size = lax.axis_size(axis)
    return lax.ppermute(rows, axis, [(place, place ^ mask) for place in range(size)])


def around(rows, shift):
    owners = lax.axis_size("seq")
    return lax.ppermute(rows, "seq", [(place, (place + shift) % owners) for place in range(owners)])


def total_of(*terms):
    return sum(term.astype(F32) for term in terms).astype(BF16)


def picked(rows, index, dim=0):
    return lax.dynamic_index_in_dim(rows, index, dim, keepdims=False)


def add_kernel(places, bits_ref, *refs):
    outs = refs[len(refs) - len(places) :]
    for out_ref, terms in zip(outs, places):
        at = 0
        for left, right in terms:
            rows = refs[left].shape[-2]
            total = refs[left][...].astype(F32) + refs[right][...].astype(F32)
            out_ref[..., at : at + rows, :] = total.reshape(out_ref.shape[:-2] + total.shape[-2:]).astype(BF16)
            at += rows


def add_pieces(kept, arrived):
    pieces, owners = kept[0].shape[:2]
    arrays = [array for pair in zip(kept, arrived) for array in pair]
    rows = sum(array.shape[2] for array in kept)
    columns = kept[0].shape[3]
    return pl.pallas_call(
        lambda *refs: add_kernel([[(0, 1), (2, 3)]], None, *refs),
        grid=(pieces,),
        in_specs=[pl.BlockSpec((1,) + array.shape[1:], lambda i: (i, 0, 0, 0)) for array in arrays],
        out_specs=pl.BlockSpec((1, owners, rows, columns), lambda i: (i, 0, 0, 0)),
        out_shape=jax.ShapeDtypeStruct((pieces, owners, rows, columns), BF16),
        compiler_params=pltpu.CompilerParams(vmem_limit_bytes=60 * MIB),
        cost_estimate=SHORT,
        name="add_pieces",
    )(*arrays)


def add_for_chips(chip, kept, arrived):
    specs, places, arrays = [], [], []
    chips, owners = kept[0].shape[:2]
    for mask in range(chips):
        terms = []
        for mine, other in zip(kept, arrived):
            terms.append((len(arrays), len(arrays) + 1))
            arrays += [mine, other]
            specs += [pl.BlockSpec((1,) + mine.shape[1:], lambda i, c, mask=mask: (c[0] ^ mask, 0, 0, 0))] * 2
        places.append(terms)
    rows = sum(array.shape[2] for array in kept)
    out = jax.ShapeDtypeStruct((owners, rows, kept[0].shape[3]), BF16)
    return pl.pallas_call(
        lambda *refs: add_kernel(places, *refs),
        grid_spec=pltpu.PrefetchScalarGridSpec(
            num_scalar_prefetch=1,
            grid=(1,),
            in_specs=specs,
            out_specs=[pl.BlockSpec(out.shape, lambda i, c: (0, 0, 0))] * chips,
        ),
        out_shape=[out] * chips,
        cost_estimate=SHORT,
        name="add_for_chips",
    )(chip[None], *arrays)


class Order:
    token = None

    def __call__(self, value):
        if self.token is None:
            return value
        return lax.optimization_barrier((value, self.token))[0]

    def done(self, token):
        self.token = token
        return token

    def also(self, *tokens):
        self.token = (self.token, tokens)


def fast_body(
    hidden,
    token_ids,
    offsets,
    end_places,
    token_table,
    norm_gain,
    norm_bias,
    qkv_weight,
    out_weight,
    in_weight,
    in_bias,
    down_weight,
    down_bias,
    cotangent,
):
    width = hidden.shape[2]
    rows = hidden.shape[1]
    owners = lax.axis_size("seq")
    pieces = lax.axis_size("batch")
    me = lax.axis_index("seq")
    core = lax.axis_index("batch") & 1
    length = rows * owners
    own_rows = width // owners
    chunks = own_rows // PAIR
    end = end_places[0]

    places = me * rows + jnp.arange(rows, dtype=jnp.int32)[:, None]
    marked = token_ids.reshape(rows, 1)
    marked = jnp.where(places == end, 2, marked)
    marked = jnp.where(places == end + 1, 1, marked)
    marked = jnp.where((places == 0) & (offsets[0] == 0), 1, marked)
    cot = cotangent.reshape(rows, width)
    stream, normed, turned = prepare(
        hidden.reshape(rows, width), marked, token_table, norm_gain[None], norm_bias[None]
    )
    cosine, sine = (jnp.asarray(table) for table in trig_tables(length))
    place = lax.axis_index("batch")
    info = jnp.stack([me, core]).astype(jnp.int32)
    spots = jnp.stack([me, end]).astype(jnp.int32)
    order = Order()

    def moved(blocks, shifts=(2, 1, 3)):
        return {shift: around(blocks[shift], shift) for shift in shifts}

    def gathered(blocks, arrived):
        return [blocks[0]] + [arrived[shift] for shift in range(1, owners)]

    def back(rows):
        return [exchange(rows, "batch", mask) for mask in (2, 4, 6)]

    shifts = lax.rem(me + jnp.arange(owners, dtype=jnp.int32), owners)
    heads = order.done(heads_of(shifts, normed, cot, qkv_weight, out_weight, cosine, sine))

    arrived = moved(order(heads[0]))
    cells = 2 * jnp.arange(owners, dtype=jnp.int32)
    cells = jnp.concatenate([cells + 1 - core, cells + core])
    away, here, in_bias_grad, out_sum, norm_sum = order.done(
        feed_forward(cells, order(normed), turned, cot, in_weight, in_bias[None], down_weight, pieces // 2)
    )
    order.also(arrived)

    feed_arrived = [exchange(array, "batch", 1) for array in order(away)]
    later = moved(order(heads[1]))
    first = order.done(attention(spots, gathered(heads[0], order(arrived)), cosine, sine))
    order.also(feed_arrived)
    feed_rows = order.done(add_pieces(order(here), feed_arrived))
    order.also(later)

    groups = [list(range(number, pieces, 2)) for number in range(2)]
    feed_rows = lax.psum_scatter(
        order(feed_rows), "batch", scatter_dimension=0, axis_index_groups=groups, tiled=False
    )
    arrived = moved(order(first))
    second = order.done(attention(spots, gathered(heads[1], order(later)), cosine, sine))
    cot_sum = order.done(jnp.sum(order(cot).astype(F32), axis=0))
    order.also(arrived)

    later = moved(order(second))
    parts = gathered(first, order(arrived))
    sums = order.done(sums_of(info, 0, chunks, order(parts), qkv_weight, out_weight, (out_sum, norm_sum)))
    first_kept, first_sent = order.done(weight_grads(info, turned, cot, order(parts), pieces // 2))
    order.also(later, feed_rows)

    feed_rows = lax.psum_scatter(order(feed_rows), "seq", scatter_dimension=0, tiled=False)
    grad_arrived = exchange(order(first_sent), "batch", 1)
    parts = gathered(second, order(later))
    second_kept, second_sent = order.done(weight_grads(info, turned, cot, parts, pieces // 2))
    order.also(grad_arrived)
    first_held = order.done(add_for_chips(place >> 1, [order(first_kept)], [grad_arrived]))

    first_arrived = [exchange(order(first_held[mask]), "batch", 2 * mask) for mask in (1, 2, 3)]
    grad_arrived = exchange(order(second_sent), "batch", 1)
    output, hidden_grad, gain_grad, bias_grad = order.done(
        sums_of(
            info, 1, chunks, order(parts), qkv_weight, out_weight, sums, (stream, cot, norm_gain[None], down_bias[None])
        )
    )
    order.also(first_arrived, grad_arrived)
    second_held = order.done(add_for_chips(place >> 1, [order(second_kept)], [grad_arrived]))

    def halve_seq(rows, number):
        bit = (me >> number) & 1
        split = rows.reshape((rows.shape[0] // 2, 2) + rows.shape[1:])
        return picked(split, bit, 1), exchange(picked(split, 1 - bit, 1), "seq", 1 << number)

    second_arrived = [exchange(order(second_held[mask]), "batch", 2 * mask) for mask in (1, 2, 3)]
    in_bias_grad = order(in_bias_grad)
    bias_low = jnp.where(core == 0, in_bias_grad[owners:], in_bias_grad[:owners])
    bias_high = jnp.where(core == 0, in_bias_grad[:owners], in_bias_grad[owners:])
    small = order.done(
        jnp.concatenate(
            [
                jnp.concatenate([bias_low, bias_high], axis=1).reshape(owners, -1),
                cot_sum.reshape(owners, -1),
                gain_grad,
                bias_grad,
            ],
            axis=1,
        )
    )
    small_arrived = exchange(order(small), "batch", 1)
    order.also(second_arrived, feed_rows, small_arrived)
    small = small + order(small_arrived)
    grad_rows = jnp.concatenate(
        [
            total_of(order(held[0]), *arrived)
            for held, arrived in ((first_held, first_arrived), (second_held, second_arrived))
        ],
        axis=1,
    )
    order.done((grad_rows, small))

    feed_rows = order(feed_rows)
    feed_back = [exchange(feed_rows, "batch", mask) for mask in (2, 4)]
    small_arrived = exchange(order(small), "batch", 2)
    grad_rows, grad_arrived = halve_seq(order(grad_rows), 0)
    order.also(feed_back, grad_arrived, small_arrived)
    small = small + order(small_arrived)
    grad_rows = total_of(order(grad_rows), grad_arrived)
    order.done((grad_rows, small))

    feed_back.append(exchange(order(feed_rows), "batch", 6))
    small_arrived = exchange(order(small), "batch", 4)
    grad_rows, grad_arrived = halve_seq(order(grad_rows), 1)
    order.also(feed_back, grad_arrived, small_arrived)
    grad_rows = total_of(order(grad_rows), grad_arrived)[0]
    small = small + order(small_arrived)
    feed_mine = jnp.stack([feed_rows] + order(feed_back))
    order.done((grad_rows, feed_mine, small))

    grad_back = back(order(grad_rows))
    small = order(small)
    small_arrived = exchange(small, "seq", 1)
    feed_other = exchange(order(feed_mine), "batch", 1)
    place_info = jnp.stack([core, place >> 1]).astype(jnp.int32)
    in_weight_grad, down_weight_grad = order.done(
        place_feed(
            place_info,
            order(feed_mine),
            feed_other,
            (own_rows, in_weight.shape[1]),
            (down_weight.shape[0] // owners, width),
        )
    )
    order.also(grad_back, small_arrived)
    small = small + order(small_arrived)
    grad_mine = jnp.stack([grad_rows] + order(grad_back))
    order.done((grad_mine, small))

    grad_other = exchange(order(grad_mine), "batch", 1)
    small = order(small)
    small_arrived = exchange(small, "seq", 2)
    qkv_weight_grad, out_weight_grad = place_heads(place_info, order(grad_mine), grad_other, own_rows, width)
    small = picked(small + small_arrived, me)
    few = own_rows
    many = in_bias.shape[0] // owners
    return (
        output[None],
        hidden_grad[None],
        small[many + few : many + 2 * few],
        small[many + 2 * few :],
        qkv_weight_grad,
        out_weight_grad,
        in_weight_grad,
        small[:many],
        down_weight_grad,
        small[many : many + few],
    )


def rotate(vectors, cosine_table, sine_table):
    even_part = vectors[..., 0:ROT:2]
    odd_part = vectors[..., 1:ROT:2]
    turned = jnp.stack(
        [
            even_part * cosine_table - odd_part * sine_table,
            odd_part * cosine_table + even_part * sine_table,
        ],
        axis=-1,
    )
    turned = turned.reshape(vectors.shape[:-1] + (ROT,))
    return jnp.concatenate([turned, vectors[..., ROT:]], axis=-1)


def angles(places):
    inverse = 10000.0 ** (-(jnp.arange(ROT // 2, dtype=jnp.float32) * 2.0) / ROT)
    phases = places.astype(jnp.float32)[:, None] * inverse[None, :]
    return (jnp.cos(phases), jnp.sin(phases))


def visible(query_places, key_places, end_places):
    query_after = query_places[None, :, None] > end_places[:, None, None]
    key_after = key_places[None, None, :] > end_places[:, None, None]
    return (key_places[None, None, :] <= query_places[None, :, None]) & (query_after == key_after)


def norm_rows(stream, gain_row, bias_row):
    centre = stream - jnp.mean(stream, axis=-1, keepdims=True)
    spread = jnp.mean(centre * centre, axis=-1, keepdims=True)
    return centre * lax.rsqrt(spread + EPSILON) * gain_row + bias_row


def gelu_rows(pre_active):
    return jax.nn.gelu(pre_active, approximate=True)


def plain_body(
    hidden,
    token_ids,
    offsets,
    end_places,
    token_table,
    norm_gain,
    norm_bias,
    qkv_weight,
    out_weight,
    in_weight,
    in_bias,
    down_weight,
    down_bias,
    cotangent,
):
    windows_here, shard_rows, model_width = hidden.shape
    head_count = model_width // HEAD_DIM
    seq_count = lax.axis_size("seq")
    seq_place = lax.axis_index("seq")
    home_places = seq_place * shard_rows + jnp.arange(shard_rows, dtype=jnp.int32)
    token_rows = shard_rows * windows_here
    marked = token_ids.T
    marked = jnp.where(home_places[:, None] == end_places[None, :], 2, marked)
    marked = jnp.where(home_places[:, None] == end_places[None, :] + 1, 1, marked)
    marked = jnp.where((home_places[:, None] == 0) & (offsets[None, :] == 0), 1, marked)
    onehot = (marked[..., None] == jnp.arange(token_table.shape[0], dtype=jnp.int32)).astype(
        jnp.bfloat16
    )
    embedded = jnp.einsum("swv,vd->swd", onehot, token_table, preferred_element_type=jnp.float32)
    stream_three = jnp.transpose(hidden, (1, 0, 2)).astype(jnp.float32) + embedded
    cot_three = jnp.transpose(cotangent, (1, 0, 2))
    own_high = jnp.max(home_places)
    stream_rows = stream_three.reshape(token_rows, model_width)
    normed, norm_back = jax.vjp(norm_rows, stream_rows, norm_gain, norm_bias)
    normed_low = normed.astype(jnp.bfloat16)
    projected = jnp.dot(normed_low, qkv_weight, preferred_element_type=jnp.float32)
    cosine_table, sine_table = angles(home_places)
    cosine_table = cosine_table[:, None, None, :]
    sine_table = sine_table[:, None, None, :]

    def turn_heads(projected_rows):
        divided = projected_rows.reshape(shard_rows, windows_here, 3, head_count, HEAD_DIM)
        return (
            rotate(divided[:, :, 0], cosine_table, sine_table),
            rotate(divided[:, :, 1], cosine_table, sine_table),
            divided[:, :, 2],
        )

    (queries, key_rows, values), turn_back = jax.vjp(turn_heads, projected)
    query_low = queries.astype(jnp.bfloat16)
    key_value = jnp.concatenate(
        [
            key_rows.reshape(shard_rows, windows_here, model_width),
            values.reshape(shard_rows, windows_here, model_width),
        ],
        axis=-1,
    ).astype(jnp.bfloat16)

    def split_block(key_block):
        row_count = key_block.shape[0]
        return (
            key_block[..., :model_width].reshape(row_count, windows_here, head_count, HEAD_DIM),
            key_block[..., model_width:].reshape(row_count, windows_here, head_count, HEAD_DIM),
        )

    def block_places(row_start, row_count):
        return row_start + jnp.arange(row_count, dtype=jnp.int32)

    def block_scores(key_block, key_start):
        key_part, value_part = split_block(key_block)
        key_places = block_places(key_start, key_block.shape[0])
        scores = (
            jnp.einsum("qwhd,kwhd->whqk", query_low, key_part, preferred_element_type=jnp.float32)
            * 0.125
        )
        scores = jnp.where(visible(home_places, key_places, end_places)[:, None], scores, BLOCKED)
        return (scores, key_part, value_part)

    def attend(carried, key_block, key_start):
        running, totals, accumulated = carried
        scores, key_part, value_part = block_scores(key_block, key_start)
        highest = jnp.maximum(running, jnp.max(scores, axis=-1))
        factor = jnp.exp(running - highest)
        raised = jnp.exp(scores - highest[..., None])
        totals = totals * factor + jnp.sum(raised, axis=-1)
        accumulated = accumulated * factor[..., None] + jnp.einsum(
            "whqk,kwhd->whqd",
            raised.astype(jnp.bfloat16),
            value_part,
            preferred_element_type=jnp.float32,
        )
        return (highest, totals, accumulated)

    start_state = (
        jnp.full((windows_here, head_count, shard_rows), BLOCKED, jnp.float32),
        jnp.zeros((windows_here, head_count, shard_rows), jnp.float32),
        jnp.zeros((windows_here, head_count, shard_rows, HEAD_DIM), jnp.float32),
    )
    carried = start_state
    fetched_rows = lax.all_gather(key_value, "seq", axis=0, tiled=True)
    row_count = fetched_rows.shape[0]
    blocks = fetched_rows.reshape((row_count // shard_rows, shard_rows) + fetched_rows.shape[1:])

    def visit_block(held_state, element):
        number, key_block = element
        key_start = number * shard_rows
        dead = jnp.min(block_places(key_start, shard_rows)) > own_high
        held_state = lax.cond(
            dead,
            lambda kept_state: kept_state,
            lambda kept_state: attend(kept_state, key_block, key_start),
            held_state,
        )
        return (held_state, None)

    carried, unused = lax.scan(
        visit_block, carried, (jnp.arange(blocks.shape[0], dtype=jnp.int32), blocks)
    )
    running, totals, accumulated = carried
    attention = accumulated / totals[..., None]
    log_total = running + jnp.log(totals)
    attention_rows = jnp.transpose(attention, (2, 0, 1, 3))
    mixed_low = attention_rows.reshape(token_rows, model_width).astype(jnp.bfloat16)
    attended = jnp.dot(mixed_low, out_weight, preferred_element_type=jnp.float32)
    pre_active = jnp.dot(normed_low, in_weight, preferred_element_type=jnp.float32) + in_bias
    active, gelu_back = jax.vjp(gelu_rows, pre_active)
    active_low = active.astype(jnp.bfloat16)
    result = (
        stream_rows
        + attended
        + jnp.dot(active_low, down_weight, preferred_element_type=jnp.float32)
        + down_bias
    )
    grad_rows = cot_three.reshape(token_rows, model_width)
    down_weight_grad = jnp.dot(active_low.T, grad_rows, preferred_element_type=jnp.float32)
    down_bias_grad = jnp.sum(grad_rows.astype(jnp.float32), axis=0)
    out_weight_grad = jnp.dot(mixed_low.T, grad_rows, preferred_element_type=jnp.float32)
    active_grad = jnp.dot(grad_rows, down_weight.T, preferred_element_type=jnp.float32)
    pre_grad = gelu_back(active_grad)[0].astype(jnp.bfloat16)
    in_weight_grad = jnp.dot(normed_low.T, pre_grad, preferred_element_type=jnp.float32)
    in_bias_grad = jnp.sum(pre_grad.astype(jnp.float32), axis=0)
    mixed_grad = jnp.dot(grad_rows, out_weight.T, preferred_element_type=jnp.float32).astype(
        jnp.bfloat16
    )
    grad_heads = mixed_grad.reshape(shard_rows, windows_here, head_count, HEAD_DIM)
    delta_rows = jnp.sum(grad_heads.astype(jnp.float32) * attention_rows, axis=-1)
    row_delta = jnp.transpose(delta_rows, (1, 2, 0))
    whole_keys = lax.all_gather(key_value, "seq", axis=0, tiled=True)
    blocks = whole_keys.reshape((seq_count, shard_rows) + whole_keys.shape[1:])
    zero_heads = jnp.zeros((shard_rows, windows_here, head_count, HEAD_DIM), jnp.float32)

    def back_block(query_grad, element):
        number, key_block = element
        key_start = number * shard_rows

        def live_block(held_grad):
            scores, key_part, value_part = block_scores(key_block, key_start)
            weighting = jnp.exp(scores - log_total[..., None])
            prob_grad = jnp.einsum(
                "qwhd,kwhd->whqk", grad_heads, value_part, preferred_element_type=jnp.float32
            )
            score_low = (weighting * (prob_grad - row_delta[..., None])).astype(jnp.bfloat16)
            held_grad = held_grad + 0.125 * jnp.einsum(
                "whqk,kwhd->qwhd", score_low, key_part, preferred_element_type=jnp.float32
            )
            key_grad = 0.125 * jnp.einsum(
                "whqk,qwhd->kwhd", score_low, query_low, preferred_element_type=jnp.float32
            )
            value_grad = jnp.einsum(
                "whqk,qwhd->kwhd",
                weighting.astype(jnp.bfloat16),
                grad_heads,
                preferred_element_type=jnp.float32,
            )
            return (
                held_grad,
                jnp.concatenate(
                    [
                        key_grad.reshape(shard_rows, windows_here, model_width),
                        value_grad.reshape(shard_rows, windows_here, model_width),
                    ],
                    axis=-1,
                ),
            )

        def dead_block(held_grad):
            return (held_grad, jnp.zeros((shard_rows, windows_here, 2 * model_width), jnp.float32))

        dead = jnp.min(block_places(key_start, shard_rows)) > own_high
        return lax.cond(dead, dead_block, live_block, query_grad)

    query_grad, key_terms = lax.scan(
        back_block, zero_heads, (jnp.arange(seq_count, dtype=jnp.int32), blocks)
    )
    key_terms = key_terms.reshape((seq_count * shard_rows,) + key_terms.shape[2:])
    summed = lax.psum_scatter(
        key_terms.astype(jnp.bfloat16), "seq", scatter_dimension=0, tiled=True
    ).astype(jnp.float32)
    key_grad = summed[..., :model_width].reshape(shard_rows, windows_here, head_count, HEAD_DIM)
    value_grad = summed[..., model_width:].reshape(shard_rows, windows_here, head_count, HEAD_DIM)
    joined_grad = turn_back((query_grad, key_grad, value_grad))[0].astype(jnp.bfloat16)
    qkv_weight_grad = jnp.dot(normed_low.T, joined_grad, preferred_element_type=jnp.float32)
    normed_grad = jnp.dot(joined_grad, qkv_weight.T, preferred_element_type=jnp.float32) + jnp.dot(
        pre_grad, in_weight.T, preferred_element_type=jnp.float32
    )
    stream_part, norm_gain_grad, norm_bias_grad = norm_back(normed_grad)
    stream_grad = grad_rows.astype(jnp.float32) + stream_part
    result_three = result.reshape(shard_rows, windows_here, model_width)
    grad_three = stream_grad.reshape(shard_rows, windows_here, model_width)
    output = jnp.transpose(result_three, (1, 0, 2)).astype(jnp.bfloat16)
    hidden_grad = jnp.transpose(grad_three, (1, 0, 2))
    shares = (
        lax.psum_scatter(
            norm_gain_grad.astype(jnp.bfloat16), "seq", scatter_dimension=0, tiled=True
        ).astype(jnp.float32),
        lax.psum_scatter(
            norm_bias_grad.astype(jnp.bfloat16), "seq", scatter_dimension=0, tiled=True
        ).astype(jnp.float32),
        lax.psum_scatter(
            qkv_weight_grad.astype(jnp.bfloat16), "seq", scatter_dimension=0, tiled=True
        ).astype(jnp.float32),
        lax.psum_scatter(
            out_weight_grad.astype(jnp.bfloat16), "seq", scatter_dimension=0, tiled=True
        ).astype(jnp.float32),
        lax.psum_scatter(
            in_weight_grad.astype(jnp.bfloat16), "seq", scatter_dimension=0, tiled=True
        ).astype(jnp.float32),
        lax.psum_scatter(
            in_bias_grad.astype(jnp.bfloat16), "seq", scatter_dimension=0, tiled=True
        ).astype(jnp.float32),
        lax.psum_scatter(
            down_weight_grad.astype(jnp.bfloat16), "seq", scatter_dimension=0, tiled=True
        ).astype(jnp.float32),
        lax.psum_scatter(
            down_bias_grad.astype(jnp.bfloat16), "seq", scatter_dimension=0, tiled=True
        ).astype(jnp.float32),
    )
    totals_all = (
        lax.psum(shares[0].astype(jnp.bfloat16), "batch").astype(jnp.float32),
        lax.psum(shares[1].astype(jnp.bfloat16), "batch").astype(jnp.float32),
        lax.psum(shares[2].astype(jnp.bfloat16), "batch").astype(jnp.float32),
        lax.psum(shares[3].astype(jnp.bfloat16), "batch").astype(jnp.float32),
        lax.psum(shares[4].astype(jnp.bfloat16), "batch").astype(jnp.float32),
        lax.psum(shares[5].astype(jnp.bfloat16), "batch").astype(jnp.float32),
        lax.psum(shares[6].astype(jnp.bfloat16), "batch").astype(jnp.float32),
        lax.psum(shares[7].astype(jnp.bfloat16), "batch").astype(jnp.float32),
    )
    return (
        output,
        hidden_grad,
        totals_all[0],
        totals_all[1],
        totals_all[2],
        totals_all[3],
        totals_all[4],
        totals_all[5],
        totals_all[6],
        totals_all[7],
    )


def solution(mesh):
    placed = (
        P("batch", "seq", None),
        P("batch", "seq"),
        P("batch"),
        P("batch"),
        P(),
        P(),
        P(),
        P(),
        P(),
        P(),
        P(),
        P(),
        P(),
        P("batch", "seq", None),
    )

    def body(*arrays):
        hidden = arrays[0]
        owners = mesh.shape["seq"]
        if hidden.shape[0] == 1 and hidden.shape[2] == 2 * PAIR * owners and owners == 4 and mesh.shape["batch"] == 8:
            return fast_body(*arrays)
        return plain_body(*arrays)

    return jax.shard_map(
        body,
        mesh=mesh,
        in_specs=placed,
        out_specs=(
            P("batch", "seq", None),
            P("batch", "seq", None),
            P("seq"),
            P("seq"),
            P("seq", None),
            P("seq", None),
            P("seq", None),
            P("seq"),
            P("seq", None),
            P("seq"),
        ),
        check_vma=False,
    )
```

```python
import math

import jax
import jax.numpy as jnp
import numpy as np
from jax import lax
from jax.experimental import pallas as pl
from jax.experimental.pallas import tpu as pltpu
from jax.sharding import PartitionSpec as P

HEAD_DIM = 64
ROT = 32
PAIR = 2 * HEAD_DIM

EPSILON = 1e-05
BLOCKED = -1e30
LOG2E = math.log2(math.e)
BF16 = jnp.bfloat16
F32 = jnp.float32
MIB = 1 << 20
SHORT = pl.CostEstimate(flops=1000, bytes_accessed=1000, transcendentals=0)
LONG = pl.CostEstimate(flops=10**11, bytes_accessed=1000, transcendentals=0)


def dot_nn(left, right):
    return lax.dot_general(left, right, (((1,), (0,)), ((), ())), preferred_element_type=F32)


def dot_nt(left, right):
    return lax.dot_general(left, right, (((1,), (1,)), ((), ())), preferred_element_type=F32)


def dot_tn(left, right):
    return lax.dot_general(left, right, (((0,), (0,)), ((), ())), preferred_element_type=F32)


def swap_pairs(rows):
    width = rows.shape[1]
    lanes = lax.broadcasted_iota(jnp.int32, rows.shape, 1)
    return jnp.where(lanes % 2 == 0, pltpu.roll(rows, width - 1, 1), pltpu.roll(rows, 1, 1))


def trig_tables(length):
    inverse = 10000.0 ** (-(np.arange(ROT // 2, dtype=np.float32) * np.float32(2.0)) / np.float32(ROT))
    phases = np.arange(length, dtype=np.float32)[:, None] * inverse.astype(np.float32)[None, :]
    cosine = np.ones((length, HEAD_DIM), np.float32)
    sine = np.zeros((length, HEAD_DIM), np.float32)
    cosine[:, :ROT] = np.repeat(np.cos(phases), 2, axis=1)
    sine[:, :ROT] = np.repeat(np.sin(phases), 2, axis=1) * np.tile(np.array([-1.0, 1.0], np.float32), ROT // 2)
    return np.tile(cosine, (1, 2)), np.tile(sine, (1, 2))


def whole(array):
    shape = array.shape
    return pl.BlockSpec(shape, lambda i: (0,) * len(shape))


SCALARS = pl.BlockSpec(memory_space=pltpu.SMEM)


def prep_kernel(hidden_ref, mark_ref, table_ref, gain_ref, bias_ref, stream_ref, normed_ref, turned_ref):
    rows = hidden_ref.shape[0]
    vocab = table_ref.shape[0]
    onehot = (mark_ref[...] == lax.broadcasted_iota(jnp.int32, (rows, vocab), 1)).astype(F32).astype(BF16)
    stream = hidden_ref[...].astype(F32) + dot_nn(onehot, table_ref[...])
    centre = stream - jnp.mean(stream, axis=-1, keepdims=True)
    spread = jnp.mean(centre * centre, axis=-1, keepdims=True)
    normed = centre * lax.rsqrt(spread + EPSILON) * gain_ref[...] + bias_ref[...]
    stream_ref[...] = stream
    normed_ref[...] = normed.astype(BF16)
    turned_ref[...] = normed.astype(BF16).T


def prepare(hidden, marked, table, gain, bias):
    rows, width = hidden.shape
    step = 128
    return pl.pallas_call(
        prep_kernel,
        grid=(rows // step,),
        in_specs=[
            pl.BlockSpec((step, width), lambda i: (i, 0)),
            pl.BlockSpec((step, 1), lambda i: (i, 0)),
            pl.BlockSpec(table.shape, lambda i: (0, 0)),
            pl.BlockSpec((1, width), lambda i: (0, 0)),
            pl.BlockSpec((1, width), lambda i: (0, 0)),
        ],
        out_specs=[
            pl.BlockSpec((step, width), lambda i: (i, 0)),
            pl.BlockSpec((step, width), lambda i: (i, 0)),
            pl.BlockSpec((width, step), lambda i: (0, i)),
        ],
        out_shape=[
            jax.ShapeDtypeStruct((rows, width), F32),
            jax.ShapeDtypeStruct((rows, width), BF16),
            jax.ShapeDtypeStruct((width, rows), BF16),
        ],
        cost_estimate=SHORT,
        name="prep",
    )(hidden, marked, table, gain, bias)


def heads_kernel(owners_ref, normed_ref, cot_ref, wq_ref, wk_ref, wv_ref, wo_ref, cos_ref, sin_ref, *out_refs):
    normed = normed_ref[...]
    shifts = pl.num_programs(0)
    chunks = wq_ref.shape[1] // PAIR
    cosine = jnp.concatenate([cos_ref[...]] * chunks, axis=1)
    sine = jnp.concatenate([sin_ref[...]] * chunks, axis=1)

    def turned(rows):
        return rows * cosine + swap_pairs(rows) * sine

    parts = (
        turned(dot_nn(normed, wq_ref[...])).astype(BF16),
        turned(dot_nn(normed, wk_ref[...])).astype(BF16),
        dot_nn(normed, wv_ref[...]).astype(BF16),
        dot_nt(cot_ref[...], wo_ref[...]).astype(BF16),
    )
    for number, out_ref in enumerate(out_refs):
        shift, chunk = divmod(number, chunks)

        @pl.when(pl.program_id(0) == shift)
        def _():
            for at, part in enumerate(parts):
                out_ref[:, at * PAIR : (at + 1) * PAIR] = part[:, chunk * PAIR : (chunk + 1) * PAIR]


def heads_of(order, normed, cot, qkv_weight, out_weight, cosine, sine):
    rows, width = normed.shape
    owners = order.shape[0]
    wide = width // owners
    chunks = wide // PAIR
    fixed = pl.BlockSpec((rows, width), lambda i, o: (0, 0))
    table = pl.BlockSpec((rows, PAIR), lambda i, o: (o[0], 0))

    def columns(part):
        return pl.BlockSpec((width, wide), lambda i, o: (0, part * owners + o[i]))

    blocks = pl.pallas_call(
        heads_kernel,
        grid_spec=pltpu.PrefetchScalarGridSpec(
            num_scalar_prefetch=1,
            grid=(owners,),
            in_specs=[fixed, fixed]
            + [columns(part) for part in range(3)]
            + [pl.BlockSpec((wide, width), lambda i, o: (o[i], 0)), table, table],
            out_specs=[pl.BlockSpec((rows, 4 * PAIR), lambda i, o: (0, 0))] * (owners * chunks),
        ),
        out_shape=[jax.ShapeDtypeStruct((rows, 4 * PAIR), BF16)] * (owners * chunks),
        compiler_params=pltpu.CompilerParams(vmem_limit_bytes=60 * MIB),
        cost_estimate=SHORT,
        name="heads",
    )(order, normed, cot, qkv_weight, qkv_weight, qkv_weight, out_weight, cosine, sine)
    return [[blocks[shift * chunks + chunk] for shift in range(owners)] for chunk in range(chunks)]


QUERY_ROWS = 512
KEY_ROWS = QUERY_ROWS


def attention_kernel(pieces, info_ref, *refs):
    piece_refs = refs[:pieces]
    cos_ref, sin_ref = refs[pieces : pieces + 2]
    out_refs = refs[pieces + 2 : -9]
    held, results, key_turned, value_turned, doubled, score_ref, raised_ref, key_sum, value_sum = refs[-9:]
    me, end = info_ref[0], info_ref[1]
    rows = piece_refs[0].shape[0]
    length = rows * pieces
    for shift in range(pieces):
        start = pl.multiple_of(lax.rem(me - shift + pieces, pieces) * rows, rows)
        held[pl.ds(start, rows), :] = piece_refs[shift][...]
    key_turned[...] = held[:, PAIR : 2 * PAIR].T
    value_turned[...] = held[:, 2 * PAIR : 3 * PAIR].T
    for head in range(2):
        keys = held[:, PAIR + head * HEAD_DIM : PAIR + (head + 1) * HEAD_DIM]
        doubled[head] = jnp.concatenate([keys, keys], axis=1)
    key_sum[...] = jnp.zeros_like(key_sum)
    value_sum[...] = jnp.zeros_like(value_sum)
    scale = 0.125 * LOG2E
    halves = lax.broadcasted_iota(jnp.int32, (QUERY_ROWS, PAIR), 1) // HEAD_DIM
    causal = lax.broadcasted_iota(jnp.int32, (KEY_ROWS, QUERY_ROWS), 0) <= lax.broadcasted_iota(
        jnp.int32, (KEY_ROWS, QUERY_ROWS), 1
    )
    key_steps = lax.broadcasted_iota(jnp.int32, (KEY_ROWS, QUERY_ROWS), 0)

    def query_block(number, carry):
        first = pl.multiple_of(number * QUERY_ROWS, QUERY_ROWS)
        query_rows = held[pl.ds(first, QUERY_ROWS), 0:PAIR]
        grad_rows = held[pl.ds(first, QUERY_ROWS), 3 * PAIR : 4 * PAIR]
        zero = jnp.zeros_like(query_rows)
        queries = [jnp.where(halves == head, query_rows, zero) for head in range(2)]
        scaled = query_rows.astype(F32) * scale
        large = scaled.astype(BF16)
        small = (scaled - large.astype(F32)).astype(BF16)
        pairs = [
            jnp.concatenate(
                [part[:, head * HEAD_DIM : (head + 1) * HEAD_DIM] for part in (large, small)], axis=1
            )
            for head in range(2)
        ]
        query_places = first + lax.broadcasted_iota(jnp.int32, (1, QUERY_ROWS), 1)
        lowest = jnp.where(query_places > end, end + 1, 0)

        def scores_of(block, highest, diagonal, parted):
            start = pl.multiple_of(block * KEY_ROWS, KEY_ROWS)
            after = []
            for head in range(2):
                scores = dot_nt(doubled[head, pl.ds(start, KEY_ROWS), :], pairs[head])
                if diagonal:
                    scores = jnp.where(causal, scores, BLOCKED)
                if parted:
                    scores = jnp.where(key_steps >= lowest - start, scores, BLOCKED)
                score_ref[head, pl.ds(start, KEY_ROWS), :] = scores
                after.append(jnp.maximum(highest[head], jnp.max(scores, axis=0, keepdims=True)))
            return tuple(after)

        def any_scores(block, highest, diagonal=False):
            parted = (first + QUERY_ROWS - 1 > end) & (block * KEY_ROWS <= end)
            return lax.cond(
                parted,
                lambda held_rows: scores_of(block, held_rows, diagonal, True),
                lambda held_rows: scores_of(block, held_rows, diagonal, False),
                highest,
            )

        start_row = jnp.full((1, QUERY_ROWS), BLOCKED, F32)
        highest = lax.fori_loop(0, number, any_scores, (start_row, start_row))
        highest = any_scores(number, highest, True)

        def mix(block, carried):
            start = pl.multiple_of(block * KEY_ROWS, KEY_ROWS)
            after = []
            for head in range(2):
                total, mixed = carried[head]
                raised = jnp.exp2(score_ref[head, pl.ds(start, KEY_ROWS), :] - highest[head])
                rounded = raised.astype(BF16)
                raised_ref[head, pl.ds(start, KEY_ROWS), :] = rounded
                values = value_turned[head * HEAD_DIM : (head + 1) * HEAD_DIM, pl.ds(start, KEY_ROWS)]
                after.append((total + jnp.sum(raised, axis=0, keepdims=True), mixed + dot_nn(values, rounded)))
            return tuple(after)

        empty = (jnp.zeros((1, QUERY_ROWS), F32), jnp.zeros((HEAD_DIM, QUERY_ROWS), F32))
        mixes = lax.fori_loop(0, number + 1, mix, (empty, empty))
        inverse = [1.0 / mixes[head][0] for head in range(2)]
        mixed = jnp.concatenate([mixes[head][1] * inverse[head] for head in range(2)], axis=0)
        turned = grad_rows.astype(F32).T
        turned = jnp.concatenate(
            [turned[head * HEAD_DIM : (head + 1) * HEAD_DIM] * inverse[head] for head in range(2)], axis=0
        )
        products = mixed * turned
        delta = [
            jnp.sum(products[head * HEAD_DIM : (head + 1) * HEAD_DIM], axis=0, keepdims=True) for head in range(2)
        ]
        divided = turned.T.astype(BF16)
        grads = [jnp.where(halves == head, divided, zero) for head in range(2)]

        def back(block, carried):
            start = pl.multiple_of(block * KEY_ROWS, KEY_ROWS)
            values = held[pl.ds(start, KEY_ROWS), 2 * PAIR : 3 * PAIR]
            after, key_terms, value_terms = [], [], []
            for head in range(2):
                raised = raised_ref[head, pl.ds(start, KEY_ROWS), :]
                score_grad = raised * (dot_nt(values, grads[head]) - delta[head]).astype(BF16)
                value_terms.append(dot_nn(raised, grads[head]))
                key_terms.append(dot_nn(score_grad, queries[head]))
                keys = key_turned[head * HEAD_DIM : (head + 1) * HEAD_DIM, pl.ds(start, KEY_ROWS)]
                after.append(carried[head] + dot_nn(keys, score_grad))
            value_sum[pl.ds(start, KEY_ROWS), :] += value_terms[0] + value_terms[1]
            key_sum[pl.ds(start, KEY_ROWS), :] += key_terms[0] + key_terms[1]
            return tuple(after)

        query_grads = lax.fori_loop(0, number + 1, back, (empty[1], empty[1]))
        query_grad = jnp.concatenate(query_grads, axis=0).T * 0.125
        cosine = cos_ref[pl.ds(first, QUERY_ROWS), :]
        sine = sin_ref[pl.ds(first, QUERY_ROWS), :]
        results[pl.ds(first, QUERY_ROWS), 0:PAIR] = (query_grad * cosine - swap_pairs(query_grad) * sine).astype(BF16)
        results[pl.ds(first, QUERY_ROWS), 3 * PAIR : 4 * PAIR] = mixed.T.astype(BF16)
        return carry

    lax.fori_loop(0, length // QUERY_ROWS, query_block, 0)
    key_grad = key_sum[...] * 0.125
    results[:, PAIR : 2 * PAIR] = (key_grad * cos_ref[...] - swap_pairs(key_grad) * sin_ref[...]).astype(BF16)
    results[:, 2 * PAIR : 3 * PAIR] = value_sum[...].astype(BF16)
    for shift in range(pieces):
        start = pl.multiple_of(lax.rem(me + shift, pieces) * rows, rows)
        out_refs[shift][...] = results[pl.ds(start, rows), :]


def attention(info, parts, cosine, sine):
    pieces = len(parts)
    rows = parts[0].shape[0]
    length = rows * pieces
    arrays = (*parts, cosine, sine)
    shapes = [jax.ShapeDtypeStruct((rows, 4 * PAIR), BF16)] * pieces
    return pl.pallas_call(
        lambda *refs: attention_kernel(pieces, *refs),
        grid=(1,),
        in_specs=[SCALARS] + [whole(array) for array in arrays],
        out_specs=[whole(shape) for shape in shapes],
        out_shape=shapes,
        scratch_shapes=[
            pltpu.VMEM((length, 4 * PAIR), BF16),
            pltpu.VMEM((length, 4 * PAIR), BF16),
            pltpu.VMEM((PAIR, length), BF16),
            pltpu.VMEM((PAIR, length), BF16),
            pltpu.VMEM((2, length, PAIR), BF16),
            pltpu.VMEM((2, length, QUERY_ROWS), F32),
            pltpu.VMEM((2, length, QUERY_ROWS), BF16),
            pltpu.VMEM((length, PAIR), F32),
            pltpu.VMEM((length, PAIR), F32),
        ],
        compiler_params=pltpu.CompilerParams(vmem_limit_bytes=60 * MIB),
        cost_estimate=SHORT,
        name="attention",
    )(info, *arrays)


def feed_kernel(cells_ref, normed_ref, turned_ref, cot_ref, in_ref, bias_ref, down_ref, *out_refs):
    sides = (out_refs[0:2], out_refs[2:4])
    bias_grad, out_sum, norm_sum = out_refs[4:]
    step = pl.program_id(0)
    steps = pl.num_programs(0) // 2
    up = math.sqrt(2.0 / math.pi)

    @pl.when(step == 0)
    def _():
        out_sum[...] = jnp.zeros_like(out_sum)
        norm_sum[...] = jnp.zeros_like(norm_sum)

    weights = in_ref[...]
    downs = down_ref[...]
    cot = cot_ref[...]
    pre = dot_nn(normed_ref[...], weights) + bias_ref[...]
    square = pre * pre
    tanh = jnp.tanh(up * pre * (1.0 + 0.044715 * square))
    half = 0.5 * (1.0 + tanh)
    active = (pre * half).astype(BF16)
    slope = half + 0.5 * pre * (1.0 - tanh * tanh) * (up * (1.0 + 3 * 0.044715 * square))
    pre_grad = (dot_nt(cot, downs) * slope).astype(BF16)
    in_term = dot_nn(turned_ref[...], pre_grad).astype(BF16)
    down_term = dot_tn(active, cot).astype(BF16)
    for side, (in_grad, down_grad) in enumerate(sides):

        @pl.when((step >= steps) == bool(side))
        def _():
            pieces, owners, kept, tile = in_grad.shape
            for owner in range(owners):
                for piece in range(pieces):
                    start = (owner * pieces + piece) * kept
                    in_grad[piece, owner] = in_term[start : start + kept]
            kept = tile // pieces
            for group in range(down_term.shape[1] // tile):
                for piece in range(pieces):
                    down_grad[piece, 0, group * kept : (group + 1) * kept] = down_term[
                        piece * kept : (piece + 1) * kept, group * tile : (group + 1) * tile
                    ]

    bias_grad[0] = jnp.sum(pre_grad.astype(F32), axis=0, keepdims=True)
    out_sum[...] += dot_nn(active, downs)
    norm_sum[...] += dot_nt(pre_grad, weights)


def feed_forward(cells, normed, turned, cot, in_weight, in_bias, down_weight, pieces):
    rows, width = normed.shape
    steps = cells.shape[0]
    owners = steps // 2
    hidden_units = in_weight.shape[1]
    tile = hidden_units // steps
    kept = width // owners // pieces
    tall = owners * kept
    wide = tile // pieces * (width // tile)
    fixed = pl.BlockSpec((rows, width), lambda i, c: (0, 0))

    def first(i):
        return jnp.minimum(i, owners - 1)

    def second(i):
        return jnp.maximum(i - owners, 0)

    def sides_of(turn):
        return [
            pl.BlockSpec((pieces, owners, kept, tile), lambda i, c: (0, 0, turn(i), 0)),
            pl.BlockSpec((pieces, 1, wide, tile), lambda i, c: (0, turn(i), 0, 0)),
        ]

    grads = [
        jax.ShapeDtypeStruct((pieces, owners, tall, tile), BF16),
        jax.ShapeDtypeStruct((pieces, owners, wide, tile), BF16),
    ]
    full = jax.ShapeDtypeStruct((rows, width), F32)
    results = pl.pallas_call(
        feed_kernel,
        grid_spec=pltpu.PrefetchScalarGridSpec(
            num_scalar_prefetch=1,
            grid=(steps,),
            in_specs=[
                fixed,
                pl.BlockSpec((width, rows), lambda i, c: (0, 0)),
                fixed,
                pl.BlockSpec((width, tile), lambda i, c: (0, c[i])),
                pl.BlockSpec((1, tile), lambda i, c: (0, c[i])),
                pl.BlockSpec((tile, width), lambda i, c: (c[i], 0)),
            ],
            out_specs=sides_of(first)
            + sides_of(second)
            + [pl.BlockSpec((1, 1, tile), lambda i, c: (i, 0, 0)), fixed, fixed],
        ),
        out_shape=grads + grads + [jax.ShapeDtypeStruct((steps, 1, tile), F32), full, full],
        compiler_params=pltpu.CompilerParams(vmem_limit_bytes=60 * MIB),
        cost_estimate=SHORT,
        name="feed",
    )(cells, normed, turned, cot, in_weight, in_bias, down_weight)
    return results[:2], results[2:4], *results[4:]


def place_columns(me_ref, piece_refs, held):
    owners = len(piece_refs)
    for shift in range(owners):
        owner = lax.rem(me_ref[0] - shift + owners, owners)
        start = pl.multiple_of(owner * PAIR, PAIR)
        for part in range(4):
            held[part, :, pl.ds(start, PAIR)] = piece_refs[shift][:, part * PAIR : (part + 1) * PAIR]


def weight_kernel(pieces, info_ref, turned_ref, cot_ref, *refs):
    owners = len(refs) - 4
    kept_ref, sent_ref, held, grad = refs[-4:]
    place_columns(info_ref, refs[:owners], held)
    kept = PAIR // pieces
    turned = turned_ref[...]
    for part in range(3):
        grad[...] = dot_nn(turned, held[part]).astype(BF16)
        for side, ref in enumerate((kept_ref, sent_ref)):
            core = info_ref[1] ^ side
            for owner in range(owners):
                for piece in range(pieces):
                    start = pl.multiple_of(((owner * 2 + core) * pieces + piece) * kept, kept)
                    ref[piece, owner, part * kept : (part + 1) * kept] = grad[pl.ds(start, kept), :]
    term = dot_tn(held[3], cot_ref[...]).astype(BF16)
    rows, half = term.shape[0], term.shape[1] // 2
    for core in range(2):
        grad[core * rows : (core + 1) * rows, :] = term[:, core * half : (core + 1) * half]
    for side, ref in enumerate((kept_ref, sent_ref)):
        core = info_ref[1] ^ side
        for owner in range(owners):
            for piece in range(pieces):
                start = pl.multiple_of(core * rows + (owner * pieces + piece) * kept, kept)
                ref[piece, owner, 3 * kept :] = grad[pl.ds(start, kept), :]


def weight_grads(info, turned, cot, parts, pieces):
    owners = len(parts)
    rows, width = cot.shape
    kept = PAIR // pieces
    arrays = (turned, cot, *parts)
    shape = jax.ShapeDtypeStruct((pieces, owners, 4 * kept, owners * PAIR), BF16)
    return pl.pallas_call(
        lambda *refs: weight_kernel(pieces, *refs),
        grid=(1,),
        in_specs=[SCALARS] + [whole(array) for array in arrays],
        out_specs=[whole(shape)] * 2,
        out_shape=[shape] * 2,
        scratch_shapes=[pltpu.VMEM((4, rows, owners * PAIR), BF16), pltpu.VMEM((width, owners * PAIR), BF16)],
        compiler_params=pltpu.CompilerParams(vmem_limit_bytes=60 * MIB),
        cost_estimate=SHORT,
        name="weight_grads",
    )(info, *arrays)


def sums_kernel(last, owners, me_ref, *refs):
    piece_refs, refs = refs[:owners], refs[owners:]
    weight_refs, refs = refs[: 3 * owners], refs[3 * owners :]
    out_weight_refs, refs = refs[:owners], refs[owners:]
    out_in, norm_in = refs[:2]
    held = refs[-1]
    place_columns(me_ref, piece_refs, held)
    norm = norm_in[...]
    for part in range(3):
        weights = jnp.concatenate([ref[...] for ref in weight_refs[part * owners : (part + 1) * owners]], axis=1)
        norm = norm + dot_nt(held[part], weights)
    weights = jnp.concatenate([ref[...] for ref in out_weight_refs], axis=0)
    out = out_in[...] + dot_nn(held[3], weights)
    if not last:
        out_ref, norm_ref = refs[2:4]
        out_ref[...] = out
        norm_ref[...] = norm
        return
    stream_ref, cot_ref, gain_ref, down_bias_ref, out_ref, hidden_ref, gain_grad, bias_grad = refs[2:-1]
    stream = stream_ref[...]
    cot = cot_ref[...].astype(F32)
    out_ref[...] = (stream + out + down_bias_ref[...]).astype(BF16)
    centre = stream - jnp.mean(stream, axis=-1, keepdims=True)
    spread = jnp.mean(centre * centre, axis=-1, keepdims=True)
    inverse = lax.rsqrt(spread + EPSILON)
    hat = centre * inverse
    gained = norm * gain_ref[...]
    hidden_ref[...] = cot + inverse * (
        gained
        - jnp.mean(gained, axis=-1, keepdims=True)
        - hat * jnp.mean(gained * hat, axis=-1, keepdims=True)
    )
    for out_ref, rows in ((gain_grad, norm * hat), (bias_grad, norm)):
        row = jnp.sum(rows, axis=0, keepdims=True)
        wide = out_ref.shape[1]
        for owner in range(owners):
            out_ref[owner : owner + 1, :] = row[:, owner * wide : (owner + 1) * wide]


def sums_of(info, chunk, chunks, parts, qkv_weight, out_weight, sums, final=()):
    owners = len(parts)
    rows = parts[0].shape[0]
    width = qkv_weight.shape[0]
    last = bool(final)

    def columns(part, owner):
        at = (part * owners + owner) * chunks + chunk
        return pl.BlockSpec((width, PAIR), lambda i: (0, at))

    def weight_rows(owner):
        return pl.BlockSpec((PAIR, width), lambda i: (owner * chunks + chunk, 0))

    full = jax.ShapeDtypeStruct((rows, width), F32)
    row = jax.ShapeDtypeStruct((owners, width // owners), F32)
    shapes = [jax.ShapeDtypeStruct((rows, width), BF16), full, row, row] if last else [full, full]
    return pl.pallas_call(
        lambda *refs: sums_kernel(last, owners, *refs),
        grid=(1,),
        in_specs=[SCALARS]
        + [whole(part) for part in parts]
        + [columns(part, owner) for part in range(3) for owner in range(owners)]
        + [weight_rows(owner) for owner in range(owners)]
        + [whole(array) for array in (*sums, *final)],
        out_specs=[whole(shape) for shape in shapes],
        out_shape=shapes,
        scratch_shapes=[pltpu.VMEM((4, rows, owners * PAIR), BF16)],
        compiler_params=pltpu.CompilerParams(vmem_limit_bytes=60 * MIB),
        cost_estimate=SHORT,
        name="sums",
    )(info, *parts, *([qkv_weight] * (3 * owners)), *([out_weight] * owners), *sums, *final)


def feed_place_kernel(info_ref, mine_ref, other_ref, in_ref, down_ref):
    masks, total, tile = mine_ref.shape
    kept = in_ref.shape[0] // masks
    tiles = in_ref.shape[1] // (2 * tile)
    half = down_ref.shape[0] // 2
    down_kept = half // masks
    for source, ref in enumerate((mine_ref, other_ref)):
        core = info_ref[0] ^ source
        for mask in range(masks):
            chip = info_ref[1] ^ mask
            rows = pl.ds(pl.multiple_of(chip * kept, kept), kept)
            for number in range(tiles):
                columns = pl.ds(pl.multiple_of((2 * number + core) * tile, tile), tile)
                in_ref[rows, columns] = ref[mask, number * kept : (number + 1) * kept].astype(F32)
            rows = pl.ds(pl.multiple_of(core * half + chip * down_kept, down_kept), down_kept)
            for group in range(down_ref.shape[1] // tile):
                at = tiles * kept + group * down_kept
                down_ref[rows, group * tile : (group + 1) * tile] = ref[mask, at : at + down_kept].astype(F32)


def place_feed(info, mine, other, in_shape, down_shape):
    shapes = [jax.ShapeDtypeStruct(in_shape, F32), jax.ShapeDtypeStruct(down_shape, F32)]
    return pl.pallas_call(
        feed_place_kernel,
        grid=(1,),
        in_specs=[SCALARS, whole(mine), whole(other)],
        out_specs=[whole(shape) for shape in shapes],
        out_shape=shapes,
        compiler_params=pltpu.CompilerParams(vmem_limit_bytes=60 * MIB),
        cost_estimate=SHORT,
        name="place_feed",
    )(info, mine, other)


def heads_place_kernel(info_ref, mine_ref, other_ref, qkv_ref, out_ref):
    core, place = info_ref[0], info_ref[1]
    masks, total, wide = mine_ref.shape
    own_rows, width = out_ref.shape
    kept = own_rows // 2 // masks
    chunks = total // (4 * kept)
    owners = wide // PAIR
    for source, ref in enumerate((mine_ref, other_ref)):
        at_core = core if source == 0 else 1 - core
        columns = pl.ds(pl.multiple_of(at_core * (width // 2), width // 2), width // 2)
        for mask in range(masks):
            piece = place ^ mask
            rows = pl.ds(pl.multiple_of(at_core * (own_rows // 2) + piece * kept, kept), kept)
            for chunk in range(chunks):
                at = chunk * 4 * kept
                for part in range(3):
                    block = ref[mask, at + part * kept : at + (part + 1) * kept].astype(F32)
                    for owner in range(owners):
                        column = part * width + (owner * chunks + chunk) * PAIR
                        qkv_ref[rows, column : column + PAIR] = block[:, owner * PAIR : (owner + 1) * PAIR]
                out_rows = pl.ds(pl.multiple_of(chunk * PAIR + piece * kept, kept), kept)
                out_ref[out_rows, columns] = ref[mask, at + 3 * kept : at + 4 * kept].astype(F32)


def place_heads(info, mine, other, own_rows, width):
    shapes = [jax.ShapeDtypeStruct((own_rows, 3 * width), F32), jax.ShapeDtypeStruct((own_rows, width), F32)]
    return pl.pallas_call(
        heads_place_kernel,
        grid=(1,),
        in_specs=[SCALARS] + [pl.BlockSpec(memory_space=pltpu.VMEM)] * 2,
        out_specs=[whole(shape) for shape in shapes],
        out_shape=shapes,
        compiler_params=pltpu.CompilerParams(vmem_limit_bytes=40 * MIB),
        cost_estimate=SHORT,
        name="place_heads",
    )(info, mine, other)


def exchange(rows, axis, mask):
    size = lax.axis_size(axis)
    return lax.ppermute(rows, axis, [(place, place ^ mask) for place in range(size)])


def around(rows, shift):
    owners = lax.axis_size("seq")
    return lax.ppermute(rows, "seq", [(place, (place + shift) % owners) for place in range(owners)])


def total_of(*terms):
    return sum(term.astype(F32) for term in terms).astype(BF16)


def picked(rows, index, dim=0):
    return lax.dynamic_index_in_dim(rows, index, dim, keepdims=False)


def add_kernel(places, bits_ref, *refs):
    outs = refs[len(refs) - len(places) :]
    for out_ref, terms in zip(outs, places):
        at = 0
        for left, right in terms:
            rows = refs[left].shape[-2]
            total = refs[left][...].astype(F32) + refs[right][...].astype(F32)
            out_ref[..., at : at + rows, :] = total.reshape(out_ref.shape[:-2] + total.shape[-2:]).astype(BF16)
            at += rows


def add_pieces(kept, arrived):
    pieces, owners = kept[0].shape[:2]
    arrays = [array for pair in zip(kept, arrived) for array in pair]
    rows = sum(array.shape[2] for array in kept)
    columns = kept[0].shape[3]
    return pl.pallas_call(
        lambda *refs: add_kernel([[(0, 1), (2, 3)]], None, *refs),
        grid=(pieces,),
        in_specs=[pl.BlockSpec((1,) + array.shape[1:], lambda i: (i, 0, 0, 0)) for array in arrays],
        out_specs=pl.BlockSpec((1, owners, rows, columns), lambda i: (i, 0, 0, 0)),
        out_shape=jax.ShapeDtypeStruct((pieces, owners, rows, columns), BF16),
        compiler_params=pltpu.CompilerParams(vmem_limit_bytes=60 * MIB),
        cost_estimate=SHORT,
        name="add_pieces",
    )(*arrays)


def chips_kernel(chip_ref, *refs):
    chips = (len(refs) - 1) // 2
    arrived_ref = refs[chips]
    for mask in range(chips):
        total = refs[mask][0].astype(F32) + arrived_ref[chip_ref[0] ^ mask].astype(F32)
        refs[chips + 1 + mask][...] = total.astype(BF16)


def add_for_chips(chip, kept, arrived):
    chips = kept.shape[0]
    block = (1,) + kept.shape[1:]
    out = jax.ShapeDtypeStruct(kept.shape[1:], BF16)
    return pl.pallas_call(
        chips_kernel,
        grid_spec=pltpu.PrefetchScalarGridSpec(
            num_scalar_prefetch=1,
            grid=(1,),
            in_specs=[
                pl.BlockSpec(block, lambda i, c, mask=mask: (c[0] ^ mask, 0, 0, 0)) for mask in range(chips)
            ]
            + [pl.BlockSpec(memory_space=pltpu.VMEM)],
            out_specs=[pl.BlockSpec(out.shape, lambda i, c: (0, 0, 0))] * chips,
        ),
        out_shape=[out] * chips,
        compiler_params=pltpu.CompilerParams(vmem_limit_bytes=40 * MIB),
        cost_estimate=SHORT,
        name="add_for_chips",
    )(chip[None], *([kept] * chips), arrived)


class Order:
    token = None

    def __call__(self, value):
        if self.token is None:
            return value
        return lax.optimization_barrier((value, self.token))[0]

    def done(self, token):
        self.token = token
        return token

    def also(self, *tokens):
        self.token = (self.token, tokens)


def fast_body(
    hidden,
    token_ids,
    offsets,
    end_places,
    token_table,
    norm_gain,
    norm_bias,
    qkv_weight,
    out_weight,
    in_weight,
    in_bias,
    down_weight,
    down_bias,
    cotangent,
):
    width = hidden.shape[2]
    rows = hidden.shape[1]
    owners = lax.axis_size("seq")
    pieces = lax.axis_size("batch")
    me = lax.axis_index("seq")
    core = lax.axis_index("batch") & 1
    length = rows * owners
    own_rows = width // owners
    chunks = own_rows // PAIR
    end = end_places[0]

    places = me * rows + jnp.arange(rows, dtype=jnp.int32)[:, None]
    marked = token_ids.reshape(rows, 1)
    marked = jnp.where(places == end, 2, marked)
    marked = jnp.where(places == end + 1, 1, marked)
    marked = jnp.where((places == 0) & (offsets[0] == 0), 1, marked)
    cot = cotangent.reshape(rows, width)
    stream, normed, turned = prepare(
        hidden.reshape(rows, width), marked, token_table, norm_gain[None], norm_bias[None]
    )
    cosine, sine = (jnp.asarray(table) for table in trig_tables(length))
    place = lax.axis_index("batch")
    info = jnp.stack([me, core]).astype(jnp.int32)
    spots = jnp.stack([me, end]).astype(jnp.int32)
    order = Order()

    def moved(blocks, shifts=(2, 1, 3)):
        return {shift: around(blocks[shift], shift) for shift in shifts}

    def gathered(blocks, arrived):
        return [blocks[0]] + [arrived[shift] for shift in range(1, owners)]

    def back(rows):
        return [exchange(rows, "batch", mask) for mask in (2, 4, 6)]

    shifts = lax.rem(me + jnp.arange(owners, dtype=jnp.int32), owners)
    heads = order.done(heads_of(shifts, normed, cot, qkv_weight, out_weight, cosine, sine))

    arrived = moved(order(heads[0]))
    cells = 2 * jnp.arange(owners, dtype=jnp.int32)
    cells = jnp.concatenate([cells + 1 - core, cells + core])
    away, here, in_bias_grad, out_sum, norm_sum = order.done(
        feed_forward(cells, order(normed), turned, cot, in_weight, in_bias[None], down_weight, pieces // 2)
    )
    order.also(arrived)

    feed_arrived = [exchange(array, "batch", 1) for array in order(away)]
    later = moved(order(heads[1]))
    first = order.done(attention(spots, gathered(heads[0], order(arrived)), cosine, sine))
    order.also(feed_arrived)
    feed_rows = order.done(add_pieces(order(here), feed_arrived))
    order.also(later)

    groups = [list(range(number, pieces, 2)) for number in range(2)]
    feed_rows = lax.psum_scatter(
        order(feed_rows), "batch", scatter_dimension=0, axis_index_groups=groups, tiled=False
    )
    arrived = moved(order(first))
    second = order.done(attention(spots, gathered(heads[1], order(later)), cosine, sine))
    cot_sum = order.done(jnp.sum(order(cot).astype(F32), axis=0))
    order.also(arrived)

    later = moved(order(second))
    parts = gathered(first, order(arrived))
    sums = order.done(sums_of(info, 0, chunks, order(parts), qkv_weight, out_weight, (out_sum, norm_sum)))
    first_kept, first_sent = order.done(weight_grads(info, turned, cot, order(parts), pieces // 2))
    order.also(later, feed_rows)

    feed_rows = lax.psum_scatter(order(feed_rows), "seq", scatter_dimension=0, tiled=False)
    grad_arrived = exchange(order(first_sent), "batch", 1)
    parts = gathered(second, order(later))
    second_kept, second_sent = order.done(weight_grads(info, turned, cot, parts, pieces // 2))
    order.also(grad_arrived)
    first_held = order.done(add_for_chips(place >> 1, order(first_kept), grad_arrived))

    first_arrived = [exchange(order(first_held[mask]), "batch", 2 * mask) for mask in (1, 2, 3)]
    grad_arrived = exchange(order(second_sent), "batch", 1)
    output, hidden_grad, gain_grad, bias_grad = order.done(
        sums_of(
            info, 1, chunks, order(parts), qkv_weight, out_weight, sums, (stream, cot, norm_gain[None], down_bias[None])
        )
    )
    order.also(first_arrived, grad_arrived)
    second_held = order.done(add_for_chips(place >> 1, order(second_kept), grad_arrived))

    def halve_seq(rows, number):
        bit = (me >> number) & 1
        split = rows.reshape((rows.shape[0] // 2, 2) + rows.shape[1:])
        return picked(split, bit, 1), exchange(picked(split, 1 - bit, 1), "seq", 1 << number)

    second_arrived = [exchange(order(second_held[mask]), "batch", 2 * mask) for mask in (1, 2, 3)]
    in_bias_grad = order(in_bias_grad)
    bias_low = jnp.where(core == 0, in_bias_grad[owners:], in_bias_grad[:owners])
    bias_high = jnp.where(core == 0, in_bias_grad[:owners], in_bias_grad[owners:])
    small = order.done(
        jnp.concatenate(
            [
                jnp.concatenate([bias_low, bias_high], axis=1).reshape(owners, -1),
                cot_sum.reshape(owners, -1),
                gain_grad,
                bias_grad,
            ],
            axis=1,
        )
    )
    small_arrived = exchange(order(small), "batch", 1)
    order.also(second_arrived, feed_rows, small_arrived)
    small = small + order(small_arrived)
    grad_rows = jnp.concatenate(
        [
            total_of(order(held[0]), *arrived)
            for held, arrived in ((first_held, first_arrived), (second_held, second_arrived))
        ],
        axis=1,
    )
    order.done((grad_rows, small))

    feed_rows = order(feed_rows)
    feed_back = [exchange(feed_rows, "batch", mask) for mask in (2, 4)]
    small_arrived = exchange(order(small), "batch", 2)
    grad_rows, grad_arrived = halve_seq(order(grad_rows), 0)
    order.also(feed_back, grad_arrived, small_arrived)
    small = small + order(small_arrived)
    grad_rows = total_of(order(grad_rows), grad_arrived)
    order.done((grad_rows, small))

    feed_back.append(exchange(order(feed_rows), "batch", 6))
    small_arrived = exchange(order(small), "batch", 4)
    grad_rows, grad_arrived = halve_seq(order(grad_rows), 1)
    order.also(feed_back, grad_arrived, small_arrived)
    grad_rows = total_of(order(grad_rows), grad_arrived)[0]
    small = small + order(small_arrived)
    feed_mine = jnp.stack([feed_rows] + order(feed_back))
    order.done((grad_rows, feed_mine, small))

    grad_back = back(order(grad_rows))
    small = order(small)
    small_arrived = exchange(small, "seq", 1)
    feed_other = exchange(order(feed_mine), "batch", 1)
    place_info = jnp.stack([core, place >> 1]).astype(jnp.int32)
    in_weight_grad, down_weight_grad = order.done(
        place_feed(
            place_info,
            order(feed_mine),
            feed_other,
            (own_rows, in_weight.shape[1]),
            (down_weight.shape[0] // owners, width),
        )
    )
    order.also(grad_back, small_arrived)
    small = small + order(small_arrived)
    grad_mine = jnp.stack([grad_rows] + order(grad_back))
    order.done((grad_mine, small))

    grad_other = exchange(order(grad_mine), "batch", 1)
    small = order(small)
    small_arrived = exchange(small, "seq", 2)
    qkv_weight_grad, out_weight_grad = place_heads(place_info, order(grad_mine), grad_other, own_rows, width)
    small = picked(small + small_arrived, me)
    few = own_rows
    many = in_bias.shape[0] // owners
    return (
        output[None],
        hidden_grad[None],
        small[many + few : many + 2 * few],
        small[many + 2 * few :],
        qkv_weight_grad,
        out_weight_grad,
        in_weight_grad,
        small[:many],
        down_weight_grad,
        small[many : many + few],
    )


def rotate(vectors, cosine_table, sine_table):
    even_part = vectors[..., 0:ROT:2]
    odd_part = vectors[..., 1:ROT:2]
    turned = jnp.stack(
        [
            even_part * cosine_table - odd_part * sine_table,
            odd_part * cosine_table + even_part * sine_table,
        ],
        axis=-1,
    )
    turned = turned.reshape(vectors.shape[:-1] + (ROT,))
    return jnp.concatenate([turned, vectors[..., ROT:]], axis=-1)


def angles(places):
    inverse = 10000.0 ** (-(jnp.arange(ROT // 2, dtype=jnp.float32) * 2.0) / ROT)
    phases = places.astype(jnp.float32)[:, None] * inverse[None, :]
    return (jnp.cos(phases), jnp.sin(phases))


def visible(query_places, key_places, end_places):
    query_after = query_places[None, :, None] > end_places[:, None, None]
    key_after = key_places[None, None, :] > end_places[:, None, None]
    return (key_places[None, None, :] <= query_places[None, :, None]) & (query_after == key_after)


def norm_rows(stream, gain_row, bias_row):
    centre = stream - jnp.mean(stream, axis=-1, keepdims=True)
    spread = jnp.mean(centre * centre, axis=-1, keepdims=True)
    return centre * lax.rsqrt(spread + EPSILON) * gain_row + bias_row


def gelu_rows(pre_active):
    return jax.nn.gelu(pre_active, approximate=True)


def plain_body(
    hidden,
    token_ids,
    offsets,
    end_places,
    token_table,
    norm_gain,
    norm_bias,
    qkv_weight,
    out_weight,
    in_weight,
    in_bias,
    down_weight,
    down_bias,
    cotangent,
):
    windows_here, shard_rows, model_width = hidden.shape
    head_count = model_width // HEAD_DIM
    seq_count = lax.axis_size("seq")
    seq_place = lax.axis_index("seq")
    home_places = seq_place * shard_rows + jnp.arange(shard_rows, dtype=jnp.int32)
    token_rows = shard_rows * windows_here
    marked = token_ids.T
    marked = jnp.where(home_places[:, None] == end_places[None, :], 2, marked)
    marked = jnp.where(home_places[:, None] == end_places[None, :] + 1, 1, marked)
    marked = jnp.where((home_places[:, None] == 0) & (offsets[None, :] == 0), 1, marked)
    onehot = (marked[..., None] == jnp.arange(token_table.shape[0], dtype=jnp.int32)).astype(
        jnp.bfloat16
    )
    embedded = jnp.einsum("swv,vd->swd", onehot, token_table, preferred_element_type=jnp.float32)
    stream_three = jnp.transpose(hidden, (1, 0, 2)).astype(jnp.float32) + embedded
    cot_three = jnp.transpose(cotangent, (1, 0, 2))
    own_high = jnp.max(home_places)
    stream_rows = stream_three.reshape(token_rows, model_width)
    normed, norm_back = jax.vjp(norm_rows, stream_rows, norm_gain, norm_bias)
    normed_low = normed.astype(jnp.bfloat16)
    projected = jnp.dot(normed_low, qkv_weight, preferred_element_type=jnp.float32)
    cosine_table, sine_table = angles(home_places)
    cosine_table = cosine_table[:, None, None, :]
    sine_table = sine_table[:, None, None, :]

    def turn_heads(projected_rows):
        divided = projected_rows.reshape(shard_rows, windows_here, 3, head_count, HEAD_DIM)
        return (
            rotate(divided[:, :, 0], cosine_table, sine_table),
            rotate(divided[:, :, 1], cosine_table, sine_table),
            divided[:, :, 2],
        )

    (queries, key_rows, values), turn_back = jax.vjp(turn_heads, projected)
    query_low = queries.astype(jnp.bfloat16)
    key_value = jnp.concatenate(
        [
            key_rows.reshape(shard_rows, windows_here, model_width),
            values.reshape(shard_rows, windows_here, model_width),
        ],
        axis=-1,
    ).astype(jnp.bfloat16)

    def split_block(key_block):
        row_count = key_block.shape[0]
        return (
            key_block[..., :model_width].reshape(row_count, windows_here, head_count, HEAD_DIM),
            key_block[..., model_width:].reshape(row_count, windows_here, head_count, HEAD_DIM),
        )

    def block_places(row_start, row_count):
        return row_start + jnp.arange(row_count, dtype=jnp.int32)

    def block_scores(key_block, key_start):
        key_part, value_part = split_block(key_block)
        key_places = block_places(key_start, key_block.shape[0])
        scores = (
            jnp.einsum("qwhd,kwhd->whqk", query_low, key_part, preferred_element_type=jnp.float32)
            * 0.125
        )
        scores = jnp.where(visible(home_places, key_places, end_places)[:, None], scores, BLOCKED)
        return (scores, key_part, value_part)

    def attend(carried, key_block, key_start):
        running, totals, accumulated = carried
        scores, key_part, value_part = block_scores(key_block, key_start)
        highest = jnp.maximum(running, jnp.max(scores, axis=-1))
        factor = jnp.exp(running - highest)
        raised = jnp.exp(scores - highest[..., None])
        totals = totals * factor + jnp.sum(raised, axis=-1)
        accumulated = accumulated * factor[..., None] + jnp.einsum(
            "whqk,kwhd->whqd",
            raised.astype(jnp.bfloat16),
            value_part,
            preferred_element_type=jnp.float32,
        )
        return (highest, totals, accumulated)

    start_state = (
        jnp.full((windows_here, head_count, shard_rows), BLOCKED, jnp.float32),
        jnp.zeros((windows_here, head_count, shard_rows), jnp.float32),
        jnp.zeros((windows_here, head_count, shard_rows, HEAD_DIM), jnp.float32),
    )
    carried = start_state
    fetched_rows = lax.all_gather(key_value, "seq", axis=0, tiled=True)
    row_count = fetched_rows.shape[0]
    blocks = fetched_rows.reshape((row_count // shard_rows, shard_rows) + fetched_rows.shape[1:])

    def visit_block(held_state, element):
        number, key_block = element
        key_start = number * shard_rows
        dead = jnp.min(block_places(key_start, shard_rows)) > own_high
        held_state = lax.cond(
            dead,
            lambda kept_state: kept_state,
            lambda kept_state: attend(kept_state, key_block, key_start),
            held_state,
        )
        return (held_state, None)

    carried, unused = lax.scan(
        visit_block, carried, (jnp.arange(blocks.shape[0], dtype=jnp.int32), blocks)
    )
    running, totals, accumulated = carried
    attention = accumulated / totals[..., None]
    log_total = running + jnp.log(totals)
    attention_rows = jnp.transpose(attention, (2, 0, 1, 3))
    mixed_low = attention_rows.reshape(token_rows, model_width).astype(jnp.bfloat16)
    attended = jnp.dot(mixed_low, out_weight, preferred_element_type=jnp.float32)
    pre_active = jnp.dot(normed_low, in_weight, preferred_element_type=jnp.float32) + in_bias
    active, gelu_back = jax.vjp(gelu_rows, pre_active)
    active_low = active.astype(jnp.bfloat16)
    result = (
        stream_rows
        + attended
        + jnp.dot(active_low, down_weight, preferred_element_type=jnp.float32)
        + down_bias
    )
    grad_rows = cot_three.reshape(token_rows, model_width)
    down_weight_grad = jnp.dot(active_low.T, grad_rows, preferred_element_type=jnp.float32)
    down_bias_grad = jnp.sum(grad_rows.astype(jnp.float32), axis=0)
    out_weight_grad = jnp.dot(mixed_low.T, grad_rows, preferred_element_type=jnp.float32)
    active_grad = jnp.dot(grad_rows, down_weight.T, preferred_element_type=jnp.float32)
    pre_grad = gelu_back(active_grad)[0].astype(jnp.bfloat16)
    in_weight_grad = jnp.dot(normed_low.T, pre_grad, preferred_element_type=jnp.float32)
    in_bias_grad = jnp.sum(pre_grad.astype(jnp.float32), axis=0)
    mixed_grad = jnp.dot(grad_rows, out_weight.T, preferred_element_type=jnp.float32).astype(
        jnp.bfloat16
    )
    grad_heads = mixed_grad.reshape(shard_rows, windows_here, head_count, HEAD_DIM)
    delta_rows = jnp.sum(grad_heads.astype(jnp.float32) * attention_rows, axis=-1)
    row_delta = jnp.transpose(delta_rows, (1, 2, 0))
    whole_keys = lax.all_gather(key_value, "seq", axis=0, tiled=True)
    blocks = whole_keys.reshape((seq_count, shard_rows) + whole_keys.shape[1:])
    zero_heads = jnp.zeros((shard_rows, windows_here, head_count, HEAD_DIM), jnp.float32)

    def back_block(query_grad, element):
        number, key_block = element
        key_start = number * shard_rows

        def live_block(held_grad):
            scores, key_part, value_part = block_scores(key_block, key_start)
            weighting = jnp.exp(scores - log_total[..., None])
            prob_grad = jnp.einsum(
                "qwhd,kwhd->whqk", grad_heads, value_part, preferred_element_type=jnp.float32
            )
            score_low = (weighting * (prob_grad - row_delta[..., None])).astype(jnp.bfloat16)
            held_grad = held_grad + 0.125 * jnp.einsum(
                "whqk,kwhd->qwhd", score_low, key_part, preferred_element_type=jnp.float32
            )
            key_grad = 0.125 * jnp.einsum(
                "whqk,qwhd->kwhd", score_low, query_low, preferred_element_type=jnp.float32
            )
            value_grad = jnp.einsum(
                "whqk,qwhd->kwhd",
                weighting.astype(jnp.bfloat16),
                grad_heads,
                preferred_element_type=jnp.float32,
            )
            return (
                held_grad,
                jnp.concatenate(
                    [
                        key_grad.reshape(shard_rows, windows_here, model_width),
                        value_grad.reshape(shard_rows, windows_here, model_width),
                    ],
                    axis=-1,
                ),
            )

        def dead_block(held_grad):
            return (held_grad, jnp.zeros((shard_rows, windows_here, 2 * model_width), jnp.float32))

        dead = jnp.min(block_places(key_start, shard_rows)) > own_high
        return lax.cond(dead, dead_block, live_block, query_grad)

    query_grad, key_terms = lax.scan(
        back_block, zero_heads, (jnp.arange(seq_count, dtype=jnp.int32), blocks)
    )
    key_terms = key_terms.reshape((seq_count * shard_rows,) + key_terms.shape[2:])
    summed = lax.psum_scatter(
        key_terms.astype(jnp.bfloat16), "seq", scatter_dimension=0, tiled=True
    ).astype(jnp.float32)
    key_grad = summed[..., :model_width].reshape(shard_rows, windows_here, head_count, HEAD_DIM)
    value_grad = summed[..., model_width:].reshape(shard_rows, windows_here, head_count, HEAD_DIM)
    joined_grad = turn_back((query_grad, key_grad, value_grad))[0].astype(jnp.bfloat16)
    qkv_weight_grad = jnp.dot(normed_low.T, joined_grad, preferred_element_type=jnp.float32)
    normed_grad = jnp.dot(joined_grad, qkv_weight.T, preferred_element_type=jnp.float32) + jnp.dot(
        pre_grad, in_weight.T, preferred_element_type=jnp.float32
    )
    stream_part, norm_gain_grad, norm_bias_grad = norm_back(normed_grad)
    stream_grad = grad_rows.astype(jnp.float32) + stream_part
    result_three = result.reshape(shard_rows, windows_here, model_width)
    grad_three = stream_grad.reshape(shard_rows, windows_here, model_width)
    output = jnp.transpose(result_three, (1, 0, 2)).astype(jnp.bfloat16)
    hidden_grad = jnp.transpose(grad_three, (1, 0, 2))
    shares = (
        lax.psum_scatter(
            norm_gain_grad.astype(jnp.bfloat16), "seq", scatter_dimension=0, tiled=True
        ).astype(jnp.float32),
        lax.psum_scatter(
            norm_bias_grad.astype(jnp.bfloat16), "seq", scatter_dimension=0, tiled=True
        ).astype(jnp.float32),
        lax.psum_scatter(
            qkv_weight_grad.astype(jnp.bfloat16), "seq", scatter_dimension=0, tiled=True
        ).astype(jnp.float32),
        lax.psum_scatter(
            out_weight_grad.astype(jnp.bfloat16), "seq", scatter_dimension=0, tiled=True
        ).astype(jnp.float32),
        lax.psum_scatter(
            in_weight_grad.astype(jnp.bfloat16), "seq", scatter_dimension=0, tiled=True
        ).astype(jnp.float32),
        lax.psum_scatter(
            in_bias_grad.astype(jnp.bfloat16), "seq", scatter_dimension=0, tiled=True
        ).astype(jnp.float32),
        lax.psum_scatter(
            down_weight_grad.astype(jnp.bfloat16), "seq", scatter_dimension=0, tiled=True
        ).astype(jnp.float32),
        lax.psum_scatter(
            down_bias_grad.astype(jnp.bfloat16), "seq", scatter_dimension=0, tiled=True
        ).astype(jnp.float32),
    )
    totals_all = (
        lax.psum(shares[0].astype(jnp.bfloat16), "batch").astype(jnp.float32),
        lax.psum(shares[1].astype(jnp.bfloat16), "batch").astype(jnp.float32),
        lax.psum(shares[2].astype(jnp.bfloat16), "batch").astype(jnp.float32),
        lax.psum(shares[3].astype(jnp.bfloat16), "batch").astype(jnp.float32),
        lax.psum(shares[4].astype(jnp.bfloat16), "batch").astype(jnp.float32),
        lax.psum(shares[5].astype(jnp.bfloat16), "batch").astype(jnp.float32),
        lax.psum(shares[6].astype(jnp.bfloat16), "batch").astype(jnp.float32),
        lax.psum(shares[7].astype(jnp.bfloat16), "batch").astype(jnp.float32),
    )
    return (
        output,
        hidden_grad,
        totals_all[0],
        totals_all[1],
        totals_all[2],
        totals_all[3],
        totals_all[4],
        totals_all[5],
        totals_all[6],
        totals_all[7],
    )


def solution(mesh):
    placed = (
        P("batch", "seq", None),
        P("batch", "seq"),
        P("batch"),
        P("batch"),
        P(),
        P(),
        P(),
        P(),
        P(),
        P(),
        P(),
        P(),
        P(),
        P("batch", "seq", None),
    )

    def body(*arrays):
        hidden = arrays[0]
        owners = mesh.shape["seq"]
        if hidden.shape[0] == 1 and hidden.shape[2] == 2 * PAIR * owners and owners == 4 and mesh.shape["batch"] == 8:
            return fast_body(*arrays)
        return plain_body(*arrays)

    return jax.shard_map(
        body,
        mesh=mesh,
        in_specs=placed,
        out_specs=(
            P("batch", "seq", None),
            P("batch", "seq", None),
            P("seq"),
            P("seq"),
            P("seq", None),
            P("seq", None),
            P("seq", None),
            P("seq"),
            P("seq", None),
            P("seq"),
        ),
        check_vma=False,
    )
```
